128 devices in a mesh: dp: 8 (over y, core), expert: 16 (over z, x).
Axes of the slice: x: 4, y: 4, z: 4, core: 2. Of those that a mesh axis runs over, the one named last changes fastest.
Arguments:
- tokens: bfloat16 [2, 16, 1024, 1024], P(None, 'expert', 'dp'), may hold values from -6 to 6
- cotangent: bfloat16 [2, 16, 1024, 1024], P(None, 'expert', 'dp'), may hold values from -6 to 6
- segments: int32 [2, 16, 1024], P(None, 'expert'), may hold values from 0 to 4, as said below
- routes: int32 [2, 16, 1024, 8], P(None, 'expert', 'dp'), may hold values from 0 to 31, all different within a row; in each aligned block of 128 rows (0 to 127, 128 to 255, ..., all dimensions but the last counted through in order) at most 48 rows name the same one
- w_qkv: bfloat16 [1024, 2048], P('dp'), may hold values from -0.1875 to 0.1875
- w_out: bfloat16 [1024, 1024], P('dp'), may hold values from -0.75 to 0.75
- attn_norm: bfloat16 [1024], P('dp'), may hold values from 0.099609375 to 1.8984375
- ffn_norm: bfloat16 [1024], P('dp'), may hold values from 0.099609375 to 1.8984375
- q_gain: bfloat16 [64], P('dp'), may hold values from 0.099609375 to 1.8984375
- k_gain: bfloat16 [64], P('dp'), may hold values from 0.099609375 to 1.8984375
- router: bfloat16 [1024, 32], P('dp'), may hold values from -0.09375 to 0.09375
- w_gate_up: bfloat16 [32, 1024, 1024], P('expert'), may hold values from -0.1875 to 0.1875
- w_down: bfloat16 [32, 512, 1024], P('expert'), may hold values from -1 to 1
Outputs:
- output: bfloat16 [2, 16, 1024, 1024], P(None, 'expert', 'dp')
- input_grad: bfloat16 [2, 16, 1024, 1024], P(None, 'expert', 'dp')
- grad_qkv: float32 [1024, 2048], P('dp')
- grad_out: float32 [1024, 1024], P('dp')
- grad_attn_norm: float32 [1024], P('dp')
- grad_ffn_norm: float32 [1024], P('dp')
- grad_q_gain: float32 [64], P('dp')
- grad_k_gain: float32 [64], P('dp')
- grad_router: float32 [1024, 32], P('dp')
- grad_gate_up: float32 [32, 1024, 1024], P('expert')
- grad_down: float32 [32, 512, 1024], P('expert')
The draws below stay inside these ranges and needn't reach their ends.
Inputs may be any that keep to these rules, and one draw needn't show every extreme that they name: `segments`: segment numbers never fall along a sequence; equal numbers mark one document. `routes`: the 8 experts of a token differ. Within each aligned block of 128 positions of one sequence in one micro-batch no expert is named more than 48 times, a bound that some block reaches.
All inputs are finite; a program needn't handle non-finite values.
Results may differ from the reference program's by a relative error of at most 0.025.
Values may be sent and summed in bfloat16 or wider, within the bound.
A program may use at most 256 MiB of HBM per device.

```python
import math
import jax
import jax.numpy as jnp
import numpy as np
from jax import lax

D = 1024
HEADS = 16
KV_HEADS = 8
HD = 64
F = 512
TOPK = 8
LEN = 1024
MB = 2
E = 32
SEQS = 16
TQ = 128
CAP = 48
QW = 1024
QKV = 2048
N_DP = 8


def draw_segments(key, part):
    key = jax.random.fold_in(key, 11)
    rows_own = LEN // N_DP
    cut_key, front_key, tail_key, pick_key = jax.random.split(key, 4)
    spread_cuts = jax.random.randint(cut_key, (MB, SEQS, 4), 1, LEN)
    front_cuts = jax.random.randint(front_key, (MB, SEQS, 2), 1, rows_own)
    tail_cuts = jax.random.randint(tail_key, (MB, SEQS, 2), LEN - rows_own + 1, LEN)
    picked = jax.random.randint(pick_key, (SEQS,), 0, MB)
    spanning = (jnp.arange(MB)[:, None] == picked[None, :])[:, :, None]
    edges = jnp.where(spanning, jnp.concatenate([front_cuts, tail_cuts], axis=-1), spread_cuts)
    position = jnp.arange(LEN)
    return jnp.sum((edges[:, :, None, :] <= position[None, None, :, None]).astype(jnp.int32), axis=-1)


def block_scale(key, dims, shards, smallest, largest):
    factor_of = 1.0
    for dim, shards_of in shards:
        draws = jax.random.uniform(jax.random.fold_in(jax.random.fold_in(key, 6), dim), (shards_of,), jnp.float32, smallest / len(shards), largest / len(shards))
        factor_of = factor_of * jnp.repeat(jnp.exp(draws), dims[dim] // shards_of).reshape((-1,) + (1,) * (len(dims) - 1 - dim))
    return factor_of


def assign_block(own_key, own, number, rows, amount, top, reach, skew):
    ranking = jax.random.permutation(own_key, amount)
    heavy_load, usual = load_shares(amount, rows * top, reach, skew, True), load_shares(amount, rows * top, reach, skew, False)
    places = jnp.arange(amount)

    def named(lengths, offset_by):
        used = int((lengths > 0).sum())
        fixed = max(1, used // 4)
        moved = fixed + (places - fixed + offset_by * (used - fixed)) % max(1, amount - fixed)
        return jnp.zeros((amount,), jnp.int32).at[ranking[jnp.where(places < fixed, places, moved)]].set(jnp.asarray(lengths, jnp.int32))

    lengths = jnp.where(number % 4 == 0, named(heavy_load, number // 4), named(usual, number - number // 4 - 1))
    mixed = jax.random.permutation(jax.random.fold_in(own, 3), amount)
    source_of, taker = mixed[0:amount // 2 * 2:2], mixed[1:amount // 2 * 2:2]
    margin = jnp.minimum(lengths[source_of] - 1, reach - lengths[taker]) // 2
    margin = jnp.where((source_of == ranking[0]) | (taker == ranking[0]) | (lengths[taker] == 0), 0, jnp.maximum(margin, 0))
    moved = jax.random.randint(jax.random.fold_in(own, 4), (amount // 2,), 0, 1 << 20) % (margin + 1)
    lengths = lengths.at[source_of].add(-moved).at[taker].add(moved)
    labels = jnp.searchsorted(jnp.cumsum(lengths), jnp.arange(rows * top), side="right").astype(jnp.int32)
    grid = labels.reshape(top, rows).T
    grid = grid[jax.random.permutation(jax.random.fold_in(own, 1), rows)]
    offset_by = jax.random.randint(jax.random.fold_in(own, 2), (rows, 1), 0, top)
    return jnp.take_along_axis(grid, (jnp.arange(top)[None, :] + offset_by) % top, axis=1)


def load_shares(number_of, total, most, lean, full):
    weights = [(1 << 20) // math.isqrt(grade ** lean) + 1 for grade in range(1, number_of + 1)]
    largest = most if full else min(most, max(-(-total // number_of), total * weights[0] // sum(weights)))
    least = 1 if total - largest >= number_of - 1 else 0
    holding, surplus = [largest] + [least] * (number_of - 1), total - largest - least * (number_of - 1)
    while surplus > 0:
        free = [i for i in range(1, number_of) if holding[i] < largest] or [i for i in range(1, number_of) if holding[i] < most]
        pool, budget = sum([weights[i] for i in free]), surplus
        for i in free:
            extra = min(most - holding[i], max(1, budget * weights[i] // pool), surplus)
            holding[i] = holding[i] + extra
            surplus = surplus - extra
    return np.array(holding)


def normal_values(own_key, shape, deviation, limit, shards=(), held_as=jnp.bfloat16):
    array = jax.random.normal(own_key, shape, jnp.float32) * deviation
    if len(shards) > 0:
        array = block_scale(own_key, shape, shards, -0.22, 0.18) * array
    return jnp.clip(array, min=-limit, max=limit).astype(held_as)


def setup_inputs(seed: int = 0) -> dict:
    splits = jax.random.split(jax.random.key(seed), 14)
    tokens = normal_values(splits[0], (MB, SEQS, LEN, D), 1.0, 6.0, ((1, 16), (2, 8)))
    cotangent = normal_values(splits[1], (MB, SEQS, LEN, D), 1.0, 6.0, ((1, 16), (2, 8)))
    segments = draw_segments(jax.random.fold_in(splits[13], 71), 0)
    routes_keys = jax.random.split(jax.random.fold_in(splits[3], 1), MB * SEQS * LEN // TQ)
    routes_turns = jax.random.permutation(jax.random.fold_in(splits[3], 3), MB * SEQS * LEN // TQ)
    routes = jax.vmap(lambda own, number: assign_block(jax.random.fold_in(splits[3], 2), own, number, TQ, E, TOPK, CAP, 2))(routes_keys, routes_turns).reshape((MB, SEQS, LEN, TOPK))
    w_qkv = normal_values(splits[4], (D, QKV), D ** -0.5, 0.1875, ((0, 8),))
    w_out = normal_values(splits[5], (QW, D), (QW // 16) ** -0.5, 0.75, ((0, 8),))
    attn_norm = jnp.clip(1.0 + 0.18 * jax.random.normal(splits[6], (D,), jnp.float32), 0.099609375, 1.8984375).astype(jnp.bfloat16)
    ffn_norm = jnp.clip(1.0 + 0.18 * jax.random.normal(splits[7], (D,), jnp.float32), 0.099609375, 1.8984375).astype(jnp.bfloat16)
    q_gain = jnp.clip(1.0 + 0.18 * jax.random.normal(splits[8], (HD,), jnp.float32), 0.099609375, 1.8984375).astype(jnp.bfloat16)
    k_gain = jnp.clip(1.0 + 0.18 * jax.random.normal(splits[9], (HD,), jnp.float32), 0.099609375, 1.8984375).astype(jnp.bfloat16)
    router = normal_values(splits[10], (D, E), (4 * D) ** -0.5, 0.09375, ((0, 8),))
    w_gate_up = normal_values(splits[11], (E, D, 2 * F), D ** -0.5, 0.1875, ((0, 16),))
    w_down = normal_values(splits[12], (E, F, D), (F // 16) ** -0.5, 1.0, ((0, 16),))
    return dict(tokens=tokens, cotangent=cotangent, segments=segments, routes=routes, w_qkv=w_qkv, w_out=w_out, attn_norm=attn_norm, ffn_norm=ffn_norm, q_gain=q_gain, k_gain=k_gain, router=router, w_gate_up=w_gate_up, w_down=w_down)


EPSILON = 1e-06
THETA = 10000.0
MASKED = -1e+30
HIGHEST = lax.Precision.HIGHEST

@jax.custom_vjp
def low(v):
    return lax.optimization_barrier(v.astype(jnp.bfloat16)).astype(jnp.float32)

@jax.custom_vjp
def low_back(v):
    return v

def low_keep(v):
    return (low(v), None)

def low_pass(kept, grad):
    return (grad,)

def back_keep(v):
    return (v, None)

def back_low(kept, grad):
    return (low(grad),)
low.defvjp(low_keep, low_pass)
low_back.defvjp(back_keep, back_low)

def hi_dot(left_mat, right_mat):
    return jnp.dot(left_mat, right_mat, precision=HIGHEST)

def rms_norm(values_in, gain_vec):
    inverse = lax.rsqrt(lax.optimization_barrier(jnp.mean(values_in * values_in, axis=-1, keepdims=True)) + EPSILON)
    return values_in * inverse * gain_vec

def rotary(values_in, cosine, sine_vals):
    half_size = values_in.shape[-1] // 2
    front_half = values_in[..., :half_size]
    back_half = values_in[..., half_size:]
    return jnp.concatenate([front_half * cosine - back_half * sine_vals, back_half * cosine + front_half * sine_vals], axis=-1)

def angles(positions):
    frequency = jnp.power(THETA, -2.0 * jnp.arange(HD // 2, dtype=jnp.float32) / HD)
    turned = positions[:, None] * frequency[None, :]
    return (jnp.cos(turned)[:, None, :], jnp.sin(turned)[:, None, :])

def sequence_forward(states, params, segment_ids, route_ids, row_lists):
    w_qkv, w_out, attn_norm, ffn_norm, q_gain, k_gain, router, w_gate_up, w_down = params
    length = states.shape[0]
    q_width = HEADS * HD
    kv_width = KV_HEADS * HD
    normed = low(rms_norm(states, attn_norm))
    projected = low_back(hi_dot(normed, w_qkv))
    cosine, sine_vals = angles(jnp.arange(length).astype(jnp.float32))
    query_vecs = projected[:, :q_width].reshape(length, HEADS, HD)
    key_vecs = projected[:, q_width:q_width + kv_width].reshape(length, KV_HEADS, HD)
    value_vecs = projected[:, q_width + kv_width:].reshape(length, KV_HEADS, HD)
    query_vecs = low(rotary(rms_norm(query_vecs, q_gain), cosine, sine_vals))
    key_vecs = low(rotary(rms_norm(key_vecs, k_gain), cosine, sine_vals))
    value_vecs = low(value_vecs)
    grouped = query_vecs.reshape(length, KV_HEADS, HEADS // KV_HEADS, HD)
    scores = low_back(jnp.einsum('qgrd,kgd->grqk', grouped, key_vecs, precision=HIGHEST) * HD ** (-0.5))
    same_doc = segment_ids[:, None] == segment_ids[None, :]
    scores = jnp.where(same_doc[None, None], scores, MASKED)
    row_max = lax.optimization_barrier(jnp.max(scores, axis=-1, keepdims=True))
    exp_scores = jnp.exp(scores - row_max)
    attn_probs = low(exp_scores / lax.optimization_barrier(jnp.sum(exp_scores, axis=-1, keepdims=True)))
    attn_mixed = jnp.einsum('grqk,kgd->qgrd', attn_probs, value_vecs, precision=HIGHEST).reshape(length, q_width)
    attn_mixed = low_back(low(attn_mixed))
    residual = states + low_back(hi_dot(attn_mixed, w_out))
    ffn_in = low(rms_norm(residual, ffn_norm))
    logits = hi_dot(ffn_in, router)
    chosen = jnp.take_along_axis(logits, route_ids, axis=1)
    gate_vals = jax.nn.softmax(chosen, axis=-1)
    copies = low_back(jnp.broadcast_to(ffn_in[:, None, :], (length, TOPK, D))).reshape(length * TOPK, D)
    padded = jnp.concatenate([copies, jnp.zeros((1, D), copies.dtype)], axis=0)

    def expert_apply(expert_item):
        row_ids, gate_up, down_mat = expert_item
        gathered = padded[row_ids]
        gate_up_out = low_back(hi_dot(gathered, gate_up))
        active = low(jax.nn.silu(gate_up_out[:, :F]) * gate_up_out[:, F:])
        return hi_dot(active, down_mat)
    results = lax.map(jax.checkpoint(expert_apply), (row_lists, w_gate_up, w_down))
    placed = jnp.zeros((length * TOPK + 1, D), results.dtype).at[row_lists.reshape(-1)].set(results.reshape(-1, D))
    returned = low_back(low(placed[:length * TOPK])).reshape(length, TOPK, D)
    return residual + lax.optimization_barrier(jnp.sum(gate_vals[:, :, None] * returned, axis=1))

def expert_lists(route_ids):
    flat_ids = route_ids.reshape(-1)

    def one_list(expert_id):
        return jnp.nonzero(flat_ids == expert_id, size=N_DP * CAP, fill_value=LEN * TOPK)[0].astype(jnp.int32)
    return jax.vmap(one_list)(jnp.arange(E, dtype=jnp.int32))

def reference(tokens, cotangent, segments, routes, w_qkv, w_out, attn_norm, ffn_norm, q_gain, k_gain, router, w_gate_up, w_down):
    params = tuple((weight.astype(jnp.float32) for weight in (w_qkv, w_out, attn_norm, ffn_norm, q_gain, k_gain, router, w_gate_up, w_down)))
    sequence_count = MB * SEQS
    inputs = (tokens.reshape(sequence_count, LEN, D), cotangent.reshape(sequence_count, LEN, D), segments.reshape(sequence_count, LEN), routes.reshape(sequence_count, LEN, TOPK))

    def accumulate(running_sum, sequence):
        states, grad_in, segment_ids, route_ids = sequence
        row_lists = expert_lists(route_ids)

        def forward(state_in, param_in):
            return sequence_forward(state_in, param_in, segment_ids, route_ids, row_lists)
        result, pullback = jax.vjp(forward, states.astype(jnp.float32), params)
        grad_states, grad_params = pullback(grad_in.astype(jnp.float32))
        running_sum = jax.tree.map(lambda running, fresh: running + fresh, running_sum, grad_params)
        return (running_sum, (result.astype(jnp.bfloat16), grad_states.astype(jnp.bfloat16)))
    zero_grads = jax.tree.map(jnp.zeros_like, params)
    totals, (results, input_grads) = lax.scan(accumulate, zero_grads, inputs)
    return (results.reshape(MB, SEQS, LEN, D), input_grads.reshape(MB, SEQS, LEN, D), totals[0], totals[1], totals[2], totals[3], totals[4], totals[5], totals[6], totals[7], totals[8])
```

```python
import jax
import jax.numpy as jnp
from jax import lax
from jax.experimental import pallas as pl
from jax.experimental.pallas import tpu as pltpu
from jax.sharding import PartitionSpec as P

HD = 64


EPSILON = 1e-06
THETA = 10000.0
MASKED = -1e30
HIGHEST = lax.Precision.HIGHEST


def in_one_piece(arrays, axis, dim, along):
    columns = [a.reshape(*a.shape[:along], -1) for a in arrays]
    both = jnp.concatenate(columns, axis=along)
    filled, at, done = (lax.all_gather(both, axis, axis=dim, tiled=True), 0, [])
    for a, column in zip(arrays, columns):
        section = filled[..., at : at + column.shape[along]]
        done.append(section.reshape(*section.shape[:along], *a.shape[along:]))
        at += column.shape[along]
    return tuple(done)


def sent_together(arrays, axis, dim, along):
    both = jnp.concatenate(arrays, axis=along)
    filled, at, done = (lax.all_gather(both, axis, axis=dim, tiled=True), 0, [])
    for a in arrays:
        done.append(lax.slice_in_dim(filled, at, at + a.shape[along], axis=along))
        at += a.shape[along]
    return tuple(done)


def in_one_piece_2(arrays, axis, dim, along):
    widths = [a.shape[along] for a in arrays]
    both = jnp.concatenate(arrays, axis=along)
    filled = lax.psum_scatter(both, axis, scatter_dimension=dim, tiled=True)
    return tuple(jnp.split(filled, [sum(widths[:k]) for k in range(1, len(widths))], axis=along))


def in_one_piece_3(arrays, axis, dim, along):
    columns = [a.reshape(*a.shape[:along], -1) for a in arrays]
    both = jnp.concatenate(columns, axis=along)
    filled, at, done = (lax.psum_scatter(both, axis, scatter_dimension=dim, tiled=True), 0, [])
    for a, column in zip(arrays, columns):
        section = filled[..., at : at + column.shape[along]]
        done.append(section.reshape(*section.shape[:along], *a.shape[along:]))
        at += column.shape[along]
    return tuple(done)


def together(arrays, axis):
    vector, at, done = (jnp.concatenate([a.reshape(-1) for a in arrays]), 0, [])
    subtotal = lax.psum(vector, axis)
    for a in arrays:
        done.append(subtotal[at : at + a.size].reshape(a.shape))
        at += a.size
    return tuple(done)


def norm_rows(values_in, gain_vec):
    inverse = lax.rsqrt(jnp.mean(values_in * values_in, axis=-1, keepdims=True) + EPSILON)
    return (values_in * inverse * gain_vec, inverse)


def norm_back(grad_in, values_in, inverse, gain_vec):
    scaled = grad_in * gain_vec
    moment = jnp.mean(scaled * values_in, axis=-1, keepdims=True)
    grad_values = inverse * (scaled - values_in * inverse * inverse * moment)
    grad_gain = grad_in * values_in * inverse
    return (grad_values, jnp.sum(grad_gain.reshape(-1, grad_gain.shape[-1]), axis=0))


def rotary(values_in, cosine, sine_vals):
    half_size = values_in.shape[-1] // 2
    front_half = values_in[..., :half_size]
    back_half = values_in[..., half_size:]
    return jnp.concatenate(
        [front_half * cosine - back_half * sine_vals, back_half * cosine + front_half * sine_vals],
        axis=-1,
    )


def angles(positions):
    frequency = jnp.power(THETA, -2.0 * jnp.arange(HD // 2, dtype=jnp.float32) / HD)
    turned = positions[:, None] * frequency[None, :]
    return (jnp.cos(turned)[:, None, :], jnp.sin(turned)[:, None, :])


BF = jnp.bfloat16
F32 = jnp.float32
SLOTS = 48
CHUNK = 256


def nn(a, b):
    return lax.dot_general(a, b, (((1,), (0,)), ((), ())), preferred_element_type=F32)


def nt(a, b):
    return lax.dot_general(a, b, (((1,), (1,)), ((), ())), preferred_element_type=F32)


def tn(a, b):
    return lax.dot_general(a, b, (((0,), (0,)), ((), ())), preferred_element_type=F32)


class Plane:
    def __init__(self):
        self.me = lax.axis_index("expert")
        self.z = self.me // 4
        self.x = self.me % 4

    def own(self, half):
        return (self.x, self.z) if half == 0 else (self.z, self.x)

    def device(self, half, p, q):
        return {"expert": q * 4 + p if half == 0 else p * 4 + q}

    def barrier(self):
        sem = pltpu.get_barrier_semaphore()
        for step in range(1, 16):
            pl.semaphore_signal(sem, inc=1, device_id={"expert": (self.me + step) % 16})
        pl.semaphore_wait(sem, 15)


def at(ref, half, p, q, rows):
    return ref.at[q, p, rows] if half == 0 else ref.at[p, q, rows]


def line(ref, half, q, rows):
    return ref.at[q, :, rows] if half == 0 else ref.at[:, q, rows]


def next_to(p):
    return (p + 1) % 4, (p + 3) % 4, (p + 2) % 4


def full_rows(half):
    return pl.ds(64 * half, 64)


def part_rows(half, part):
    return pl.ds(64 * half + 32 * part, 32)


class Gather:
    def __init__(self, plane, ref, send, recv):
        self.plane, self.ref, self.send, self.recv = plane, ref, send, recv

    def message(self, half, i):
        p, q = self.plane.own(half)
        pn, pp, _ = next_to(p)
        qn, qp, _ = next_to(q)
        ref, full = self.ref, full_rows(half)
        first, second = part_rows(half, 0), part_rows(half, 1)
        view, to = [
            lambda: (at(ref, half, p, q, full), (pn, q)),
            lambda: (at(ref, half, p, q, full), (pp, q)),
            lambda: (at(ref, half, pp, q, first), (pn, q)),
            lambda: (at(ref, half, pn, q, second), (pp, q)),
            lambda: (line(ref, half, q, full), (p, qn)),
            lambda: (line(ref, half, q, full), (p, qp)),
            lambda: (line(ref, half, qp, first), (p, qn)),
            lambda: (line(ref, half, qn, second), (p, qp)),
        ][i]()
        return pltpu.make_async_remote_copy(
            src_ref=view,
            dst_ref=view,
            send_sem=self.send.at[half, i],
            recv_sem=self.recv.at[half, i],
            device_id=self.plane.device(half, *to),
        )

    def step(self, n):
        waits, starts = [
            ((), (0, 1)),
            ((0, 1), (2, 3)),
            ((2, 3), (4, 5)),
            ((4, 5), (6, 7)),
            ((6, 7), ()),
        ][n]
        for half in range(2):
            for i in waits:
                self.message(half, i).wait_recv()
            for i in starts:
                self.message(half, i).start()
        if n == 4:
            for half in range(2):
                for i in range(8):
                    self.message(half, i).wait_send()


class Scatter:
    def __init__(self, plane, ref, r1, r2, r3, r4, send, recv, free, out):
        self.plane, self.ref, self.out = plane, ref, out
        self.r1, self.r2, self.r3, self.r4 = r1, r2, r3, r4
        self.send, self.recv, self.free = send, recv, free

    def message(self, half, i):
        p, q = self.plane.own(half)
        pn, pp, po = next_to(p)
        qn, qp, qo = next_to(q)
        ref, full = self.ref, full_rows(half)
        first, second = part_rows(half, 0), part_rows(half, 1)
        view, slot, to = [
            lambda: (line(ref, half, qo, first), self.r1.at[half, 0], (p, qn)),
            lambda: (line(ref, half, qo, second), self.r1.at[half, 1], (p, qp)),
            lambda: (line(ref, half, qn, full), self.r2.at[half, 0], (p, qn)),
            lambda: (line(ref, half, qp, full), self.r2.at[half, 1], (p, qp)),
            lambda: (at(ref, half, po, q, first), self.r3.at[half, 0], (pn, q)),
            lambda: (at(ref, half, po, q, second), self.r3.at[half, 1], (pp, q)),
            lambda: (at(ref, half, pn, q, full), self.r4.at[half, 0], (pn, q)),
            lambda: (at(ref, half, pp, q, full), self.r4.at[half, 1], (pp, q)),
        ][i]()
        return pltpu.make_async_remote_copy(
            src_ref=view,
            dst_ref=slot,
            send_sem=self.send.at[half, i],
            recv_sem=self.recv.at[half, i],
            device_id=self.plane.device(half, *to),
        )

    def add_line(self, half, q, offset, count, slots):
        @pl.loop(0, 4)
        def _(j):
            @pl.loop(0, count // 16)
            def _(k):
                rows = pl.ds(pl.multiple_of(offset + k * 16, 16), 16)
                place = (q, j, rows) if half == 0 else (j, q, rows)
                total = self.ref[place].astype(F32)
                for slot in slots:
                    total += self.r_line(half, slot, j, k)
                self.ref[place] = total.astype(BF)

    def r_line(self, half, slot, j, k):
        ref, side = slot
        return ref[half, side, j, pl.ds(pl.multiple_of(k * 16, 16), 16)].astype(F32)

    def add_at(self, half, p, q, part, slot):
        @pl.loop(0, 2)
        def _(k):
            rows = pl.ds(pl.multiple_of(64 * half + 32 * part + k * 16, 16), 16)
            place = (q, p, rows) if half == 0 else (p, q, rows)
            ref, side = slot
            got = ref[half, side, pl.ds(pl.multiple_of(k * 16, 16), 16)].astype(F32)
            self.ref[place] = (self.ref[place].astype(F32) + got).astype(BF)

    def step(self, n):
        for half in range(2):
            p, q = self.plane.own(half)
            pn, pp, po = next_to(p)
            qn, qp, qo = next_to(q)
            if n == 0:
                self.message(half, 0).start()
                self.message(half, 1).start()
            elif n == 1:
                self.message(half, 0).wait_recv()
                self.add_line(half, qn, 64 * half, 32, [(self.r1, 0)])
                self.message(half, 2).start()
                self.message(half, 1).wait_recv()
                self.add_line(half, qp, 64 * half + 32, 32, [(self.r1, 1)])
                self.message(half, 3).start()
            elif n == 2:
                self.message(half, 2).wait_recv()
                self.message(half, 3).wait_recv()
                self.add_line(half, q, 64 * half, 64, [(self.r2, 0), (self.r2, 1)])
                self.message(half, 4).start()
                self.message(half, 5).start()
            elif n == 3:
                self.message(half, 4).wait_recv()
                self.add_at(half, pn, q, 0, (self.r3, 0))
                self.message(half, 6).start()
                self.message(half, 5).wait_recv()
                self.add_at(half, pp, q, 1, (self.r3, 1))
                self.message(half, 7).start()
            elif n == 4:
                self.message(half, 6).wait_recv()
                self.message(half, 7).wait_recv()

                @pl.loop(0, 4)
                def _(k):
                    rows = pl.ds(pl.multiple_of(64 * half + k * 16, 16), 16)
                    place = (q, p, rows) if half == 0 else (p, q, rows)
                    some = pl.ds(pl.multiple_of(k * 16, 16), 16)
                    total = self.ref[place].astype(F32)
                    total += self.r4[half, 0, some].astype(F32)
                    total += self.r4[half, 1, some].astype(F32)
                    self.out[rows] = total
        if n == 4:
            for half in range(2):
                for i in range(8):
                    self.message(half, i).wait_send()

    def give_credit(self):
        for half in range(2):
            p, q = self.plane.own(half)
            for to in (p + 1) % 4, (p + 3) % 4:
                pl.semaphore_signal(self.free, inc=1, device_id=self.plane.device(half, to, q))

    def take_credit(self):
        pl.semaphore_wait(self.free, 4)


def moe_kernel(
    ffn_ref, cot_ref, gates_ref, wgu_hbm, wd_hbm,
    out_ref, dx_ref, h_ref, dgu_ref, dd_ref,
    x_all, dy_all, r1, r2, r3, r4, xs, ds, os, act, a1, a2, ggu, g_all, ranks, hcol, hs,
    wgu, wd, send, recv, gsend, grecv, hsend, hrecv, free, local,
):
    plane = Plane()
    me, z, x = plane.me, plane.z, plane.x
    w1 = pltpu.make_async_copy(wgu_hbm, wgu, local.at[0])
    w2 = pltpu.make_async_copy(wd_hbm, wd, local.at[1])
    w1.start()
    w2.start()
    own = []
    for mb in range(2):
        own.append(pltpu.make_async_copy(cot_ref.at[mb], dy_all.at[mb, z, x], local.at[2 + mb]))
        own.append(pltpu.make_async_copy(ffn_ref.at[mb], x_all.at[mb, z, x], local.at[4 + mb]))
    for copy in own:
        copy.start()
    plane.barrier()
    for copy in own:
        copy.wait()

    def gate_message(step):
        to = (me + step) % 16
        return pltpu.make_async_remote_copy(
            src_ref=gates_ref.at[to], dst_ref=g_all.at[me],
            send_sem=gsend.at[step], recv_sem=grecv.at[step], device_id={"expert": to},
        )

    def h_message(step):
        to = (me + step) % 16
        return pltpu.make_async_remote_copy(
            src_ref=hs.at[to], dst_ref=h_ref.at[me],
            send_sem=hsend.at[step], recv_sem=hrecv.at[step], device_id={"expert": to},
        )

    for step in range(1, 16):
        gate_message(step).start()
    g_all[me] = gates_ref[me]
    gx = [Gather(plane, x_all.at[mb], send.at[mb], recv.at[mb]) for mb in range(2)]
    gdy = [Gather(plane, dy_all.at[mb], send.at[2 + mb], recv.at[2 + mb]) for mb in range(2)]
    sout = [
        Scatter(plane, x_all.at[mb], r1.at[0], r2.at[0], r3.at[0], r4.at[0],
                send.at[4 + mb], recv.at[4 + mb], free.at[0], out_ref.at[mb])
        for mb in range(2)
    ]
    sdx = [
        Scatter(plane, dy_all.at[mb], r1.at[1], r2.at[1], r3.at[1], r4.at[1],
                send.at[6 + mb], recv.at[6 + mb], free.at[1], dx_ref.at[mb])
        for mb in range(2)
    ]
    for n in range(5):
        gx[0].step(n)
        gdy[0].step(n)
    gx[1].step(0)
    gdy[1].step(0)
    for step in range(1, 16):
        gate_message(step).wait_recv()
    for step in range(1, 16):
        gate_message(step).wait_send()

    earlier = (
        lax.broadcasted_iota(jnp.int32, (128, 128), 0)
        < lax.broadcasted_iota(jnp.int32, (128, 128), 1)
    ).astype(F32).astype(BF)

    @pl.loop(0, 16)
    def _(s):
        named = g_all[s] > 0.0
        before = nn(named.astype(F32).astype(BF), earlier)
        ranks[s] = jnp.where(named, before, -1.0)

    slot_ids = lax.broadcasted_iota(jnp.int32, (SLOTS, 128), 0).astype(F32)

    def places(s, mb):
        r = ranks[s]
        return [(slot_ids == r[2 * mb + e : 2 * mb + e + 1]).astype(F32) for e in range(2)]

    def gated(s, mb, hot):
        g = g_all[s]
        return [hot[e] * g[2 * mb + e : 2 * mb + e + 1] for e in range(2)]

    def span(s):
        return pl.ds(pl.multiple_of(s * SLOTS, 16), SLOTS)

    def select(mb):
        @pl.loop(0, 16)
        def _(s):
            hot = places(s, mb)
            pick = jnp.concatenate(hot, axis=0).astype(BF)
            scaled = jnp.concatenate(gated(s, mb, hot), axis=0).astype(BF)
            rows = nn(pick, x_all[mb, s // 4, s % 4]).astype(BF)
            drows = nn(scaled, dy_all[mb, s // 4, s % 4]).astype(BF)
            for e in range(2):
                xs[e, span(s)] = rows[SLOTS * e : SLOTS * (e + 1)]
                ds[e, span(s)] = drows[SLOTS * e : SLOTS * (e + 1)]

    chunks = 16 * SLOTS // CHUNK

    def forward(e):
        @pl.loop(0, chunks)
        def _(c):
            r = pl.ds(pl.multiple_of(c * CHUNK, CHUNK), CHUNK)
            gu = nn(xs[e, r], wgu[e])
            g, u = gu[:, :512], gu[:, 512:]
            sig = 1.0 / (1.0 + jnp.exp(-g))
            silu = g * sig
            active = (silu * u).astype(BF)
            act[e, r] = active
            a1[e, r] = (u * sig * (1.0 + g * (1.0 - sig))).astype(BF)
            a2[e, r] = silu.astype(BF)
            o = nn(active, wd[e]).astype(BF)
            os[e, r] = o
            hcol[e, r] = jnp.sum(o.astype(F32) * ds[e, r].astype(F32), axis=-1, keepdims=True)

    def combine_out(mb):
        @pl.loop(0, 16)
        def _(s):
            hot = places(s, mb)
            scaled = jnp.concatenate(gated(s, mb, hot), axis=0).astype(BF)
            both = jnp.concatenate([os[0, span(s)], os[1, span(s)]], axis=0)
            x_all[mb, s // 4, s % 4] = tn(scaled, both).astype(BF)
            for e in range(2):
                row = 2 * mb + e
                hs[s, row : row + 1] = jnp.sum(hot[e] * hcol[e, span(s)], axis=0, keepdims=True)

    def backward(mb, e):
        @pl.loop(0, chunks)
        def _(c):
            r = pl.ds(pl.multiple_of(c * CHUNK, CHUNK), CHUNK)
            ga = nt(ds[e, r], wd[e])
            grad = jnp.concatenate(
                [ga * a1[e, r].astype(F32), ga * a2[e, r].astype(F32)], axis=1
            ).astype(BF)
            ggu[r] = grad
            os[e, r] = nt(grad, wgu[e]).astype(BF)

        @pl.loop(0, 4)
        def _(m):
            cols = pl.ds(pl.multiple_of(m * 256, 256), 256)
            fresh = tn(xs[e, :, cols], ggu[...])
            dgu_ref[e, cols] = fresh if mb == 0 else dgu_ref[e, cols] + fresh

        @pl.loop(0, 2)
        def _(m):
            cols = pl.ds(pl.multiple_of(m * 256, 256), 256)
            fresh = tn(act[e, :, cols], ds[e])
            dd_ref[e, cols] = fresh if mb == 0 else dd_ref[e, cols] + fresh

    def combine_dx(mb):
        @pl.loop(0, 16)
        def _(s):
            pick = jnp.concatenate(places(s, mb), axis=0).astype(BF)
            both = jnp.concatenate([os[0, span(s)], os[1, span(s)]], axis=0)
            dy_all[mb, s // 4, s % 4] = tn(pick, both).astype(BF)

    w1.wait()
    w2.wait()
    select(0)
    gx[1].step(1)
    gdy[1].step(1)
    forward(0)
    gx[1].step(2)
    gdy[1].step(2)
    forward(1)
    combine_out(0)
    gx[1].step(3)
    gdy[1].step(3)
    sout[0].step(0)
    backward(0, 0)
    gx[1].step(4)
    gdy[1].step(4)
    sout[0].step(1)
    backward(0, 1)
    combine_dx(0)
    sout[0].step(2)
    sdx[0].step(0)
    select(1)
    sout[0].step(3)
    sdx[0].step(1)
    forward(0)
    sout[0].step(4)
    sout[0].give_credit()
    sdx[0].step(2)
    forward(1)
    sdx[0].step(3)
    combine_out(1)
    hs_own = hs[me]
    h_ref[me] = hs_own
    for step in range(1, 16):
        h_message(step).start()
    sout[1].take_credit()
    sout[1].step(0)
    sdx[0].step(4)
    sdx[0].give_credit()
    backward(1, 0)
    sout[1].step(1)
    backward(1, 1)
    sout[1].step(2)
    combine_dx(1)
    sdx[1].take_credit()
    sdx[1].step(0)
    sout[1].step(3)
    sdx[1].step(1)
    sout[1].step(4)
    for n in range(2, 5):
        sdx[1].step(n)
    for step in range(1, 16):
        h_message(step).wait_recv()
    for step in range(1, 16):
        h_message(step).wait_send()


def moe(ffn, cot, gates, w_gate_up, w_down):
    vmem = pl.BlockSpec(memory_space=pltpu.VMEM)
    anywhere = pl.BlockSpec(memory_space=pl.ANY)
    rows = 16 * SLOTS
    return pl.pallas_call(
        moe_kernel,
        out_shape=(
            jax.ShapeDtypeStruct((2, 128, 1024), F32),
            jax.ShapeDtypeStruct((2, 128, 1024), F32),
            jax.ShapeDtypeStruct((16, 8, 128), F32),
            jax.ShapeDtypeStruct((2, 1024, 1024), F32),
            jax.ShapeDtypeStruct((2, 512, 1024), F32),
        ),
        in_specs=[anywhere, anywhere, vmem, anywhere, anywhere],
        out_specs=(vmem,) * 5,
        scratch_shapes=[
            pltpu.VMEM((2, 4, 4, 128, 1024), BF),
            pltpu.VMEM((2, 4, 4, 128, 1024), BF),
            pltpu.VMEM((2, 2, 2, 4, 32, 1024), BF),
            pltpu.VMEM((2, 2, 2, 4, 64, 1024), BF),
            pltpu.VMEM((2, 2, 2, 32, 1024), BF),
            pltpu.VMEM((2, 2, 2, 64, 1024), BF),
            pltpu.VMEM((2, rows, 1024), BF),
            pltpu.VMEM((2, rows, 1024), BF),
            pltpu.VMEM((2, rows, 1024), BF),
            pltpu.VMEM((2, rows, 512), BF),
            pltpu.VMEM((2, rows, 512), BF),
            pltpu.VMEM((2, rows, 512), BF),
            pltpu.VMEM((rows, 1024), BF),
            pltpu.VMEM((16, 8, 128), F32),
            pltpu.VMEM((16, 8, 128), F32),
            pltpu.VMEM((2, rows, 1), F32),
            pltpu.VMEM((16, 8, 128), F32),
            pltpu.VMEM((2, 1024, 1024), BF),
            pltpu.VMEM((2, 512, 1024), BF),
            pltpu.SemaphoreType.DMA((8, 2, 8)),
            pltpu.SemaphoreType.DMA((8, 2, 8)),
            pltpu.SemaphoreType.DMA((16,)),
            pltpu.SemaphoreType.DMA((16,)),
            pltpu.SemaphoreType.DMA((16,)),
            pltpu.SemaphoreType.DMA((16,)),
            pltpu.SemaphoreType.REGULAR((2,)),
            pltpu.SemaphoreType.DMA((6,)),
        ],
        compiler_params=pltpu.CompilerParams(
            collective_id=0, has_side_effects=True, vmem_limit_bytes=63 * 1024 * 1024
        ),
        cost_estimate=pl.CostEstimate(
            flops=30_000_000_000, bytes_accessed=30_000_000, transcendentals=2_000_000
        ),
    )(ffn, cot, gates, w_gate_up, w_down)


def body(
    tokens,
    cotangent,
    segments,
    routes,
    w_qkv,
    w_out,
    attn_norm,
    ffn_norm,
    q_gain,
    k_gain,
    router,
    w_gate_up,
    w_down,
):
    micro_count, seq_count, query_rows, width = tokens.shape
    seq_length = segments.shape[2]
    experts_here = w_gate_up.shape[0]
    owners = lax.axis_size("expert")
    dp_size = lax.axis_size("dp")
    experts_all = experts_here * owners
    top_count = routes.shape[3]
    q_width = w_out.shape[0] * dp_size
    kv_width = (w_qkv.shape[1] - q_width) // 2
    kv_heads = kv_width // HD
    head_group = q_width // HD // kv_heads
    scaling = HD ** (-0.5)
    tok_rows = seq_count * query_rows
    dp_index = lax.axis_index("dp")
    cosine, sine_vals = angles((dp_index * query_rows + jnp.arange(query_rows)).astype(jnp.float32))
    expert_ids = jnp.arange(experts_all, dtype=jnp.int32)
    attn_totals = [
        jnp.zeros((piece.shape[0] * dp_size,) + piece.shape[1:], jnp.float32)
        for piece in (w_qkv, w_out, attn_norm, ffn_norm, q_gain, k_gain, router)
    ]
    outputs = []
    input_grads = []
    kept = []
    gathered = (
        *in_one_piece((w_qkv, w_out, attn_norm, ffn_norm), "dp", 0, 1),
        lax.all_gather(q_gain, "dp", axis=0, tiled=True),
        lax.all_gather(k_gain, "dp", axis=0, tiled=True),
        lax.all_gather(router, "dp", axis=0, tiled=True),
    )
    full_qkv, full_out, full_attn_norm, full_ffn_norm, full_q_gain, full_k_gain, full_router = (
        gathered
    )
    attn_gain = full_attn_norm.astype(jnp.float32)
    ffn_gain = full_ffn_norm.astype(jnp.float32)
    query_gain = full_q_gain.astype(jnp.float32)
    key_gain = full_k_gain.astype(jnp.float32)
    for micro_index in range(micro_count):
        states = tokens[micro_index].astype(jnp.float32).reshape(tok_rows, width)
        normed, inv_attn = norm_rows(states, attn_gain)
        normed_low = normed.astype(jnp.bfloat16)
        projected = jnp.dot(normed_low, full_qkv, preferred_element_type=jnp.float32)
        query_raw = projected[:, :q_width].reshape(seq_count, query_rows, q_width // HD, HD)
        key_raw = projected[:, q_width : q_width + kv_width].reshape(
            seq_count, query_rows, kv_heads, HD
        )
        value_low = (
            projected[:, q_width + kv_width :]
            .astype(jnp.bfloat16)
            .reshape(seq_count, query_rows, kv_width)
        )
        query_normed, inv_query = norm_rows(query_raw, query_gain)
        key_normed, inv_key = norm_rows(key_raw, key_gain)
        query_low = (
            rotary(query_normed, cosine, sine_vals)
            .astype(jnp.bfloat16)
            .reshape(seq_count, query_rows, kv_heads, head_group, HD)
        )
        key_low = (
            rotary(key_normed, cosine, sine_vals)
            .astype(jnp.bfloat16)
            .reshape(seq_count, query_rows, kv_width)
        )
        key_all, value_all = sent_together((key_low, value_low), "dp", 1, 0)
        key_all = key_all.reshape(seq_count, seq_length, kv_heads, HD)
        value_all = value_all.reshape(seq_count, seq_length, kv_heads, HD)
        segment_all = segments[micro_index]
        segment_own = lax.dynamic_slice_in_dim(segment_all, dp_index * query_rows, query_rows, 1)
        same_doc = (segment_own[:, :, None] == segment_all[:, None, :])[:, None, None]

        def attn_scores():
            raw_scores = (
                jnp.einsum(
                    "sqgrd,skgd->sgrqk", query_low, key_all, preferred_element_type=jnp.float32
                )
                * scaling
            )
            return jnp.where(same_doc, raw_scores, MASKED)

        scores = attn_scores()
        row_max = jnp.max(scores, axis=-1, keepdims=True)
        exp_scores = jnp.exp(scores - row_max)
        row_sum = jnp.sum(exp_scores, axis=-1, keepdims=True)
        log_norm = row_max + jnp.log(row_sum)
        probs_low = (exp_scores / row_sum).astype(jnp.bfloat16)
        mixed = jnp.einsum(
            "sgrqk,skgd->sqgrd", probs_low, value_all, preferred_element_type=jnp.float32
        )
        mixed_low = mixed.reshape(tok_rows, q_width).astype(jnp.bfloat16)
        residual = states + jnp.dot(mixed_low, full_out, preferred_element_type=jnp.float32)
        ffn_normed, inv_ffn = norm_rows(residual, ffn_gain)
        ffn_low = ffn_normed.astype(jnp.bfloat16)
        logits = jnp.dot(ffn_low, full_router, preferred_element_type=jnp.float32)
        route_ids = routes[micro_index].reshape(tok_rows, top_count)
        route_hot = (route_ids[:, :, None] == expert_ids[None, None, :])
        routed = jnp.any(route_hot, axis=1)
        top = jnp.max(jnp.where(routed, logits, MASKED), axis=1, keepdims=True)
        weight = jnp.where(routed, jnp.exp(logits - top), 0.0)
        gates = weight / jnp.sum(weight, axis=1, keepdims=True)
        kept.append((
            states, normed_low, inv_attn, query_raw, key_raw, inv_query, inv_key, query_low,
            key_all, value_all, same_doc, log_norm, mixed_low, residual, inv_ffn, ffn_low, gates,
        ))
    gates_sent = jnp.stack([k[-1].T.reshape(owners, experts_here, tok_rows) for k in kept], axis=1)
    gates_sent = gates_sent.reshape(owners, micro_count * experts_here, tok_rows)
    gates_sent = jnp.pad(gates_sent, ((0, 0), (0, 8 - micro_count * experts_here), (0, 0)))
    moved_out, moved_dx, weighed, gate_up_total, down_total = moe(
        jnp.stack([k[-2] for k in kept]),
        cotangent.reshape(micro_count, tok_rows, width),
        gates_sent,
        w_gate_up,
        w_down,
    )
    weighed = weighed[:, : micro_count * experts_here].reshape(
        owners, micro_count, experts_here, tok_rows
    )
    for micro_index in range(micro_count):
        (
            states, normed_low, inv_attn, query_raw, key_raw, inv_query, inv_key, query_low,
            key_all, value_all, same_doc, log_norm, mixed_low, residual, inv_ffn, ffn_low, gates,
        ) = kept[micro_index]

        def attn_scores():
            raw_scores = (
                jnp.einsum(
                    "sqgrd,skgd->sgrqk", query_low, key_all, preferred_element_type=jnp.float32
                )
                * scaling
            )
            return jnp.where(same_doc, raw_scores, MASKED)

        final = residual + moved_out[micro_index]
        outputs.append(final.astype(jnp.bfloat16).reshape(seq_count, query_rows, width))
        grad_final = cotangent[micro_index].astype(jnp.float32).reshape(tok_rows, width)
        share = weighed[:, micro_index].reshape(experts_all, tok_rows).T
        grad_logits = share - gates * jnp.sum(share, axis=1, keepdims=True)
        grad_router_now = jnp.einsum(
            "rd,re->de", ffn_low.astype(jnp.float32), grad_logits, precision=HIGHEST
        )
        grad_ffn_in = jnp.einsum(
            "re,de->rd", grad_logits, full_router.astype(jnp.float32), precision=HIGHEST
        )
        grad_ffn_in = grad_ffn_in + moved_dx[micro_index]
        grad_residual_part, ffn_gain_grad = norm_back(grad_ffn_in, residual, inv_ffn, ffn_gain)
        grad_residual = grad_final + grad_residual_part
        grad_branch = grad_residual.astype(jnp.bfloat16)
        grad_out_now = jnp.einsum(
            "rq,rd->qd", mixed_low, grad_branch, preferred_element_type=jnp.float32
        )
        grad_mixed = jnp.einsum(
            "rd,qd->rq", grad_branch, full_out, preferred_element_type=jnp.float32
        )
        grad_mixed = grad_mixed.astype(jnp.bfloat16).reshape(
            seq_count, query_rows, kv_heads, head_group, HD
        )
        probs = jnp.exp(attn_scores() - log_norm)
        grad_probs = jnp.einsum(
            "sqgrd,skgd->sgrqk", grad_mixed, value_all, preferred_element_type=jnp.float32
        )
        inner = jnp.sum(probs * grad_probs, axis=-1, keepdims=True)
        grad_scores = (probs * (grad_probs - inner)).astype(jnp.bfloat16)
        grad_query = (
            jnp.einsum(
                "sgrqk,skgd->sqgrd", grad_scores, key_all, preferred_element_type=jnp.float32
            )
            * scaling
        )
        grad_key_part = (
            jnp.einsum(
                "sgrqk,sqgrd->skgd", grad_scores, query_low, preferred_element_type=jnp.float32
            )
            * scaling
        )
        grad_value_part = jnp.einsum(
            "sgrqk,sqgrd->skgd",
            probs.astype(jnp.bfloat16),
            grad_mixed,
            preferred_element_type=jnp.float32,
        )
        grad_key, grad_value = tuple(
            (
                part.astype(jnp.float32)
                for part in in_one_piece_2(
                    (
                        grad_key_part.reshape(seq_count, seq_length, kv_width).astype(jnp.bfloat16),
                        grad_value_part.reshape(seq_count, seq_length, kv_width).astype(
                            jnp.bfloat16
                        ),
                    ),
                    "dp",
                    1,
                    0,
                )
            )
        )
        grad_query = rotary(
            grad_query.reshape(seq_count, query_rows, q_width // HD, HD), cosine, -sine_vals
        )
        grad_query_raw, query_gain_grad = norm_back(grad_query, query_raw, inv_query, query_gain)
        grad_key = rotary(grad_key.reshape(seq_count, query_rows, kv_heads, HD), cosine, -sine_vals)
        grad_key_raw, key_gain_grad = norm_back(grad_key, key_raw, inv_key, key_gain)
        grad_projected = jnp.concatenate(
            [
                grad_query_raw.reshape(tok_rows, q_width),
                grad_key_raw.reshape(tok_rows, kv_width),
                grad_value.reshape(tok_rows, kv_width),
            ],
            axis=1,
        ).astype(jnp.bfloat16)
        grad_qkv_now = jnp.einsum(
            "rd,rf->df", normed_low, grad_projected, preferred_element_type=jnp.float32
        )
        grad_normed = jnp.einsum(
            "rf,df->rd", grad_projected, full_qkv, preferred_element_type=jnp.float32
        )
        grad_states_part, attn_gain_grad = norm_back(grad_normed, states, inv_attn, attn_gain)
        input_grads.append(
            (grad_residual + grad_states_part)
            .astype(jnp.bfloat16)
            .reshape(seq_count, query_rows, width)
        )
        fresh_terms = (
            grad_qkv_now,
            grad_out_now,
            attn_gain_grad,
            ffn_gain_grad,
            query_gain_grad,
            key_gain_grad,
            grad_router_now,
        )
        attn_totals = [running + fresh for running, fresh in zip(attn_totals, fresh_terms)]
    attn_full = (
        attn_totals[0],
        attn_totals[1],
        attn_totals[2],
        attn_totals[3],
        attn_totals[4],
        attn_totals[5],
        attn_totals[6],
    )
    shard_part = (
        *tuple(
            (
                part.astype(jnp.float32)
                for part in in_one_piece_3(
                    (
                        attn_full[0].astype(jnp.bfloat16),
                        attn_full[1].astype(jnp.bfloat16),
                        attn_full[2].astype(jnp.bfloat16),
                        attn_full[3].astype(jnp.bfloat16),
                    ),
                    "dp",
                    0,
                    1,
                )
            )
        ),
        lax.psum_scatter(
            attn_full[4].astype(jnp.bfloat16), "dp", scatter_dimension=0, tiled=True
        ).astype(jnp.float32),
        lax.psum_scatter(
            attn_full[5].astype(jnp.bfloat16), "dp", scatter_dimension=0, tiled=True
        ).astype(jnp.float32),
        lax.psum_scatter(
            attn_full[6].astype(jnp.bfloat16), "dp", scatter_dimension=0, tiled=True
        ).astype(jnp.float32),
    )
    shard_grads = (
        lax.psum(shard_part[0].astype(jnp.bfloat16), "expert").astype(jnp.float32),
        lax.psum(shard_part[1].astype(jnp.bfloat16), "expert").astype(jnp.float32),
        lax.psum(shard_part[2].astype(jnp.bfloat16), "expert").astype(jnp.float32),
        lax.psum(shard_part[3].astype(jnp.bfloat16), "expert").astype(jnp.float32),
        lax.psum(shard_part[4].astype(jnp.bfloat16), "expert").astype(jnp.float32),
        lax.psum(shard_part[5].astype(jnp.bfloat16), "expert").astype(jnp.float32),
        lax.psum(shard_part[6].astype(jnp.bfloat16), "expert").astype(jnp.float32),
    )
    grad_gate_up, grad_down = tuple(
        (
            part.astype(jnp.float32)
            for part in together(
                (gate_up_total.astype(jnp.bfloat16), down_total.astype(jnp.bfloat16)), "dp"
            )
        )
    )
    return (
        jnp.stack(outputs),
        jnp.stack(input_grads),
        shard_grads[0],
        shard_grads[1],
        shard_grads[2],
        shard_grads[3],
        shard_grads[4],
        shard_grads[5],
        shard_grads[6],
        grad_gate_up,
        grad_down,
    )


def solution(mesh):
    return jax.shard_map(
        body,
        mesh=mesh,
        in_specs=(
            P(None, "expert", "dp", None),
            P(None, "expert", "dp", None),
            P(None, "expert", None),
            P(None, "expert", "dp", None),
            P("dp", None),
            P("dp", None),
            P("dp"),
            P("dp"),
            P("dp"),
            P("dp"),
            P("dp", None),
            P("expert", None, None),
            P("expert", None, None),
        ),
        out_specs=(
            P(None, "expert", "dp", None),
            P(None, "expert", "dp", None),
            P("dp", None),
            P("dp", None),
            P("dp"),
            P("dp"),
            P("dp"),
            P("dp"),
            P("dp", None),
            P("expert", None, None),
            P("expert", None, None),
        ),
        check_vma=False,
    )
```

```python
import jax
import jax.numpy as jnp
import numpy as np
from jax import lax
from jax.experimental import pallas as pl
from jax.experimental.pallas import tpu as pltpu
from jax.sharding import PartitionSpec as P

HD = 64
EPSILON = 1e-06
THETA = 10000.0
MASKED = -1e30

BF = jnp.bfloat16
F32 = jnp.float32
SLOTS = 48
CHUNK = 256
MIB = 1024 * 1024


def nn(a, b):
    return lax.dot_general(a, b, (((1,), (0,)), ((), ())), preferred_element_type=F32)


def nt(a, b):
    return lax.dot_general(a, b, (((1,), (1,)), ((), ())), preferred_element_type=F32)


def tn(a, b):
    return lax.dot_general(a, b, (((0,), (0,)), ((), ())), preferred_element_type=F32)


def send(src, dst, send_sem, recv_sem, device):
    return pltpu.make_async_remote_copy(
        src_ref=src, dst_ref=dst, send_sem=send_sem, recv_sem=recv_sem, device_id=device
    )


def next_to(p):
    return (p + 1) % 4, (p + 3) % 4, (p + 2) % 4


def greet(devices):
    sem = pltpu.get_barrier_semaphore()
    for device in devices:
        pl.semaphore_signal(sem, inc=1, device_id=device)
    pl.semaphore_wait(sem, len(devices))


class Plane:
    def __init__(self):
        self.me = lax.axis_index("expert")
        self.z = self.me // 4
        self.x = self.me % 4

    def own(self, half):
        return (self.x, self.z) if half == 0 else (self.z, self.x)

    def device(self, half, p, q):
        return {"expert": q * 4 + p if half == 0 else p * 4 + q}

    def others(self):
        return [{"expert": (self.me + step) % 16} for step in range(1, 16)]

    def neighbours(self):
        zn, zp, _ = next_to(self.z)
        xn, xp, _ = next_to(self.x)
        return [{"expert": k} for k in (zn * 4 + self.x, zp * 4 + self.x, self.z * 4 + xn, self.z * 4 + xp)]


class Column:
    def __init__(self):
        self.me = lax.axis_index("dp")
        self.y = self.me // 2
        self.c = self.me % 2

    def neighbours(self):
        yn, yp, _ = next_to(self.y)
        return [self.to(yn), self.to(yp), self.other()]

    def to(self, y):
        return {"dp": y * 2 + self.c}

    def other(self):
        return {"dp": self.y * 2 + 1 - self.c}


class PlaneStep:
    def at(self, half, p, q, rows):
        return self.ref.at[q, p, rows] if half == 0 else self.ref.at[p, q, rows]

    def line(self, half, q, rows):
        return self.ref.at[q, :, rows] if half == 0 else self.ref.at[:, q, rows]

    def rows(self, half):
        quarter = self.height // 4
        base = 2 * quarter * half
        return pl.ds(base, 2 * quarter), pl.ds(base, quarter), pl.ds(base + quarter, quarter)


class Gather(PlaneStep):
    def __init__(self, plane, ref, sems, height=128):
        self.plane, self.ref, self.sems, self.height = plane, ref, sems, height

    def message(self, half, i):
        p, q = self.plane.own(half)
        pn, pp, _ = next_to(p)
        qn, qp, _ = next_to(q)
        full, first, second = self.rows(half)
        view, to = [
            lambda: (self.at(half, p, q, full), (pn, q)),
            lambda: (self.at(half, p, q, full), (pp, q)),
            lambda: (self.at(half, pp, q, first), (pn, q)),
            lambda: (self.at(half, pn, q, second), (pp, q)),
            lambda: (self.line(half, q, full), (p, qn)),
            lambda: (self.line(half, q, full), (p, qp)),
            lambda: (self.line(half, qp, first), (p, qn)),
            lambda: (self.line(half, qn, second), (p, qp)),
        ][i]()
        sems = self.sems
        return send(view, view, sems.at[0, half, i], sems.at[1, half, i], self.plane.device(half, *to))

    def step(self, n):
        waits, starts = [
            ((), (0, 1)),
            ((0, 1), (2, 3)),
            ((2, 3), (4, 5)),
            ((4, 5), (6, 7)),
            ((6, 7), ()),
        ][n]
        for half in range(2):
            for i in waits:
                self.message(half, i).wait_recv()
            for i in starts:
                self.message(half, i).start()
        if n == 4:
            for half in range(2):
                for i in range(8):
                    self.message(half, i).wait_send()


class Scatter(PlaneStep):
    def __init__(self, plane, ref, slots, sems, store, free=None, height=128):
        self.plane, self.ref, self.slots, self.sems = plane, ref, slots, sems
        self.store, self.free, self.height = store, free, height

    def message(self, half, i):
        p, q = self.plane.own(half)
        pn, pp, po = next_to(p)
        qn, qp, qo = next_to(q)
        full, first, second = self.rows(half)
        r1, r2, r3, r4 = self.slots
        view, slot, to = [
            lambda: (self.line(half, qo, first), r1.at[half, 0], (p, qn)),
            lambda: (self.line(half, qo, second), r1.at[half, 1], (p, qp)),
            lambda: (self.line(half, qn, full), r2.at[half, 0], (p, qn)),
            lambda: (self.line(half, qp, full), r2.at[half, 1], (p, qp)),
            lambda: (self.at(half, po, q, first), r3.at[half, 0], (pn, q)),
            lambda: (self.at(half, po, q, second), r3.at[half, 1], (pp, q)),
            lambda: (self.at(half, pn, q, full), r4.at[half, 0], (pn, q)),
            lambda: (self.at(half, pp, q, full), r4.at[half, 1], (pp, q)),
        ][i]()
        sems = self.sems
        return send(view, slot, sems.at[0, half, i], sems.at[1, half, i], self.plane.device(half, *to))

    def add_line(self, half, q, part, parts, slots):
        quarter = self.height // 4
        offset = quarter * (2 * half + part)
        groups = quarter * parts // 16

        @pl.loop(0, 4 * groups)
        def _(n):
            j, k = n // groups, n % groups
            rows = pl.ds(pl.multiple_of(offset + k * 16, 16), 16)
            some = pl.ds(pl.multiple_of(k * 16, 16), 16)
            place = (q, j, rows) if half == 0 else (j, q, rows)
            total = self.ref[place].astype(F32)
            for ref, side in slots:
                total += ref[half, side, j, some].astype(F32)
            self.ref[place] = total.astype(BF)

    def add_at(self, half, p, q, part, slot):
        quarter = self.height // 4
        ref, side = slot

        @pl.loop(0, quarter // 16)
        def _(k):
            rows = pl.ds(pl.multiple_of(quarter * (2 * half + part) + k * 16, 16), 16)
            place = (q, p, rows) if half == 0 else (p, q, rows)
            got = ref[half, side, pl.ds(pl.multiple_of(k * 16, 16), 16)].astype(F32)
            self.ref[place] = (self.ref[place].astype(F32) + got).astype(BF)

    def step(self, n):
        r1, r2, r3, r4 = self.slots
        for half in range(2):
            p, q = self.plane.own(half)
            pn, pp, po = next_to(p)
            qn, qp, qo = next_to(q)
            if n == 0:
                self.message(half, 0).start()
                self.message(half, 1).start()
            elif n == 1:
                self.message(half, 0).wait_recv()
                self.add_line(half, qn, 0, 1, [(r1, 0)])
                self.message(half, 2).start()
                self.message(half, 1).wait_recv()
                self.add_line(half, qp, 1, 1, [(r1, 1)])
                self.message(half, 3).start()
            elif n == 2:
                self.message(half, 2).wait_recv()
                self.message(half, 3).wait_recv()
                self.add_line(half, q, 0, 2, [(r2, 0), (r2, 1)])
                self.message(half, 4).start()
                self.message(half, 5).start()
            elif n == 3:
                self.message(half, 4).wait_recv()
                self.add_at(half, pn, q, 0, (r3, 0))
                self.message(half, 6).start()
                self.message(half, 5).wait_recv()
                self.add_at(half, pp, q, 1, (r3, 1))
                self.message(half, 7).start()
            elif n == 4:
                self.message(half, 6).wait_recv()
                self.message(half, 7).wait_recv()

                @pl.loop(0, self.height // 32)
                def _(k):
                    rows = pl.ds(pl.multiple_of(self.height // 2 * half + k * 16, 16), 16)
                    place = (q, p, rows) if half == 0 else (p, q, rows)
                    some = pl.ds(pl.multiple_of(k * 16, 16), 16)
                    total = self.ref[place].astype(F32)
                    total += r4[half, 0, some].astype(F32)
                    total += r4[half, 1, some].astype(F32)
                    self.store(place, rows, total)
        if n == 4:
            for half in range(2):
                for i in range(8):
                    self.message(half, i).wait_send()

    def give_credit(self):
        for device in self.plane.neighbours():
            pl.semaphore_signal(self.free, inc=1, device_id=device)

    def take_credit(self):
        pl.semaphore_wait(self.free, 4)


def scatter_slots(height, width, lead=()):
    quarter = height // 4
    return [
        pltpu.VMEM((*lead, 2, 2, 4, quarter, width), BF),
        pltpu.VMEM((*lead, 2, 2, 4, 2 * quarter, width), BF),
        pltpu.VMEM((*lead, 2, 2, quarter, width), BF),
        pltpu.VMEM((*lead, 2, 2, 2 * quarter, width), BF),
    ]


class ColumnGather:
    def __init__(self, column, ref, sems, count):
        self.column, self.ref, self.sems, self.count = column, ref, sems, count

    def message(self, i):
        y, c = self.column.y, self.column.c
        yn, yp, yo = next_to(y)
        half = self.count // 2
        ref, column = self.ref, self.column
        view, device = [
            lambda: (ref.at[y, c], column.to(yn)),
            lambda: (ref.at[y, c], column.to(yp)),
            lambda: (ref.at[y, c], column.other()),
            lambda: (ref.at[yp, c, pl.ds(0, half)], column.to(yn)),
            lambda: (ref.at[yn, c, pl.ds(half, half)], column.to(yp)),
            lambda: (ref.at[yp, c], column.other()),
            lambda: (ref.at[yn, c], column.other()),
            lambda: (ref.at[yo, c], column.other()),
        ][i]()
        return send(view, view, self.sems.at[0, i], self.sems.at[1, i], device)

    def step(self, n):
        order = [
            [("s", 0), ("s", 1), ("s", 2)],
            [("w", 0), ("s", 3), ("s", 5), ("w", 1), ("s", 4), ("s", 6)],
            [("w", 3), ("w", 4), ("s", 7)],
            [("w", 2), ("w", 5), ("w", 6), ("w", 7)],
        ][n]
        for what, i in order:
            if what == "s":
                self.message(i).start()
            else:
                self.message(i).wait_recv()
        if n == 3:
            for i in range(8):
                self.message(i).wait_send()


class ColumnScatter:
    def __init__(self, column, ref, slots, sems, count, store, group=16):
        self.column, self.ref, self.slots, self.sems = column, ref, slots, sems
        self.count, self.store, self.group = count, store, group

    def message(self, i):
        y, c = self.column.y, self.column.c
        yn, yp, yo = next_to(y)
        half = self.count // 2
        ref, column = self.ref, self.column
        ra, rb, rc = self.slots
        view, slot, device = [
            lambda: (ref.at[:, 1 - c], ra, column.other()),
            lambda: (ref.at[yo, c, pl.ds(0, half)], rb.at[0], column.to(yn)),
            lambda: (ref.at[yo, c, pl.ds(half, half)], rb.at[1], column.to(yp)),
            lambda: (ref.at[yn, c], rc.at[0], column.to(yn)),
            lambda: (ref.at[yp, c], rc.at[1], column.to(yp)),
        ][i]()
        return send(view, slot, self.sems.at[0, i], self.sems.at[1, i], device)

    def some(self, k, base=0):
        return pl.ds(pl.multiple_of(base + k * self.group, self.group), self.group)

    def step(self, n):
        y, c = self.column.y, self.column.c
        yn, yp, yo = next_to(y)
        ref, (ra, rb, rc) = self.ref, self.slots
        low = ref.dtype
        half = self.count // 2
        groups = self.count // self.group
        if n == 0:
            self.message(0).start()
        elif n == 1:
            self.message(0).wait_recv()

            @pl.loop(0, 4 * groups)
            def _(k):
                j, r = k // groups, self.some(k % groups)
                ref[j, c, r] = (ref[j, c, r].astype(F32) + ra[j, r].astype(F32)).astype(low)

            self.message(1).start()
            self.message(2).start()
        elif n == 2:
            for side, to in ((0, yn), (1, yp)):
                self.message(1 + side).wait_recv()

                @pl.loop(0, groups // 2)
                def _(k):
                    r = self.some(k, side * half)
                    got = rb[side, self.some(k)].astype(F32)
                    ref[to, c, r] = (ref[to, c, r].astype(F32) + got).astype(low)

                self.message(3 + side).start()
        else:
            self.message(3).wait_recv()
            self.message(4).wait_recv()

            @pl.loop(0, groups)
            def _(k):
                r = self.some(k)
                total = ref[y, c, r].astype(F32) + rc[0, r].astype(F32) + rc[1, r].astype(F32)
                self.store(r, total)

            for i in range(5):
                self.message(i).wait_send()


def column_slots(shape, dtype=BF, lead=()):
    count, rest = shape[0], shape[1:]
    return [
        pltpu.VMEM((*lead, 4, count, *rest), dtype),
        pltpu.VMEM((*lead, 2, count // 2, *rest), dtype),
        pltpu.VMEM((*lead, 2, count, *rest), dtype),
    ]


def turned(v, cosine, sine):
    a, b = v[:32], v[32:]
    return jnp.concatenate([a * cosine - b * sine, b * cosine + a * sine], axis=0)


def inverse_rms(v, axis):
    return lax.rsqrt(jnp.mean(v * v, axis=axis, keepdims=True) + EPSILON)


def head_gain(small_t, row):
    pieces = [small_t[:, 128 * b : 128 * (b + 1)] for b in range(8)]
    tall = jnp.concatenate([piece.T[:8] for piece in pieces], axis=0)
    return jnp.broadcast_to(tall[:, row : row + 1], (64, 128))


def document_bias(seg_ref, bias, mb, mine):
    own = seg_ref[mb, mine]
    for b in range(8):
        keys = jnp.broadcast_to(seg_ref[mb, b], (128, 128)).T
        bias[mb, 128 * b : 128 * (b + 1)] = jnp.where(keys == own, 0.0, MASKED)


def pair_columns(ref, mb, g):
    both = ref[mb, pl.ds(pl.multiple_of(g * 128, 128), 128)]
    return jnp.concatenate([both[:64], both[64:]], axis=1)


def front_kernel(
    tok, cot, wq, wo, small, seg_ref, routes_ref, turn_hbm,
    dy_all, wq_all, wo_all, small_t, raw_t, q_t, kv_all, mix_t, lsum, res, ffn, gates_t, sent,
    small_all, normed, bias, turn, plane_sems, column_sems, local,
):
    plane, column = Plane(), Column()
    y, c = column.y, column.c
    copies = [
        pltpu.make_async_copy(wq, wq_all.at[y, c], local.at[0]),
        pltpu.make_async_copy(wo, wo_all.at[y, c], local.at[1]),
        pltpu.make_async_copy(small, small_all.at[y, c], local.at[2]),
        pltpu.make_async_copy(turn_hbm.at[column.me], turn, local.at[3]),
        pltpu.make_async_copy(cot.at[0], dy_all.at[0, plane.z, plane.x], local.at[4]),
        pltpu.make_async_copy(cot.at[1], dy_all.at[1, plane.z, plane.x], local.at[5]),
    ]
    for copy in copies:
        copy.start()
    greet(plane.neighbours() + column.neighbours())
    for copy in copies:
        copy.wait()
    gdy = [Gather(plane, dy_all.at[mb], plane_sems.at[mb]) for mb in range(2)]
    w_small = ColumnGather(column, small_all, column_sems.at[0], 128)
    w_q = ColumnGather(column, wq_all, column_sems.at[1], 128)
    w_o = ColumnGather(column, wo_all, column_sems.at[2], 128)
    kv = [ColumnGather(column, kv_all.at[mb], column_sems.at[3 + mb], 8) for mb in range(2)]
    w_small.step(0)
    w_q.step(0)
    gdy[0].step(0)
    w_small.step(1)
    w_small.step(2)
    w_small.step(3)
    for b in range(8):
        small_t[:, 128 * b : 128 * (b + 1)] = small_all[b // 2, b % 2].astype(F32).T
    for mb in range(2):
        document_bias(seg_ref, bias, mb, column.me)
    attn_gain = small_t[32:33]
    for mb in range(2):
        v = tok[mb].astype(F32)
        normed[128 * mb : 128 * (mb + 1)] = (v * inverse_rms(v, 1) * attn_gain).astype(BF)
    gdy[0].step(1)
    w_q.step(1)
    w_o.step(0)
    w_q.step(2)
    gdy[0].step(2)
    w_q.step(3)

    @pl.loop(0, 4)
    def _(n):
        cols = pl.ds(pl.multiple_of(n * 512, 512), 512)
        got = nn(normed[...], wq_all[:, :, :, cols].reshape(1024, 512))
        for mb in range(2):
            raw_t[mb, cols] = got[128 * mb : 128 * (mb + 1)].T

    query_gain = head_gain(small_t[...], 34)
    key_gain = head_gain(small_t[...], 35)
    cosine, sine = turn[:32], turn[32:]

    def heads(mb):
        @pl.loop(0, 8)
        def _(g):
            v = raw_t[mb, pl.ds(pl.multiple_of(1024 + g * 64, 64), 64)]
            key = turned(v * inverse_rms(v, 0) * key_gain, cosine, sine)
            value = raw_t[mb, pl.ds(pl.multiple_of(1536 + g * 64, 64), 64)]
            kv_all[mb, y, c, g] = jnp.concatenate([key, value], axis=0).T.astype(BF)

        kv[mb].step(0)

        @pl.loop(0, 16)
        def _(h):
            rows = pl.ds(pl.multiple_of(h * 64, 64), 64)
            v = raw_t[mb, rows]
            query = turned(v * inverse_rms(v, 0) * query_gain, cosine, sine)
            q_t[mb, rows] = (query.astype(BF).astype(F32) * HD ** (-0.5)).astype(BF)

    def attend(mb, start, stop):
        @pl.loop(start, stop)
        def _(g):
            query = pair_columns(q_t, mb, g)
            query = jnp.concatenate([query, jnp.zeros_like(query)], axis=0)
            total = jnp.zeros((1, 256), F32)
            mixed = jnp.zeros((128, 256), F32)
            for j in range(4):
                keys = kv_all[mb, j, :, g].reshape(256, 128)
                there = bias[mb, 256 * j : 256 * (j + 1)]
                p = jnp.exp(nn(keys, query) + jnp.concatenate([there, there], axis=1))
                total += jnp.sum(p, axis=0, keepdims=True)
                mixed += tn(keys, p.astype(BF))
            lsum[mb, g] = total
            mixed = (mixed[64:] / total).astype(BF)
            both = jnp.concatenate([mixed[:, :128], mixed[:, 128:]], axis=0)
            mix_t[mb, pl.ds(pl.multiple_of(g * 128, 128), 128)] = both

    def finish(mb):
        @pl.loop(0, 2)
        def _(n):
            cols = pl.ds(pl.multiple_of(n * 512, 512), 512)
            got = tn(mix_t[mb], wo_all[:, :, :, cols].reshape(1024, 512))
            res[mb, :, cols] = tok[mb, :, cols].astype(F32) + got

        v = res[mb]
        low = (v * inverse_rms(v, 1) * small_t[33:34]).astype(BF)
        ffn[mb] = low
        logits = nt(small_t[:32].astype(BF), low)
        ids = lax.broadcasted_iota(jnp.int32, (32, 128), 0)
        routed = ids == routes_ref[mb, 0:1]
        for k in range(1, 8):
            routed = routed | (ids == routes_ref[mb, k : k + 1])
        top = jnp.max(jnp.where(routed, logits, MASKED), axis=0, keepdims=True)
        weight = jnp.where(routed, jnp.exp(logits - top), 0.0)
        gates = weight / jnp.sum(weight, axis=0, keepdims=True)
        gates_t[mb] = gates
        for k in range(16):
            sent[k, 2 * mb : 2 * mb + 2] = gates[2 * k : 2 * k + 2]

    sent[...] = jnp.zeros_like(sent)
    heads(0)
    heads(1)
    gdy[0].step(3)
    kv[0].step(1)
    w_o.step(1)
    kv[0].step(2)
    kv[1].step(1)
    kv[0].step(3)
    gdy[0].step(4)
    gdy[1].step(0)
    attend(0, 0, 4)
    w_o.step(2)
    kv[1].step(2)
    gdy[1].step(1)
    attend(0, 4, 8)
    gdy[1].step(2)
    w_o.step(3)
    finish(0)
    kv[1].step(3)
    attend(1, 0, 4)
    gdy[1].step(3)
    attend(1, 4, 8)
    finish(1)
    gdy[1].step(4)


def front(tok, cot, wq, wo, small, seg, routes_t, turn):
    vmem = pl.BlockSpec(memory_space=pltpu.VMEM)
    anywhere = pl.BlockSpec(memory_space=pl.ANY)
    return pl.pallas_call(
        front_kernel,
        out_shape=(
            jax.ShapeDtypeStruct((2, 4, 4, 128, 1024), BF),
            jax.ShapeDtypeStruct((4, 2, 128, 2048), BF),
            jax.ShapeDtypeStruct((4, 2, 128, 1024), BF),
            jax.ShapeDtypeStruct((128, 1024), F32),
            jax.ShapeDtypeStruct((2, 2048, 128), F32),
            jax.ShapeDtypeStruct((2, 1024, 128), BF),
            jax.ShapeDtypeStruct((2, 4, 2, 8, 128, 128), BF),
            jax.ShapeDtypeStruct((2, 1024, 128), BF),
            jax.ShapeDtypeStruct((2, 8, 1, 256), F32),
            jax.ShapeDtypeStruct((2, 128, 1024), F32),
            jax.ShapeDtypeStruct((2, 128, 1024), BF),
            jax.ShapeDtypeStruct((2, 32, 128), F32),
            jax.ShapeDtypeStruct((16, 8, 128), F32),
        ),
        in_specs=[vmem, anywhere, anywhere, anywhere, anywhere, vmem, vmem, anywhere],
        out_specs=(anywhere,) + (vmem,) * 12,
        scratch_shapes=[
            pltpu.VMEM((4, 2, 128, 128), BF),
            pltpu.VMEM((256, 1024), BF),
            pltpu.VMEM((2, 1024, 128), F32),
            pltpu.VMEM((64, 128), F32),
            pltpu.SemaphoreType.DMA((2, 2, 2, 8)),
            pltpu.SemaphoreType.DMA((5, 2, 8)),
            pltpu.SemaphoreType.DMA((6,)),
        ],
        compiler_params=pltpu.CompilerParams(
            collective_id=0, has_side_effects=True, vmem_limit_bytes=56 * MIB
        ),
        cost_estimate=pl.CostEstimate(
            flops=5_000_000_000, bytes_accessed=30_000_000, transcendentals=5_000_000
        ),
    )(tok, cot, wq, wo, small, seg, routes_t, turn)


def moe_kernel(
    ffn_ref, dy_hbm, gates_ref, wgu_hbm, wd_hbm,
    out_ref, dx_ref, h_ref, dw,
    x_all, dy_all, r1, r2, r3, r4, xs, ds, os, act, a1, a2, ggu, g_all, ranks, hcol, hs,
    wgu, wd, ra, rb, rc, sems, column_sems, gsend, grecv, hsend, hrecv, free, dfree, local,
):
    plane, column = Plane(), Column()
    me, z, x = plane.me, plane.z, plane.x
    w1 = pltpu.make_async_copy(wgu_hbm, wgu, local.at[0])
    w2 = pltpu.make_async_copy(wd_hbm, wd, local.at[1])
    w1.start()
    w2.start()
    own = [pltpu.make_async_copy(ffn_ref.at[mb], x_all.at[mb, z, x], local.at[4 + mb]) for mb in range(2)]
    dys = [pltpu.make_async_copy(dy_hbm.at[mb], dy_all.at[mb], local.at[2 + mb]) for mb in range(2)]
    for copy in own + dys:
        copy.start()
    greet(plane.others() + column.neighbours())
    for copy in own:
        copy.wait()

    def gate_message(step):
        to = (me + step) % 16
        return pltpu.make_async_remote_copy(
            src_ref=gates_ref.at[to], dst_ref=g_all.at[me],
            send_sem=gsend.at[step], recv_sem=grecv.at[step], device_id={"expert": to},
        )

    def h_message(step):
        to = (me + step) % 16
        return pltpu.make_async_remote_copy(
            src_ref=hs.at[to], dst_ref=h_ref.at[me],
            send_sem=hsend.at[step], recv_sem=hrecv.at[step], device_id={"expert": to},
        )

    for step in range(1, 16):
        gate_message(step).start()
    g_all[me] = gates_ref[me]
    gx = [Gather(plane, x_all.at[mb], sems.at[mb]) for mb in range(2)]

    def into(ref, mb):
        def store(place, rows, total):
            ref[mb, rows] = total

        return store

    def slots(k):
        return [r.at[k] for r in (r1, r2, r3, r4)]

    sout = [
        Scatter(plane, x_all.at[mb], slots(0), sems.at[2 + mb], into(out_ref, mb), free.at[0])
        for mb in range(2)
    ]
    sdx = [
        Scatter(plane, dy_all.at[mb], slots(1), sems.at[4 + mb], into(dx_ref, mb), free.at[1])
        for mb in range(2)
    ]

    def own_part(k):
        def store(r, total):
            dw[k, column.y, column.c, r] = total.astype(BF)

        return store

    dsum = [
        ColumnScatter(
            column, dw.at[k], (ra.at[k], rb.at[k], rc.at[k]), column_sems.at[k], 128, own_part(k)
        )
        for k in range(3)
    ]
    dall = [ColumnGather(column, dw.at[k], column_sems.at[3 + k], 128) for k in range(3)]

    def parts_free(k):
        for device in column.neighbours():
            pl.semaphore_signal(dfree.at[k], inc=1, device_id=device)

    def gather_part(k):
        pl.semaphore_wait(dfree.at[k], 3)
        dall[k].step(0)

    for n in range(5):
        gx[0].step(n)
    gx[1].step(0)
    for step in range(1, 16):
        gate_message(step).wait_recv()
    for step in range(1, 16):
        gate_message(step).wait_send()

    earlier = (
        lax.broadcasted_iota(jnp.int32, (128, 128), 0)
        < lax.broadcasted_iota(jnp.int32, (128, 128), 1)
    ).astype(F32).astype(BF)

    @pl.loop(0, 16)
    def _(s):
        named = g_all[s] > 0.0
        before = nn(named.astype(F32).astype(BF), earlier)
        ranks[s] = jnp.where(named, before, -1.0)

    slot_ids = lax.broadcasted_iota(jnp.int32, (SLOTS, 128), 0).astype(F32)

    def places(s, mb):
        r = ranks[s]
        return [(slot_ids == r[2 * mb + e : 2 * mb + e + 1]).astype(F32) for e in range(2)]

    def gated(s, mb, hot):
        g = g_all[s]
        return [hot[e] * g[2 * mb + e : 2 * mb + e + 1] for e in range(2)]

    def span(s):
        return pl.ds(pl.multiple_of(s * SLOTS, 16), SLOTS)

    def select(mb):
        @pl.loop(0, 16)
        def _(s):
            hot = places(s, mb)
            pick = jnp.concatenate(hot, axis=0).astype(BF)
            scaled = jnp.concatenate(gated(s, mb, hot), axis=0).astype(BF)
            rows = nn(pick, x_all[mb, s // 4, s % 4]).astype(BF)
            drows = nn(scaled, dy_all[mb, s // 4, s % 4]).astype(BF)
            for e in range(2):
                xs[e, span(s)] = rows[SLOTS * e : SLOTS * (e + 1)]
                ds[e, span(s)] = drows[SLOTS * e : SLOTS * (e + 1)]

    chunks = 16 * SLOTS // CHUNK

    def forward(e):
        @pl.loop(0, chunks)
        def _(c):
            r = pl.ds(pl.multiple_of(c * CHUNK, CHUNK), CHUNK)
            gu = nn(xs[e, r], wgu[e])
            g, u = gu[:, :512], gu[:, 512:]
            sig = 1.0 / (1.0 + jnp.exp(-g))
            silu = g * sig
            active = (silu * u).astype(BF)
            act[e, r] = active
            a1[e, r] = (u * sig * (1.0 + g * (1.0 - sig))).astype(BF)
            a2[e, r] = silu.astype(BF)
            o = nn(active, wd[e]).astype(BF)
            os[e, r] = o
            hcol[e, r] = jnp.sum(o.astype(F32) * ds[e, r].astype(F32), axis=-1, keepdims=True)

    def combine_out(mb):
        @pl.loop(0, 16)
        def _(s):
            hot = places(s, mb)
            scaled = jnp.concatenate(gated(s, mb, hot), axis=0).astype(BF)
            both = jnp.concatenate([os[0, span(s)], os[1, span(s)]], axis=0)
            x_all[mb, s // 4, s % 4] = tn(scaled, both).astype(BF)
            for e in range(2):
                row = 2 * mb + e
                hs[s, row : row + 1] = jnp.sum(hot[e] * hcol[e, span(s)], axis=0, keepdims=True)

    def add_part(mb, k, n, fresh):
        fresh = fresh.reshape(2, 128, 1024)
        if mb == 1:
            fresh += dw[k, n].astype(F32)
        dw[k, n] = fresh.astype(BF)

    def backward(mb, e):
        @pl.loop(0, chunks)
        def _(c):
            r = pl.ds(pl.multiple_of(c * CHUNK, CHUNK), CHUNK)
            ga = nt(ds[e, r], wd[e])
            grad = jnp.concatenate(
                [ga * a1[e, r].astype(F32), ga * a2[e, r].astype(F32)], axis=1
            ).astype(BF)
            ggu[r] = grad
            os[e, r] = nt(grad, wgu[e]).astype(BF)

        @pl.loop(0, 4)
        def _(m):
            cols = pl.ds(pl.multiple_of(m * 256, 256), 256)
            add_part(mb, e, m, tn(xs[e, :, cols], ggu[...]))

        @pl.loop(0, 2)
        def _(m):
            cols = pl.ds(pl.multiple_of(m * 256, 256), 256)
            add_part(mb, 2, 2 * e + m, tn(act[e, :, cols], ds[e]))

    def combine_dx(mb):
        @pl.loop(0, 16)
        def _(s):
            pick = jnp.concatenate(places(s, mb), axis=0).astype(BF)
            both = jnp.concatenate([os[0, span(s)], os[1, span(s)]], axis=0)
            dy_all[mb, s // 4, s % 4] = tn(pick, both).astype(BF)

    w1.wait()
    w2.wait()
    for copy in dys:
        copy.wait()
    select(0)
    gx[1].step(1)
    forward(0)
    gx[1].step(2)
    forward(1)
    combine_out(0)
    gx[1].step(3)
    sout[0].step(0)
    backward(0, 0)
    gx[1].step(4)
    sout[0].step(1)
    backward(0, 1)
    combine_dx(0)
    sout[0].step(2)
    sdx[0].step(0)
    select(1)
    sout[0].step(3)
    sdx[0].step(1)
    forward(0)
    sout[0].step(4)
    sout[0].give_credit()
    sdx[0].step(2)
    forward(1)
    sdx[0].step(3)
    combine_out(1)
    h_ref[me] = hs[me]
    for step in range(1, 16):
        h_message(step).start()
    sout[1].take_credit()
    sout[1].step(0)
    sdx[0].step(4)
    sdx[0].give_credit()
    backward(1, 0)
    dsum[0].step(0)
    sout[1].step(1)
    backward(1, 1)
    dsum[1].step(0)
    dsum[2].step(0)
    dsum[0].step(1)
    sout[1].step(2)
    combine_dx(1)
    sdx[1].take_credit()
    sdx[1].step(0)
    dsum[1].step(1)
    sout[1].step(3)
    dsum[0].step(2)
    sdx[1].step(1)
    dsum[2].step(1)
    sout[1].step(4)
    dsum[0].step(3)
    parts_free(0)
    dsum[1].step(2)
    gather_part(0)
    sdx[1].step(2)
    dsum[2].step(2)
    dsum[1].step(3)
    parts_free(1)
    dall[0].step(1)
    gather_part(1)
    sdx[1].step(3)
    dsum[2].step(3)
    parts_free(2)
    dall[1].step(1)
    dall[0].step(2)
    gather_part(2)
    sdx[1].step(4)
    dall[2].step(1)
    dall[1].step(2)
    dall[2].step(2)
    for k in range(3):
        dall[k].step(3)
    for step in range(1, 16):
        h_message(step).wait_recv()
    for step in range(1, 16):
        h_message(step).wait_send()


def moe(ffn, dy, gates, w_gate_up, w_down):
    vmem = pl.BlockSpec(memory_space=pltpu.VMEM)
    anywhere = pl.BlockSpec(memory_space=pl.ANY)
    rows = 16 * SLOTS
    return pl.pallas_call(
        moe_kernel,
        out_shape=(
            jax.ShapeDtypeStruct((2, 128, 1024), F32),
            jax.ShapeDtypeStruct((2, 128, 1024), F32),
            jax.ShapeDtypeStruct((16, 8, 128), F32),
            jax.ShapeDtypeStruct((3, 4, 2, 128, 1024), BF),
        ),
        in_specs=[anywhere, anywhere, vmem, anywhere, anywhere],
        out_specs=(vmem,) * 4,
        scratch_shapes=[
            pltpu.VMEM((2, 4, 4, 128, 1024), BF),
            pltpu.VMEM((2, 4, 4, 128, 1024), BF),
            *scatter_slots(128, 1024, lead=(2,)),
            pltpu.VMEM((2, rows, 1024), BF),
            pltpu.VMEM((2, rows, 1024), BF),
            pltpu.VMEM((2, rows, 1024), BF),
            pltpu.VMEM((2, rows, 512), BF),
            pltpu.VMEM((2, rows, 512), BF),
            pltpu.VMEM((2, rows, 512), BF),
            pltpu.VMEM((rows, 1024), BF),
            pltpu.VMEM((16, 8, 128), F32),
            pltpu.VMEM((16, 8, 128), F32),
            pltpu.VMEM((2, rows, 1), F32),
            pltpu.VMEM((16, 8, 128), F32),
            pltpu.VMEM((2, 1024, 1024), BF),
            pltpu.VMEM((2, 512, 1024), BF),
            *column_slots((128, 1024), lead=(3,)),
            pltpu.SemaphoreType.DMA((6, 2, 2, 8)),
            pltpu.SemaphoreType.DMA((6, 2, 8)),
            pltpu.SemaphoreType.DMA((16,)),
            pltpu.SemaphoreType.DMA((16,)),
            pltpu.SemaphoreType.DMA((16,)),
            pltpu.SemaphoreType.DMA((16,)),
            pltpu.SemaphoreType.REGULAR((2,)),
            pltpu.SemaphoreType.REGULAR((3,)),
            pltpu.SemaphoreType.DMA((6,)),
        ],
        compiler_params=pltpu.CompilerParams(
            collective_id=1, has_side_effects=True, vmem_limit_bytes=63 * MIB
        ),
        cost_estimate=pl.CostEstimate(
            flops=30_000_000_000, bytes_accessed=30_000_000, transcendentals=2_000_000
        ),
    )(ffn, dy, gates, w_gate_up, w_down)


def norm_grad(grad, v, inverse, gain, axis):
    scaled = grad * gain
    moment = jnp.mean(scaled * v, axis=axis, keepdims=True)
    return inverse * (scaled - v * (inverse * inverse * moment)), grad * (v * inverse)


def back_kernel(
    tok, cot, seg_ref, turn_hbm, wq_hbm, wo_hbm, small_t, raw_hbm, q_t, kv_hbm, mix_t, lsum,
    res, ffn, gates_t, share_ref, dx,
    in_grad, gq, go, gs,
    wq_all, wo_all, kv_all, raw_t, turn, bias, gres, branch, gm_t, dq_t, own_kv, gp, normed_t, gn,
    part_kv, part_w, part_s, q_sum, k_sum, ra, rb, rc, sa, sb, sc, plane_buf, plane_all, p1, p2, p3, p4, ta, tb, tc,
    logits, routers, router_sum,
    column_sems, plane_sems, local,
):
    plane, column = Plane(), Column()
    y, c = column.y, column.c
    copies = [
        pltpu.make_async_copy(wo_hbm, wo_all, local.at[0]),
        pltpu.make_async_copy(kv_hbm, kv_all, local.at[1]),
        pltpu.make_async_copy(raw_hbm, raw_t, local.at[2]),
        pltpu.make_async_copy(wq_hbm, wq_all, local.at[3]),
        pltpu.make_async_copy(turn_hbm.at[column.me], turn, local.at[4]),
    ]
    for copy in copies:
        copy.start()
    greet(plane.neighbours() + column.neighbours())
    plane_buf[...] = jnp.zeros_like(plane_buf)
    part_s[...] = jnp.zeros_like(part_s)
    q_sum[...] = jnp.zeros_like(q_sum)
    k_sum[...] = jnp.zeros_like(k_sum)
    for mb in range(2):
        document_bias(seg_ref, bias, mb, column.me)

    def place_w(first):
        def store(r, total):
            low = total.astype(BF)
            half = r.start // 64
            some = pl.ds(pl.multiple_of(r.start % 64, 16), 16)
            for k in range(2):
                n = half * 8 + first + k
                plane_buf[n // 4, n % 4, some] = low[:, 512 * k : 512 * (k + 1)]

        return store

    def place_s(r, total):
        plane_buf[1, 2, r, 0:128] = total.astype(BF)

    def place_kv(mb):
        def store(r, total):
            own_kv[mb, r] = total

        return store

    w_sums = [
        ColumnScatter(
            column, part_w.at[k], (ra.at[k], rb.at[k], rc.at[k]), column_sems.at[k], 128,
            place_w(first),
        )
        for k, first in ((0, 4), (1, 0), (2, 2))
    ]
    kv_sums = [
        ColumnScatter(
            column, part_kv.at[mb],
            (sa.at[mb], sb.at[mb], sc.at[mb]),
            column_sems.at[3 + mb], 8, place_kv(mb), group=1,
        )
        for mb in range(2)
    ]

    s_sum = ColumnScatter(column, part_s, (ta, tb, tc), column_sems.at[5], 64, place_s)
    def tokens_of(mb):
        return pl.ds(128 * mb, 128)

    router = small_t[:32].astype(BF)
    ffn_gain, attn_gain = small_t[33:34], small_t[32:33]
    routers[0:32] = router
    routers[32:64] = router
    ffn_gain_grad = jnp.zeros((1, 1024), F32)
    for mb in range(2):
        share = jnp.concatenate([share_ref[k, 2 * mb : 2 * mb + 2] for k in range(16)], axis=0)
        logit = share - gates_t[mb] * jnp.sum(share, axis=0, keepdims=True)
        high = logit.astype(BF)
        logits[0:32, tokens_of(mb)] = high
        logits[32:64, tokens_of(mb)] = (logit - high.astype(F32)).astype(BF)

    @pl.loop(0, 4)
    def _(n):
        cols = pl.ds(pl.multiple_of(n * 256, 256), 256)
        gn[:, cols] = tn(logits[...], routers[:, cols])
        router_sum[:, cols] = nn(logits[...], ffn[:, :, cols].reshape(256, 256))

    for mb in range(2):
        into = dx[mb] + gn[tokens_of(mb)]
        v = res[mb]
        inv = inverse_rms(v, 1)
        grad, gain = norm_grad(into, v, inv, ffn_gain, 1)
        ffn_gain_grad += jnp.sum(gain, axis=0, keepdims=True)
        total = cot[mb].astype(F32) + grad
        gres[mb] = total
        branch[128 * mb : 128 * (mb + 1)] = total.astype(BF)
    copies[0].wait()

    @pl.loop(0, 4)
    def _(n):
        rows = pl.ds(pl.multiple_of(n * 256, 256), 256)
        got = nt(wo_all[n].reshape(256, 1024), branch[...])
        gm_t[0, rows] = got[:, :128].astype(BF)
        gm_t[1, rows] = got[:, 128:].astype(BF)
        mixed = jnp.concatenate([mix_t[0, rows], mix_t[1, rows]], axis=1)
        part_w[0, n] = nn(mixed, branch[...]).astype(BF).reshape(2, 128, 1024)

    w_sums[0].step(0)
    copies[1].wait()

    def attend(mb, start, stop):
        @pl.loop(start, stop)
        def _(g):
            query = pair_columns(q_t, mb, g)
            grad = pair_columns(gm_t, mb, g)
            mixed = pair_columns(mix_t, mb, g)
            blank = jnp.zeros_like(query)
            inner = jnp.sum(grad.astype(F32) * mixed.astype(F32), axis=0, keepdims=True)
            query = jnp.concatenate([query, blank], axis=0)
            grad = jnp.concatenate([blank, grad], axis=0)
            both = jnp.concatenate([query, grad], axis=1)
            scale = 1.0 / lsum[mb, g]
            dq = jnp.zeros((128, 256), F32)
            for j in range(4):
                keys = kv_all[mb, j, :, g].reshape(256, 128)
                there = bias[mb, 256 * j : 256 * (j + 1)]
                got = nn(keys, both)
                p = jnp.exp(got[:, :256] + jnp.concatenate([there, there], axis=1)) * scale
                ds = (p * (got[:, 256:] - inner)).astype(BF)
                dq += tn(keys, ds)
                dkv = nt(jnp.concatenate([ds, p.astype(BF)], axis=1), both)
                part_kv[mb, j, :, g] = dkv.astype(BF).reshape(2, 128, 128)
            dq = dq[:64] * HD ** (-0.5)
            rows = pl.ds(pl.multiple_of(g * 128, 128), 128)
            dq_t[mb, rows] = jnp.concatenate([dq[:, :128], dq[:, 128:]], axis=0)

    attend(0, 0, 4)
    w_sums[0].step(1)
    attend(0, 4, 8)
    kv_sums[0].step(0)
    w_sums[0].step(2)
    attend(1, 0, 4)
    kv_sums[0].step(1)
    w_sums[0].step(3)
    attend(1, 4, 8)
    kv_sums[1].step(0)
    kv_sums[0].step(2)
    copies[2].wait()
    copies[4].wait()
    cosine, sine = turn[:32], turn[32:]
    query_gain = head_gain(small_t[...], 34)
    key_gain = head_gain(small_t[...], 35)

    def head_back(grad, v, gain, total):
        inv = inverse_rms(v, 0)
        grad = turned(grad, cosine, -sine)
        grad_v, gain_part = norm_grad(grad, v, inv, gain, 0)
        total[...] += gain_part
        return grad_v

    @pl.loop(0, 8)
    def _(g):
        for mb in range(2):
            pieces = []
            for r in range(2):
                rows = pl.ds(pl.multiple_of(g * 128 + r * 64, 64), 64)
                pieces.append(head_back(dq_t[mb, rows], raw_t[mb, rows], query_gain, q_sum))
            cols = pl.ds(pl.multiple_of(g * 128, 128), 128)
            gp[tokens_of(mb), cols] = jnp.concatenate(pieces, axis=0).T.astype(BF)

    kv_sums[0].step(3)
    kv_sums[1].step(1)
    for mb in range(2):
        v = tok[mb].astype(F32)
        normed = (v * inverse_rms(v, 1) * attn_gain).astype(BF).astype(F32)
        for k in range(8):
            normed_t[128 * k : 128 * (k + 1), tokens_of(mb)] = (
                normed[:, 128 * k : 128 * (k + 1)].T.astype(BF)
            )

    def weight_part(which):
        cols = pl.ds(1024 * (which - 1), 1024)

        @pl.loop(0, 4)
        def _(n):
            rows = pl.ds(pl.multiple_of(n * 256, 256), 256)
            part_w[which, n] = nn(normed_t[rows], gp[:, cols]).astype(BF).reshape(2, 128, 1024)

    def keys_back(mb):
        @pl.loop(0, 4)
        def _(k):
            keys, values = [], []
            for r in range(2):
                g = 2 * k + r
                grad = own_kv[mb, g].T
                rows = pl.ds(pl.multiple_of(1024 + g * 64, 64), 64)
                keys.append(head_back(grad[:64], raw_t[mb, rows], key_gain, k_sum))
                values.append(grad[64:])
            cols = pl.ds(pl.multiple_of(1024 + k * 128, 128), 128)
            gp[tokens_of(mb), cols] = jnp.concatenate(keys, axis=0).T.astype(BF)
            cols = pl.ds(pl.multiple_of(1536 + k * 128, 128), 128)
            gp[tokens_of(mb), cols] = jnp.concatenate(values, axis=0).T.astype(BF)

    weight_part(1)
    w_sums[1].step(0)
    kv_sums[1].step(2)
    keys_back(0)
    w_sums[1].step(1)
    kv_sums[1].step(3)
    keys_back(1)
    weight_part(2)
    w_sums[2].step(0)
    w_sums[1].step(2)
    copies[3].wait()

    @pl.loop(0, 4)
    def _(n):
        cols = pl.ds(pl.multiple_of(n * 256, 256), 256)
        gn[:, cols] = nt(gp[...], wq_all[n].reshape(256, 2048))

    w_sums[2].step(1)
    attn_gain_grad = jnp.zeros((1, 1024), F32)
    for mb in range(2):
        v = tok[mb].astype(F32)
        grad, gain = norm_grad(gn[tokens_of(mb)], v, inverse_rms(v, 1), attn_gain, 1)
        attn_gain_grad += jnp.sum(gain, axis=0, keepdims=True)
        in_grad[mb] = (gres[mb] + grad).astype(BF)
    for b in range(8):
        cols = slice(128 * b, 128 * (b + 1))
        heads = slice(8 * b, 8 * (b + 1))
        part_s[b // 2, b % 2, 0:32] = router_sum[0:32, cols] + router_sum[32:64, cols]
        part_s[b // 2, b % 2, 32:33] = attn_gain_grad[:, cols]
        part_s[b // 2, b % 2, 33:34] = ffn_gain_grad[:, cols]
        part_s[b // 2, b % 2, 40:48] = jnp.broadcast_to(
            jnp.sum(q_sum[heads], axis=1, keepdims=True), (8, 128)
        )
        part_s[b // 2, b % 2, 48:56] = jnp.broadcast_to(
            jnp.sum(k_sum[heads], axis=1, keepdims=True), (8, 128)
        )
    s_sum.step(0)
    s_sum.step(1)
    w_sums[1].step(3)
    w_sums[2].step(2)
    s_sum.step(2)
    w_sums[2].step(3)
    s_sum.step(3)

    def keep(place, rows, total):
        plane_all[place] = total.astype(BF)

    over = Scatter(plane, plane_buf, (p1, p2, p3, p4), plane_sems.at[0], keep, height=64)
    back = Gather(plane, plane_all, plane_sems.at[1], height=64)
    for n in range(5):
        over.step(n)
    for n in range(5):
        back.step(n)
    for half in range(2):
        rows = pl.ds(64 * half, 64)
        for k in range(4):
            n = half * 8 + k
            gq[rows, 512 * k : 512 * (k + 1)] = plane_all[n // 4, n % 4].astype(F32)
        for k in range(2):
            n = half * 8 + 4 + k
            go[rows, 512 * k : 512 * (k + 1)] = plane_all[n // 4, n % 4].astype(F32)
    gs[...] = plane_all[1, 2, :, 0:128].astype(F32)


def back(tok, cot, seg, turn, wq_all, wo_all, small_t, raw_t, q_t, kv_all, mix_t, lsum, res, ffn, gates_t, share, dx):
    vmem = pl.BlockSpec(memory_space=pltpu.VMEM)
    anywhere = pl.BlockSpec(memory_space=pl.ANY)
    kv_slots = column_slots((8, 128, 128), lead=(2,))
    return pl.pallas_call(
        back_kernel,
        out_shape=(
            jax.ShapeDtypeStruct((2, 128, 1024), BF),
            jax.ShapeDtypeStruct((128, 2048), F32),
            jax.ShapeDtypeStruct((128, 1024), F32),
            jax.ShapeDtypeStruct((64, 128), F32),
        ),
        in_specs=[
            vmem, vmem, vmem, anywhere, anywhere, anywhere, vmem, anywhere, vmem, anywhere,
            vmem, vmem, vmem, vmem, vmem, vmem, vmem,
        ],
        out_specs=(vmem,) * 4,
        scratch_shapes=[
            pltpu.VMEM((4, 2, 128, 2048), BF),
            pltpu.VMEM((4, 2, 128, 1024), BF),
            pltpu.VMEM((2, 4, 2, 8, 128, 128), BF),
            pltpu.VMEM((2, 2048, 128), F32),
            pltpu.VMEM((64, 128), F32),
            pltpu.VMEM((2, 1024, 128), F32),
            pltpu.VMEM((2, 128, 1024), F32),
            pltpu.VMEM((256, 1024), BF),
            pltpu.VMEM((2, 1024, 128), BF),
            pltpu.VMEM((2, 1024, 128), F32),
            pltpu.VMEM((2, 8, 128, 128), F32),
            pltpu.VMEM((256, 2048), BF),
            pltpu.VMEM((1024, 256), BF),
            pltpu.VMEM((256, 1024), F32),
            pltpu.VMEM((2, 4, 2, 8, 128, 128), BF),
            pltpu.VMEM((3, 4, 2, 128, 1024), BF),
            pltpu.VMEM((4, 2, 64, 128), F32),
            pltpu.VMEM((64, 128), F32),
            pltpu.VMEM((64, 128), F32),
            *column_slots((128, 1024), lead=(3,)),
            *kv_slots,
            pltpu.VMEM((4, 4, 64, 512), BF),
            pltpu.VMEM((4, 4, 64, 512), BF),
            *scatter_slots(64, 512),
            *column_slots((64, 128), F32),
            pltpu.VMEM((64, 256), BF),
            pltpu.VMEM((64, 1024), BF),
            pltpu.VMEM((64, 1024), F32),
            pltpu.SemaphoreType.DMA((6, 2, 8)),
            pltpu.SemaphoreType.DMA((2, 2, 2, 8)),
            pltpu.SemaphoreType.DMA((5,)),
        ],
        compiler_params=pltpu.CompilerParams(
            collective_id=2, has_side_effects=True, vmem_limit_bytes=60 * MIB
        ),
        cost_estimate=pl.CostEstimate(
            flops=12_000_000_000, bytes_accessed=30_000_000, transcendentals=5_000_000
        ),
    )(tok, cot, seg, turn, wq_all, wo_all, small_t, raw_t, q_t, kv_all, mix_t, lsum, res, ffn, gates_t, share, dx)


def turn_table(length):
    frequency = np.power(np.float32(THETA), -2.0 * np.arange(HD // 2, dtype=np.float32) / HD)
    angle = np.arange(length, dtype=np.float32)[:, None] * frequency.astype(np.float32)[None, :]
    both = np.concatenate([np.cos(angle), np.sin(angle)], axis=1).astype(np.float32)
    return both.reshape(length // 128, 128, HD).transpose(0, 2, 1)


def body(
    tokens,
    cotangent,
    segments,
    routes,
    w_qkv,
    w_out,
    attn_norm,
    ffn_norm,
    q_gain,
    k_gain,
    router,
    w_gate_up,
    w_down,
):
    tok = tokens.reshape(2, 128, 1024)
    cot = cotangent.reshape(2, 128, 1024)
    seg = segments.reshape(2, 8, 1, 128).astype(F32)
    routes_t = routes.reshape(2, 128, 8).transpose(0, 2, 1)
    turn = jnp.asarray(turn_table(1024))
    gains = jnp.zeros((128, 2), BF).at[:8, 0].set(q_gain).at[:8, 1].set(k_gain)
    small = jnp.concatenate(
        [router, attn_norm[:, None], ffn_norm[:, None], gains, jnp.zeros((128, 92), BF)], axis=1
    )
    dy_all, wq_all, wo_all, small_t, raw_t, q_t, kv_all, mix_t, lsum, res, ffn, gates_t, sent = front(
        tok, cot, w_qkv, w_out, small, seg, routes_t, turn
    )
    moved_out, moved_dx, share, dw = moe(ffn, dy_all, sent, w_gate_up, w_down)
    in_grad, gq, go, gs = back(
        tok, cot, seg, turn, wq_all, wo_all, small_t, raw_t, q_t, kv_all, mix_t, lsum, res, ffn,
        gates_t, share, moved_dx,
    )
    output = (res + moved_out).astype(BF).reshape(tokens.shape)
    return (
        output,
        in_grad.reshape(tokens.shape),
        gq,
        go,
        gs[32],
        gs[33],
        gs[40:48, 0],
        gs[48:56, 0],
        gs[:32].T,
        dw[:2].astype(F32).reshape(2, 1024, 1024),
        dw[2].astype(F32).reshape(2, 512, 1024),
    )


def solution(mesh):
    return jax.shard_map(
        body,
        mesh=mesh,
        in_specs=(
            P(None, "expert", "dp", None),
            P(None, "expert", "dp", None),
            P(None, "expert", None),
            P(None, "expert", "dp", None),
            P("dp", None),
            P("dp", None),
            P("dp"),
            P("dp"),
            P("dp"),
            P("dp"),
            P("dp", None),
            P("expert", None, None),
            P("expert", None, None),
        ),
        out_specs=(
            P(None, "expert", "dp", None),
            P(None, "expert", "dp", None),
            P("dp", None),
            P("dp", None),
            P("dp"),
            P("dp"),
            P("dp"),
            P("dp"),
            P("dp", None),
            P("expert", None, None),
            P("expert", None, None),
        ),
        check_vma=False,
    )
```

```python
import jax
import jax.numpy as jnp
import numpy as np
from jax import lax
from jax.experimental import pallas as pl
from jax.experimental.pallas import tpu as pltpu
from jax.sharding import PartitionSpec as P

HD = 64
EPSILON = 1e-06
THETA = 10000.0
MASKED = -1e30

BF = jnp.bfloat16
F32 = jnp.float32
SLOTS = 48
CHUNK = 256
MIB = 1024 * 1024


def nn(a, b):
    return lax.dot_general(a, b, (((1,), (0,)), ((), ())), preferred_element_type=F32)


def nt(a, b):
    return lax.dot_general(a, b, (((1,), (1,)), ((), ())), preferred_element_type=F32)


def tn(a, b):
    return lax.dot_general(a, b, (((0,), (0,)), ((), ())), preferred_element_type=F32)


def send(src, dst, send_sem, recv_sem, device):
    return pltpu.make_async_remote_copy(
        src_ref=src, dst_ref=dst, send_sem=send_sem, recv_sem=recv_sem, device_id=device
    )


def next_to(p):
    return (p + 1) % 4, (p + 3) % 4, (p + 2) % 4


def greet(devices):
    sem = pltpu.get_barrier_semaphore()
    for device in devices:
        pl.semaphore_signal(sem, inc=1, device_id=device)
    pl.semaphore_wait(sem, len(devices))


class Plane:
    def __init__(self):
        self.me = lax.axis_index("expert")
        self.z = self.me // 4
        self.x = self.me % 4

    def own(self, half):
        return (self.x, self.z) if half == 0 else (self.z, self.x)

    def device(self, half, p, q):
        return {"expert": q * 4 + p if half == 0 else p * 4 + q}

    def others(self):
        return [{"expert": (self.me + step) % 16} for step in range(1, 16)]

    def neighbours(self):
        zn, zp, _ = next_to(self.z)
        xn, xp, _ = next_to(self.x)
        return [{"expert": k} for k in (zn * 4 + self.x, zp * 4 + self.x, self.z * 4 + xn, self.z * 4 + xp)]


class Column:
    def __init__(self):
        self.me = lax.axis_index("dp")
        self.y = self.me // 2
        self.c = self.me % 2

    def neighbours(self):
        yn, yp, _ = next_to(self.y)
        return [self.to(yn), self.to(yp), self.other()]

    def to(self, y):
        return {"dp": y * 2 + self.c}

    def other(self):
        return {"dp": self.y * 2 + 1 - self.c}


class PlaneStep:
    def at(self, half, p, q, rows):
        return self.ref.at[q, p, rows] if half == 0 else self.ref.at[p, q, rows]

    def line(self, half, q, rows):
        return self.ref.at[q, :, rows] if half == 0 else self.ref.at[:, q, rows]

    def rows(self, half):
        quarter = self.height // 4
        base = 2 * quarter * half
        return pl.ds(base, 2 * quarter), pl.ds(base, quarter), pl.ds(base + quarter, quarter)


class Gather(PlaneStep):
    def __init__(self, plane, ref, sems, height=128):
        self.plane, self.ref, self.sems, self.height = plane, ref, sems, height

    def message(self, half, i):
        p, q = self.plane.own(half)
        pn, pp, _ = next_to(p)
        qn, qp, _ = next_to(q)
        full, first, second = self.rows(half)
        view, to = [
            lambda: (self.at(half, p, q, full), (pn, q)),
            lambda: (self.at(half, p, q, full), (pp, q)),
            lambda: (self.at(half, pp, q, first), (pn, q)),
            lambda: (self.at(half, pn, q, second), (pp, q)),
            lambda: (self.line(half, q, full), (p, qn)),
            lambda: (self.line(half, q, full), (p, qp)),
            lambda: (self.line(half, qp, first), (p, qn)),
            lambda: (self.line(half, qn, second), (p, qp)),
        ][i]()
        sems = self.sems
        return send(view, view, sems.at[0, half, i], sems.at[1, half, i], self.plane.device(half, *to))

    def step(self, n):
        waits, starts = [
            ((), (0, 1)),
            ((0, 1), (2, 3)),
            ((2, 3), (4, 5)),
            ((4, 5), (6, 7)),
            ((6, 7), ()),
        ][n]
        for half in range(2):
            for i in waits:
                self.message(half, i).wait_recv()
            for i in starts:
                self.message(half, i).start()
        if n == 4:
            for half in range(2):
                for i in range(8):
                    self.message(half, i).wait_send()


class Scatter(PlaneStep):
    def __init__(self, plane, ref, slots, sems, store, free=None, height=128):
        self.plane, self.ref, self.slots, self.sems = plane, ref, slots, sems
        self.store, self.free, self.height = store, free, height

    def message(self, half, i):
        p, q = self.plane.own(half)
        pn, pp, po = next_to(p)
        qn, qp, qo = next_to(q)
        full, first, second = self.rows(half)
        r1, r2, r3, r4 = self.slots
        view, slot, to = [
            lambda: (self.line(half, qo, first), r1.at[half, 0], (p, qn)),
            lambda: (self.line(half, qo, second), r1.at[half, 1], (p, qp)),
            lambda: (self.line(half, qn, full), r2.at[half, 0], (p, qn)),
            lambda: (self.line(half, qp, full), r2.at[half, 1], (p, qp)),
            lambda: (self.at(half, po, q, first), r3.at[half, 0], (pn, q)),
            lambda: (self.at(half, po, q, second), r3.at[half, 1], (pp, q)),
            lambda: (self.at(half, pn, q, full), r4.at[half, 0], (pn, q)),
            lambda: (self.at(half, pp, q, full), r4.at[half, 1], (pp, q)),
        ][i]()
        sems = self.sems
        return send(view, slot, sems.at[0, half, i], sems.at[1, half, i], self.plane.device(half, *to))

    def add_line(self, half, q, part, parts, slots):
        quarter = self.height // 4
        offset = quarter * (2 * half + part)
        groups = quarter * parts // 16

        @pl.loop(0, 4 * groups)
        def _(n):
            j, k = n // groups, n % groups
            rows = pl.ds(pl.multiple_of(offset + k * 16, 16), 16)
            some = pl.ds(pl.multiple_of(k * 16, 16), 16)
            place = (q, j, rows) if half == 0 else (j, q, rows)
            total = self.ref[place].astype(F32)
            for ref, side in slots:
                total += ref[half, side, j, some].astype(F32)
            self.ref[place] = total.astype(BF)

    def add_at(self, half, p, q, part, slot):
        quarter = self.height // 4
        ref, side = slot

        @pl.loop(0, quarter // 16)
        def _(k):
            rows = pl.ds(pl.multiple_of(quarter * (2 * half + part) + k * 16, 16), 16)
            place = (q, p, rows) if half == 0 else (p, q, rows)
            got = ref[half, side, pl.ds(pl.multiple_of(k * 16, 16), 16)].astype(F32)
            self.ref[place] = (self.ref[place].astype(F32) + got).astype(BF)

    def step(self, n):
        r1, r2, r3, r4 = self.slots
        for half in range(2):
            p, q = self.plane.own(half)
            pn, pp, po = next_to(p)
            qn, qp, qo = next_to(q)
            if n == 0:
                self.message(half, 0).start()
                self.message(half, 1).start()
            elif n == 1:
                self.message(half, 0).wait_recv()
                self.add_line(half, qn, 0, 1, [(r1, 0)])
                self.message(half, 2).start()
                self.message(half, 1).wait_recv()
                self.add_line(half, qp, 1, 1, [(r1, 1)])
                self.message(half, 3).start()
            elif n == 2:
                self.message(half, 2).wait_recv()
                self.message(half, 3).wait_recv()
                self.add_line(half, q, 0, 2, [(r2, 0), (r2, 1)])
                self.message(half, 4).start()
                self.message(half, 5).start()
            elif n == 3:
                self.message(half, 4).wait_recv()
                self.add_at(half, pn, q, 0, (r3, 0))
                self.message(half, 6).start()
                self.message(half, 5).wait_recv()
                self.add_at(half, pp, q, 1, (r3, 1))
                self.message(half, 7).start()
            elif n == 4:
                self.message(half, 6).wait_recv()
                self.message(half, 7).wait_recv()

                @pl.loop(0, self.height // 32)
                def _(k):
                    rows = pl.ds(pl.multiple_of(self.height // 2 * half + k * 16, 16), 16)
                    place = (q, p, rows) if half == 0 else (p, q, rows)
                    some = pl.ds(pl.multiple_of(k * 16, 16), 16)
                    total = self.ref[place].astype(F32)
                    total += r4[half, 0, some].astype(F32)
                    total += r4[half, 1, some].astype(F32)
                    self.store(place, rows, total)
        if n == 4:
            for half in range(2):
                for i in range(8):
                    self.message(half, i).wait_send()

    def give_credit(self):
        for device in self.plane.neighbours():
            pl.semaphore_signal(self.free, inc=1, device_id=device)

    def take_credit(self):
        pl.semaphore_wait(self.free, 4)


def scatter_slots(height, width, lead=()):
    quarter = height // 4
    return [
        pltpu.VMEM((*lead, 2, 2, 4, quarter, width), BF),
        pltpu.VMEM((*lead, 2, 2, 4, 2 * quarter, width), BF),
        pltpu.VMEM((*lead, 2, 2, quarter, width), BF),
        pltpu.VMEM((*lead, 2, 2, 2 * quarter, width), BF),
    ]


class ColumnGather:
    def __init__(self, column, ref, sems, count):
        self.column, self.ref, self.sems, self.count = column, ref, sems, count

    def message(self, i):
        y, c = self.column.y, self.column.c
        yn, yp, yo = next_to(y)
        half = self.count // 2
        ref, column = self.ref, self.column
        view, device = [
            lambda: (ref.at[y, c], column.to(yn)),
            lambda: (ref.at[y, c], column.to(yp)),
            lambda: (ref.at[y, c], column.other()),
            lambda: (ref.at[yp, c, pl.ds(0, half)], column.to(yn)),
            lambda: (ref.at[yn, c, pl.ds(half, half)], column.to(yp)),
            lambda: (ref.at[yp, c], column.other()),
            lambda: (ref.at[yn, c], column.other()),
            lambda: (ref.at[yo, c], column.other()),
        ][i]()
        return send(view, view, self.sems.at[0, i], self.sems.at[1, i], device)

    def step(self, n):
        order = [
            [("s", 0), ("s", 1), ("s", 2)],
            [("w", 0), ("s", 3), ("s", 5), ("w", 1), ("s", 4), ("s", 6)],
            [("w", 3), ("w", 4), ("s", 7)],
            [("w", 2), ("w", 5), ("w", 6), ("w", 7)],
        ][n]
        for what, i in order:
            if what == "s":
                self.message(i).start()
            else:
                self.message(i).wait_recv()
        if n == 3:
            for i in range(8):
                self.message(i).wait_send()


class ColumnScatter:
    def __init__(self, column, ref, slots, sems, count, store, group=16):
        self.column, self.ref, self.slots, self.sems = column, ref, slots, sems
        self.count, self.store, self.group = count, store, group

    def message(self, i):
        y, c = self.column.y, self.column.c
        yn, yp, yo = next_to(y)
        half = self.count // 2
        ref, column = self.ref, self.column
        ra, rb, rc = self.slots
        view, slot, device = [
            lambda: (ref.at[:, 1 - c], ra, column.other()),
            lambda: (ref.at[yo, c, pl.ds(0, half)], rb.at[0], column.to(yn)),
            lambda: (ref.at[yo, c, pl.ds(half, half)], rb.at[1], column.to(yp)),
            lambda: (ref.at[yn, c], rc.at[0], column.to(yn)),
            lambda: (ref.at[yp, c], rc.at[1], column.to(yp)),
        ][i]()
        return send(view, slot, self.sems.at[0, i], self.sems.at[1, i], device)

    def some(self, k, base=0):
        return pl.ds(pl.multiple_of(base + k * self.group, self.group), self.group)

    def step(self, n):
        y, c = self.column.y, self.column.c
        yn, yp, yo = next_to(y)
        ref, (ra, rb, rc) = self.ref, self.slots
        low = ref.dtype
        half = self.count // 2
        groups = self.count // self.group
        if n == 0:
            self.message(0).start()
        elif n == 1:
            self.message(0).wait_recv()

            @pl.loop(0, 4 * groups)
            def _(k):
                j, r = k // groups, self.some(k % groups)
                ref[j, c, r] = (ref[j, c, r].astype(F32) + ra[j, r].astype(F32)).astype(low)

            self.message(1).start()
            self.message(2).start()
        elif n == 2:
            for side, to in ((0, yn), (1, yp)):
                self.message(1 + side).wait_recv()

                @pl.loop(0, groups // 2)
                def _(k):
                    r = self.some(k, side * half)
                    got = rb[side, self.some(k)].astype(F32)
                    ref[to, c, r] = (ref[to, c, r].astype(F32) + got).astype(low)

                self.message(3 + side).start()
        else:
            self.message(3).wait_recv()
            self.message(4).wait_recv()

            @pl.loop(0, groups)
            def _(k):
                r = self.some(k)
                total = ref[y, c, r].astype(F32) + rc[0, r].astype(F32) + rc[1, r].astype(F32)
                self.store(r, total)

            for i in range(5):
                self.message(i).wait_send()


def column_slots(shape, dtype=BF, lead=()):
    count, rest = shape[0], shape[1:]
    return [
        pltpu.VMEM((*lead, 4, count, *rest), dtype),
        pltpu.VMEM((*lead, 2, count // 2, *rest), dtype),
        pltpu.VMEM((*lead, 2, count, *rest), dtype),
    ]


def turned(v, cosine, sine):
    a, b = v[:32], v[32:]
    return jnp.concatenate([a * cosine - b * sine, b * cosine + a * sine], axis=0)


def inverse_rms(v, axis):
    return lax.rsqrt(jnp.mean(v * v, axis=axis, keepdims=True) + EPSILON)


def head_gain(small_t, row):
    pieces = [small_t[:, 128 * b : 128 * (b + 1)] for b in range(8)]
    tall = jnp.concatenate([piece.T[:8] for piece in pieces], axis=0)
    return jnp.broadcast_to(tall[:, row : row + 1], (64, 128))


def document_bias(seg_ref, bias, mb, mine):
    own = seg_ref[mb, mine].astype(F32)
    for b in range(8):
        keys = jnp.broadcast_to(seg_ref[mb, b].astype(F32), (128, 128)).T
        bias[mb, 128 * b : 128 * (b + 1)] = jnp.where(keys == own, 0.0, MASKED).astype(bias.dtype)


def pair_columns(ref, mb, g):
    both = ref[mb, pl.ds(pl.multiple_of(g * 128, 128), 128)]
    return jnp.concatenate([both[:64], both[64:]], axis=1)


def front_kernel(
    tok, cot, wq, wo, small, seg_ref, routes_ref, turn_hbm,
    dy_all, x0_all, wq_out, wo_out, kv_out, raw_out,
    small_t, q_t, mix_t, lsum, res, ffn, gates_t, sent,
    wq_all, wo_all, kv_all, raw_t, small_all, normed, bias, turn, plane_sems, column_sems, local,
):
    plane, column = Plane(), Column()
    y, c = column.y, column.c
    copies = [
        pltpu.make_async_copy(small, small_all.at[y, c], local.at[0]),
        pltpu.make_async_copy(wq.at[:, 1024:2048], wq_all.at[1, y, c], local.at[1]),
        pltpu.make_async_copy(cot.at[0], dy_all.at[0, plane.z, plane.x], local.at[2]),
        pltpu.make_async_copy(wq.at[:, 0:1024], wq_all.at[0, y, c], local.at[3]),
        pltpu.make_async_copy(cot.at[1], dy_all.at[1, plane.z, plane.x], local.at[4]),
        pltpu.make_async_copy(wo, wo_all.at[y, c], local.at[5]),
        pltpu.make_async_copy(turn_hbm.at[column.me], turn, local.at[6]),
    ]
    for copy in copies:
        copy.start()
    outs = [
        pltpu.make_async_copy(wq_all, wq_out, local.at[7]),
        pltpu.make_async_copy(wo_all, wo_out, local.at[8]),
        pltpu.make_async_copy(kv_all, kv_out, local.at[9]),
        pltpu.make_async_copy(raw_t, raw_out, local.at[10]),
    ]
    own_x = pltpu.make_async_copy(ffn.at[0], x0_all.at[plane.z, plane.x], local.at[11])
    greet(plane.neighbours() + column.neighbours())
    gdy = [Gather(plane, dy_all.at[mb], plane_sems.at[mb]) for mb in range(2)]
    gx = Gather(plane, x0_all, plane_sems.at[2])
    w_small = ColumnGather(column, small_all, column_sems.at[0], 64)
    w_q = ColumnGather(column, wq_all.at[0], column_sems.at[1], 128)
    w_kv = ColumnGather(column, wq_all.at[1], column_sems.at[2], 128)
    w_o = ColumnGather(column, wo_all, column_sems.at[3], 128)
    kv = [ColumnGather(column, kv_all.at[mb], column_sems.at[4 + mb], 8) for mb in range(2)]
    copies[0].wait()
    w_small.step(0)
    copies[1].wait()
    w_kv.step(0)
    copies[2].wait()
    gdy[0].step(0)
    for mb in range(2):
        document_bias(seg_ref, bias, mb, column.me)
    w_small.step(1)
    w_small.step(2)
    w_small.step(3)
    for b in range(8):
        small_t[:, 128 * b : 128 * (b + 1)] = small_all[b // 2, b % 2].astype(F32)
    attn_gain = small_t[32:33]
    for mb in range(2):
        v = tok[mb].astype(F32)
        normed[128 * mb : 128 * (mb + 1)] = (v * inverse_rms(v, 1) * attn_gain).astype(BF)
    w_kv.step(1)
    gdy[0].step(1)
    copies[4].wait()
    gdy[1].step(0)
    w_kv.step(2)
    copies[3].wait()
    w_q.step(0)
    gdy[0].step(2)
    w_kv.step(3)

    def project(k):
        @pl.loop(0, 2)
        def _(n):
            cols = pl.ds(pl.multiple_of(n * 512, 512), 512)
            rows = pl.ds(pl.multiple_of(1024 * k + n * 512, 512), 512)
            got = nn(normed[...], wq_all[k, :, :, :, cols].reshape(1024, 512))
            for mb in range(2):
                raw_t[mb, rows] = got[128 * mb : 128 * (mb + 1)].T

    query_gain = head_gain(small_t[...], 34)
    key_gain = head_gain(small_t[...], 35)
    copies[6].wait()
    cosine, sine = turn[:32], turn[32:]

    def key_heads(mb):
        @pl.loop(0, 8)
        def _(g):
            v = raw_t[mb, pl.ds(pl.multiple_of(1024 + g * 64, 64), 64)]
            key = turned(v * inverse_rms(v, 0) * key_gain, cosine, sine)
            value = raw_t[mb, pl.ds(pl.multiple_of(1536 + g * 64, 64), 64)]
            kv_all[mb, y, c, g] = jnp.concatenate([key, value], axis=0).T.astype(BF)

    def query_heads(mb):
        @pl.loop(0, 16)
        def _(h):
            rows = pl.ds(pl.multiple_of(h * 64, 64), 64)
            v = raw_t[mb, rows]
            query = turned(v * inverse_rms(v, 0) * query_gain, cosine, sine)
            q_t[mb, rows] = (query.astype(BF).astype(F32) * HD ** (-0.5)).astype(BF)

    def attend(mb, start, stop):
        @pl.loop(start, stop)
        def _(g):
            query = pair_columns(q_t, mb, g)
            query = jnp.concatenate([query, jnp.zeros_like(query)], axis=0)
            total = jnp.zeros((1, 256), F32)
            mixed = jnp.zeros((128, 256), F32)
            for j in range(4):
                keys = kv_all[mb, j, :, g].reshape(256, 128)
                there = bias[mb, 256 * j : 256 * (j + 1)].astype(F32)
                p = jnp.exp(nn(keys, query) + jnp.concatenate([there, there], axis=1))
                total += jnp.sum(p, axis=0, keepdims=True)
                mixed += tn(keys, p.astype(BF))
            lsum[mb, g] = total
            mixed = (mixed[64:] / total).astype(BF)
            both = jnp.concatenate([mixed[:, :128], mixed[:, 128:]], axis=0)
            mix_t[mb, pl.ds(pl.multiple_of(g * 128, 128), 128)] = both

    def finish(mb):
        @pl.loop(0, 2)
        def _(n):
            cols = pl.ds(pl.multiple_of(n * 512, 512), 512)
            got = tn(mix_t[mb], wo_all[:, :, :, cols].reshape(1024, 512))
            res[mb, :, cols] = tok[mb, :, cols].astype(F32) + got

        v = res[mb]
        low = (v * inverse_rms(v, 1) * small_t[33:34]).astype(BF)
        ffn[mb] = low
        logits = nt(small_t[:32].astype(BF), low)
        ids = lax.broadcasted_iota(jnp.int32, (32, 128), 0)
        routed = ids == routes_ref[mb, 0:1]
        for k in range(1, 8):
            routed = routed | (ids == routes_ref[mb, k : k + 1])
        top = jnp.max(jnp.where(routed, logits, MASKED), axis=0, keepdims=True)
        weight = jnp.where(routed, jnp.exp(logits - top), 0.0)
        gates = weight / jnp.sum(weight, axis=0, keepdims=True)
        gates_t[mb] = gates
        for k in range(16):
            sent[k, 2 * mb : 2 * mb + 2] = gates[2 * k : 2 * k + 2]

    project(1)
    key_heads(0)
    kv[0].step(0)
    w_q.step(1)
    key_heads(1)
    kv[0].step(1)
    w_q.step(2)
    copies[5].wait()
    w_o.step(0)
    sent[...] = jnp.zeros_like(sent)
    w_q.step(3)
    outs[0].start()
    project(0)
    outs[3].start()
    kv[0].step(2)
    kv[1].step(0)
    gdy[1].step(1)
    query_heads(0)
    kv[0].step(3)
    attend(0, 0, 4)
    w_o.step(1)
    gdy[0].step(3)
    attend(0, 4, 8)
    w_o.step(2)
    kv[1].step(1)
    gdy[0].step(4)
    query_heads(1)
    w_o.step(3)
    outs[1].start()
    finish(0)
    own_x.start()
    kv[1].step(2)
    gdy[1].step(2)
    own_x.wait()
    gx.step(0)
    kv[1].step(3)
    outs[2].start()
    attend(1, 0, 4)
    gx.step(1)
    attend(1, 4, 8)
    gx.step(2)
    gdy[1].step(3)
    finish(1)
    gdy[1].step(4)
    gx.step(3)
    gx.step(4)
    for copy in outs:
        copy.wait()


def front(tok, cot, wq, wo, small, seg, routes_t, turn):
    vmem = pl.BlockSpec(memory_space=pltpu.VMEM)
    anywhere = pl.BlockSpec(memory_space=pl.ANY)
    return pl.pallas_call(
        front_kernel,
        out_shape=(
            jax.ShapeDtypeStruct((2, 4, 4, 128, 1024), BF),
            jax.ShapeDtypeStruct((4, 4, 128, 1024), BF),
            jax.ShapeDtypeStruct((2, 4, 2, 128, 1024), BF),
            jax.ShapeDtypeStruct((4, 2, 128, 1024), BF),
            jax.ShapeDtypeStruct((2, 4, 2, 8, 128, 128), BF),
            jax.ShapeDtypeStruct((2, 2048, 128), F32),
            jax.ShapeDtypeStruct((64, 1024), F32),
            jax.ShapeDtypeStruct((2, 1024, 128), BF),
            jax.ShapeDtypeStruct((2, 1024, 128), BF),
            jax.ShapeDtypeStruct((2, 8, 1, 256), F32),
            jax.ShapeDtypeStruct((2, 128, 1024), F32),
            jax.ShapeDtypeStruct((2, 128, 1024), BF),
            jax.ShapeDtypeStruct((2, 32, 128), F32),
            jax.ShapeDtypeStruct((16, 8, 128), F32),
        ),
        in_specs=[vmem, vmem, anywhere, anywhere, anywhere, vmem, vmem, anywhere],
        out_specs=(anywhere,) * 6 + (vmem,) * 8,
        scratch_shapes=[
            pltpu.VMEM((2, 4, 2, 128, 1024), BF),
            pltpu.VMEM((4, 2, 128, 1024), BF),
            pltpu.VMEM((2, 4, 2, 8, 128, 128), BF),
            pltpu.VMEM((2, 2048, 128), F32),
            pltpu.VMEM((4, 2, 64, 128), BF),
            pltpu.VMEM((256, 1024), BF),
            pltpu.VMEM((2, 1024, 128), F32),
            pltpu.VMEM((64, 128), F32),
            pltpu.SemaphoreType.DMA((3, 2, 2, 8)),
            pltpu.SemaphoreType.DMA((6, 2, 8)),
            pltpu.SemaphoreType.DMA((12,)),
        ],
        compiler_params=pltpu.CompilerParams(
            collective_id=0, has_side_effects=True, vmem_limit_bytes=56 * MIB
        ),
        cost_estimate=pl.CostEstimate(
            flops=5_000_000_000, bytes_accessed=30_000_000, transcendentals=5_000_000
        ),
    )(tok, cot, wq, wo, small, seg, routes_t, turn)


def moe_kernel(
    ffn_ref, x0_hbm, dy_hbm, gates_ref, wgu_hbm, wd_hbm,
    out_hbm, dx_ref, h_ref, dw_own,
    dw, x_all, dy_all, r1, r2, r3, r4, xs, ds, os, gc, act, a1, a2, ggu, g_all, ranks, hcol, hs,
    wgu, wd, ra, rb, rc, sems, column_sems, gsend, grecv, hsend, hrecv, free, local,
):
    plane, column = Plane(), Column()
    me, z, x = plane.me, plane.z, plane.x
    w1 = pltpu.make_async_copy(wgu_hbm, wgu, local.at[0])
    w2 = pltpu.make_async_copy(wd_hbm, wd, local.at[1])
    w1.start()
    w2.start()
    own = [
        pltpu.make_async_copy(ffn_ref.at[1], x_all.at[1, z, x], local.at[4]),
        pltpu.make_async_copy(x0_hbm, x_all.at[0], local.at[5]),
    ]
    outs = [pltpu.make_async_copy(x_all.at[mb], out_hbm.at[mb], local.at[6 + mb]) for mb in range(2)]
    dys = [pltpu.make_async_copy(dy_hbm.at[mb], dy_all.at[mb], local.at[2 + mb]) for mb in range(2)]
    for copy in own + dys:
        copy.start()
    greet(plane.others() + column.neighbours())
    own[0].wait()

    def gate_message(step):
        to = (me + step) % 16
        return pltpu.make_async_remote_copy(
            src_ref=gates_ref.at[to], dst_ref=g_all.at[me],
            send_sem=gsend.at[step], recv_sem=grecv.at[step], device_id={"expert": to},
        )

    def h_message(step):
        to = (me + step) % 16
        return pltpu.make_async_remote_copy(
            src_ref=hs.at[to], dst_ref=h_ref.at[me],
            send_sem=hsend.at[step], recv_sem=hrecv.at[step], device_id={"expert": to},
        )

    for step in range(1, 16):
        gate_message(step).start()
    g_all[me] = gates_ref[me]
    gx = Gather(plane, x_all.at[1], sems.at[0])
    gx.step(0)

    def into(mb):
        def store(place, rows, total):
            dx_ref[mb, rows] = total

        return store

    sdx = [
        Scatter(plane, dy_all.at[mb], (r1, r2, r3, r4), sems.at[1 + mb], into(mb), free)
        for mb in range(2)
    ]

    def own_part(k):
        def store(r, total):
            dw_own[k, r] = total.astype(BF)

        return store

    dsum = [
        ColumnScatter(
            column, dw.at[k], (ra.at[k], rb.at[k], rc.at[k]), column_sems.at[k], 128, own_part(k)
        )
        for k in range(3)
    ]
    for step in range(1, 16):
        gate_message(step).wait_recv()
    for step in range(1, 16):
        gate_message(step).wait_send()

    earlier = (
        lax.broadcasted_iota(jnp.int32, (128, 128), 0)
        < lax.broadcasted_iota(jnp.int32, (128, 128), 1)
    ).astype(F32).astype(BF)

    @pl.loop(0, 16)
    def _(s):
        named = g_all[s] > 0.0
        before = nn(named.astype(F32).astype(BF), earlier)
        ranks[s] = jnp.where(named, before, -1.0)

    slot_ids = lax.broadcasted_iota(jnp.int32, (SLOTS, 128), 0).astype(F32)

    def places(s, mb):
        r = ranks[s]
        return [(slot_ids == r[2 * mb + e : 2 * mb + e + 1]).astype(F32) for e in range(2)]

    def gated(s, mb, hot):
        g = g_all[s]
        return [hot[e] * g[2 * mb + e : 2 * mb + e + 1] for e in range(2)]

    def span(s):
        return pl.ds(pl.multiple_of(s * SLOTS, 16), SLOTS)

    def select(mb):
        @pl.loop(0, 16)
        def _(s):
            hot = places(s, mb)
            pick = jnp.concatenate(hot, axis=0).astype(BF)
            scaled = jnp.concatenate(gated(s, mb, hot), axis=0).astype(BF)
            rows = nn(pick, x_all[mb, s // 4, s % 4]).astype(BF)
            drows = nn(scaled, dy_all[mb, s // 4, s % 4]).astype(BF)
            for e in range(2):
                xs[e, span(s)] = rows[SLOTS * e : SLOTS * (e + 1)]
                ds[e, span(s)] = drows[SLOTS * e : SLOTS * (e + 1)]

    chunks = 16 * SLOTS // CHUNK

    def forward(e):
        @pl.loop(0, chunks)
        def _(c):
            r = pl.ds(pl.multiple_of(c * CHUNK, CHUNK), CHUNK)
            gu = nn(xs[e, r], wgu[e])
            g, u = gu[:, :512], gu[:, 512:]
            sig = 1.0 / (1.0 + jnp.exp(-g))
            silu = g * sig
            active = (silu * u).astype(BF)
            act[e, r] = active
            a1[e, r] = (u * sig * (1.0 + g * (1.0 - sig))).astype(BF)
            a2[e, r] = silu.astype(BF)
            o = nn(active, wd[e]).astype(BF)
            os[e, r] = o
            hcol[e, r] = jnp.sum(o.astype(F32) * ds[e, r].astype(F32), axis=-1, keepdims=True)

    def combine_out(mb):
        @pl.loop(0, 16)
        def _(s):
            hot = places(s, mb)
            scaled = jnp.concatenate(gated(s, mb, hot), axis=0).astype(BF)
            both = jnp.concatenate([os[0, span(s)], os[1, span(s)]], axis=0)
            x_all[mb, s // 4, s % 4] = tn(scaled, both).astype(BF)
            for e in range(2):
                row = 2 * mb + e
                hs[s, row : row + 1] = jnp.sum(hot[e] * hcol[e, span(s)], axis=0, keepdims=True)

    def add_part(mb, k, n, fresh):
        fresh = fresh.reshape(2, 128, 1024)
        if mb == 1:
            fresh += dw[k, n].astype(F32)
        dw[k, n] = fresh.astype(BF)

    def backward(mb, e):
        @pl.loop(0, chunks)
        def _(c):
            r = pl.ds(pl.multiple_of(c * CHUNK, CHUNK), CHUNK)
            ga = nt(ds[e, r], wd[e])
            grad = jnp.concatenate(
                [ga * a1[e, r].astype(F32), ga * a2[e, r].astype(F32)], axis=1
            ).astype(BF)
            ggu[r] = grad
            gc[e, r] = nt(grad, wgu[e]).astype(BF)

        @pl.loop(0, 4)
        def _(m):
            cols = pl.ds(pl.multiple_of(m * 256, 256), 256)
            add_part(mb, e, m, tn(xs[e, :, cols], ggu[...]))

        @pl.loop(0, 2)
        def _(m):
            cols = pl.ds(pl.multiple_of(m * 256, 256), 256)
            add_part(mb, 2, 2 * e + m, tn(act[e, :, cols], ds[e]))

    def combine_dx(mb):
        @pl.loop(0, 16)
        def _(s):
            pick = jnp.concatenate(places(s, mb), axis=0).astype(BF)
            both = jnp.concatenate([gc[0, span(s)], gc[1, span(s)]], axis=0)
            dy_all[mb, s // 4, s % 4] = tn(pick, both).astype(BF)

    own[1].wait()
    for copy in dys:
        copy.wait()
    select(0)
    gx.step(1)
    w1.wait()
    w2.wait()
    forward(0)
    gx.step(2)
    forward(1)
    backward(0, 0)
    gx.step(3)
    backward(0, 1)
    combine_dx(0)
    sdx[0].step(0)
    gx.step(4)
    combine_out(0)
    outs[0].start()
    sdx[0].step(1)
    select(1)
    forward(0)
    sdx[0].step(2)
    backward(1, 0)
    dsum[0].step(0)
    sdx[0].step(3)
    forward(1)
    dsum[0].step(1)
    sdx[0].step(4)
    sdx[0].give_credit()
    backward(1, 1)
    dsum[1].step(0)
    dsum[2].step(0)
    dsum[0].step(2)
    combine_dx(1)
    sdx[1].take_credit()
    sdx[1].step(0)
    dsum[1].step(1)
    dsum[2].step(1)
    combine_out(1)
    outs[1].start()
    sdx[1].step(1)
    dsum[0].step(3)
    h_ref[me] = hs[me]
    for step in range(1, 16):
        h_message(step).start()
    dsum[1].step(2)
    sdx[1].step(2)
    dsum[2].step(2)
    dsum[1].step(3)
    sdx[1].step(3)
    dsum[2].step(3)
    sdx[1].step(4)
    for step in range(1, 16):
        h_message(step).wait_recv()
    for step in range(1, 16):
        h_message(step).wait_send()
    for copy in outs:
        copy.wait()


def moe(ffn, x0, dy, gates, w_gate_up, w_down):
    vmem = pl.BlockSpec(memory_space=pltpu.VMEM)
    anywhere = pl.BlockSpec(memory_space=pl.ANY)
    rows = 16 * SLOTS
    return pl.pallas_call(
        moe_kernel,
        out_shape=(
            jax.ShapeDtypeStruct((2, 4, 4, 128, 1024), BF),
            jax.ShapeDtypeStruct((2, 128, 1024), F32),
            jax.ShapeDtypeStruct((16, 8, 128), F32),
            jax.ShapeDtypeStruct((3, 128, 1024), BF),
        ),
        in_specs=[anywhere, anywhere, anywhere, vmem, anywhere, anywhere],
        out_specs=(anywhere,) + (vmem,) * 3,
        scratch_shapes=[
            pltpu.VMEM((3, 4, 2, 128, 1024), BF),
            pltpu.VMEM((2, 4, 4, 128, 1024), BF),
            pltpu.VMEM((2, 4, 4, 128, 1024), BF),
            *scatter_slots(128, 1024),
            pltpu.VMEM((2, rows, 1024), BF),
            pltpu.VMEM((2, rows, 1024), BF),
            pltpu.VMEM((2, rows, 1024), BF),
            pltpu.VMEM((2, rows, 1024), BF),
            pltpu.VMEM((2, rows, 512), BF),
            pltpu.VMEM((2, rows, 512), BF),
            pltpu.VMEM((2, rows, 512), BF),
            pltpu.VMEM((rows, 1024), BF),
            pltpu.VMEM((16, 8, 128), F32),
            pltpu.VMEM((16, 8, 128), F32),
            pltpu.VMEM((2, rows, 1), F32),
            pltpu.VMEM((16, 8, 128), F32),
            pltpu.VMEM((2, 1024, 1024), BF),
            pltpu.VMEM((2, 512, 1024), BF),
            *column_slots((128, 1024), lead=(3,)),
            pltpu.SemaphoreType.DMA((3, 2, 2, 8)),
            pltpu.SemaphoreType.DMA((3, 2, 8)),
            pltpu.SemaphoreType.DMA((16,)),
            pltpu.SemaphoreType.DMA((16,)),
            pltpu.SemaphoreType.DMA((16,)),
            pltpu.SemaphoreType.DMA((16,)),
            pltpu.SemaphoreType.REGULAR,
            pltpu.SemaphoreType.DMA((8,)),
        ],
        compiler_params=pltpu.CompilerParams(
            collective_id=1, has_side_effects=True, vmem_limit_bytes=63 * MIB
        ),
        cost_estimate=pl.CostEstimate(
            flops=30_000_000_000, bytes_accessed=30_000_000, transcendentals=2_000_000
        ),
    )(ffn, x0, dy, gates, w_gate_up, w_down)


def norm_grad(grad, v, inverse, gain, axis):
    scaled = grad * gain
    moment = jnp.mean(scaled * v, axis=axis, keepdims=True)
    return inverse * (scaled - v * (inverse * inverse * moment)), grad * (v * inverse)


def back_kernel(
    tok, cot, seg_ref, turn_hbm, wq_hbm, wo_hbm, small_t, raw_hbm, q_t, kv_hbm, mix_t, lsum,
    res, ffn, gates_t, share_ref, dx, out_hbm, dw_own,
    dgu_all, dd_all, output, in_grad, gq, go, gs,
    wq_all, wo_all, kv_all, raw_t, turn, bias, gres, branch, gm_t, dq_t, own_kv, gp, normed_t, gn,
    part_kv, part_w, part_s, q_sum, k_sum, ra, rb, rc, sa, sb, sc, plane_buf, plane_all, p1, p2, p3, p4, ta, tb, tc,
    logits, routers, router_sum, out_part, r1, r2, r3, r4, parcels, got_parcels, small_own, kv_total,
    column_sems, plane_sems, far_send, far_recv, all_send, all_recv, free, local,
):
    plane, column = Plane(), Column()
    y, c = column.y, column.c
    copies = [
        pltpu.make_async_copy(wo_hbm, wo_all, local.at[0]),
        pltpu.make_async_copy(kv_hbm, kv_all, local.at[1]),
        pltpu.make_async_copy(raw_hbm, raw_t, local.at[2]),
        pltpu.make_async_copy(wq_hbm, wq_all, local.at[3]),
        pltpu.make_async_copy(turn_hbm.at[column.me], turn, local.at[4]),
    ]
    parts = [pltpu.make_async_copy(out_hbm.at[mb], out_part, local.at[5 + mb]) for mb in range(2)]
    dw_refs = [dgu_all.at[0], dgu_all.at[1], dd_all]
    owns = [pltpu.make_async_copy(dw_own.at[n], dw_refs[n].at[y, c], local.at[7 + n]) for n in range(3)]
    for copy in parts[:1] + owns + copies:
        copy.start()
    greet(plane.others() + column.neighbours())
    dall = [ColumnGather(column, dw_refs[n], column_sems.at[8 + n], 128) for n in range(3)]

    def add_residual(mb):
        def store(place, rows, total):
            output[mb, rows] = (res[mb, rows] + total).astype(BF)

        return store

    sout = [
        Scatter(plane, out_part, (r1, r2, r3, r4), plane_sems.at[mb], add_residual(mb), free)
        for mb in range(2)
    ]
    parts[0].wait()
    sout[0].step(0)
    for copy in owns:
        copy.wait()
    dall[0].step(0)
    part_s[...] = jnp.zeros_like(part_s)
    q_sum[...] = jnp.zeros_like(q_sum)
    k_sum[...] = jnp.zeros_like(k_sum)
    for mb in range(2):
        document_bias(seg_ref, bias, mb, column.me)

    def place_w(which):
        def store(r, total):
            low = total.astype(BF)
            half = r.start // 64
            some = pl.ds(pl.multiple_of(r.start % 64, 16), 16)
            for k in range(8):
                n = half * 8 + k
                piece = low[:, 128 * k : 128 * (k + 1)]
                if which == 2:
                    parcels[n, some] = piece
                else:
                    plane_buf[which, n // 4, n % 4, some] = piece

        return store

    def place_s(r, total):
        small_own[r] = total.astype(BF)

    def place_kv(mb, half):
        def store(r, total):
            own_kv[mb, pl.ds(r.start + 4 * half, 1)] = total

        return store

    w_sums = [
        ColumnScatter(
            column, part_w.at[n], (ra.at[n], rb.at[n], rc.at[n]), column_sems.at[n], 128, place_w(n)
        )
        for n in range(3)
    ]
    kv_sums = [
        [
            ColumnScatter(
                column, part_kv.at[mb, half],
                (sa.at[mb, half], sb.at[mb, half], sc.at[mb, half]),
                column_sems.at[4 + 2 * mb + half], 4, place_kv(mb, half), group=1,
            )
            for half in range(2)
        ]
        for mb in range(2)
    ]
    s_sum = ColumnScatter(column, part_s, (ta, tb, tc), column_sems.at[3], 64, place_s)

    def keep(n):
        def store(place, rows, total):
            plane_all[(n, *place)] = total.astype(BF)

        return store

    over = [
        Scatter(
            plane, plane_buf.at[n], (p1.at[n], p2.at[n], p3.at[n], p4.at[n]), plane_sems.at[2 + n],
            keep(n), height=64,
        )
        for n in range(2)
    ]
    spread = [Gather(plane, plane_all.at[n], plane_sems.at[4 + n], height=64) for n in range(2)]

    def tokens_of(mb):
        return pl.ds(128 * mb, 128)

    router = small_t[:32].astype(BF)
    ffn_gain, attn_gain = small_t[33:34], small_t[32:33]
    routers[0:32] = router
    routers[32:64] = router
    ffn_gain_grad = jnp.zeros((1, 1024), F32)
    for mb in range(2):
        share = jnp.concatenate([share_ref[k, 2 * mb : 2 * mb + 2] for k in range(16)], axis=0)
        logit = share - gates_t[mb] * jnp.sum(share, axis=0, keepdims=True)
        high = logit.astype(BF)
        logits[0:32, tokens_of(mb)] = high
        logits[32:64, tokens_of(mb)] = (logit - high.astype(F32)).astype(BF)

    @pl.loop(0, 4)
    def _(n):
        cols = pl.ds(pl.multiple_of(n * 256, 256), 256)
        gn[:, cols] = tn(logits[...], routers[:, cols])
        router_sum[:, cols] = nn(logits[...], ffn[:, :, cols].reshape(256, 256))

    for mb in range(2):
        into = dx[mb] + gn[tokens_of(mb)]
        v = res[mb]
        inv = inverse_rms(v, 1)
        grad, gain = norm_grad(into, v, inv, ffn_gain, 1)
        ffn_gain_grad += jnp.sum(gain, axis=0, keepdims=True)
        total = cot[mb].astype(F32) + grad
        gres[mb] = total
        branch[128 * mb : 128 * (mb + 1)] = total.astype(BF)
    copies[0].wait()

    @pl.loop(0, 4)
    def _(n):
        rows = pl.ds(pl.multiple_of(n * 256, 256), 256)
        got = nt(wo_all[n].reshape(256, 1024), branch[...])
        gm_t[0, rows] = got[:, :128].astype(BF)
        gm_t[1, rows] = got[:, 128:].astype(BF)
        mixed = jnp.concatenate([mix_t[0, rows], mix_t[1, rows]], axis=1)
        part_w[0, n] = nn(mixed, branch[...]).astype(BF).reshape(2, 128, 1024)

    w_sums[0].step(0)
    dall[1].step(0)
    copies[1].wait()

    def attend(mb, start, stop):
        @pl.loop(start, stop)
        def _(g):
            query = pair_columns(q_t, mb, g)
            grad = pair_columns(gm_t, mb, g)
            mixed = pair_columns(mix_t, mb, g)
            blank = jnp.zeros_like(query)
            inner = jnp.sum(grad.astype(F32) * mixed.astype(F32), axis=0, keepdims=True)
            query = jnp.concatenate([query, blank], axis=0)
            grad = jnp.concatenate([blank, grad], axis=0)
            both = jnp.concatenate([query, grad], axis=1)
            scale = 1.0 / lsum[mb, g]
            dq = jnp.zeros((128, 256), F32)
            for j in range(4):
                keys = kv_all[mb, j, :, g].reshape(256, 128)
                there = bias[mb, 256 * j : 256 * (j + 1)].astype(F32)
                got = nn(keys, both)
                p = jnp.exp(got[:, :256] + jnp.concatenate([there, there], axis=1)) * scale
                ds = (p * (got[:, 256:] - inner)).astype(BF)
                dq += tn(keys, ds)
                dkv = nt(jnp.concatenate([ds, p.astype(BF)], axis=1), both)
                part_kv[mb, g // 4, j, :, g % 4] = dkv.astype(BF).reshape(2, 128, 128)
            dq = dq[:64] * HD ** (-0.5)
            rows = pl.ds(pl.multiple_of(g * 128, 128), 128)
            dq_t[mb, rows] = jnp.concatenate([dq[:, :128], dq[:, 128:]], axis=0)

    attend(0, 0, 2)
    dall[0].step(1)
    sout[0].step(1)
    attend(0, 2, 4)
    kv_sums[0][0].step(0)
    w_sums[0].step(1)
    dall[0].step(2)
    dall[1].step(1)
    dall[2].step(0)
    attend(0, 4, 6)
    kv_sums[0][0].step(1)
    sout[0].step(2)
    attend(0, 6, 8)
    kv_sums[0][1].step(0)
    w_sums[0].step(2)
    dall[1].step(2)
    dall[2].step(1)
    attend(1, 0, 2)
    kv_sums[0][1].step(1)
    kv_sums[0][0].step(2)
    sout[0].step(3)
    dall[0].step(3)
    attend(1, 2, 4)
    kv_sums[1][0].step(0)
    w_sums[0].step(3)
    sout[0].step(4)
    parts[1].start()
    sout[0].give_credit()
    dall[2].step(2)
    attend(1, 4, 6)
    kv_sums[1][0].step(1)
    kv_sums[0][1].step(2)
    kv_sums[0][0].step(3)
    over[0].step(0)
    parts[1].wait()
    sout[1].take_credit()
    sout[1].step(0)
    attend(1, 6, 8)
    kv_sums[1][1].step(0)
    dall[1].step(3)
    over[0].step(1)
    copies[2].wait()
    copies[4].wait()
    cosine, sine = turn[:32], turn[32:]
    query_gain = head_gain(small_t[...], 34)
    key_gain = head_gain(small_t[...], 35)

    def head_back(grad, v, gain, total):
        inv = inverse_rms(v, 0)
        grad = turned(grad, cosine, -sine)
        grad_v, gain_part = norm_grad(grad, v, inv, gain, 0)
        total[...] += gain_part
        return grad_v

    def queries_back(mb):
        @pl.loop(0, 8)
        def _(g):
            pieces = []
            for r in range(2):
                rows = pl.ds(pl.multiple_of(g * 128 + r * 64, 64), 64)
                pieces.append(head_back(dq_t[mb, rows], raw_t[mb, rows], query_gain, q_sum))
            cols = pl.ds(pl.multiple_of(g * 128, 128), 128)
            gp[tokens_of(mb), cols] = jnp.concatenate(pieces, axis=0).T.astype(BF)

    queries_back(0)
    kv_sums[1][1].step(1)
    kv_sums[1][0].step(2)
    queries_back(1)
    kv_sums[0][1].step(3)
    over[0].step(2)
    sout[1].step(1)
    dall[2].step(3)
    for mb in range(2):
        v = tok[mb].astype(F32)
        normed = (v * inverse_rms(v, 1) * attn_gain).astype(BF).astype(F32)
        for k in range(8):
            normed_t[128 * k : 128 * (k + 1), tokens_of(mb)] = (
                normed[:, 128 * k : 128 * (k + 1)].T.astype(BF)
            )

    def weight_part(which):
        cols = pl.ds(1024 * (which - 1), 1024)

        @pl.loop(0, 4)
        def _(n):
            rows = pl.ds(pl.multiple_of(n * 256, 256), 256)
            part_w[which, n] = nn(normed_t[rows], gp[:, cols]).astype(BF).reshape(2, 128, 1024)

    def keys_back(mb):
        @pl.loop(0, 4)
        def _(k):
            keys, values = [], []
            for r in range(2):
                g = 2 * k + r
                grad = own_kv[mb, g].T
                rows = pl.ds(pl.multiple_of(1024 + g * 64, 64), 64)
                keys.append(head_back(grad[:64], raw_t[mb, rows], key_gain, k_sum))
                values.append(grad[64:])
            cols = pl.ds(pl.multiple_of(1024 + k * 128, 128), 128)
            gp[tokens_of(mb), cols] = jnp.concatenate(keys, axis=0).T.astype(BF)
            cols = pl.ds(pl.multiple_of(1536 + k * 128, 128), 128)
            gp[tokens_of(mb), cols] = jnp.concatenate(values, axis=0).T.astype(BF)

    weight_part(1)
    w_sums[1].step(0)
    kv_sums[1][1].step(2)
    kv_sums[1][0].step(3)
    over[0].step(3)
    keys_back(0)
    w_sums[1].step(1)
    sout[1].step(2)
    copies[3].wait()

    @pl.loop(0, 4)
    def _(n):
        cols = pl.ds(pl.multiple_of(n * 256, 256), 256)
        gn[:, cols] = nt(gp[:, 0:1024], wq_all[0, n].reshape(256, 1024))

    kv_sums[1][1].step(3)
    keys_back(1)
    weight_part(2)
    w_sums[2].step(0)
    w_sums[1].step(2)
    over[0].step(4)
    spread[0].step(0)
    sout[1].step(3)

    @pl.loop(0, 4)
    def _(n):
        cols = pl.ds(pl.multiple_of(n * 256, 256), 256)
        gn[:, cols] = gn[:, cols] + nt(gp[:, 1024:2048], wq_all[1, n].reshape(256, 1024))

    w_sums[2].step(1)
    w_sums[1].step(3)
    over[1].step(0)
    spread[0].step(1)
    attn_gain_grad = jnp.zeros((1, 1024), F32)
    for mb in range(2):
        v = tok[mb].astype(F32)
        grad, gain = norm_grad(gn[tokens_of(mb)], v, inverse_rms(v, 1), attn_gain, 1)
        attn_gain_grad += jnp.sum(gain, axis=0, keepdims=True)
        in_grad[mb] = (gres[mb] + grad).astype(BF)
    for b in range(8):
        cols = slice(128 * b, 128 * (b + 1))
        heads = slice(8 * b, 8 * (b + 1))
        part_s[b // 2, b % 2, 0:32] = router_sum[0:32, cols] + router_sum[32:64, cols]
        part_s[b // 2, b % 2, 32:33] = attn_gain_grad[:, cols]
        part_s[b // 2, b % 2, 33:34] = ffn_gain_grad[:, cols]
        part_s[b // 2, b % 2, 40:48] = jnp.broadcast_to(
            jnp.sum(q_sum[heads], axis=1, keepdims=True), (8, 128)
        )
        part_s[b // 2, b % 2, 48:56] = jnp.broadcast_to(
            jnp.sum(k_sum[heads], axis=1, keepdims=True), (8, 128)
        )
    s_sum.step(0)
    over[1].step(1)
    spread[0].step(2)
    s_sum.step(1)
    w_sums[2].step(2)
    s_sum.step(2)
    over[1].step(2)
    spread[0].step(3)
    sout[1].step(4)
    over[1].step(3)
    s_sum.step(3)
    w_sums[2].step(3)
    me = plane.me

    @pl.loop(0, 16)
    def _(n):
        parcels[n, 64:128] = small_own[...]

    def parcel(step):
        to = (me + step) % 16
        return send(
            parcels.at[to], got_parcels.at[me], far_send.at[step], far_recv.at[step], {"expert": to}
        )

    def total_message(step):
        to = (me + step) % 16
        return send(
            kv_total.at[me], kv_total.at[me], all_send.at[step], all_recv.at[step], {"expert": to}
        )

    for step in range(1, 16):
        parcel(step).start()
    got_parcels[me] = parcels[me]
    over[1].step(4)
    spread[1].step(0)
    spread[0].step(4)
    for step in range(1, 16):
        parcel(step).wait_recv()
    total = got_parcels[0].astype(F32)
    for n in range(1, 16):
        total += got_parcels[n].astype(F32)
    kv_total[me] = total[:64].astype(BF)
    for step in range(1, 16):
        total_message(step).start()
    gs[...] = total[64:]
    for n in range(16):
        place = slice(64 * (n // 8), 64 * (n // 8) + 64), slice(128 * (n % 8), 128 * (n % 8) + 128)
        go[place] = plane_all[0, n // 4, n % 4].astype(F32)
    for n in range(1, 5):
        spread[1].step(n)
    for n in range(16):
        place = slice(64 * (n // 8), 64 * (n // 8) + 64), slice(128 * (n % 8), 128 * (n % 8) + 128)
        gq[place] = plane_all[1, n // 4, n % 4].astype(F32)
    for step in range(1, 16):
        total_message(step).wait_recv()
    for n in range(16):
        first = 1024 + 128 * (n % 8)
        gq[64 * (n // 8) : 64 * (n // 8) + 64, first : first + 128] = kv_total[n].astype(F32)
    for step in range(1, 16):
        parcel(step).wait_send()
        total_message(step).wait_send()


def back(tok, cot, seg, turn, wq_all, wo_all, small_t, raw_t, q_t, kv_all, mix_t, lsum, res, ffn, gates_t, share, dx, out_part, dw_own):
    vmem = pl.BlockSpec(memory_space=pltpu.VMEM)
    anywhere = pl.BlockSpec(memory_space=pl.ANY)
    kv_slots = column_slots((4, 128, 128), lead=(2, 2))
    return pl.pallas_call(
        back_kernel,
        out_shape=(
            jax.ShapeDtypeStruct((2, 4, 2, 128, 1024), BF),
            jax.ShapeDtypeStruct((4, 2, 128, 1024), BF),
            jax.ShapeDtypeStruct((2, 128, 1024), BF),
            jax.ShapeDtypeStruct((2, 128, 1024), BF),
            jax.ShapeDtypeStruct((128, 2048), F32),
            jax.ShapeDtypeStruct((128, 1024), F32),
            jax.ShapeDtypeStruct((64, 128), F32),
        ),
        in_specs=[
            vmem, vmem, vmem, anywhere, anywhere, anywhere, vmem, anywhere, vmem, anywhere,
            vmem, vmem, vmem, vmem, vmem, vmem, vmem, anywhere, vmem,
        ],
        out_specs=(anywhere,) * 2 + (vmem,) * 5,
        scratch_shapes=[
            pltpu.VMEM((2, 4, 2, 128, 1024), BF),
            pltpu.VMEM((4, 2, 128, 1024), BF),
            pltpu.VMEM((2, 4, 2, 8, 128, 128), BF),
            pltpu.VMEM((2, 2048, 128), F32),
            pltpu.VMEM((64, 128), F32),
            pltpu.VMEM((2, 1024, 128), BF),
            pltpu.VMEM((2, 128, 1024), F32),
            pltpu.VMEM((256, 1024), BF),
            pltpu.VMEM((2, 1024, 128), BF),
            pltpu.VMEM((2, 1024, 128), F32),
            pltpu.VMEM((2, 8, 128, 128), F32),
            pltpu.VMEM((256, 2048), BF),
            pltpu.VMEM((1024, 256), BF),
            pltpu.VMEM((256, 1024), F32),
            pltpu.VMEM((2, 2, 4, 2, 4, 128, 128), BF),
            pltpu.VMEM((3, 4, 2, 128, 1024), BF),
            pltpu.VMEM((4, 2, 64, 128), F32),
            pltpu.VMEM((64, 128), F32),
            pltpu.VMEM((64, 128), F32),
            *column_slots((128, 1024), lead=(3,)),
            *kv_slots,
            pltpu.VMEM((2, 4, 4, 64, 128), BF),
            pltpu.VMEM((2, 4, 4, 64, 128), BF),
            *scatter_slots(64, 128, lead=(2,)),
            *column_slots((64, 128), F32),
            pltpu.VMEM((64, 256), BF),
            pltpu.VMEM((64, 1024), BF),
            pltpu.VMEM((64, 1024), F32),
            pltpu.VMEM((4, 4, 128, 1024), BF),
            *scatter_slots(128, 1024),
            pltpu.VMEM((16, 128, 128), BF),
            pltpu.VMEM((16, 128, 128), BF),
            pltpu.VMEM((64, 128), BF),
            pltpu.VMEM((16, 64, 128), BF),
            pltpu.SemaphoreType.DMA((11, 2, 8)),
            pltpu.SemaphoreType.DMA((6, 2, 2, 8)),
            pltpu.SemaphoreType.DMA((16,)),
            pltpu.SemaphoreType.DMA((16,)),
            pltpu.SemaphoreType.DMA((16,)),
            pltpu.SemaphoreType.DMA((16,)),
            pltpu.SemaphoreType.REGULAR,
            pltpu.SemaphoreType.DMA((10,)),
        ],
        compiler_params=pltpu.CompilerParams(
            collective_id=2, has_side_effects=True, vmem_limit_bytes=63 * MIB
        ),
        cost_estimate=pl.CostEstimate(
            flops=12_000_000_000, bytes_accessed=30_000_000, transcendentals=5_000_000
        ),
    )(tok, cot, seg, turn, wq_all, wo_all, small_t, raw_t, q_t, kv_all, mix_t, lsum, res, ffn, gates_t, share, dx, out_part, dw_own)


def turn_table(length):
    frequency = np.power(np.float32(THETA), -2.0 * np.arange(HD // 2, dtype=np.float32) / HD)
    angle = np.arange(length, dtype=np.float32)[:, None] * frequency.astype(np.float32)[None, :]
    both = np.concatenate([np.cos(angle), np.sin(angle)], axis=1).astype(np.float32)
    return both.reshape(length // 128, 128, HD).transpose(0, 2, 1)


def body(
    tokens,
    cotangent,
    segments,
    routes,
    w_qkv,
    w_out,
    attn_norm,
    ffn_norm,
    q_gain,
    k_gain,
    router,
    w_gate_up,
    w_down,
):
    tok = tokens.reshape(2, 128, 1024)
    cot = cotangent.reshape(2, 128, 1024)
    seg = segments.reshape(2, 8, 1, 128)
    routes_t = routes.reshape(2, 128, 8).transpose(0, 2, 1)
    turn = jnp.asarray(turn_table(1024))
    gains = jnp.pad(jnp.stack([q_gain, k_gain]), ((0, 28), (0, 120)))
    small = jnp.concatenate([router.T, attn_norm[None], ffn_norm[None], gains])
    (
        dy_all, x0, wq_all, wo_all, kv_all, raw_t, small_t, q_t, mix_t, lsum, res, ffn, gates_t, sent
    ) = front(tok, cot, w_qkv, w_out, small, seg, routes_t, turn)
    out_part, moved_dx, share, dw_own = moe(ffn, x0, dy_all, sent, w_gate_up, w_down)
    dgu, dd, output, in_grad, gq, go, gs = back(
        tok, cot, seg, turn, wq_all, wo_all, small_t, raw_t, q_t, kv_all, mix_t, lsum, res, ffn,
        gates_t, share, moved_dx, out_part, dw_own,
    )
    return (
        output.reshape(tokens.shape),
        in_grad.reshape(tokens.shape),
        gq,
        go,
        gs[32],
        gs[33],
        gs[40:48, 0],
        gs[48:56, 0],
        gs[:32].T,
        dgu.astype(F32).reshape(2, 1024, 1024),
        dd.astype(F32).reshape(2, 512, 1024),
    )


def solution(mesh):
    return jax.shard_map(
        body,
        mesh=mesh,
        in_specs=(
            P(None, "expert", "dp", None),
            P(None, "expert", "dp", None),
            P(None, "expert", None),
            P(None, "expert", "dp", None),
            P("dp", None),
            P("dp", None),
            P("dp"),
            P("dp"),
            P("dp"),
            P("dp"),
            P("dp", None),
            P("expert", None, None),
            P("expert", None, None),
        ),
        out_specs=(
            P(None, "expert", "dp", None),
            P(None, "expert", "dp", None),
            P("dp", None),
            P("dp", None),
            P("dp"),
            P("dp"),
            P("dp"),
            P("dp"),
            P("dp", None),
            P("expert", None, None),
            P("expert", None, None),
        ),
        check_vma=False,
    )
```

```python
import jax
import jax.numpy as jnp
import numpy as np
from jax import lax
from jax.experimental import pallas as pl
from jax.experimental.pallas import tpu as pltpu
from jax.sharding import PartitionSpec as P

HD = 64
EPSILON = 1e-06
THETA = 10000.0
MASKED = -1e30

BF = jnp.bfloat16
F32 = jnp.float32
SLOTS = 48
CHUNK = 256
MIB = 1024 * 1024


def nn(a, b):
    return lax.dot_general(a, b, (((1,), (0,)), ((), ())), preferred_element_type=F32)


def nt(a, b):
    return lax.dot_general(a, b, (((1,), (1,)), ((), ())), preferred_element_type=F32)


def tn(a, b):
    return lax.dot_general(a, b, (((0,), (0,)), ((), ())), preferred_element_type=F32)


def send(src, dst, send_sem, recv_sem, device):
    return pltpu.make_async_remote_copy(
        src_ref=src, dst_ref=dst, send_sem=send_sem, recv_sem=recv_sem, device_id=device
    )


def next_to(p):
    return (p + 1) % 4, (p + 3) % 4, (p + 2) % 4


def greet(devices):
    sem = pltpu.get_barrier_semaphore()
    for device in devices:
        pl.semaphore_signal(sem, inc=1, device_id=device)
    pl.semaphore_wait(sem, len(devices))


class Plane:
    def __init__(self):
        self.me = lax.axis_index("expert")
        self.z = self.me // 4
        self.x = self.me % 4

    def own(self, half):
        return (self.x, self.z) if half == 0 else (self.z, self.x)

    def device(self, half, p, q):
        return {"expert": q * 4 + p if half == 0 else p * 4 + q}

    def others(self):
        return [{"expert": (self.me + step) % 16} for step in range(1, 16)]

    def neighbours(self):
        zn, zp, _ = next_to(self.z)
        xn, xp, _ = next_to(self.x)
        return [{"expert": k} for k in (zn * 4 + self.x, zp * 4 + self.x, self.z * 4 + xn, self.z * 4 + xp)]


class Column:
    def __init__(self):
        self.me = lax.axis_index("dp")
        self.y = self.me // 2
        self.c = self.me % 2

    def neighbours(self):
        yn, yp, _ = next_to(self.y)
        return [self.to(yn), self.to(yp), self.other()]

    def to(self, y):
        return {"dp": y * 2 + self.c}

    def other(self):
        return {"dp": self.y * 2 + 1 - self.c}


class PlaneStep:
    def at(self, half, p, q, rows):
        return self.ref.at[q, p, rows] if half == 0 else self.ref.at[p, q, rows]

    def line(self, half, q, rows):
        return self.ref.at[q, :, rows] if half == 0 else self.ref.at[:, q, rows]

    def rows(self, half):
        quarter = self.height // 4
        base = 2 * quarter * half
        return pl.ds(base, 2 * quarter), pl.ds(base, quarter), pl.ds(base + quarter, quarter)


class Gather(PlaneStep):
    def __init__(self, plane, ref, sems, height=128):
        self.plane, self.ref, self.sems, self.height = plane, ref, sems, height

    def message(self, half, i):
        p, q = self.plane.own(half)
        pn, pp, _ = next_to(p)
        qn, qp, _ = next_to(q)
        full, first, second = self.rows(half)
        view, to = [
            lambda: (self.at(half, p, q, full), (pn, q)),
            lambda: (self.at(half, p, q, full), (pp, q)),
            lambda: (self.at(half, pp, q, first), (pn, q)),
            lambda: (self.at(half, pn, q, second), (pp, q)),
            lambda: (self.line(half, q, full), (p, qn)),
            lambda: (self.line(half, q, full), (p, qp)),
            lambda: (self.line(half, qp, first), (p, qn)),
            lambda: (self.line(half, qn, second), (p, qp)),
        ][i]()
        sems = self.sems
        return send(view, view, sems.at[0, half, i], sems.at[1, half, i], self.plane.device(half, *to))

    def step(self, n):
        waits, starts = [
            ((), (0, 1)),
            ((0, 1), (2, 3)),
            ((2, 3), (4, 5)),
            ((4, 5), (6, 7)),
            ((6, 7), ()),
        ][n]
        for half in range(2):
            for i in waits:
                self.message(half, i).wait_recv()
            for i in starts:
                self.message(half, i).start()
        if n == 4:
            for half in range(2):
                for i in range(8):
                    self.message(half, i).wait_send()


class Scatter(PlaneStep):
    def __init__(self, plane, ref, slots, sems, store, free=None, height=128):
        self.plane, self.ref, self.slots, self.sems = plane, ref, slots, sems
        self.store, self.free, self.height = store, free, height

    def message(self, half, i):
        p, q = self.plane.own(half)
        pn, pp, po = next_to(p)
        qn, qp, qo = next_to(q)
        full, first, second = self.rows(half)
        r1, r2, r3, r4 = self.slots
        view, slot, to = [
            lambda: (self.line(half, qo, first), r1.at[half, 0], (p, qn)),
            lambda: (self.line(half, qo, second), r1.at[half, 1], (p, qp)),
            lambda: (self.line(half, qn, full), r2.at[half, 0], (p, qn)),
            lambda: (self.line(half, qp, full), r2.at[half, 1], (p, qp)),
            lambda: (self.at(half, po, q, first), r3.at[half, 0], (pn, q)),
            lambda: (self.at(half, po, q, second), r3.at[half, 1], (pp, q)),
            lambda: (self.at(half, pn, q, full), r4.at[half, 0], (pn, q)),
            lambda: (self.at(half, pp, q, full), r4.at[half, 1], (pp, q)),
        ][i]()
        sems = self.sems
        return send(view, slot, sems.at[0, half, i], sems.at[1, half, i], self.plane.device(half, *to))

    def add_line(self, half, q, part, parts, slots):
        quarter = self.height // 4
        offset = quarter * (2 * half + part)
        groups = quarter * parts // 16

        @pl.loop(0, 4 * groups)
        def _(n):
            j, k = n // groups, n % groups
            rows = pl.ds(pl.multiple_of(offset + k * 16, 16), 16)
            some = pl.ds(pl.multiple_of(k * 16, 16), 16)
            place = (q, j, rows) if half == 0 else (j, q, rows)
            total = self.ref[place].astype(F32)
            for ref, side in slots:
                total += ref[half, side, j, some].astype(F32)
            self.ref[place] = total.astype(BF)

    def add_at(self, half, p, q, part, slot):
        quarter = self.height // 4
        ref, side = slot

        @pl.loop(0, quarter // 16)
        def _(k):
            rows = pl.ds(pl.multiple_of(quarter * (2 * half + part) + k * 16, 16), 16)
            place = (q, p, rows) if half == 0 else (p, q, rows)
            got = ref[half, side, pl.ds(pl.multiple_of(k * 16, 16), 16)].astype(F32)
            self.ref[place] = (self.ref[place].astype(F32) + got).astype(BF)

    def step(self, n):
        r1, r2, r3, r4 = self.slots
        for half in range(2):
            p, q = self.plane.own(half)
            pn, pp, po = next_to(p)
            qn, qp, qo = next_to(q)
            if n == 0:
                self.message(half, 0).start()
                self.message(half, 1).start()
            elif n == 1:
                self.message(half, 0).wait_recv()
                self.add_line(half, qn, 0, 1, [(r1, 0)])
                self.message(half, 2).start()
                self.message(half, 1).wait_recv()
                self.add_line(half, qp, 1, 1, [(r1, 1)])
                self.message(half, 3).start()
            elif n == 2:
                self.message(half, 2).wait_recv()
                self.message(half, 3).wait_recv()
                self.add_line(half, q, 0, 2, [(r2, 0), (r2, 1)])
                self.message(half, 4).start()
                self.message(half, 5).start()
            elif n == 3:
                self.message(half, 4).wait_recv()
                self.add_at(half, pn, q, 0, (r3, 0))
                self.message(half, 6).start()
                self.message(half, 5).wait_recv()
                self.add_at(half, pp, q, 1, (r3, 1))
                self.message(half, 7).start()
            elif n == 4:
                self.message(half, 6).wait_recv()
                self.message(half, 7).wait_recv()

                @pl.loop(0, self.height // 32)
                def _(k):
                    rows = pl.ds(pl.multiple_of(self.height // 2 * half + k * 16, 16), 16)
                    place = (q, p, rows) if half == 0 else (p, q, rows)
                    some = pl.ds(pl.multiple_of(k * 16, 16), 16)
                    total = self.ref[place].astype(F32)
                    total += r4[half, 0, some].astype(F32)
                    total += r4[half, 1, some].astype(F32)
                    self.store(place, rows, total)
        if n == 4:
            for half in range(2):
                for i in range(8):
                    self.message(half, i).wait_send()

    def give_credit(self):
        for device in self.plane.neighbours():
            pl.semaphore_signal(self.free, inc=1, device_id=device)

    def take_credit(self):
        pl.semaphore_wait(self.free, 4)


def scatter_slots(height, width, lead=()):
    quarter = height // 4
    return [
        pltpu.VMEM((*lead, 2, 2, 4, quarter, width), BF),
        pltpu.VMEM((*lead, 2, 2, 4, 2 * quarter, width), BF),
        pltpu.VMEM((*lead, 2, 2, quarter, width), BF),
        pltpu.VMEM((*lead, 2, 2, 2 * quarter, width), BF),
    ]


class ColumnGather:
    def __init__(self, column, ref, sems, count, own=None):
        self.column, self.ref, self.sems, self.count = column, ref, sems, count
        self.own = own

    def message(self, i):
        y, c = self.column.y, self.column.c
        yn, yp, yo = next_to(y)
        half = self.count // 2
        ref, column = self.ref, self.column
        view, device = [
            lambda: (ref.at[y, c], column.to(yn)),
            lambda: (ref.at[y, c], column.to(yp)),
            lambda: (ref.at[y, c], column.other()),
            lambda: (ref.at[yp, c, pl.ds(0, half)], column.to(yn)),
            lambda: (ref.at[yn, c, pl.ds(half, half)], column.to(yp)),
            lambda: (ref.at[yp, c], column.other()),
            lambda: (ref.at[yn, c], column.other()),
            lambda: (ref.at[yo, c], column.other()),
        ][i]()
        source = self.own if i < 3 and self.own is not None else view
        return send(source, view, self.sems.at[0, i], self.sems.at[1, i], device)

    def step(self, n):
        order = [
            [("s", 0), ("s", 1), ("s", 2)],
            [("w", 0), ("s", 3), ("s", 5), ("w", 1), ("s", 4), ("s", 6)],
            [("w", 3), ("w", 4), ("s", 7)],
            [("w", 2), ("w", 5), ("w", 6), ("w", 7)],
        ][n]
        for what, i in order:
            if what == "s":
                self.message(i).start()
            else:
                self.message(i).wait_recv()
        if n == 3:
            for i in range(8):
                self.message(i).wait_send()


class ColumnScatter:
    def __init__(self, column, ref, slots, sems, count, store, group=16):
        self.column, self.ref, self.slots, self.sems = column, ref, slots, sems
        self.count, self.store, self.group = count, store, group

    def message(self, i):
        y, c = self.column.y, self.column.c
        yn, yp, yo = next_to(y)
        half = self.count // 2
        ref, column = self.ref, self.column
        ra, rb, rc = self.slots
        view, slot, device = [
            lambda: (ref.at[:, 1 - c], ra, column.other()),
            lambda: (ref.at[yo, c, pl.ds(0, half)], rb.at[0], column.to(yn)),
            lambda: (ref.at[yo, c, pl.ds(half, half)], rb.at[1], column.to(yp)),
            lambda: (ref.at[yn, c], rc.at[0], column.to(yn)),
            lambda: (ref.at[yp, c], rc.at[1], column.to(yp)),
        ][i]()
        return send(view, slot, self.sems.at[0, i], self.sems.at[1, i], device)

    def some(self, k, base=0):
        return pl.ds(pl.multiple_of(base + k * self.group, self.group), self.group)

    def step(self, n):
        y, c = self.column.y, self.column.c
        yn, yp, yo = next_to(y)
        ref, (ra, rb, rc) = self.ref, self.slots
        low = ref.dtype
        half = self.count // 2
        groups = self.count // self.group
        if n == 0:
            self.message(0).start()
        elif n == 1:
            self.message(0).wait_recv()

            @pl.loop(0, 4 * groups)
            def _(k):
                j, r = k // groups, self.some(k % groups)
                ref[j, c, r] = (ref[j, c, r].astype(F32) + ra[j, r].astype(F32)).astype(low)

            self.message(1).start()
            self.message(2).start()
        elif n == 2:
            for side, to in ((0, yn), (1, yp)):
                self.message(1 + side).wait_recv()

                @pl.loop(0, groups // 2)
                def _(k):
                    r = self.some(k, side * half)
                    got = rb[side, self.some(k)].astype(F32)
                    ref[to, c, r] = (ref[to, c, r].astype(F32) + got).astype(low)

                self.message(3 + side).start()
        else:
            self.message(3).wait_recv()
            self.message(4).wait_recv()

            @pl.loop(0, groups)
            def _(k):
                r = self.some(k)
                total = ref[y, c, r].astype(F32) + rc[0, r].astype(F32) + rc[1, r].astype(F32)
                self.store(r, total)

            for i in range(5):
                self.message(i).wait_send()


def column_slots(shape, dtype=BF, lead=()):
    count, rest = shape[0], shape[1:]
    return [
        pltpu.VMEM((*lead, 4, count, *rest), dtype),
        pltpu.VMEM((*lead, 2, count // 2, *rest), dtype),
        pltpu.VMEM((*lead, 2, count, *rest), dtype),
    ]


def turned(v, cosine, sine):
    a, b = v[:32], v[32:]
    return jnp.concatenate([a * cosine - b * sine, b * cosine + a * sine], axis=0)


def inverse_rms(v, axis):
    return lax.rsqrt(jnp.mean(v * v, axis=axis, keepdims=True) + EPSILON)


def head_gain(small_t, row):
    pieces = [small_t[:, 128 * b : 128 * (b + 1)] for b in range(8)]
    tall = jnp.concatenate([piece.T[:8] for piece in pieces], axis=0)
    return jnp.broadcast_to(tall[:, row : row + 1], (64, 128))


def document_bias(seg_ref, bias, mb, mine):
    own = seg_ref[mb, mine].astype(F32)
    for b in range(8):
        keys = jnp.broadcast_to(seg_ref[mb, b].astype(F32), (128, 128)).T
        bias[mb, 128 * b : 128 * (b + 1)] = jnp.where(keys == own, 0.0, MASKED).astype(bias.dtype)


def pair_columns(ref, mb, g):
    both = ref[mb, pl.ds(pl.multiple_of(g * 128, 128), 128)]
    return jnp.concatenate([both[:64], both[64:]], axis=1)


def front_kernel(
    tok, cot, wq, wo, small, seg_ref, routes_ref, turn_hbm,
    dy_out, x0_out, wq_out, wo_out, kv_out, raw_out,
    small_t, q_t, mix_t, lsum, res, ffn, gates_t, sent,
    dy_all, x0_all, wq_all, wo_all, kv_all, raw_t, small_all, normed, bias, turn, plane_sems, column_sems,
    local,
):
    plane, column = Plane(), Column()
    y, c = column.y, column.c
    copies = [
        pltpu.make_async_copy(small, small_all.at[y, c], local.at[0]),
        pltpu.make_async_copy(wq.at[:, 1024:2048], wq_all.at[1, y, c], local.at[1]),
        pltpu.make_async_copy(wq.at[:, 0:1024], wq_all.at[0, y, c], local.at[3]),
        pltpu.make_async_copy(wo, wo_all.at[y, c], local.at[5]),
        pltpu.make_async_copy(turn_hbm.at[column.me], turn, local.at[6]),
    ]
    for copy in copies:
        copy.start()
    outs = [
        pltpu.make_async_copy(wq_all, wq_out, local.at[7]),
        pltpu.make_async_copy(wo_all, wo_out, local.at[8]),
        pltpu.make_async_copy(kv_all, kv_out, local.at[9]),
        pltpu.make_async_copy(raw_t, raw_out, local.at[10]),
        pltpu.make_async_copy(dy_all.at[0], dy_out.at[0], local.at[11]),
        pltpu.make_async_copy(dy_all.at[1], dy_out.at[1], local.at[2]),
        pltpu.make_async_copy(x0_all, x0_out, local.at[4]),
    ]
    for mb in range(2):
        dy_all[mb, plane.z, plane.x] = cot[mb]
    greet(plane.neighbours() + column.neighbours())
    gdy = [Gather(plane, dy_all.at[mb], plane_sems.at[mb]) for mb in range(2)]
    gx = Gather(plane, x0_all, plane_sems.at[2])
    w_small = ColumnGather(column, small_all, column_sems.at[0], 64)
    w_q = ColumnGather(column, wq_all.at[0], column_sems.at[1], 128)
    w_kv = ColumnGather(column, wq_all.at[1], column_sems.at[2], 128)
    w_o = ColumnGather(column, wo_all, column_sems.at[3], 128)
    kv = [ColumnGather(column, kv_all.at[mb], column_sems.at[4 + mb], 8) for mb in range(2)]
    def both_biases():
        for mb in range(2):
            document_bias(seg_ref, bias, mb, column.me)

    def norm_tokens():
        for b in range(8):
            small_t[:, 128 * b : 128 * (b + 1)] = small_all[b // 2, b % 2].astype(F32)
        attn_gain = small_t[32:33]
        for mb in range(2):
            v = tok[mb].astype(F32)
            normed[128 * mb : 128 * (mb + 1)] = (v * inverse_rms(v, 1) * attn_gain).astype(BF)

    def project(k):
        @pl.loop(0, 2)
        def _(n):
            cols = pl.ds(pl.multiple_of(n * 512, 512), 512)
            rows = pl.ds(pl.multiple_of(1024 * k + n * 512, 512), 512)
            got = nn(normed[...], wq_all[k, :, :, :, cols].reshape(1024, 512))
            for mb in range(2):
                raw_t[mb, rows] = got[128 * mb : 128 * (mb + 1)].T

    def key_heads(mb):
        @pl.loop(0, 8)
        def _(g):
            v = raw_t[mb, pl.ds(pl.multiple_of(1024 + g * 64, 64), 64)]
            key = turned(v * inverse_rms(v, 0) * key_gain, cosine, sine)
            value = raw_t[mb, pl.ds(pl.multiple_of(1536 + g * 64, 64), 64)]
            kv_all[mb, y, c, g] = jnp.concatenate([key, value], axis=0).T.astype(BF)

    def query_heads(mb):
        @pl.loop(0, 16)
        def _(h):
            rows = pl.ds(pl.multiple_of(h * 64, 64), 64)
            v = raw_t[mb, rows]
            query = turned(v * inverse_rms(v, 0) * query_gain, cosine, sine)
            q_t[mb, rows] = (query.astype(BF).astype(F32) * HD ** (-0.5)).astype(BF)

    def attend(mb, start, stop):
        @pl.loop(start, stop)
        def _(g):
            query = pair_columns(q_t, mb, g)
            query = jnp.concatenate([query, jnp.zeros_like(query)], axis=0)
            total = jnp.zeros((1, 256), F32)
            mixed = jnp.zeros((128, 256), F32)
            for j in range(4):
                keys = kv_all[mb, j, :, g].reshape(256, 128)
                there = bias[mb, 256 * j : 256 * (j + 1)].astype(F32)
                p = jnp.exp(nn(keys, query) + jnp.concatenate([there, there], axis=1))
                total += jnp.sum(p, axis=0, keepdims=True)
                mixed += tn(keys, p.astype(BF))
            lsum[mb, g] = total
            mixed = (mixed[64:] / total).astype(BF)
            both = jnp.concatenate([mixed[:, :128], mixed[:, 128:]], axis=0)
            mix_t[mb, pl.ds(pl.multiple_of(g * 128, 128), 128)] = both

    def finish(mb):
        @pl.loop(0, 2)
        def _(n):
            cols = pl.ds(pl.multiple_of(n * 512, 512), 512)
            got = tn(mix_t[mb], wo_all[:, :, :, cols].reshape(1024, 512))
            res[mb, :, cols] = tok[mb, :, cols].astype(F32) + got

        v = res[mb]
        low = (v * inverse_rms(v, 1) * small_t[33:34]).astype(BF)
        ffn[mb] = low
        logits = nt(small_t[:32].astype(BF), low)
        ids = lax.broadcasted_iota(jnp.int32, (32, 128), 0)
        routed = ids == routes_ref[mb, 0:1]
        for k in range(1, 8):
            routed = routed | (ids == routes_ref[mb, k : k + 1])
        top = jnp.max(jnp.where(routed, logits, MASKED), axis=0, keepdims=True)
        weight = jnp.where(routed, jnp.exp(logits - top), 0.0)
        gates = weight / jnp.sum(weight, axis=0, keepdims=True)
        gates_t[mb] = gates
        for k in range(16):
            sent[k, 2 * mb : 2 * mb + 2] = gates[2 * k : 2 * k + 2]

    sent[...] = jnp.zeros_like(sent)
    copies[1].wait()
    w_kv.step(0)
    copies[0].wait()
    w_small.step(0)
    gdy[1].step(0)
    gdy[1].step(1)
    gdy[0].step(0)
    copies[2].wait()
    w_q.step(0)
    w_small.step(1)
    w_kv.step(1)
    w_small.step(2)
    gdy[1].step(2)
    w_small.step(3)
    norm_tokens()
    copies[3].wait()
    w_o.step(0)
    gdy[0].step(1)
    w_kv.step(2)
    w_kv.step(3)
    project(1)
    w_q.step(1)
    query_gain = head_gain(small_t[...], 34)
    key_gain = head_gain(small_t[...], 35)
    copies[4].wait()
    cosine, sine = turn[:32], turn[32:]
    key_heads(0)
    kv[0].step(0)
    gdy[0].step(2)
    w_q.step(2)
    both_biases()
    w_o.step(1)
    kv[0].step(1)
    w_q.step(3)
    outs[0].start()
    gdy[1].step(3)
    project(0)
    outs[3].start()
    kv[0].step(2)
    query_heads(0)
    gdy[0].step(3)
    key_heads(1)
    w_o.step(2)
    kv[0].step(3)
    attend(0, 0, 4)
    attend(0, 4, 8)
    w_o.step(3)
    outs[1].start()
    finish(0)
    x0_all[plane.z, plane.x] = ffn[0]
    gx.step(0)
    query_heads(1)
    kv[1].step(0)
    gx.step(1)
    gx.step(2)
    gdy[1].step(4)
    outs[5].start()
    kv[1].step(1)
    kv[1].step(2)
    kv[1].step(3)
    outs[2].start()
    attend(1, 0, 4)
    attend(1, 4, 8)
    gx.step(3)
    finish(1)
    gdy[0].step(4)
    outs[4].start()
    gx.step(4)
    outs[6].start()
    for copy in outs:
        copy.wait()


def front(tok, cot, wq, wo, small, seg, routes_t, turn):
    vmem = pl.BlockSpec(memory_space=pltpu.VMEM)
    anywhere = pl.BlockSpec(memory_space=pl.ANY)
    return pl.pallas_call(
        front_kernel,
        out_shape=(
            jax.ShapeDtypeStruct((2, 4, 4, 128, 1024), BF),
            jax.ShapeDtypeStruct((4, 4, 128, 1024), BF),
            jax.ShapeDtypeStruct((2, 4, 2, 128, 1024), BF),
            jax.ShapeDtypeStruct((4, 2, 128, 1024), BF),
            jax.ShapeDtypeStruct((2, 4, 2, 8, 128, 128), BF),
            jax.ShapeDtypeStruct((2, 2048, 128), F32),
            jax.ShapeDtypeStruct((64, 1024), F32),
            jax.ShapeDtypeStruct((2, 1024, 128), BF),
            jax.ShapeDtypeStruct((2, 1024, 128), BF),
            jax.ShapeDtypeStruct((2, 8, 1, 256), F32),
            jax.ShapeDtypeStruct((2, 128, 1024), F32),
            jax.ShapeDtypeStruct((2, 128, 1024), BF),
            jax.ShapeDtypeStruct((2, 32, 128), F32),
            jax.ShapeDtypeStruct((16, 8, 128), F32),
        ),
        in_specs=[vmem, vmem, anywhere, anywhere, anywhere, vmem, vmem, anywhere],
        out_specs=(anywhere,) * 6 + (vmem,) * 8,
        scratch_shapes=[
            pltpu.VMEM((2, 4, 4, 128, 1024), BF),
            pltpu.VMEM((4, 4, 128, 1024), BF),
            pltpu.VMEM((2, 4, 2, 128, 1024), BF),
            pltpu.VMEM((4, 2, 128, 1024), BF),
            pltpu.VMEM((2, 4, 2, 8, 128, 128), BF),
            pltpu.VMEM((2, 2048, 128), F32),
            pltpu.VMEM((4, 2, 64, 128), BF),
            pltpu.VMEM((256, 1024), BF),
            pltpu.VMEM((2, 1024, 128), F32),
            pltpu.VMEM((64, 128), F32),
            pltpu.SemaphoreType.DMA((3, 2, 2, 8)),
            pltpu.SemaphoreType.DMA((6, 2, 8)),
            pltpu.SemaphoreType.DMA((12,)),
        ],
        compiler_params=pltpu.CompilerParams(
            collective_id=0, has_side_effects=True, vmem_limit_bytes=56 * MIB
        ),
        cost_estimate=pl.CostEstimate(
            flops=5_000_000_000, bytes_accessed=30_000_000, transcendentals=5_000_000
        ),
    )(tok, cot, wq, wo, small, seg, routes_t, turn)


def moe_kernel(
    ffn_ref, x0_hbm, dy_hbm, gates_ref, wgu_hbm, wd_hbm,
    out_hbm, dx_ref, h_ref, dw_own,
    dw, x_all, dy_all, r1, r2, r3, r4, xs, ds, os, gc, act, a1, a2, ggu, g_all, ranks, hcol, hs,
    wgu, wd, ra, rb, rc, sems, column_sems, gsend, grecv, hsend, hrecv, free, local,
):
    plane, column = Plane(), Column()
    me, z, x = plane.me, plane.z, plane.x
    w1 = pltpu.make_async_copy(wgu_hbm, wgu, local.at[0])
    w2 = pltpu.make_async_copy(wd_hbm, wd, local.at[1])
    w1.start()
    w2.start()
    own = [
        pltpu.make_async_copy(ffn_ref.at[1], x_all.at[1, z, x], local.at[4]),
        pltpu.make_async_copy(x0_hbm, x_all.at[0], local.at[5]),
    ]
    outs = [pltpu.make_async_copy(x_all.at[mb], out_hbm.at[mb], local.at[6 + mb]) for mb in range(2)]
    dys = [pltpu.make_async_copy(dy_hbm.at[mb], dy_all.at[mb], local.at[2 + mb]) for mb in range(2)]
    for copy in own + dys:
        copy.start()
    greet(plane.others() + column.neighbours())
    own[0].wait()

    def gate_message(step):
        to = (me + step) % 16
        return pltpu.make_async_remote_copy(
            src_ref=gates_ref.at[to], dst_ref=g_all.at[me],
            send_sem=gsend.at[step], recv_sem=grecv.at[step], device_id={"expert": to},
        )

    def h_message(step):
        to = (me + step) % 16
        return pltpu.make_async_remote_copy(
            src_ref=hs.at[to], dst_ref=h_ref.at[me],
            send_sem=hsend.at[step], recv_sem=hrecv.at[step], device_id={"expert": to},
        )

    for step in range(1, 16):
        gate_message(step).start()
    g_all[me] = gates_ref[me]
    gx = Gather(plane, x_all.at[1], sems.at[0])

    def into(mb):
        def store(place, rows, total):
            dx_ref[mb, rows] = total

        return store

    sdx = [
        Scatter(plane, dy_all.at[mb], (r1, r2, r3, r4), sems.at[1 + mb], into(mb), free)
        for mb in range(2)
    ]

    def own_part(k):
        def store(r, total):
            dw_own[k, r] = total.astype(BF)

        return store

    dsum = [
        ColumnScatter(
            column, dw.at[k], (ra.at[k], rb.at[k], rc.at[k]), column_sems.at[k], 128, own_part(k)
        )
        for k in range(3)
    ]
    def gates_here():
        for step in range(1, 16):
            gate_message(step).wait_recv()
        for step in range(1, 16):
            gate_message(step).wait_send()

        earlier = (
            lax.broadcasted_iota(jnp.int32, (128, 128), 0)
            < lax.broadcasted_iota(jnp.int32, (128, 128), 1)
        ).astype(F32).astype(BF)

        @pl.loop(0, 16)
        def _(s):
            named = g_all[s] > 0.0
            before = nn(named.astype(F32).astype(BF), earlier)
            ranks[s] = jnp.where(named, before, -1.0)

    slot_ids = lax.broadcasted_iota(jnp.int32, (SLOTS, 128), 0).astype(F32)

    def places(s, mb):
        r = ranks[s]
        return [(slot_ids == r[2 * mb + e : 2 * mb + e + 1]).astype(F32) for e in range(2)]

    def gated(s, mb, hot):
        g = g_all[s]
        return [hot[e] * g[2 * mb + e : 2 * mb + e + 1] for e in range(2)]

    def span(s):
        return pl.ds(pl.multiple_of(s * SLOTS, 16), SLOTS)

    def select(mb):
        @pl.loop(0, 16)
        def _(s):
            hot = places(s, mb)
            pick = jnp.concatenate(hot, axis=0).astype(BF)
            scaled = jnp.concatenate(gated(s, mb, hot), axis=0).astype(BF)
            rows = nn(pick, x_all[mb, s // 4, s % 4]).astype(BF)
            drows = nn(scaled, dy_all[mb, s // 4, s % 4]).astype(BF)
            for e in range(2):
                xs[e, span(s)] = rows[SLOTS * e : SLOTS * (e + 1)]
                ds[e, span(s)] = drows[SLOTS * e : SLOTS * (e + 1)]

    chunks = 16 * SLOTS // CHUNK

    def forward(e):
        @pl.loop(0, chunks)
        def _(c):
            r = pl.ds(pl.multiple_of(c * CHUNK, CHUNK), CHUNK)
            gu = nn(xs[e, r], wgu[e])
            g, u = gu[:, :512], gu[:, 512:]
            sig = 1.0 / (1.0 + jnp.exp(-g))
            silu = g * sig
            active = (silu * u).astype(BF)
            act[e, r] = active
            a1[e, r] = (u * sig * (1.0 + g * (1.0 - sig))).astype(BF)
            a2[e, r] = silu.astype(BF)
            o = nn(active, wd[e]).astype(BF)
            os[e, r] = o
            hcol[e, r] = jnp.sum(o.astype(F32) * ds[e, r].astype(F32), axis=-1, keepdims=True)

    def combine_out(mb):
        @pl.loop(0, 16)
        def _(s):
            hot = places(s, mb)
            scaled = jnp.concatenate(gated(s, mb, hot), axis=0).astype(BF)
            both = jnp.concatenate([os[0, span(s)], os[1, span(s)]], axis=0)
            x_all[mb, s // 4, s % 4] = tn(scaled, both).astype(BF)
            for e in range(2):
                row = 2 * mb + e
                hs[s, row : row + 1] = jnp.sum(hot[e] * hcol[e, span(s)], axis=0, keepdims=True)

    def add_part(mb, k, n, fresh):
        fresh = fresh.reshape(2, 128, 1024)
        if mb == 1:
            fresh += dw[k, n].astype(F32)
        dw[k, n] = fresh.astype(BF)

    def backward(mb, e):
        @pl.loop(0, chunks)
        def _(c):
            r = pl.ds(pl.multiple_of(c * CHUNK, CHUNK), CHUNK)
            ga = nt(ds[e, r], wd[e])
            grad = jnp.concatenate(
                [ga * a1[e, r].astype(F32), ga * a2[e, r].astype(F32)], axis=1
            ).astype(BF)
            ggu[r] = grad
            gc[e, r] = nt(grad, wgu[e]).astype(BF)

        @pl.loop(0, 4)
        def _(m):
            cols = pl.ds(pl.multiple_of(m * 256, 256), 256)
            add_part(mb, e, m, tn(xs[e, :, cols], ggu[...]))

        @pl.loop(0, 2)
        def _(m):
            cols = pl.ds(pl.multiple_of(m * 256, 256), 256)
            add_part(mb, 2, 2 * e + m, tn(act[e, :, cols], ds[e]))

    def combine_dx(mb):
        @pl.loop(0, 16)
        def _(s):
            pick = jnp.concatenate(places(s, mb), axis=0).astype(BF)
            both = jnp.concatenate([gc[0, span(s)], gc[1, span(s)]], axis=0)
            dy_all[mb, s // 4, s % 4] = tn(pick, both).astype(BF)

    gx.step(0)
    gates_here()
    own[1].wait()
    for copy in dys:
        copy.wait()
    select(0)
    w1.wait()
    w2.wait()
    gx.step(1)
    forward(1)
    forward(0)
    gx.step(2)
    backward(0, 0)
    backward(0, 1)
    gx.step(3)
    combine_dx(0)
    sdx[0].step(0)
    combine_out(0)
    outs[0].start()
    gx.step(4)
    select(1)
    sdx[0].step(1)
    forward(0)
    backward(1, 0)
    forward(1)
    sdx[0].step(2)
    backward(1, 1)
    sdx[0].step(3)
    dsum[0].step(0)
    combine_dx(1)
    sdx[0].step(4)
    sdx[0].give_credit()
    sdx[1].take_credit()
    sdx[1].step(0)
    dsum[1].step(0)
    dsum[0].step(1)
    combine_out(1)
    outs[1].start()
    dsum[2].step(0)
    dsum[0].step(2)
    sdx[1].step(1)
    dsum[1].step(1)
    h_ref[me] = hs[me]
    for step in range(1, 16):
        h_message(step).start()
    dsum[2].step(1)
    dsum[1].step(2)
    dsum[2].step(2)
    sdx[1].step(2)
    sdx[1].step(3)
    dsum[1].step(3)
    dsum[0].step(3)
    dsum[2].step(3)
    sdx[1].step(4)
    for step in range(1, 16):
        h_message(step).wait_recv()
    for step in range(1, 16):
        h_message(step).wait_send()
    for copy in outs:
        copy.wait()


def moe(ffn, x0, dy, gates, w_gate_up, w_down):
    vmem = pl.BlockSpec(memory_space=pltpu.VMEM)
    anywhere = pl.BlockSpec(memory_space=pl.ANY)
    rows = 16 * SLOTS
    return pl.pallas_call(
        moe_kernel,
        out_shape=(
            jax.ShapeDtypeStruct((2, 4, 4, 128, 1024), BF),
            jax.ShapeDtypeStruct((2, 128, 1024), F32),
            jax.ShapeDtypeStruct((16, 8, 128), F32),
            jax.ShapeDtypeStruct((3, 128, 1024), BF),
        ),
        in_specs=[anywhere, anywhere, anywhere, vmem, anywhere, anywhere],
        out_specs=(anywhere,) + (vmem,) * 3,
        scratch_shapes=[
            pltpu.VMEM((3, 4, 2, 128, 1024), BF),
            pltpu.VMEM((2, 4, 4, 128, 1024), BF),
            pltpu.VMEM((2, 4, 4, 128, 1024), BF),
            *scatter_slots(128, 1024),
            pltpu.VMEM((2, rows, 1024), BF),
            pltpu.VMEM((2, rows, 1024), BF),
            pltpu.VMEM((2, rows, 1024), BF),
            pltpu.VMEM((2, rows, 1024), BF),
            pltpu.VMEM((2, rows, 512), BF),
            pltpu.VMEM((2, rows, 512), BF),
            pltpu.VMEM((2, rows, 512), BF),
            pltpu.VMEM((rows, 1024), BF),
            pltpu.VMEM((16, 8, 128), F32),
            pltpu.VMEM((16, 8, 128), F32),
            pltpu.VMEM((2, rows, 1), F32),
            pltpu.VMEM((16, 8, 128), F32),
            pltpu.VMEM((2, 1024, 1024), BF),
            pltpu.VMEM((2, 512, 1024), BF),
            *column_slots((128, 1024), lead=(3,)),
            pltpu.SemaphoreType.DMA((3, 2, 2, 8)),
            pltpu.SemaphoreType.DMA((3, 2, 8)),
            pltpu.SemaphoreType.DMA((16,)),
            pltpu.SemaphoreType.DMA((16,)),
            pltpu.SemaphoreType.DMA((16,)),
            pltpu.SemaphoreType.DMA((16,)),
            pltpu.SemaphoreType.REGULAR,
            pltpu.SemaphoreType.DMA((8,)),
        ],
        compiler_params=pltpu.CompilerParams(
            collective_id=1, has_side_effects=True, vmem_limit_bytes=63 * MIB
        ),
        cost_estimate=pl.CostEstimate(
            flops=30_000_000_000, bytes_accessed=30_000_000, transcendentals=2_000_000
        ),
    )(ffn, x0, dy, gates, w_gate_up, w_down)


def norm_grad(grad, v, inverse, gain, axis):
    scaled = grad * gain
    moment = jnp.mean(scaled * v, axis=axis, keepdims=True)
    return inverse * (scaled - v * (inverse * inverse * moment)), grad * (v * inverse)


def back_kernel(
    tok, cot, seg_ref, turn_hbm, wq_hbm, wo_hbm, small_t, raw_hbm, q_t, kv_hbm, mix_t, lsum,
    res, ffn, gates_t, share_ref, dx, out_hbm, dw_own,
    dgu_all, dd_all, output, in_grad, gq, go, gs,
    wq_all, wo_all, kv_all, raw_t, turn, bias, gres, branch, gm_t, dq_t, own_kv, gp, normed_t, gn,
    part_kv, part_w, part_s, q_sum, k_sum, ra, rb, rc, sa, sb, sc, plane_buf, plane_all, p1, p2, p3, p4, ta, tb, tc,
    logits, routers, router_sum, out_part, r1, r2, r3, r4, parcels, got_parcels, small_own, kv_total,
    column_sems, plane_sems, far_send, far_recv, all_send, all_recv, free, local, gain_sums,
):
    plane, column = Plane(), Column()
    y, c = column.y, column.c
    copies = [
        pltpu.make_async_copy(wo_hbm, wo_all, local.at[0]),
        pltpu.make_async_copy(kv_hbm, kv_all, local.at[1]),
        pltpu.make_async_copy(raw_hbm, raw_t, local.at[2]),
        pltpu.make_async_copy(wq_hbm, wq_all, local.at[3]),
        pltpu.make_async_copy(turn_hbm.at[column.me], turn, local.at[4]),
    ]
    parts = [pltpu.make_async_copy(out_hbm.at[mb], out_part, local.at[5 + mb]) for mb in range(2)]
    dw_refs = [dgu_all.at[0], dgu_all.at[1], dd_all]
    owns = [pltpu.make_async_copy(dw_own.at[n], dw_refs[n].at[y, c], local.at[7 + n]) for n in range(3)]
    for copy in parts[:1] + owns + copies:
        copy.start()
    greet(plane.others() + column.neighbours())
    dall = [ColumnGather(column, dw_refs[n], column_sems.at[8 + n], 128, dw_own.at[n]) for n in range(3)]

    def add_residual(mb):
        def store(place, rows, total):
            output[mb, rows] = (res[mb, rows] + total).astype(BF)

        return store

    sout = [
        Scatter(plane, out_part, (r1, r2, r3, r4), plane_sems.at[mb], add_residual(mb), free)
        for mb in range(2)
    ]
    part_s[...] = jnp.zeros_like(part_s)
    q_sum[...] = jnp.zeros_like(q_sum)
    k_sum[...] = jnp.zeros_like(k_sum)
    for mb in range(2):
        document_bias(seg_ref, bias, mb, column.me)

    def place_w(which):
        def store(r, total):
            low = total.astype(BF)
            half = r.start // 64
            some = pl.ds(pl.multiple_of(r.start % 64, 16), 16)
            for k in range(8):
                n = half * 8 + k
                piece = low[:, 128 * k : 128 * (k + 1)]
                if which == 2:
                    parcels[n, some] = piece
                else:
                    plane_buf[which, n // 4, n % 4, some] = piece

        return store

    def place_s(r, total):
        small_own[r] = total.astype(BF)

    def place_kv(mb, half):
        def store(r, total):
            own_kv[mb, pl.ds(r.start + 4 * half, 1)] = total

        return store

    w_sums = [
        ColumnScatter(
            column, part_w.at[n], (ra.at[n], rb.at[n], rc.at[n]), column_sems.at[n], 128, place_w(n)
        )
        for n in range(3)
    ]
    kv_sums = [
        [
            ColumnScatter(
                column, part_kv.at[mb, half],
                (sa.at[mb, half], sb.at[mb, half], sc.at[mb, half]),
                column_sems.at[4 + 2 * mb + half], 4, place_kv(mb, half), group=1,
            )
            for half in range(2)
        ]
        for mb in range(2)
    ]
    s_sum = ColumnScatter(column, part_s, (ta, tb, tc), column_sems.at[3], 64, place_s)

    def keep(n):
        def store(place, rows, total):
            plane_all[(n, *place)] = total.astype(BF)

        return store

    over = [
        Scatter(
            plane, plane_buf.at[n], (p1.at[n], p2.at[n], p3.at[n], p4.at[n]), plane_sems.at[2 + n],
            keep(n), height=64,
        )
        for n in range(2)
    ]
    spread = [Gather(plane, plane_all.at[n], plane_sems.at[4 + n], height=64) for n in range(2)]

    def tokens_of(mb):
        return pl.ds(128 * mb, 128)

    router = small_t[:32].astype(BF)
    ffn_gain, attn_gain = small_t[33:34], small_t[32:33]
    routers[0:32] = router
    routers[32:64] = router
    def router_and_norm():
        ffn_gain_grad = jnp.zeros((1, 1024), F32)
        for mb in range(2):
            share = jnp.concatenate([share_ref[k, 2 * mb : 2 * mb + 2] for k in range(16)], axis=0)
            logit = share - gates_t[mb] * jnp.sum(share, axis=0, keepdims=True)
            high = logit.astype(BF)
            logits[0:32, tokens_of(mb)] = high
            logits[32:64, tokens_of(mb)] = (logit - high.astype(F32)).astype(BF)

        @pl.loop(0, 4)
        def _(n):
            cols = pl.ds(pl.multiple_of(n * 256, 256), 256)
            gn[:, cols] = tn(logits[...], routers[:, cols])
            router_sum[:, cols] = nn(logits[...], ffn[:, :, cols].reshape(256, 256))

        for mb in range(2):
            into = dx[mb] + gn[tokens_of(mb)]
            v = res[mb]
            inv = inverse_rms(v, 1)
            grad, gain = norm_grad(into, v, inv, ffn_gain, 1)
            ffn_gain_grad += jnp.sum(gain, axis=0, keepdims=True)
            total = cot[mb].astype(F32) + grad
            gres[mb] = total
            branch[128 * mb : 128 * (mb + 1)] = total.astype(BF)
        gain_sums[1:2] = ffn_gain_grad

    def out_projection():
        copies[0].wait()

        @pl.loop(0, 4)
        def _(n):
            rows = pl.ds(pl.multiple_of(n * 256, 256), 256)
            got = nt(wo_all[n].reshape(256, 1024), branch[...])
            gm_t[0, rows] = got[:, :128].astype(BF)
            gm_t[1, rows] = got[:, 128:].astype(BF)
            mixed = jnp.concatenate([mix_t[0, rows], mix_t[1, rows]], axis=1)
            part_w[0, n] = nn(mixed, branch[...]).astype(BF).reshape(2, 128, 1024)

    def attend(mb, start, stop):
        @pl.loop(start, stop)
        def _(g):
            query = pair_columns(q_t, mb, g)
            grad = pair_columns(gm_t, mb, g)
            mixed = pair_columns(mix_t, mb, g)
            blank = jnp.zeros_like(query)
            inner = jnp.sum(grad.astype(F32) * mixed.astype(F32), axis=0, keepdims=True)
            query = jnp.concatenate([query, blank], axis=0)
            grad = jnp.concatenate([blank, grad], axis=0)
            both = jnp.concatenate([query, grad], axis=1)
            scale = 1.0 / lsum[mb, g]
            dq = jnp.zeros((128, 256), F32)
            for j in range(4):
                keys = kv_all[mb, j, :, g].reshape(256, 128)
                there = bias[mb, 256 * j : 256 * (j + 1)].astype(F32)
                got = nn(keys, both)
                p = jnp.exp(got[:, :256] + jnp.concatenate([there, there], axis=1)) * scale
                ds = (p * (got[:, 256:] - inner)).astype(BF)
                dq += tn(keys, ds)
                dkv = nt(jnp.concatenate([ds, p.astype(BF)], axis=1), both)
                part_kv[mb, g // 4, j, :, g % 4] = dkv.astype(BF).reshape(2, 128, 128)
            dq = dq[:64] * HD ** (-0.5)
            rows = pl.ds(pl.multiple_of(g * 128, 128), 128)
            dq_t[mb, rows] = jnp.concatenate([dq[:, :128], dq[:, 128:]], axis=0)

    copies[4].wait()
    cosine, sine = turn[:32], turn[32:]
    query_gain = head_gain(small_t[...], 34)
    key_gain = head_gain(small_t[...], 35)

    def head_back(grad, v, gain, total):
        inv = inverse_rms(v, 0)
        grad = turned(grad, cosine, -sine)
        grad_v, gain_part = norm_grad(grad, v, inv, gain, 0)
        total[...] += gain_part
        return grad_v

    def queries_back(mb):
        @pl.loop(0, 8)
        def _(g):
            pieces = []
            for r in range(2):
                rows = pl.ds(pl.multiple_of(g * 128 + r * 64, 64), 64)
                pieces.append(head_back(dq_t[mb, rows], raw_t[mb, rows], query_gain, q_sum))
            cols = pl.ds(pl.multiple_of(g * 128, 128), 128)
            gp[tokens_of(mb), cols] = jnp.concatenate(pieces, axis=0).T.astype(BF)

    def turn_normed():
        for mb in range(2):
            v = tok[mb].astype(F32)
            normed = (v * inverse_rms(v, 1) * attn_gain).astype(BF).astype(F32)
            for k in range(8):
                normed_t[128 * k : 128 * (k + 1), tokens_of(mb)] = (
                    normed[:, 128 * k : 128 * (k + 1)].T.astype(BF)
                )

    def weight_part(which):
        cols = pl.ds(1024 * (which - 1), 1024)

        @pl.loop(0, 4)
        def _(n):
            rows = pl.ds(pl.multiple_of(n * 256, 256), 256)
            part_w[which, n] = nn(normed_t[rows], gp[:, cols]).astype(BF).reshape(2, 128, 1024)

    def keys_back(mb):
        @pl.loop(0, 4)
        def _(k):
            keys, values = [], []
            for r in range(2):
                g = 2 * k + r
                grad = own_kv[mb, g].T
                rows = pl.ds(pl.multiple_of(1024 + g * 64, 64), 64)
                keys.append(head_back(grad[:64], raw_t[mb, rows], key_gain, k_sum))
                values.append(grad[64:])
            cols = pl.ds(pl.multiple_of(1024 + k * 128, 128), 128)
            gp[tokens_of(mb), cols] = jnp.concatenate(keys, axis=0).T.astype(BF)
            cols = pl.ds(pl.multiple_of(1536 + k * 128, 128), 128)
            gp[tokens_of(mb), cols] = jnp.concatenate(values, axis=0).T.astype(BF)

    def normed_grad(k):
        @pl.loop(0, 4)
        def _(n):
            cols = pl.ds(pl.multiple_of(n * 256, 256), 256)
            got = nt(gp[:, 1024 * k : 1024 * (k + 1)], wq_all[k, n].reshape(256, 1024))
            gn[:, cols] = got if k == 0 else gn[:, cols] + got

    def finish():
        attn_gain_grad = jnp.zeros((1, 1024), F32)
        for mb in range(2):
            v = tok[mb].astype(F32)
            grad, gain = norm_grad(gn[tokens_of(mb)], v, inverse_rms(v, 1), attn_gain, 1)
            attn_gain_grad += jnp.sum(gain, axis=0, keepdims=True)
            in_grad[mb] = (gres[mb] + grad).astype(BF)
        for b in range(8):
            cols = slice(128 * b, 128 * (b + 1))
            heads = slice(8 * b, 8 * (b + 1))
            part_s[b // 2, b % 2, 0:32] = router_sum[0:32, cols] + router_sum[32:64, cols]
            part_s[b // 2, b % 2, 32:33] = attn_gain_grad[:, cols]
            part_s[b // 2, b % 2, 33:34] = gain_sums[1:2, cols]
            part_s[b // 2, b % 2, 40:48] = jnp.broadcast_to(
                jnp.sum(q_sum[heads], axis=1, keepdims=True), (8, 128)
            )
            part_s[b // 2, b % 2, 48:56] = jnp.broadcast_to(
                jnp.sum(k_sum[heads], axis=1, keepdims=True), (8, 128)
            )

    me = plane.me

    def parcel(step):
        to = (me + step) % 16
        return send(
            parcels.at[to], got_parcels.at[me], far_send.at[step], far_recv.at[step], {"expert": to}
        )

    def total_message(step):
        to = (me + step) % 16
        return send(
            kv_total.at[me], kv_total.at[me], all_send.at[step], all_recv.at[step], {"expert": to}
        )

    def send_parcels():
        @pl.loop(0, 16)
        def _(n):
            parcels[n, 64:128] = small_own[...]

        for step in range(1, 16):
            parcel(step).start()
        got_parcels[me] = parcels[me]

    def add_parcels():
        for step in range(1, 16):
            parcel(step).wait_recv()
        total = got_parcels[0].astype(F32)
        for n in range(1, 16):
            total += got_parcels[n].astype(F32)
        kv_total[me] = total[:64].astype(BF)
        for step in range(1, 16):
            total_message(step).start()
        gs[...] = total[64:]

    def write_out(k):
        for n in range(16):
            rows = slice(64 * (n // 8), 64 * (n // 8) + 64)
            cols = slice(128 * (n % 8), 128 * (n % 8) + 128)
            (go, gq)[k][rows, cols] = plane_all[k, n // 4, n % 4].astype(F32)

    def take_totals():
        for step in range(1, 16):
            total_message(step).wait_recv()
        for n in range(16):
            first = 1024 + 128 * (n % 8)
            gq[64 * (n // 8) : 64 * (n // 8) + 64, first : first + 128] = kv_total[n].astype(F32)

    parts[0].wait()
    sout[0].step(0)
    dall[1].step(0)
    router_and_norm()
    dall[2].step(0)
    out_projection()
    w_sums[0].step(0)
    copies[1].wait()
    attend(1, 0, 2)
    dall[1].step(1)
    attend(0, 0, 2)
    w_sums[0].step(1)
    attend(0, 2, 4)
    kv_sums[0][0].step(0)
    dall[0].step(0)
    sout[0].step(1)
    attend(1, 2, 4)
    w_sums[0].step(2)
    attend(0, 4, 6)
    attend(1, 4, 6)
    attend(1, 6, 8)
    attend(0, 6, 8)
    kv_sums[1][1].step(0)
    sout[0].step(2)
    kv_sums[0][1].step(0)
    kv_sums[0][0].step(1)
    kv_sums[1][0].step(0)
    dall[2].step(1)
    w_sums[0].step(3)
    sout[0].step(3)
    over[0].step(0)
    dall[0].step(1)
    turn_normed()
    kv_sums[0][1].step(1)
    kv_sums[0][0].step(2)
    copies[2].wait()
    queries_back(0)
    queries_back(1)
    weight_part(1)
    kv_sums[1][1].step(1)
    kv_sums[1][0].step(1)
    sout[0].step(4)
    parts[1].start()
    sout[0].give_credit()
    w_sums[1].step(0)
    kv_sums[0][1].step(2)
    over[0].step(1)
    parts[1].wait()
    sout[1].take_credit()
    sout[1].step(0)
    over[0].step(2)
    kv_sums[1][1].step(2)
    dall[1].step(2)
    kv_sums[0][0].step(3)
    dall[0].step(2)
    copies[3].wait()
    normed_grad(0)
    kv_sums[1][0].step(2)
    over[0].step(3)
    kv_sums[0][1].step(3)
    keys_back(0)
    w_sums[1].step(1)
    sout[1].step(1)
    over[0].step(4)
    kv_sums[1][1].step(3)
    kv_sums[1][0].step(3)
    keys_back(1)
    weight_part(2)
    w_sums[1].step(2)
    dall[2].step(2)
    normed_grad(1)
    spread[0].step(0)
    w_sums[2].step(0)
    spread[0].step(1)
    finish()
    w_sums[2].step(1)
    w_sums[1].step(3)
    s_sum.step(0)
    over[1].step(0)
    spread[0].step(2)
    s_sum.step(1)
    over[1].step(1)
    w_sums[2].step(2)
    spread[0].step(3)
    s_sum.step(2)
    over[1].step(2)
    over[1].step(3)
    s_sum.step(3)
    dall[1].step(3)
    sout[1].step(2)
    over[1].step(4)
    spread[1].step(0)
    w_sums[2].step(3)
    send_parcels()
    spread[1].step(1)
    spread[1].step(2)
    dall[2].step(3)
    spread[0].step(4)
    dall[0].step(3)
    write_out(0)
    sout[1].step(3)
    spread[1].step(3)
    add_parcels()
    spread[1].step(4)
    write_out(1)
    sout[1].step(4)
    take_totals()
    for step in range(1, 16):
        parcel(step).wait_send()
        total_message(step).wait_send()
    for copy in owns:
        copy.wait()


def back(tok, cot, seg, turn, wq_all, wo_all, small_t, raw_t, q_t, kv_all, mix_t, lsum, res, ffn, gates_t, share, dx, out_part, dw_own):
    vmem = pl.BlockSpec(memory_space=pltpu.VMEM)
    anywhere = pl.BlockSpec(memory_space=pl.ANY)
    kv_slots = column_slots((4, 128, 128), lead=(2, 2))
    return pl.pallas_call(
        back_kernel,
        out_shape=(
            jax.ShapeDtypeStruct((2, 4, 2, 128, 1024), BF),
            jax.ShapeDtypeStruct((4, 2, 128, 1024), BF),
            jax.ShapeDtypeStruct((2, 128, 1024), BF),
            jax.ShapeDtypeStruct((2, 128, 1024), BF),
            jax.ShapeDtypeStruct((128, 2048), F32),
            jax.ShapeDtypeStruct((128, 1024), F32),
            jax.ShapeDtypeStruct((64, 128), F32),
        ),
        in_specs=[
            vmem, vmem, vmem, anywhere, anywhere, anywhere, vmem, anywhere, vmem, anywhere,
            vmem, vmem, vmem, vmem, vmem, vmem, vmem, anywhere, vmem,
        ],
        out_specs=(anywhere,) * 2 + (vmem,) * 5,
        scratch_shapes=[
            pltpu.VMEM((2, 4, 2, 128, 1024), BF),
            pltpu.VMEM((4, 2, 128, 1024), BF),
            pltpu.VMEM((2, 4, 2, 8, 128, 128), BF),
            pltpu.VMEM((2, 2048, 128), F32),
            pltpu.VMEM((64, 128), F32),
            pltpu.VMEM((2, 1024, 128), BF),
            pltpu.VMEM((2, 128, 1024), F32),
            pltpu.VMEM((256, 1024), BF),
            pltpu.VMEM((2, 1024, 128), BF),
            pltpu.VMEM((2, 1024, 128), F32),
            pltpu.VMEM((2, 8, 128, 128), F32),
            pltpu.VMEM((256, 2048), BF),
            pltpu.VMEM((1024, 256), BF),
            pltpu.VMEM((256, 1024), F32),
            pltpu.VMEM((2, 2, 4, 2, 4, 128, 128), BF),
            pltpu.VMEM((3, 4, 2, 128, 1024), BF),
            pltpu.VMEM((4, 2, 64, 128), F32),
            pltpu.VMEM((64, 128), F32),
            pltpu.VMEM((64, 128), F32),
            *column_slots((128, 1024), lead=(3,)),
            *kv_slots,
            pltpu.VMEM((2, 4, 4, 64, 128), BF),
            pltpu.VMEM((2, 4, 4, 64, 128), BF),
            *scatter_slots(64, 128, lead=(2,)),
            *column_slots((64, 128), F32),
            pltpu.VMEM((64, 256), BF),
            pltpu.VMEM((64, 1024), BF),
            pltpu.VMEM((64, 1024), F32),
            pltpu.VMEM((4, 4, 128, 1024), BF),
            *scatter_slots(128, 1024),
            pltpu.VMEM((16, 128, 128), BF),
            pltpu.VMEM((16, 128, 128), BF),
            pltpu.VMEM((64, 128), BF),
            pltpu.VMEM((16, 64, 128), BF),
            pltpu.SemaphoreType.DMA((11, 2, 8)),
            pltpu.SemaphoreType.DMA((6, 2, 2, 8)),
            pltpu.SemaphoreType.DMA((16,)),
            pltpu.SemaphoreType.DMA((16,)),
            pltpu.SemaphoreType.DMA((16,)),
            pltpu.SemaphoreType.DMA((16,)),
            pltpu.SemaphoreType.REGULAR,
            pltpu.SemaphoreType.DMA((10,)),
            pltpu.VMEM((8, 1024), F32),
        ],
        compiler_params=pltpu.CompilerParams(
            collective_id=2, has_side_effects=True, vmem_limit_bytes=63 * MIB
        ),
        cost_estimate=pl.CostEstimate(
            flops=12_000_000_000, bytes_accessed=30_000_000, transcendentals=5_000_000
        ),
    )(tok, cot, seg, turn, wq_all, wo_all, small_t, raw_t, q_t, kv_all, mix_t, lsum, res, ffn, gates_t, share, dx, out_part, dw_own)


def turn_table(length):
    frequency = np.power(np.float32(THETA), -2.0 * np.arange(HD // 2, dtype=np.float32) / HD)
    angle = np.arange(length, dtype=np.float32)[:, None] * frequency.astype(np.float32)[None, :]
    both = np.concatenate([np.cos(angle), np.sin(angle)], axis=1).astype(np.float32)
    return both.reshape(length // 128, 128, HD).transpose(0, 2, 1)


def body(
    tokens,
    cotangent,
    segments,
    routes,
    w_qkv,
    w_out,
    attn_norm,
    ffn_norm,
    q_gain,
    k_gain,
    router,
    w_gate_up,
    w_down,
):
    tok = tokens.reshape(2, 128, 1024)
    cot = cotangent.reshape(2, 128, 1024)
    seg = segments.reshape(2, 8, 1, 128)
    routes_t = routes.reshape(2, 128, 8).transpose(0, 2, 1)
    turn = jnp.asarray(turn_table(1024))
    gains = jnp.pad(jnp.stack([q_gain, k_gain]), ((0, 28), (0, 120)))
    small = jnp.concatenate([router.T, attn_norm[None], ffn_norm[None], gains])
    (
        dy_all, x0, wq_all, wo_all, kv_all, raw_t, small_t, q_t, mix_t, lsum, res, ffn, gates_t, sent
    ) = front(tok, cot, w_qkv, w_out, small, seg, routes_t, turn)
    out_part, moved_dx, share, dw_own = moe(ffn, x0, dy_all, sent, w_gate_up, w_down)
    dgu, dd, output, in_grad, gq, go, gs = back(
        tok, cot, seg, turn, wq_all, wo_all, small_t, raw_t, q_t, kv_all, mix_t, lsum, res, ffn,
        gates_t, share, moved_dx, out_part, dw_own,
    )
    return (
        output.reshape(tokens.shape),
        in_grad.reshape(tokens.shape),
        gq,
        go,
        gs[32],
        gs[33],
        gs[40:48, 0],
        gs[48:56, 0],
        gs[:32].T,
        dgu.astype(F32).reshape(2, 1024, 1024),
        dd.astype(F32).reshape(2, 512, 1024),
    )


def solution(mesh):
    return jax.shard_map(
        body,
        mesh=mesh,
        in_specs=(
            P(None, "expert", "dp", None),
            P(None, "expert", "dp", None),
            P(None, "expert", None),
            P(None, "expert", "dp", None),
            P("dp", None),
            P("dp", None),
            P("dp"),
            P("dp"),
            P("dp"),
            P("dp"),
            P("dp", None),
            P("expert", None, None),
            P("expert", None, None),
        ),
        out_specs=(
            P(None, "expert", "dp", None),
            P(None, "expert", "dp", None),
            P("dp", None),
            P("dp", None),
            P("dp"),
            P("dp"),
            P("dp"),
            P("dp"),
            P("dp", None),
            P("expert", None, None),
            P("expert", None, None),
        ),
        check_vma=False,
    )
```

```python
import jax
import jax.numpy as jnp
import numpy as np
from jax import lax
from jax.experimental import pallas as pl
from jax.experimental.pallas import tpu as pltpu
from jax.sharding import PartitionSpec as P

HD = 64
EPSILON = 1e-06
THETA = 10000.0
MASKED = -1e30

BF = jnp.bfloat16
F32 = jnp.float32
SLOTS = 48
CHUNK = 256
MIB = 1024 * 1024


def nn(a, b):
    return lax.dot_general(a, b, (((1,), (0,)), ((), ())), preferred_element_type=F32)


def nt(a, b):
    return lax.dot_general(a, b, (((1,), (1,)), ((), ())), preferred_element_type=F32)


def tn(a, b):
    return lax.dot_general(a, b, (((0,), (0,)), ((), ())), preferred_element_type=F32)


def send(src, dst, send_sem, recv_sem, device):
    return pltpu.make_async_remote_copy(
        src_ref=src, dst_ref=dst, send_sem=send_sem, recv_sem=recv_sem, device_id=device
    )


def next_to(p):
    return (p + 1) % 4, (p + 3) % 4, (p + 2) % 4


def greet(devices):
    sem = pltpu.get_barrier_semaphore()
    for device in devices:
        pl.semaphore_signal(sem, inc=1, device_id=device)
    pl.semaphore_wait(sem, len(devices))


class Plane:
    def __init__(self):
        self.me = lax.axis_index("expert")
        self.z = self.me // 4
        self.x = self.me % 4

    def own(self, half):
        return (self.x, self.z) if half == 0 else (self.z, self.x)

    def device(self, half, p, q):
        return {"expert": q * 4 + p if half == 0 else p * 4 + q}

    def others(self):
        return [{"expert": (self.me + step) % 16} for step in range(1, 16)]

    def neighbours(self):
        zn, zp, _ = next_to(self.z)
        xn, xp, _ = next_to(self.x)
        return [{"expert": k} for k in (zn * 4 + self.x, zp * 4 + self.x, self.z * 4 + xn, self.z * 4 + xp)]


class Column:
    def __init__(self):
        self.me = lax.axis_index("dp")
        self.y = self.me // 2
        self.c = self.me % 2

    def neighbours(self):
        yn, yp, _ = next_to(self.y)
        return [self.to(yn), self.to(yp), self.other()]

    def to(self, y):
        return {"dp": y * 2 + self.c}

    def other(self):
        return {"dp": self.y * 2 + 1 - self.c}


class PlaneStep:
    def at(self, half, p, q, rows):
        return self.ref.at[q, p, rows] if half == 0 else self.ref.at[p, q, rows]

    def line(self, half, q, rows):
        return self.ref.at[q, :, rows] if half == 0 else self.ref.at[:, q, rows]

    def rows(self, half):
        quarter = self.height // 4
        base = 2 * quarter * half
        return pl.ds(base, 2 * quarter), pl.ds(base, quarter), pl.ds(base + quarter, quarter)


class Gather(PlaneStep):
    def __init__(self, plane, ref, sems, height=128):
        self.plane, self.ref, self.sems, self.height = plane, ref, sems, height

    def message(self, half, i):
        p, q = self.plane.own(half)
        pn, pp, _ = next_to(p)
        qn, qp, _ = next_to(q)
        full, first, second = self.rows(half)
        view, to = [
            lambda: (self.at(half, p, q, full), (pn, q)),
            lambda: (self.at(half, p, q, full), (pp, q)),
            lambda: (self.at(half, pp, q, first), (pn, q)),
            lambda: (self.at(half, pn, q, second), (pp, q)),
            lambda: (self.line(half, q, full), (p, qn)),
            lambda: (self.line(half, q, full), (p, qp)),
            lambda: (self.line(half, qp, first), (p, qn)),
            lambda: (self.line(half, qn, second), (p, qp)),
        ][i]()
        sems = self.sems
        return send(view, view, sems.at[0, half, i], sems.at[1, half, i], self.plane.device(half, *to))

    def step(self, n):
        waits, starts = [
            ((), (0, 1)),
            ((0, 1), (2, 3)),
            ((2, 3), (4, 5)),
            ((4, 5), (6, 7)),
            ((6, 7), ()),
        ][n]
        for half in range(2):
            for i in waits:
                self.message(half, i).wait_recv()
            for i in starts:
                self.message(half, i).start()
        if n == 4:
            for half in range(2):
                for i in range(8):
                    self.message(half, i).wait_send()


class Scatter(PlaneStep):
    def __init__(self, plane, ref, slots, sems, store, free=None, height=128):
        self.plane, self.ref, self.slots, self.sems = plane, ref, slots, sems
        self.store, self.free, self.height = store, free, height

    def message(self, half, i):
        p, q = self.plane.own(half)
        pn, pp, po = next_to(p)
        qn, qp, qo = next_to(q)
        full, first, second = self.rows(half)
        r1, r2, r3, r4 = self.slots
        view, slot, to = [
            lambda: (self.line(half, qo, first), r1.at[half, 0], (p, qn)),
            lambda: (self.line(half, qo, second), r1.at[half, 1], (p, qp)),
            lambda: (self.line(half, qn, full), r2.at[half, 0], (p, qn)),
            lambda: (self.line(half, qp, full), r2.at[half, 1], (p, qp)),
            lambda: (self.at(half, po, q, first), r3.at[half, 0], (pn, q)),
            lambda: (self.at(half, po, q, second), r3.at[half, 1], (pp, q)),
            lambda: (self.at(half, pn, q, full), r4.at[half, 0], (pn, q)),
            lambda: (self.at(half, pp, q, full), r4.at[half, 1], (pp, q)),
        ][i]()
        sems = self.sems
        return send(view, slot, sems.at[0, half, i], sems.at[1, half, i], self.plane.device(half, *to))

    def add_line(self, half, q, part, parts, slots):
        quarter = self.height // 4
        offset = quarter * (2 * half + part)
        groups = quarter * parts // 16

        @pl.loop(0, 4 * groups)
        def _(n):
            j, k = n // groups, n % groups
            rows = pl.ds(pl.multiple_of(offset + k * 16, 16), 16)
            some = pl.ds(pl.multiple_of(k * 16, 16), 16)
            place = (q, j, rows) if half == 0 else (j, q, rows)
            total = self.ref[place].astype(F32)
            for ref, side in slots:
                total += ref[half, side, j, some].astype(F32)
            self.ref[place] = total.astype(BF)

    def add_at(self, half, p, q, part, slot):
        quarter = self.height // 4
        ref, side = slot

        @pl.loop(0, quarter // 16)
        def _(k):
            rows = pl.ds(pl.multiple_of(quarter * (2 * half + part) + k * 16, 16), 16)
            place = (q, p, rows) if half == 0 else (p, q, rows)
            got = ref[half, side, pl.ds(pl.multiple_of(k * 16, 16), 16)].astype(F32)
            self.ref[place] = (self.ref[place].astype(F32) + got).astype(BF)

    def step(self, n):
        r1, r2, r3, r4 = self.slots
        for half in range(2):
            p, q = self.plane.own(half)
            pn, pp, po = next_to(p)
            qn, qp, qo = next_to(q)
            if n == 0:
                self.message(half, 0).start()
                self.message(half, 1).start()
            elif n == 1:
                self.message(half, 0).wait_recv()
                self.add_line(half, qn, 0, 1, [(r1, 0)])
                self.message(half, 2).start()
                self.message(half, 1).wait_recv()
                self.add_line(half, qp, 1, 1, [(r1, 1)])
                self.message(half, 3).start()
            elif n == 2:
                self.message(half, 2).wait_recv()
                self.message(half, 3).wait_recv()
                self.add_line(half, q, 0, 2, [(r2, 0), (r2, 1)])
                self.message(half, 4).start()
                self.message(half, 5).start()
            elif n == 3:
                self.message(half, 4).wait_recv()
                self.add_at(half, pn, q, 0, (r3, 0))
                self.message(half, 6).start()
                self.message(half, 5).wait_recv()
                self.add_at(half, pp, q, 1, (r3, 1))
                self.message(half, 7).start()
            elif n == 4:
                self.message(half, 6).wait_recv()
                self.message(half, 7).wait_recv()

                @pl.loop(0, self.height // 32)
                def _(k):
                    rows = pl.ds(pl.multiple_of(self.height // 2 * half + k * 16, 16), 16)
                    place = (q, p, rows) if half == 0 else (p, q, rows)
                    some = pl.ds(pl.multiple_of(k * 16, 16), 16)
                    total = self.ref[place].astype(F32)
                    total += r4[half, 0, some].astype(F32)
                    total += r4[half, 1, some].astype(F32)
                    self.store(place, rows, total)
        if n == 4:
            for half in range(2):
                for i in range(8):
                    self.message(half, i).wait_send()

    def give_credit(self):
        for device in self.plane.neighbours():
            pl.semaphore_signal(self.free, inc=1, device_id=device)

    def take_credit(self):
        pl.semaphore_wait(self.free, 4)


def scatter_slots(height, width, lead=()):
    quarter = height // 4
    return [
        pltpu.VMEM((*lead, 2, 2, 4, quarter, width), BF),
        pltpu.VMEM((*lead, 2, 2, 4, 2 * quarter, width), BF),
        pltpu.VMEM((*lead, 2, 2, quarter, width), BF),
        pltpu.VMEM((*lead, 2, 2, 2 * quarter, width), BF),
    ]


class ColumnGather:
    def __init__(self, column, ref, sems, count, own=None):
        self.column, self.ref, self.sems, self.count = column, ref, sems, count
        self.own = own

    def message(self, i):
        y, c = self.column.y, self.column.c
        yn, yp, yo = next_to(y)
        half = self.count // 2
        ref, column = self.ref, self.column
        view, device = [
            lambda: (ref.at[y, c], column.to(yn)),
            lambda: (ref.at[y, c], column.to(yp)),
            lambda: (ref.at[y, c], column.other()),
            lambda: (ref.at[yp, c, pl.ds(0, half)], column.to(yn)),
            lambda: (ref.at[yn, c, pl.ds(half, half)], column.to(yp)),
            lambda: (ref.at[yp, c], column.other()),
            lambda: (ref.at[yn, c], column.other()),
            lambda: (ref.at[yo, c], column.other()),
        ][i]()
        source = self.own if i < 3 and self.own is not None else view
        return send(source, view, self.sems.at[0, i], self.sems.at[1, i], device)

    def step(self, n):
        order = [
            [("s", 0), ("s", 1), ("s", 2)],
            [("w", 0), ("s", 3), ("s", 5), ("w", 1), ("s", 4), ("s", 6)],
            [("w", 3), ("w", 4), ("s", 7)],
            [("w", 2), ("w", 5), ("w", 6), ("w", 7)],
        ][n]
        for what, i in order:
            if what == "s":
                self.message(i).start()
            else:
                self.message(i).wait_recv()
        if n == 3:
            for i in range(8):
                self.message(i).wait_send()


class ColumnScatter:
    def __init__(self, column, ref, slots, sems, count, store, group=16):
        self.column, self.ref, self.slots, self.sems = column, ref, slots, sems
        self.count, self.store, self.group = count, store, group

    def message(self, i):
        y, c = self.column.y, self.column.c
        yn, yp, yo = next_to(y)
        half = self.count // 2
        ref, column = self.ref, self.column
        ra, rb, rc = self.slots
        view, slot, device = [
            lambda: (ref.at[:, 1 - c], ra, column.other()),
            lambda: (ref.at[yo, c, pl.ds(0, half)], rb.at[0], column.to(yn)),
            lambda: (ref.at[yo, c, pl.ds(half, half)], rb.at[1], column.to(yp)),
            lambda: (ref.at[yn, c], rc.at[0], column.to(yn)),
            lambda: (ref.at[yp, c], rc.at[1], column.to(yp)),
        ][i]()
        return send(view, slot, self.sems.at[0, i], self.sems.at[1, i], device)

    def some(self, k, base=0):
        return pl.ds(pl.multiple_of(base + k * self.group, self.group), self.group)

    def step(self, n):
        y, c = self.column.y, self.column.c
        yn, yp, yo = next_to(y)
        ref, (ra, rb, rc) = self.ref, self.slots
        low = ref.dtype
        half = self.count // 2
        groups = self.count // self.group
        if n == 0:
            self.message(0).start()
        elif n == 1:
            self.message(0).wait_recv()

            @pl.loop(0, 4 * groups)
            def _(k):
                j, r = k // groups, self.some(k % groups)
                ref[j, c, r] = (ref[j, c, r].astype(F32) + ra[j, r].astype(F32)).astype(low)

            self.message(1).start()
            self.message(2).start()
        elif n == 2:
            for side, to in ((0, yn), (1, yp)):
                self.message(1 + side).wait_recv()

                @pl.loop(0, groups // 2)
                def _(k):
                    r = self.some(k, side * half)
                    got = rb[side, self.some(k)].astype(F32)
                    ref[to, c, r] = (ref[to, c, r].astype(F32) + got).astype(low)

                self.message(3 + side).start()
        else:
            self.message(3).wait_recv()
            self.message(4).wait_recv()

            @pl.loop(0, groups)
            def _(k):
                r = self.some(k)
                total = ref[y, c, r].astype(F32) + rc[0, r].astype(F32) + rc[1, r].astype(F32)
                self.store(r, total)

            for i in range(5):
                self.message(i).wait_send()


def column_slots(shape, dtype=BF, lead=()):
    count, rest = shape[0], shape[1:]
    return [
        pltpu.VMEM((*lead, 4, count, *rest), dtype),
        pltpu.VMEM((*lead, 2, count // 2, *rest), dtype),
        pltpu.VMEM((*lead, 2, count, *rest), dtype),
    ]


def turned(v, cosine, sine):
    a, b = v[:32], v[32:]
    return jnp.concatenate([a * cosine - b * sine, b * cosine + a * sine], axis=0)


def inverse_rms(v, axis):
    return lax.rsqrt(jnp.mean(v * v, axis=axis, keepdims=True) + EPSILON)


def head_gain(small_t, row):
    pieces = [small_t[:, 128 * b : 128 * (b + 1)] for b in range(8)]
    tall = jnp.concatenate([piece.T[:8] for piece in pieces], axis=0)
    return jnp.broadcast_to(tall[:, row : row + 1], (64, 128))


def document_bias(seg_ref, bias, mb, mine):
    own = seg_ref[mb, mine].astype(F32)
    for b in range(8):
        keys = jnp.broadcast_to(seg_ref[mb, b].astype(F32), (128, 128)).T
        bias[mb, 128 * b : 128 * (b + 1)] = jnp.where(keys == own, 0.0, MASKED).astype(bias.dtype)


def pair_columns(ref, mb, g):
    both = ref[mb, pl.ds(pl.multiple_of(g * 128, 128), 128)]
    return jnp.concatenate([both[:64], both[64:]], axis=1)


def front_kernel(
    tok, cot, wq, wo, small, seg_ref, routes_ref, turn_hbm,
    dy_out, x0_out, wq_out, wo_out, kv_out, raw_out,
    small_t, q_t, mix_t, lsum, res, ffn, gates_t, g_all,
    dy_all, x0_all, wq_all, wo_all, kv_all, raw_t, small_all, normed, bias, turn, plane_sems, column_sems,
    sent, gsend, grecv, local,
):
    plane, column = Plane(), Column()
    y, c = column.y, column.c
    copies = [
        pltpu.make_async_copy(small, small_all.at[y, c], local.at[0]),
        pltpu.make_async_copy(wq.at[:, 1024:2048], wq_all.at[1, y, c], local.at[1]),
        pltpu.make_async_copy(wq.at[:, 0:1024], wq_all.at[0, y, c], local.at[3]),
        pltpu.make_async_copy(wo, wo_all.at[y, c], local.at[5]),
        pltpu.make_async_copy(turn_hbm.at[column.me], turn, local.at[6]),
    ]
    for copy in copies:
        copy.start()
    outs = [
        pltpu.make_async_copy(wq_all, wq_out, local.at[7]),
        pltpu.make_async_copy(wo_all, wo_out, local.at[8]),
        pltpu.make_async_copy(kv_all, kv_out, local.at[9]),
        pltpu.make_async_copy(raw_t, raw_out, local.at[10]),
        pltpu.make_async_copy(dy_all.at[0], dy_out.at[0], local.at[11]),
        pltpu.make_async_copy(dy_all.at[1], dy_out.at[1], local.at[2]),
        pltpu.make_async_copy(x0_all, x0_out, local.at[4]),
    ]
    for mb in range(2):
        dy_all[mb, plane.z, plane.x] = cot[mb]
    greet(plane.others() + column.neighbours())
    gdy = [Gather(plane, dy_all.at[mb], plane_sems.at[mb]) for mb in range(2)]
    gx = Gather(plane, x0_all, plane_sems.at[2])
    w_small = ColumnGather(column, small_all, column_sems.at[0], 64)
    w_q = ColumnGather(column, wq_all.at[0], column_sems.at[1], 128)
    w_kv = ColumnGather(column, wq_all.at[1], column_sems.at[2], 128)
    w_o = ColumnGather(column, wo_all, column_sems.at[3], 128)
    kv = [ColumnGather(column, kv_all.at[mb], column_sems.at[4 + mb], 8) for mb in range(2)]
    def both_biases():
        for mb in range(2):
            document_bias(seg_ref, bias, mb, column.me)

    def norm_tokens():
        for b in range(8):
            small_t[:, 128 * b : 128 * (b + 1)] = small_all[b // 2, b % 2].astype(F32)
        attn_gain = small_t[32:33]
        for mb in range(2):
            v = tok[mb].astype(F32)
            normed[128 * mb : 128 * (mb + 1)] = (v * inverse_rms(v, 1) * attn_gain).astype(BF)

    def project(k):
        @pl.loop(0, 2)
        def _(n):
            cols = pl.ds(pl.multiple_of(n * 512, 512), 512)
            rows = pl.ds(pl.multiple_of(1024 * k + n * 512, 512), 512)
            got = nn(normed[...], wq_all[k, :, :, :, cols].reshape(1024, 512))
            for mb in range(2):
                raw_t[mb, rows] = got[128 * mb : 128 * (mb + 1)].T

    def key_heads(mb):
        @pl.loop(0, 8)
        def _(g):
            v = raw_t[mb, pl.ds(pl.multiple_of(1024 + g * 64, 64), 64)]
            key = turned(v * inverse_rms(v, 0) * key_gain, cosine, sine)
            value = raw_t[mb, pl.ds(pl.multiple_of(1536 + g * 64, 64), 64)]
            kv_all[mb, y, c, g] = jnp.concatenate([key, value], axis=0).T.astype(BF)

    def query_heads(mb):
        @pl.loop(0, 16)
        def _(h):
            rows = pl.ds(pl.multiple_of(h * 64, 64), 64)
            v = raw_t[mb, rows]
            query = turned(v * inverse_rms(v, 0) * query_gain, cosine, sine)
            q_t[mb, rows] = (query.astype(BF).astype(F32) * HD ** (-0.5)).astype(BF)

    def attend(mb, start, stop):
        @pl.loop(start, stop)
        def _(g):
            query = pair_columns(q_t, mb, g)
            query = jnp.concatenate([query, jnp.zeros_like(query)], axis=0)
            total = jnp.zeros((1, 256), F32)
            mixed = jnp.zeros((128, 256), F32)
            for j in range(4):
                keys = kv_all[mb, j, :, g].reshape(256, 128)
                there = bias[mb, 256 * j : 256 * (j + 1)].astype(F32)
                p = jnp.exp(nn(keys, query) + jnp.concatenate([there, there], axis=1))
                total += jnp.sum(p, axis=0, keepdims=True)
                mixed += tn(keys, p.astype(BF))
            lsum[mb, g] = total
            mixed = (mixed[64:] / total).astype(BF)
            both = jnp.concatenate([mixed[:, :128], mixed[:, 128:]], axis=0)
            mix_t[mb, pl.ds(pl.multiple_of(g * 128, 128), 128)] = both

    def finish(mb):
        @pl.loop(0, 2)
        def _(n):
            cols = pl.ds(pl.multiple_of(n * 512, 512), 512)
            got = tn(mix_t[mb], wo_all[:, :, :, cols].reshape(1024, 512))
            res[mb, :, cols] = tok[mb, :, cols].astype(F32) + got

        v = res[mb]
        low = (v * inverse_rms(v, 1) * small_t[33:34]).astype(BF)
        ffn[mb] = low
        logits = nt(small_t[:32].astype(BF), low)
        ids = lax.broadcasted_iota(jnp.int32, (32, 128), 0)
        routed = ids == routes_ref[mb, 0:1]
        for k in range(1, 8):
            routed = routed | (ids == routes_ref[mb, k : k + 1])
        top = jnp.max(jnp.where(routed, logits, MASKED), axis=0, keepdims=True)
        weight = jnp.where(routed, jnp.exp(logits - top), 0.0)
        gates = weight / jnp.sum(weight, axis=0, keepdims=True)
        gates_t[mb] = gates
        for k in range(16):
            sent[k, 2 * mb : 2 * mb + 2] = gates[2 * k : 2 * k + 2]

    def gate_message(step):
        to = (plane.me + step) % 16
        return send(
            sent.at[to], g_all.at[plane.me], gsend.at[step], grecv.at[step], {"expert": to}
        )

    def send_gates():
        for step in range(1, 16):
            gate_message(step).start()
        g_all[plane.me] = sent[plane.me]

    def take_gates():
        for step in range(1, 16):
            gate_message(step).wait_recv()
        for step in range(1, 16):
            gate_message(step).wait_send()

    sent[...] = jnp.zeros_like(sent)
    copies[0].wait()
    w_small.step(0)
    gdy[0].step(0)
    copies[1].wait()
    w_kv.step(0)
    w_small.step(1)
    gdy[1].step(0)
    copies[2].wait()
    w_q.step(0)
    gdy[0].step(1)
    gdy[0].step(2)
    w_small.step(2)
    w_kv.step(1)
    gdy[1].step(1)
    w_q.step(1)
    copies[3].wait()
    w_o.step(0)
    w_small.step(3)
    norm_tokens()
    w_kv.step(2)
    w_kv.step(3)
    project(1)
    gdy[1].step(2)
    query_gain = head_gain(small_t[...], 34)
    key_gain = head_gain(small_t[...], 35)
    copies[4].wait()
    cosine, sine = turn[:32], turn[32:]
    key_heads(0)
    kv[0].step(0)
    kv[0].step(1)
    both_biases()
    key_heads(1)
    w_q.step(2)
    gdy[0].step(3)
    w_o.step(1)
    kv[0].step(2)
    w_q.step(3)
    outs[0].start()
    project(0)
    outs[3].start()
    kv[1].step(0)
    w_o.step(2)
    gdy[1].step(3)
    query_heads(0)
    kv[0].step(3)
    attend(0, 0, 4)
    attend(0, 4, 8)
    w_o.step(3)
    outs[1].start()
    finish(0)
    x0_all[plane.z, plane.x] = ffn[0]
    gx.step(0)
    query_heads(1)
    kv[1].step(1)
    gx.step(1)
    kv[1].step(2)
    gdy[1].step(4)
    outs[5].start()
    gx.step(2)
    kv[1].step(3)
    outs[2].start()
    attend(1, 0, 4)
    gx.step(3)
    attend(1, 4, 8)
    finish(1)
    send_gates()
    gdy[0].step(4)
    outs[4].start()
    take_gates()
    gx.step(4)
    outs[6].start()
    for copy in outs:
        copy.wait()


def front(tok, cot, wq, wo, small, seg, routes_t, turn):
    vmem = pl.BlockSpec(memory_space=pltpu.VMEM)
    anywhere = pl.BlockSpec(memory_space=pl.ANY)
    return pl.pallas_call(
        front_kernel,
        out_shape=(
            jax.ShapeDtypeStruct((2, 4, 4, 128, 1024), BF),
            jax.ShapeDtypeStruct((4, 4, 128, 1024), BF),
            jax.ShapeDtypeStruct((2, 4, 2, 128, 1024), BF),
            jax.ShapeDtypeStruct((4, 2, 128, 1024), BF),
            jax.ShapeDtypeStruct((2, 4, 2, 8, 128, 128), BF),
            jax.ShapeDtypeStruct((2, 2048, 128), F32),
            jax.ShapeDtypeStruct((64, 1024), F32),
            jax.ShapeDtypeStruct((2, 1024, 128), BF),
            jax.ShapeDtypeStruct((2, 1024, 128), BF),
            jax.ShapeDtypeStruct((2, 8, 1, 256), F32),
            jax.ShapeDtypeStruct((2, 128, 1024), F32),
            jax.ShapeDtypeStruct((2, 128, 1024), BF),
            jax.ShapeDtypeStruct((2, 32, 128), F32),
            jax.ShapeDtypeStruct((16, 8, 128), F32),
        ),
        in_specs=[vmem, vmem, anywhere, anywhere, anywhere, vmem, vmem, anywhere],
        out_specs=(anywhere,) * 6 + (vmem,) * 8,
        scratch_shapes=[
            pltpu.VMEM((2, 4, 4, 128, 1024), BF),
            pltpu.VMEM((4, 4, 128, 1024), BF),
            pltpu.VMEM((2, 4, 2, 128, 1024), BF),
            pltpu.VMEM((4, 2, 128, 1024), BF),
            pltpu.VMEM((2, 4, 2, 8, 128, 128), BF),
            pltpu.VMEM((2, 2048, 128), F32),
            pltpu.VMEM((4, 2, 64, 128), BF),
            pltpu.VMEM((256, 1024), BF),
            pltpu.VMEM((2, 1024, 128), F32),
            pltpu.VMEM((64, 128), F32),
            pltpu.SemaphoreType.DMA((3, 2, 2, 8)),
            pltpu.SemaphoreType.DMA((6, 2, 8)),
            pltpu.VMEM((16, 8, 128), F32),
            pltpu.SemaphoreType.DMA((16,)),
            pltpu.SemaphoreType.DMA((16,)),
            pltpu.SemaphoreType.DMA((12,)),
        ],
        compiler_params=pltpu.CompilerParams(
            collective_id=0, has_side_effects=True, vmem_limit_bytes=56 * MIB
        ),
        cost_estimate=pl.CostEstimate(
            flops=5_000_000_000, bytes_accessed=30_000_000, transcendentals=5_000_000
        ),
    )(tok, cot, wq, wo, small, seg, routes_t, turn)


def moe_kernel(
    ffn_ref, x0_hbm, dy_hbm, g_all, wgu_hbm, wd_hbm,
    out_hbm, dx_ref, h_ref, dw_own,
    dw, x_all, dy_all, r1, r2, r3, r4, xs, ds, os, gc, act, a1, a2, ggu, ranks, hcol, hs,
    wgu, wd, ra, rb, rc, sems, column_sems, hsend, hrecv, free, local,
):
    plane, column = Plane(), Column()
    me, z, x = plane.me, plane.z, plane.x
    own = [
        pltpu.make_async_copy(ffn_ref.at[1], x_all.at[1, z, x], local.at[0]),
        pltpu.make_async_copy(x0_hbm, x_all.at[0], local.at[2]),
        pltpu.make_async_copy(dy_hbm.at[0], dy_all.at[0], local.at[3]),
        pltpu.make_async_copy(wgu_hbm, wgu, local.at[4]),
        pltpu.make_async_copy(wd_hbm, wd, local.at[5]),
        pltpu.make_async_copy(dy_hbm.at[1], dy_all.at[1], local.at[1]),
    ]
    outs = [pltpu.make_async_copy(x_all.at[mb], out_hbm.at[mb], local.at[6 + mb]) for mb in range(2)]
    for copy in own:
        copy.start()
    greet(plane.others() + column.neighbours())
    own[0].wait()

    def h_message(step):
        to = (me + step) % 16
        return pltpu.make_async_remote_copy(
            src_ref=hs.at[to], dst_ref=h_ref.at[me],
            send_sem=hsend.at[step], recv_sem=hrecv.at[step], device_id={"expert": to},
        )

    gx = Gather(plane, x_all.at[1], sems.at[0])

    def into(mb):
        def store(place, rows, total):
            dx_ref[mb, rows] = total

        return store

    sdx = [
        Scatter(plane, dy_all.at[mb], (r1, r2, r3, r4), sems.at[1 + mb], into(mb), free)
        for mb in range(2)
    ]

    def own_part(k):
        def store(r, total):
            dw_own[k, r] = total.astype(BF)

        return store

    dsum = [
        ColumnScatter(
            column, dw.at[k], (ra.at[k], rb.at[k], rc.at[k]), column_sems.at[k], 128, own_part(k)
        )
        for k in range(3)
    ]
    earlier = (
        lax.broadcasted_iota(jnp.int32, (128, 128), 0)
        < lax.broadcasted_iota(jnp.int32, (128, 128), 1)
    ).astype(F32).astype(BF)

    @pl.loop(0, 16)
    def _(s):
        named = g_all[s] > 0.0
        before = nn(named.astype(F32).astype(BF), earlier)
        ranks[s] = jnp.where(named, before, -1.0)

    slot_ids = lax.broadcasted_iota(jnp.int32, (SLOTS, 128), 0).astype(F32)

    def places(p, mb):
        ranked = [ranks[2 * p + k] for k in range(2)]
        return [
            [(slot_ids == ranked[k][2 * mb + e : 2 * mb + e + 1]).astype(F32) for k in range(2)]
            for e in range(2)
        ]

    def gated(p, mb, hot):
        gates = [g_all[2 * p + k] for k in range(2)]
        return [
            [hot[e][k] * gates[k][2 * mb + e : 2 * mb + e + 1] for k in range(2)] for e in range(2)
        ]

    def spread(hot):
        blank = jnp.zeros((SLOTS, 128), F32)
        rows = []
        for e in range(2):
            rows.append(jnp.concatenate([hot[e][0], blank], axis=1))
            rows.append(jnp.concatenate([blank, hot[e][1]], axis=1))
        return jnp.concatenate(rows, axis=0).astype(BF)

    def span(p):
        return pl.ds(pl.multiple_of(p * 2 * SLOTS, 32), 2 * SLOTS)

    def pair(p):
        return p // 2, pl.ds(2 * (p % 2), 2)

    def select(mb):
        @pl.loop(0, 8)
        def _(p):
            hot = places(p, mb)
            line, two = pair(p)
            rows = nn(spread(hot), x_all[mb, line, two].reshape(256, 1024)).astype(BF)
            drows = nn(spread(gated(p, mb, hot)), dy_all[mb, line, two].reshape(256, 1024)).astype(BF)
            for e in range(2):
                xs[e, span(p)] = rows[2 * SLOTS * e : 2 * SLOTS * (e + 1)]
                ds[e, span(p)] = drows[2 * SLOTS * e : 2 * SLOTS * (e + 1)]

    chunks = 16 * SLOTS // CHUNK

    def forward(e):
        @pl.loop(0, chunks)
        def _(c):
            r = pl.ds(pl.multiple_of(c * CHUNK, CHUNK), CHUNK)
            gu = nn(xs[e, r], wgu[e])
            g, u = gu[:, :512], gu[:, 512:]
            sig = 1.0 / (1.0 + jnp.exp(-g))
            silu = g * sig
            active = (silu * u).astype(BF)
            act[e, r] = active
            a1[e, r] = (u * sig * (1.0 + g * (1.0 - sig))).astype(BF)
            a2[e, r] = silu.astype(BF)
            o = nn(active, wd[e]).astype(BF)
            os[e, r] = o
            hcol[e, r] = jnp.sum(o.astype(F32) * ds[e, r].astype(F32), axis=-1, keepdims=True)

    def combine_out(mb):
        @pl.loop(0, 8)
        def _(p):
            hot = places(p, mb)
            line, two = pair(p)
            both = jnp.concatenate([os[0, span(p)], os[1, span(p)]], axis=0)
            got = tn(spread(gated(p, mb, hot)), both).astype(BF)
            x_all[mb, line, two] = got.reshape(2, 128, 1024)
            for e in range(2):
                column_of = hcol[e, span(p)]
                for k in range(2):
                    row = 2 * mb + e
                    part = hot[e][k] * column_of[SLOTS * k : SLOTS * (k + 1)]
                    hs[2 * p + k, row : row + 1] = jnp.sum(part, axis=0, keepdims=True)

    def add_part(mb, k, n, fresh):
        fresh = fresh.reshape(2, 128, 1024)
        if mb == 1:
            fresh += dw[k, n].astype(F32)
        dw[k, n] = fresh.astype(BF)

    def backward(mb, e):
        @pl.loop(0, chunks)
        def _(c):
            r = pl.ds(pl.multiple_of(c * CHUNK, CHUNK), CHUNK)
            ga = nt(ds[e, r], wd[e])
            grad = jnp.concatenate(
                [ga * a1[e, r].astype(F32), ga * a2[e, r].astype(F32)], axis=1
            ).astype(BF)
            ggu[r] = grad
            gc[e, r] = nt(grad, wgu[e]).astype(BF)

        @pl.loop(0, 4)
        def _(m):
            cols = pl.ds(pl.multiple_of(m * 256, 256), 256)
            add_part(mb, e, m, tn(xs[e, :, cols], ggu[...]))

        @pl.loop(0, 2)
        def _(m):
            cols = pl.ds(pl.multiple_of(m * 256, 256), 256)
            add_part(mb, 2, 2 * e + m, tn(act[e, :, cols], ds[e]))

    def combine_dx(mb):
        @pl.loop(0, 8)
        def _(p):
            line, two = pair(p)
            both = jnp.concatenate([gc[0, span(p)], gc[1, span(p)]], axis=0)
            got = tn(spread(places(p, mb)), both).astype(BF)
            dy_all[mb, line, two] = got.reshape(2, 128, 1024)

    gx.step(0)
    own[1].wait()
    own[2].wait()
    select(0)
    gx.step(1)
    own[3].wait()
    own[4].wait()
    forward(0)
    gx.step(2)
    forward(1)
    combine_out(0)
    outs[0].start()
    backward(0, 0)
    gx.step(3)
    backward(0, 1)
    combine_dx(0)
    sdx[0].step(0)
    gx.step(4)
    own[5].wait()
    select(1)
    forward(1)
    sdx[0].step(1)
    forward(0)
    backward(1, 0)
    dsum[0].step(0)
    sdx[0].step(2)
    backward(1, 1)
    sdx[0].step(3)
    dsum[1].step(0)
    dsum[2].step(0)
    dsum[0].step(1)
    combine_dx(1)
    sdx[0].step(4)
    sdx[0].give_credit()
    sdx[1].take_credit()
    sdx[1].step(0)
    dsum[2].step(1)
    combine_out(1)
    outs[1].start()
    dsum[1].step(1)
    sdx[1].step(1)
    dsum[0].step(2)
    dsum[1].step(2)
    dsum[2].step(2)
    sdx[1].step(2)
    h_ref[me] = hs[me]
    for step in range(1, 16):
        h_message(step).start()
    sdx[1].step(3)
    dsum[0].step(3)
    dsum[2].step(3)
    dsum[1].step(3)
    sdx[1].step(4)
    for step in range(1, 16):
        h_message(step).wait_recv()
    for step in range(1, 16):
        h_message(step).wait_send()
    for copy in outs:
        copy.wait()


def moe(ffn, x0, dy, gates, w_gate_up, w_down):
    vmem = pl.BlockSpec(memory_space=pltpu.VMEM)
    anywhere = pl.BlockSpec(memory_space=pl.ANY)
    rows = 16 * SLOTS
    return pl.pallas_call(
        moe_kernel,
        out_shape=(
            jax.ShapeDtypeStruct((2, 4, 4, 128, 1024), BF),
            jax.ShapeDtypeStruct((2, 128, 1024), F32),
            jax.ShapeDtypeStruct((16, 8, 128), F32),
            jax.ShapeDtypeStruct((3, 128, 1024), BF),
        ),
        in_specs=[anywhere, anywhere, anywhere, vmem, anywhere, anywhere],
        out_specs=(anywhere,) + (vmem,) * 3,
        scratch_shapes=[
            pltpu.VMEM((3, 4, 2, 128, 1024), BF),
            pltpu.VMEM((2, 4, 4, 128, 1024), BF),
            pltpu.VMEM((2, 4, 4, 128, 1024), BF),
            *scatter_slots(128, 1024),
            pltpu.VMEM((2, rows, 1024), BF),
            pltpu.VMEM((2, rows, 1024), BF),
            pltpu.VMEM((2, rows, 1024), BF),
            pltpu.VMEM((2, rows, 1024), BF),
            pltpu.VMEM((2, rows, 512), BF),
            pltpu.VMEM((2, rows, 512), BF),
            pltpu.VMEM((2, rows, 512), BF),
            pltpu.VMEM((rows, 1024), BF),
            pltpu.VMEM((16, 8, 128), F32),
            pltpu.VMEM((2, rows, 1), F32),
            pltpu.VMEM((16, 8, 128), F32),
            pltpu.VMEM((2, 1024, 1024), BF),
            pltpu.VMEM((2, 512, 1024), BF),
            *column_slots((128, 1024), lead=(3,)),
            pltpu.SemaphoreType.DMA((3, 2, 2, 8)),
            pltpu.SemaphoreType.DMA((3, 2, 8)),
            pltpu.SemaphoreType.DMA((16,)),
            pltpu.SemaphoreType.DMA((16,)),
            pltpu.SemaphoreType.REGULAR,
            pltpu.SemaphoreType.DMA((8,)),
        ],
        compiler_params=pltpu.CompilerParams(
            collective_id=1, has_side_effects=True, vmem_limit_bytes=63 * MIB
        ),
        cost_estimate=pl.CostEstimate(
            flops=30_000_000_000, bytes_accessed=30_000_000, transcendentals=2_000_000
        ),
    )(ffn, x0, dy, gates, w_gate_up, w_down)


def norm_grad(grad, v, inverse, gain, axis):
    scaled = grad * gain
    moment = jnp.mean(scaled * v, axis=axis, keepdims=True)
    return inverse * (scaled - v * (inverse * inverse * moment)), grad * (v * inverse)


def back_kernel(
    tok, cot, seg_ref, turn_hbm, wq_hbm, wo_hbm, small_t, raw_hbm, q_t, kv_hbm, mix_t, lsum,
    res, ffn, gates_t, share_ref, dx, out_hbm, dw_own,
    dgu_all, dd_all, output, in_grad, gq, go, gs,
    wq_all, wo_all, kv_all, raw_t, turn, bias, gres, branch, gm_t, dq_t, own_kv, gp, normed_t, gn,
    part_kv, part_w, part_s, q_sum, k_sum, ra, rb, rc, sa, sb, sc, plane_buf, plane_all, p1, p2, p3, p4, ta, tb, tc,
    logits, routers, router_sum, out_part, r1, r2, r3, r4, parcels, got_parcels, small_own, kv_total,
    column_sems, plane_sems, far_send, far_recv, all_send, all_recv, free, local, gain_sums,
):
    plane, column = Plane(), Column()
    y, c = column.y, column.c
    copies = [
        pltpu.make_async_copy(wo_hbm, wo_all, local.at[0]),
        pltpu.make_async_copy(kv_hbm, kv_all, local.at[1]),
        pltpu.make_async_copy(raw_hbm, raw_t, local.at[2]),
        pltpu.make_async_copy(wq_hbm, wq_all, local.at[3]),
        pltpu.make_async_copy(turn_hbm.at[column.me], turn, local.at[4]),
    ]
    parts = [pltpu.make_async_copy(out_hbm.at[mb], out_part, local.at[5 + mb]) for mb in range(2)]
    dw_refs = [dgu_all.at[0], dgu_all.at[1], dd_all]
    owns = [pltpu.make_async_copy(dw_own.at[n], dw_refs[n].at[y, c], local.at[7 + n]) for n in range(3)]
    for copy in parts[:1] + owns + copies:
        copy.start()
    greet(plane.others() + column.neighbours())
    dall = [ColumnGather(column, dw_refs[n], column_sems.at[8 + n], 128, dw_own.at[n]) for n in range(3)]

    def add_residual(mb):
        def store(place, rows, total):
            output[mb, rows] = (res[mb, rows] + total).astype(BF)

        return store

    sout = [
        Scatter(plane, out_part, (r1, r2, r3, r4), plane_sems.at[mb], add_residual(mb), free)
        for mb in range(2)
    ]
    part_s[...] = jnp.zeros_like(part_s)
    q_sum[...] = jnp.zeros_like(q_sum)
    k_sum[...] = jnp.zeros_like(k_sum)
    for mb in range(2):
        document_bias(seg_ref, bias, mb, column.me)

    def place_w(which):
        def store(r, total):
            low = total.astype(BF)
            half = r.start // 64
            some = pl.ds(pl.multiple_of(r.start % 64, 16), 16)
            for k in range(8):
                n = half * 8 + k
                piece = low[:, 128 * k : 128 * (k + 1)]
                if which == 2:
                    parcels[n, some] = piece
                else:
                    plane_buf[n // 4, n % 4, some, 128 * which : 128 * (which + 1)] = piece

        return store

    def place_s(r, total):
        small_own[r] = total.astype(BF)

    def place_kv(mb, half):
        def store(r, total):
            own_kv[mb, pl.ds(r.start + 4 * half, 1)] = total

        return store

    w_sums = [
        ColumnScatter(
            column, part_w.at[n], (ra.at[n], rb.at[n], rc.at[n]), column_sems.at[n], 128, place_w(n)
        )
        for n in range(3)
    ]
    kv_sums = [
        [
            ColumnScatter(
                column, part_kv.at[mb, half],
                (sa.at[mb, half], sb.at[mb, half], sc.at[mb, half]),
                column_sems.at[4 + 2 * mb + half], 4, place_kv(mb, half), group=1,
            )
            for half in range(2)
        ]
        for mb in range(2)
    ]
    s_sum = ColumnScatter(column, part_s, (ta, tb, tc), column_sems.at[3], 64, place_s)

    def keep(place, rows, total):
        plane_all[place] = total.astype(BF)

    over = Scatter(plane, plane_buf, (p1, p2, p3, p4), plane_sems.at[2], keep, height=64)
    spread = Gather(plane, plane_all, plane_sems.at[3], height=64)

    def tokens_of(mb):
        return pl.ds(128 * mb, 128)

    router = small_t[:32].astype(BF)
    ffn_gain, attn_gain = small_t[33:34], small_t[32:33]
    routers[0:32] = router
    routers[32:64] = router
    def router_and_norm():
        ffn_gain_grad = jnp.zeros((1, 1024), F32)
        for mb in range(2):
            share = jnp.concatenate([share_ref[k, 2 * mb : 2 * mb + 2] for k in range(16)], axis=0)
            logit = share - gates_t[mb] * jnp.sum(share, axis=0, keepdims=True)
            high = logit.astype(BF)
            logits[0:32, tokens_of(mb)] = high
            logits[32:64, tokens_of(mb)] = (logit - high.astype(F32)).astype(BF)

        @pl.loop(0, 4)
        def _(n):
            cols = pl.ds(pl.multiple_of(n * 256, 256), 256)
            gn[:, cols] = tn(logits[...], routers[:, cols])
            router_sum[:, cols] = nn(logits[...], ffn[:, :, cols].reshape(256, 256))

        for mb in range(2):
            into = dx[mb] + gn[tokens_of(mb)]
            v = res[mb]
            inv = inverse_rms(v, 1)
            grad, gain = norm_grad(into, v, inv, ffn_gain, 1)
            ffn_gain_grad += jnp.sum(gain, axis=0, keepdims=True)
            total = cot[mb].astype(F32) + grad
            gres[mb] = total
            branch[128 * mb : 128 * (mb + 1)] = total.astype(BF)
        gain_sums[1:2] = ffn_gain_grad

    def out_projection():
        copies[0].wait()

        @pl.loop(0, 4)
        def _(n):
            rows = pl.ds(pl.multiple_of(n * 256, 256), 256)
            got = nt(wo_all[n].reshape(256, 1024), branch[...])
            gm_t[0, rows] = got[:, :128].astype(BF)
            gm_t[1, rows] = got[:, 128:].astype(BF)
            mixed = jnp.concatenate([mix_t[0, rows], mix_t[1, rows]], axis=1)
            part_w[0, n] = nn(mixed, branch[...]).astype(BF).reshape(2, 128, 1024)

    def attend(mb, start, stop):
        @pl.loop(start, stop)
        def _(g):
            query = pair_columns(q_t, mb, g)
            grad = pair_columns(gm_t, mb, g)
            mixed = pair_columns(mix_t, mb, g)
            blank = jnp.zeros_like(query)
            inner = jnp.sum(grad.astype(F32) * mixed.astype(F32), axis=0, keepdims=True)
            query = jnp.concatenate([query, blank], axis=0)
            grad = jnp.concatenate([blank, grad], axis=0)
            both = jnp.concatenate([query, grad], axis=1)
            scale = 1.0 / lsum[mb, g]
            dq = jnp.zeros((128, 256), F32)
            for j in range(4):
                keys = kv_all[mb, j, :, g].reshape(256, 128)
                there = bias[mb, 256 * j : 256 * (j + 1)].astype(F32)
                got = nn(keys, both)
                p = jnp.exp(got[:, :256] + jnp.concatenate([there, there], axis=1)) * scale
                ds = (p * (got[:, 256:] - inner)).astype(BF)
                dq += tn(keys, ds)
                dkv = nt(jnp.concatenate([ds, p.astype(BF)], axis=1), both)
                part_kv[mb, g // 4, j, :, g % 4] = dkv.astype(BF).reshape(2, 128, 128)
            dq = dq[:64] * HD ** (-0.5)
            rows = pl.ds(pl.multiple_of(g * 128, 128), 128)
            dq_t[mb, rows] = jnp.concatenate([dq[:, :128], dq[:, 128:]], axis=0)

    copies[4].wait()
    cosine, sine = turn[:32], turn[32:]
    query_gain = head_gain(small_t[...], 34)
    key_gain = head_gain(small_t[...], 35)

    def head_back(grad, v, gain, total):
        inv = inverse_rms(v, 0)
        grad = turned(grad, cosine, -sine)
        grad_v, gain_part = norm_grad(grad, v, inv, gain, 0)
        total[...] += gain_part
        return grad_v

    def queries_back(mb):
        @pl.loop(0, 8)
        def _(g):
            pieces = []
            for r in range(2):
                rows = pl.ds(pl.multiple_of(g * 128 + r * 64, 64), 64)
                pieces.append(head_back(dq_t[mb, rows], raw_t[mb, rows], query_gain, q_sum))
            cols = pl.ds(pl.multiple_of(g * 128, 128), 128)
            gp[tokens_of(mb), cols] = jnp.concatenate(pieces, axis=0).T.astype(BF)

    def turn_normed():
        for mb in range(2):
            v = tok[mb].astype(F32)
            normed = (v * inverse_rms(v, 1) * attn_gain).astype(BF).astype(F32)
            for k in range(8):
                normed_t[128 * k : 128 * (k + 1), tokens_of(mb)] = (
                    normed[:, 128 * k : 128 * (k + 1)].T.astype(BF)
                )

    def weight_part(which):
        cols = pl.ds(1024 * (which - 1), 1024)

        @pl.loop(0, 4)
        def _(n):
            rows = pl.ds(pl.multiple_of(n * 256, 256), 256)
            part_w[which, n] = nn(normed_t[rows], gp[:, cols]).astype(BF).reshape(2, 128, 1024)

    def keys_back(mb):
        @pl.loop(0, 4)
        def _(k):
            keys, values = [], []
            for r in range(2):
                g = 2 * k + r
                grad = own_kv[mb, g].T
                rows = pl.ds(pl.multiple_of(1024 + g * 64, 64), 64)
                keys.append(head_back(grad[:64], raw_t[mb, rows], key_gain, k_sum))
                values.append(grad[64:])
            cols = pl.ds(pl.multiple_of(1024 + k * 128, 128), 128)
            gp[tokens_of(mb), cols] = jnp.concatenate(keys, axis=0).T.astype(BF)
            cols = pl.ds(pl.multiple_of(1536 + k * 128, 128), 128)
            gp[tokens_of(mb), cols] = jnp.concatenate(values, axis=0).T.astype(BF)

    def normed_grad(k):
        @pl.loop(0, 4)
        def _(n):
            cols = pl.ds(pl.multiple_of(n * 256, 256), 256)
            got = nt(gp[:, 1024 * k : 1024 * (k + 1)], wq_all[k, n].reshape(256, 1024))
            gn[:, cols] = got if k == 0 else gn[:, cols] + got

    def finish():
        attn_gain_grad = jnp.zeros((1, 1024), F32)
        for mb in range(2):
            v = tok[mb].astype(F32)
            grad, gain = norm_grad(gn[tokens_of(mb)], v, inverse_rms(v, 1), attn_gain, 1)
            attn_gain_grad += jnp.sum(gain, axis=0, keepdims=True)
            in_grad[mb] = (gres[mb] + grad).astype(BF)
        for b in range(8):
            cols = slice(128 * b, 128 * (b + 1))
            heads = slice(8 * b, 8 * (b + 1))
            part_s[b // 2, b % 2, 0:32] = router_sum[0:32, cols] + router_sum[32:64, cols]
            part_s[b // 2, b % 2, 32:33] = attn_gain_grad[:, cols]
            part_s[b // 2, b % 2, 33:34] = gain_sums[1:2, cols]
            part_s[b // 2, b % 2, 40:48] = jnp.broadcast_to(
                jnp.sum(q_sum[heads], axis=1, keepdims=True), (8, 128)
            )
            part_s[b // 2, b % 2, 48:56] = jnp.broadcast_to(
                jnp.sum(k_sum[heads], axis=1, keepdims=True), (8, 128)
            )

    me = plane.me

    def parcel(step):
        to = (me + step) % 16
        return send(
            parcels.at[to], got_parcels.at[me], far_send.at[step], far_recv.at[step], {"expert": to}
        )

    def total_message(step):
        to = (me + step) % 16
        return send(
            kv_total.at[me], kv_total.at[me], all_send.at[step], all_recv.at[step], {"expert": to}
        )

    def send_parcels():
        @pl.loop(0, 16)
        def _(n):
            parcels[n, 64:128] = small_own[...]

        for step in range(1, 16):
            parcel(step).start()
        got_parcels[me] = parcels[me]

    def add_parcels():
        for step in range(1, 16):
            parcel(step).wait_recv()
        total = got_parcels[0].astype(F32)
        for n in range(1, 16):
            total += got_parcels[n].astype(F32)
        kv_total[me] = total[:64].astype(BF)
        for step in range(1, 16):
            total_message(step).start()
        gs[...] = total[64:]

    def write_out(k):
        for n in range(16):
            rows = slice(64 * (n // 8), 64 * (n // 8) + 64)
            cols = slice(128 * (n % 8), 128 * (n % 8) + 128)
            (go, gq)[k][rows, cols] = plane_all[n // 4, n % 4, :, 128 * k : 128 * (k + 1)].astype(F32)

    def take_totals():
        for step in range(1, 16):
            total_message(step).wait_recv()
        for n in range(16):
            first = 1024 + 128 * (n % 8)
            gq[64 * (n // 8) : 64 * (n // 8) + 64, first : first + 128] = kv_total[n].astype(F32)

    dall[2].step(0)
    router_and_norm()
    parts[0].wait()
    sout[0].step(0)
    dall[0].step(0)
    out_projection()
    dall[1].step(0)
    copies[1].wait()
    attend(1, 0, 2)
    attend(1, 2, 4)
    attend(0, 0, 2)
    kv_sums[1][0].step(0)
    w_sums[0].step(0)
    sout[0].step(1)
    attend(1, 4, 6)
    attend(1, 6, 8)
    dall[0].step(1)
    kv_sums[1][0].step(1)
    kv_sums[1][1].step(0)
    attend(0, 2, 4)
    w_sums[0].step(1)
    attend(0, 4, 6)
    dall[2].step(1)
    kv_sums[1][1].step(1)
    sout[0].step(2)
    w_sums[0].step(2)
    attend(0, 6, 8)
    sout[0].step(3)
    kv_sums[0][1].step(0)
    kv_sums[0][0].step(0)
    kv_sums[1][1].step(2)
    turn_normed()
    copies[2].wait()
    queries_back(1)
    queries_back(0)
    kv_sums[1][0].step(2)
    kv_sums[0][1].step(1)
    weight_part(1)
    copies[3].wait()
    normed_grad(0)
    sout[0].step(4)
    parts[1].start()
    sout[0].give_credit()
    w_sums[1].step(0)
    kv_sums[0][0].step(1)
    kv_sums[0][1].step(2)
    parts[1].wait()
    sout[1].take_credit()
    sout[1].step(0)
    dall[0].step(2)
    w_sums[1].step(1)
    kv_sums[1][1].step(3)
    kv_sums[0][1].step(3)
    kv_sums[0][0].step(2)
    w_sums[1].step(2)
    sout[1].step(1)
    kv_sums[0][0].step(3)
    kv_sums[1][0].step(3)
    keys_back(0)
    dall[2].step(2)
    keys_back(1)
    dall[1].step(1)
    weight_part(2)
    w_sums[2].step(0)
    w_sums[0].step(3)
    normed_grad(1)
    w_sums[1].step(3)
    over.step(0)
    finish()
    dall[0].step(3)
    dall[1].step(2)
    s_sum.step(0)
    w_sums[2].step(1)
    over.step(1)
    dall[2].step(3)
    sout[1].step(2)
    s_sum.step(1)
    w_sums[2].step(2)
    over.step(2)
    over.step(3)
    s_sum.step(2)
    sout[1].step(3)
    dall[1].step(3)
    over.step(4)
    s_sum.step(3)
    spread.step(0)
    w_sums[2].step(3)
    send_parcels()
    spread.step(1)
    spread.step(2)
    sout[1].step(4)
    add_parcels()
    spread.step(3)
    spread.step(4)
    write_out(0)
    write_out(1)
    take_totals()
    for step in range(1, 16):
        parcel(step).wait_send()
        total_message(step).wait_send()
    for copy in owns:
        copy.wait()


def back(tok, cot, seg, turn, wq_all, wo_all, small_t, raw_t, q_t, kv_all, mix_t, lsum, res, ffn, gates_t, share, dx, out_part, dw_own):
    vmem = pl.BlockSpec(memory_space=pltpu.VMEM)
    anywhere = pl.BlockSpec(memory_space=pl.ANY)
    kv_slots = column_slots((4, 128, 128), lead=(2, 2))
    return pl.pallas_call(
        back_kernel,
        out_shape=(
            jax.ShapeDtypeStruct((2, 4, 2, 128, 1024), BF),
            jax.ShapeDtypeStruct((4, 2, 128, 1024), BF),
            jax.ShapeDtypeStruct((2, 128, 1024), BF),
            jax.ShapeDtypeStruct((2, 128, 1024), BF),
            jax.ShapeDtypeStruct((128, 2048), F32),
            jax.ShapeDtypeStruct((128, 1024), F32),
            jax.ShapeDtypeStruct((64, 128), F32),
        ),
        in_specs=[
            vmem, vmem, vmem, anywhere, anywhere, anywhere, vmem, anywhere, vmem, anywhere,
            vmem, vmem, vmem, vmem, vmem, vmem, vmem, anywhere, vmem,
        ],
        out_specs=(anywhere,) * 2 + (vmem,) * 5,
        scratch_shapes=[
            pltpu.VMEM((2, 4, 2, 128, 1024), BF),
            pltpu.VMEM((4, 2, 128, 1024), BF),
            pltpu.VMEM((2, 4, 2, 8, 128, 128), BF),
            pltpu.VMEM((2, 2048, 128), F32),
            pltpu.VMEM((64, 128), F32),
            pltpu.VMEM((2, 1024, 128), BF),
            pltpu.VMEM((2, 128, 1024), F32),
            pltpu.VMEM((256, 1024), BF),
            pltpu.VMEM((2, 1024, 128), BF),
            pltpu.VMEM((2, 1024, 128), F32),
            pltpu.VMEM((2, 8, 128, 128), F32),
            pltpu.VMEM((256, 2048), BF),
            pltpu.VMEM((1024, 256), BF),
            pltpu.VMEM((256, 1024), F32),
            pltpu.VMEM((2, 2, 4, 2, 4, 128, 128), BF),
            pltpu.VMEM((3, 4, 2, 128, 1024), BF),
            pltpu.VMEM((4, 2, 64, 128), F32),
            pltpu.VMEM((64, 128), F32),
            pltpu.VMEM((64, 128), F32),
            *column_slots((128, 1024), lead=(3,)),
            *kv_slots,
            pltpu.VMEM((4, 4, 64, 256), BF),
            pltpu.VMEM((4, 4, 64, 256), BF),
            *scatter_slots(64, 256),
            *column_slots((64, 128), F32),
            pltpu.VMEM((64, 256), BF),
            pltpu.VMEM((64, 1024), BF),
            pltpu.VMEM((64, 1024), F32),
            pltpu.VMEM((4, 4, 128, 1024), BF),
            *scatter_slots(128, 1024),
            pltpu.VMEM((16, 128, 128), BF),
            pltpu.VMEM((16, 128, 128), BF),
            pltpu.VMEM((64, 128), BF),
            pltpu.VMEM((16, 64, 128), BF),
            pltpu.SemaphoreType.DMA((11, 2, 8)),
            pltpu.SemaphoreType.DMA((4, 2, 2, 8)),
            pltpu.SemaphoreType.DMA((16,)),
            pltpu.SemaphoreType.DMA((16,)),
            pltpu.SemaphoreType.DMA((16,)),
            pltpu.SemaphoreType.DMA((16,)),
            pltpu.SemaphoreType.REGULAR,
            pltpu.SemaphoreType.DMA((10,)),
            pltpu.VMEM((8, 1024), F32),
        ],
        compiler_params=pltpu.CompilerParams(
            collective_id=2, has_side_effects=True, vmem_limit_bytes=63 * MIB
        ),
        cost_estimate=pl.CostEstimate(
            flops=12_000_000_000, bytes_accessed=30_000_000, transcendentals=5_000_000
        ),
    )(tok, cot, seg, turn, wq_all, wo_all, small_t, raw_t, q_t, kv_all, mix_t, lsum, res, ffn, gates_t, share, dx, out_part, dw_own)


def turn_table(length):
    frequency = np.power(np.float32(THETA), -2.0 * np.arange(HD // 2, dtype=np.float32) / HD)
    angle = np.arange(length, dtype=np.float32)[:, None] * frequency.astype(np.float32)[None, :]
    both = np.concatenate([np.cos(angle), np.sin(angle)], axis=1).astype(np.float32)
    return both.reshape(length // 128, 128, HD).transpose(0, 2, 1)


def body(
    tokens,
    cotangent,
    segments,
    routes,
    w_qkv,
    w_out,
    attn_norm,
    ffn_norm,
    q_gain,
    k_gain,
    router,
    w_gate_up,
    w_down,
):
    tok = tokens.reshape(2, 128, 1024)
    cot = cotangent.reshape(2, 128, 1024)
    seg = segments.reshape(2, 8, 1, 128)
    routes_t = routes.reshape(2, 128, 8).transpose(0, 2, 1)
    turn = jnp.asarray(turn_table(1024))
    gains = jnp.pad(jnp.stack([q_gain, k_gain]), ((0, 28), (0, 120)))
    small = jnp.concatenate([router.T, attn_norm[None], ffn_norm[None], gains])
    (
        dy_all, x0, wq_all, wo_all, kv_all, raw_t, small_t, q_t, mix_t, lsum, res, ffn, gates_t, sent
    ) = front(tok, cot, w_qkv, w_out, small, seg, routes_t, turn)
    out_part, moved_dx, share, dw_own = moe(ffn, x0, dy_all, sent, w_gate_up, w_down)
    dgu, dd, output, in_grad, gq, go, gs = back(
        tok, cot, seg, turn, wq_all, wo_all, small_t, raw_t, q_t, kv_all, mix_t, lsum, res, ffn,
        gates_t, share, moved_dx, out_part, dw_own,
    )
    return (
        output.reshape(tokens.shape),
        in_grad.reshape(tokens.shape),
        gq,
        go,
        gs[32],
        gs[33],
        gs[40:48, 0],
        gs[48:56, 0],
        gs[:32].T,
        dgu.astype(F32).reshape(2, 1024, 1024),
        dd.astype(F32).reshape(2, 512, 1024),
    )


def solution(mesh):
    return jax.shard_map(
        body,
        mesh=mesh,
        in_specs=(
            P(None, "expert", "dp", None),
            P(None, "expert", "dp", None),
            P(None, "expert", None),
            P(None, "expert", "dp", None),
            P("dp", None),
            P("dp", None),
            P("dp"),
            P("dp"),
            P("dp"),
            P("dp"),
            P("dp", None),
            P("expert", None, None),
            P("expert", None, None),
        ),
        out_specs=(
            P(None, "expert", "dp", None),
            P(None, "expert", "dp", None),
            P("dp", None),
            P("dp", None),
            P("dp"),
            P("dp"),
            P("dp"),
            P("dp"),
            P("dp", None),
            P("expert", None, None),
            P("expert", None, None),
        ),
        check_vma=False,
    )
```

```python
import jax
import jax.numpy as jnp
import numpy as np
from jax import lax
from jax.experimental import pallas as pl
from jax.experimental.pallas import tpu as pltpu
from jax.sharding import PartitionSpec as P

HD = 64
EPSILON = 1e-06
THETA = 10000.0
MASKED = -1e30

BF = jnp.bfloat16
F32 = jnp.float32
SLOTS = 48
CHUNK = 384
MIB = 1024 * 1024


def nn(a, b):
    return lax.dot_general(a, b, (((1,), (0,)), ((), ())), preferred_element_type=F32)


def nt(a, b):
    return lax.dot_general(a, b, (((1,), (1,)), ((), ())), preferred_element_type=F32)


def tn(a, b):
    return lax.dot_general(a, b, (((0,), (0,)), ((), ())), preferred_element_type=F32)


def send(src, dst, send_sem, recv_sem, device):
    return pltpu.make_async_remote_copy(
        src_ref=src, dst_ref=dst, send_sem=send_sem, recv_sem=recv_sem, device_id=device
    )


def next_to(p):
    return (p + 1) % 4, (p + 3) % 4, (p + 2) % 4


def greet(devices):
    sem = pltpu.get_barrier_semaphore()
    for device in devices:
        pl.semaphore_signal(sem, inc=1, device_id=device)
    pl.semaphore_wait(sem, len(devices))


class Plane:
    def __init__(self):
        self.me = lax.axis_index("expert")
        self.z = self.me // 4
        self.x = self.me % 4

    def own(self, half):
        return (self.x, self.z) if half == 0 else (self.z, self.x)

    def device(self, half, p, q):
        return {"expert": q * 4 + p if half == 0 else p * 4 + q}

    def others(self):
        return [{"expert": (self.me + step) % 16} for step in range(1, 16)]

    def neighbours(self):
        zn, zp, _ = next_to(self.z)
        xn, xp, _ = next_to(self.x)
        return [{"expert": k} for k in (zn * 4 + self.x, zp * 4 + self.x, self.z * 4 + xn, self.z * 4 + xp)]


class Column:
    def __init__(self):
        self.me = lax.axis_index("dp")
        self.y = self.me // 2
        self.c = self.me % 2

    def neighbours(self):
        yn, yp, _ = next_to(self.y)
        return [self.to(yn), self.to(yp), self.other()]

    def to(self, y):
        return {"dp": y * 2 + self.c}

    def other(self):
        return {"dp": self.y * 2 + 1 - self.c}


class PlaneStep:
    def at(self, half, p, q, rows):
        return self.ref.at[q, p, rows] if half == 0 else self.ref.at[p, q, rows]

    def line(self, half, q, rows):
        return self.ref.at[q, :, rows] if half == 0 else self.ref.at[:, q, rows]

    def rows(self, half):
        quarter = self.height // 4
        base = 2 * quarter * half
        return pl.ds(base, 2 * quarter), pl.ds(base, quarter), pl.ds(base + quarter, quarter)


class Gather(PlaneStep):
    def __init__(self, plane, ref, sems, height=128):
        self.plane, self.ref, self.sems, self.height = plane, ref, sems, height

    def message(self, half, i):
        p, q = self.plane.own(half)
        pn, pp, _ = next_to(p)
        qn, qp, _ = next_to(q)
        full, first, second = self.rows(half)
        view, to = [
            lambda: (self.at(half, p, q, full), (pn, q)),
            lambda: (self.at(half, p, q, full), (pp, q)),
            lambda: (self.at(half, pp, q, first), (pn, q)),
            lambda: (self.at(half, pn, q, second), (pp, q)),
            lambda: (self.line(half, q, full), (p, qn)),
            lambda: (self.line(half, q, full), (p, qp)),
            lambda: (self.line(half, qp, first), (p, qn)),
            lambda: (self.line(half, qn, second), (p, qp)),
        ][i]()
        sems = self.sems
        return send(view, view, sems.at[0, half, i], sems.at[1, half, i], self.plane.device(half, *to))

    def step(self, n):
        waits, starts = [
            ((), (0, 1)),
            ((0, 1), (2, 3)),
            ((2, 3), (4, 5)),
            ((4, 5), (6, 7)),
            ((6, 7), ()),
        ][n]
        for half in range(2):
            for i in waits:
                self.message(half, i).wait_recv()
            for i in starts:
                self.message(half, i).start()
        if n == 4:
            for half in range(2):
                for i in range(8):
                    self.message(half, i).wait_send()


class Scatter(PlaneStep):
    def __init__(self, plane, ref, slots, sems, store, free=None, height=128):
        self.plane, self.ref, self.slots, self.sems = plane, ref, slots, sems
        self.store, self.free, self.height = store, free, height

    def message(self, half, i):
        p, q = self.plane.own(half)
        pn, pp, po = next_to(p)
        qn, qp, qo = next_to(q)
        full, first, second = self.rows(half)
        r1, r2, r3, r4 = self.slots
        view, slot, to = [
            lambda: (self.line(half, qo, first), r1.at[half, 0], (p, qn)),
            lambda: (self.line(half, qo, second), r1.at[half, 1], (p, qp)),
            lambda: (self.line(half, qn, full), r2.at[half, 0], (p, qn)),
            lambda: (self.line(half, qp, full), r2.at[half, 1], (p, qp)),
            lambda: (self.at(half, po, q, first), r3.at[half, 0], (pn, q)),
            lambda: (self.at(half, po, q, second), r3.at[half, 1], (pp, q)),
            lambda: (self.at(half, pn, q, full), r4.at[half, 0], (pn, q)),
            lambda: (self.at(half, pp, q, full), r4.at[half, 1], (pp, q)),
        ][i]()
        sems = self.sems
        return send(view, slot, sems.at[0, half, i], sems.at[1, half, i], self.plane.device(half, *to))

    def add_line(self, half, q, part, parts, slots):
        quarter = self.height // 4
        offset = quarter * (2 * half + part)
        groups = quarter * parts // 16

        @pl.loop(0, 4 * groups)
        def _(n):
            j, k = n // groups, n % groups
            rows = pl.ds(pl.multiple_of(offset + k * 16, 16), 16)
            some = pl.ds(pl.multiple_of(k * 16, 16), 16)
            place = (q, j, rows) if half == 0 else (j, q, rows)
            total = self.ref[place].astype(F32)
            for ref, side in slots:
                total += ref[half, side, j, some].astype(F32)
            self.ref[place] = total.astype(BF)

    def add_at(self, half, p, q, part, slot):
        quarter = self.height // 4
        ref, side = slot

        @pl.loop(0, quarter // 16)
        def _(k):
            rows = pl.ds(pl.multiple_of(quarter * (2 * half + part) + k * 16, 16), 16)
            place = (q, p, rows) if half == 0 else (p, q, rows)
            got = ref[half, side, pl.ds(pl.multiple_of(k * 16, 16), 16)].astype(F32)
            self.ref[place] = (self.ref[place].astype(F32) + got).astype(BF)

    def step(self, n):
        r1, r2, r3, r4 = self.slots
        for half in range(2):
            p, q = self.plane.own(half)
            pn, pp, po = next_to(p)
            qn, qp, qo = next_to(q)
            if n == 0:
                self.message(half, 0).start()
                self.message(half, 1).start()
            elif n == 1:
                self.message(half, 0).wait_recv()
                self.add_line(half, qn, 0, 1, [(r1, 0)])
                self.message(half, 2).start()
                self.message(half, 1).wait_recv()
                self.add_line(half, qp, 1, 1, [(r1, 1)])
                self.message(half, 3).start()
            elif n == 2:
                self.message(half, 2).wait_recv()
                self.message(half, 3).wait_recv()
                self.add_line(half, q, 0, 2, [(r2, 0), (r2, 1)])
                self.message(half, 4).start()
                self.message(half, 5).start()
            elif n == 3:
                self.message(half, 4).wait_recv()
                self.add_at(half, pn, q, 0, (r3, 0))
                self.message(half, 6).start()
                self.message(half, 5).wait_recv()
                self.add_at(half, pp, q, 1, (r3, 1))
                self.message(half, 7).start()
            elif n == 4:
                self.message(half, 6).wait_recv()
                self.message(half, 7).wait_recv()

                @pl.loop(0, self.height // 32)
                def _(k):
                    rows = pl.ds(pl.multiple_of(self.height // 2 * half + k * 16, 16), 16)
                    place = (q, p, rows) if half == 0 else (p, q, rows)
                    some = pl.ds(pl.multiple_of(k * 16, 16), 16)
                    total = self.ref[place].astype(F32)
                    total += r4[half, 0, some].astype(F32)
                    total += r4[half, 1, some].astype(F32)
                    self.store(place, rows, total)
        if n == 4:
            for half in range(2):
                for i in range(8):
                    self.message(half, i).wait_send()

    def give_credit(self):
        for device in self.plane.neighbours():
            pl.semaphore_signal(self.free, inc=1, device_id=device)

    def take_credit(self):
        pl.semaphore_wait(self.free, 4)


def scatter_slots(height, width, lead=()):
    quarter = height // 4
    return [
        pltpu.VMEM((*lead, 2, 2, 4, quarter, width), BF),
        pltpu.VMEM((*lead, 2, 2, 4, 2 * quarter, width), BF),
        pltpu.VMEM((*lead, 2, 2, quarter, width), BF),
        pltpu.VMEM((*lead, 2, 2, 2 * quarter, width), BF),
    ]


class ColumnGather:
    def __init__(self, column, ref, sems, count, own=None):
        self.column, self.ref, self.sems, self.count = column, ref, sems, count
        self.own = own

    def message(self, i):
        y, c = self.column.y, self.column.c
        yn, yp, yo = next_to(y)
        half = self.count // 2
        ref, column = self.ref, self.column
        view, device = [
            lambda: (ref.at[y, c], column.to(yn)),
            lambda: (ref.at[y, c], column.to(yp)),
            lambda: (ref.at[y, c], column.other()),
            lambda: (ref.at[yp, c, pl.ds(0, half)], column.to(yn)),
            lambda: (ref.at[yn, c, pl.ds(half, half)], column.to(yp)),
            lambda: (ref.at[yp, c], column.other()),
            lambda: (ref.at[yn, c], column.other()),
            lambda: (ref.at[yo, c], column.other()),
        ][i]()
        source = self.own if i < 3 and self.own is not None else view
        return send(source, view, self.sems.at[0, i], self.sems.at[1, i], device)

    def step(self, n):
        order = [
            [("s", 0), ("s", 1), ("s", 2)],
            [("w", 0), ("s", 3), ("s", 5), ("w", 1), ("s", 4), ("s", 6)],
            [("w", 3), ("w", 4), ("s", 7)],
            [("w", 2), ("w", 5), ("w", 6), ("w", 7)],
        ][n]
        for what, i in order:
            if what == "s":
                self.message(i).start()
            else:
                self.message(i).wait_recv()
        if n == 3:
            for i in range(8):
                self.message(i).wait_send()


class ColumnScatter:
    def __init__(self, column, ref, slots, sems, count, store, group=16):
        self.column, self.ref, self.slots, self.sems = column, ref, slots, sems
        self.count, self.store, self.group = count, store, group

    def message(self, i):
        y, c = self.column.y, self.column.c
        yn, yp, yo = next_to(y)
        half = self.count // 2
        ref, column = self.ref, self.column
        ra, rb, rc = self.slots
        view, slot, device = [
            lambda: (ref.at[:, 1 - c], ra, column.other()),
            lambda: (ref.at[yo, c, pl.ds(0, half)], rb.at[0], column.to(yn)),
            lambda: (ref.at[yo, c, pl.ds(half, half)], rb.at[1], column.to(yp)),
            lambda: (ref.at[yn, c], rc.at[0], column.to(yn)),
            lambda: (ref.at[yp, c], rc.at[1], column.to(yp)),
        ][i]()
        return send(view, slot, self.sems.at[0, i], self.sems.at[1, i], device)

    def some(self, k, base=0):
        return pl.ds(pl.multiple_of(base + k * self.group, self.group), self.group)

    def step(self, n):
        y, c = self.column.y, self.column.c
        yn, yp, yo = next_to(y)
        ref, (ra, rb, rc) = self.ref, self.slots
        low = ref.dtype
        half = self.count // 2
        groups = self.count // self.group
        if n == 0:
            self.message(0).start()
        elif n == 1:
            self.message(0).wait_recv()

            @pl.loop(0, 4 * groups)
            def _(k):
                j, r = k // groups, self.some(k % groups)
                ref[j, c, r] = (ref[j, c, r].astype(F32) + ra[j, r].astype(F32)).astype(low)

            self.message(1).start()
            self.message(2).start()
        elif n == 2:
            for side, to in ((0, yn), (1, yp)):
                self.message(1 + side).wait_recv()

                @pl.loop(0, groups // 2)
                def _(k):
                    r = self.some(k, side * half)
                    got = rb[side, self.some(k)].astype(F32)
                    ref[to, c, r] = (ref[to, c, r].astype(F32) + got).astype(low)

                self.message(3 + side).start()
        else:
            self.message(3).wait_recv()
            self.message(4).wait_recv()

            @pl.loop(0, groups)
            def _(k):
                r = self.some(k)
                total = ref[y, c, r].astype(F32) + rc[0, r].astype(F32) + rc[1, r].astype(F32)
                self.store(r, total)

            for i in range(5):
                self.message(i).wait_send()


def column_slots(shape, dtype=BF, lead=()):
    count, rest = shape[0], shape[1:]
    return [
        pltpu.VMEM((*lead, 4, count, *rest), dtype),
        pltpu.VMEM((*lead, 2, count // 2, *rest), dtype),
        pltpu.VMEM((*lead, 2, count, *rest), dtype),
    ]


def turned(v, cosine, sine):
    a, b = v[:32], v[32:]
    return jnp.concatenate([a * cosine - b * sine, b * cosine + a * sine], axis=0)


def inverse_rms(v, axis):
    return lax.rsqrt(jnp.mean(v * v, axis=axis, keepdims=True) + EPSILON)


def head_gain(small_t, row):
    pieces = [small_t[:, 128 * b : 128 * (b + 1)] for b in range(8)]
    tall = jnp.concatenate([piece.T[:8] for piece in pieces], axis=0)
    return jnp.broadcast_to(tall[:, row : row + 1], (64, 128))


def document_bias(seg_ref, bias, mb, mine):
    own = seg_ref[mb, mine].astype(F32)
    for b in range(8):
        keys = jnp.broadcast_to(seg_ref[mb, b].astype(F32), (128, 128)).T
        bias[mb, 128 * b : 128 * (b + 1)] = jnp.where(keys == own, 0.0, MASKED).astype(bias.dtype)


def pair_columns(ref, mb, g):
    both = ref[mb, pl.ds(pl.multiple_of(g * 128, 128), 128)]
    return jnp.concatenate([both[:64], both[64:]], axis=1)


def front_kernel(
    tok, cot, wq, wo, small, seg_ref, routes_ref, turn_hbm,
    dy_out, x0_out, wq_out, wo_out, kv_out, raw_out,
    small_t, q_t, mix_t, lsum, res, ffn, gates_t, g_all,
    dy_all, x0_all, wq_all, wo_all, kv_all, raw_t, small_all, normed, bias, turn, plane_sems, column_sems,
    sent, gsend, grecv, local,
):
    plane, column = Plane(), Column()
    y, c = column.y, column.c
    copies = [
        pltpu.make_async_copy(small, small_all.at[y, c], local.at[0]),
        pltpu.make_async_copy(wq.at[:, 1024:2048], wq_all.at[1, y, c], local.at[1]),
        pltpu.make_async_copy(wq.at[:, 0:1024], wq_all.at[0, y, c], local.at[3]),
        pltpu.make_async_copy(wo, wo_all.at[y, c], local.at[5]),
        pltpu.make_async_copy(turn_hbm.at[column.me], turn, local.at[6]),
    ]
    for copy in copies:
        copy.start()
    outs = [
        pltpu.make_async_copy(wq_all, wq_out, local.at[7]),
        pltpu.make_async_copy(wo_all, wo_out, local.at[8]),
        pltpu.make_async_copy(kv_all, kv_out, local.at[9]),
        pltpu.make_async_copy(raw_t, raw_out, local.at[10]),
        pltpu.make_async_copy(dy_all.at[0], dy_out.at[0], local.at[11]),
        pltpu.make_async_copy(dy_all.at[1], dy_out.at[1], local.at[2]),
        pltpu.make_async_copy(x0_all, x0_out, local.at[4]),
    ]
    for mb in range(2):
        dy_all[mb, plane.z, plane.x] = cot[mb]
    greet(plane.others() + column.neighbours())
    gdy = [Gather(plane, dy_all.at[mb], plane_sems.at[mb]) for mb in range(2)]
    gx = Gather(plane, x0_all, plane_sems.at[2])
    w_small = ColumnGather(column, small_all, column_sems.at[0], 64)
    w_q = ColumnGather(column, wq_all.at[0], column_sems.at[1], 128)
    w_kv = ColumnGather(column, wq_all.at[1], column_sems.at[2], 128)
    w_o = ColumnGather(column, wo_all, column_sems.at[3], 128)
    kv = [ColumnGather(column, kv_all.at[mb], column_sems.at[4 + mb], 8) for mb in range(2)]
    def both_biases():
        for mb in range(2):
            document_bias(seg_ref, bias, mb, column.me)

    def norm_tokens():
        for b in range(8):
            small_t[:, 128 * b : 128 * (b + 1)] = small_all[b // 2, b % 2].astype(F32)
        attn_gain = small_t[32:33]
        for mb in range(2):
            v = tok[mb].astype(F32)
            normed[128 * mb : 128 * (mb + 1)] = (v * inverse_rms(v, 1) * attn_gain).astype(BF)

    def project(k):
        @pl.loop(0, 2)
        def _(n):
            cols = pl.ds(pl.multiple_of(n * 512, 512), 512)
            rows = pl.ds(pl.multiple_of(1024 * k + n * 512, 512), 512)
            got = nn(normed[...], wq_all[k, :, :, :, cols].reshape(1024, 512))
            for mb in range(2):
                raw_t[mb, rows] = got[128 * mb : 128 * (mb + 1)].T

    def key_heads(mb):
        @pl.loop(0, 8)
        def _(g):
            v = raw_t[mb, pl.ds(pl.multiple_of(1024 + g * 64, 64), 64)]
            key = turned(v * inverse_rms(v, 0) * key_gain, cosine, sine)
            value = raw_t[mb, pl.ds(pl.multiple_of(1536 + g * 64, 64), 64)]
            kv_all[mb, y, c, g] = jnp.concatenate([key, value], axis=0).T.astype(BF)

    def query_heads(mb):
        @pl.loop(0, 16)
        def _(h):
            rows = pl.ds(pl.multiple_of(h * 64, 64), 64)
            v = raw_t[mb, rows]
            query = turned(v * inverse_rms(v, 0) * query_gain, cosine, sine)
            q_t[mb, rows] = (query.astype(BF).astype(F32) * HD ** (-0.5)).astype(BF)

    def attend(mb, start, stop):
        @pl.loop(start, stop)
        def _(g):
            query = pair_columns(q_t, mb, g)
            query = jnp.concatenate([query, jnp.zeros_like(query)], axis=0)
            total = jnp.zeros((1, 256), F32)
            mixed = jnp.zeros((128, 256), F32)
            for j in range(4):
                keys = kv_all[mb, j, :, g].reshape(256, 128)
                there = bias[mb, 256 * j : 256 * (j + 1)].astype(F32)
                p = jnp.exp(nn(keys, query) + jnp.concatenate([there, there], axis=1))
                total += jnp.sum(p, axis=0, keepdims=True)
                mixed += tn(keys, p.astype(BF))
            lsum[mb, g] = total
            mixed = (mixed[64:] / total).astype(BF)
            both = jnp.concatenate([mixed[:, :128], mixed[:, 128:]], axis=0)
            mix_t[mb, pl.ds(pl.multiple_of(g * 128, 128), 128)] = both

    def finish(mb):
        @pl.loop(0, 2)
        def _(n):
            cols = pl.ds(pl.multiple_of(n * 512, 512), 512)
            got = tn(mix_t[mb], wo_all[:, :, :, cols].reshape(1024, 512))
            res[mb, :, cols] = tok[mb, :, cols].astype(F32) + got

        v = res[mb]
        low = (v * inverse_rms(v, 1) * small_t[33:34]).astype(BF)
        ffn[mb] = low
        logits = nt(small_t[:32].astype(BF), low)
        ids = lax.broadcasted_iota(jnp.int32, (32, 128), 0)
        routed = ids == routes_ref[mb, 0:1]
        for k in range(1, 8):
            routed = routed | (ids == routes_ref[mb, k : k + 1])
        top = jnp.max(jnp.where(routed, logits, MASKED), axis=0, keepdims=True)
        weight = jnp.where(routed, jnp.exp(logits - top), 0.0)
        gates = weight / jnp.sum(weight, axis=0, keepdims=True)
        gates_t[mb] = gates
        for k in range(16):
            sent[k, 2 * mb : 2 * mb + 2] = gates[2 * k : 2 * k + 2]

    def gate_message(step):
        to = (plane.me + step) % 16
        return send(
            sent.at[to], g_all.at[plane.me], gsend.at[step], grecv.at[step], {"expert": to}
        )

    def send_gates():
        for step in range(1, 16):
            gate_message(step).start()
        g_all[plane.me] = sent[plane.me]

    def take_gates():
        for step in range(1, 16):
            gate_message(step).wait_recv()
        for step in range(1, 16):
            gate_message(step).wait_send()

    sent[...] = jnp.zeros_like(sent)
    copies[0].wait()
    w_small.step(0)
    gdy[0].step(0)
    copies[1].wait()
    w_kv.step(0)
    w_small.step(1)
    gdy[1].step(0)
    copies[2].wait()
    w_q.step(0)
    gdy[0].step(1)
    gdy[0].step(2)
    w_small.step(2)
    w_kv.step(1)
    gdy[1].step(1)
    w_q.step(1)
    copies[3].wait()
    w_o.step(0)
    w_small.step(3)
    norm_tokens()
    w_kv.step(2)
    w_kv.step(3)
    project(1)
    gdy[1].step(2)
    query_gain = head_gain(small_t[...], 34)
    key_gain = head_gain(small_t[...], 35)
    copies[4].wait()
    cosine, sine = turn[:32], turn[32:]
    key_heads(0)
    kv[0].step(0)
    kv[0].step(1)
    both_biases()
    key_heads(1)
    w_q.step(2)
    gdy[0].step(3)
    w_o.step(1)
    kv[0].step(2)
    w_q.step(3)
    outs[0].start()
    project(0)
    outs[3].start()
    kv[1].step(0)
    w_o.step(2)
    gdy[1].step(3)
    query_heads(0)
    kv[0].step(3)
    attend(0, 0, 4)
    attend(0, 4, 8)
    w_o.step(3)
    outs[1].start()
    finish(0)
    x0_all[plane.z, plane.x] = ffn[0]
    gx.step(0)
    query_heads(1)
    kv[1].step(1)
    gx.step(1)
    kv[1].step(2)
    gdy[1].step(4)
    outs[5].start()
    gx.step(2)
    kv[1].step(3)
    outs[2].start()
    attend(1, 0, 4)
    gx.step(3)
    attend(1, 4, 8)
    finish(1)
    send_gates()
    gdy[0].step(4)
    outs[4].start()
    take_gates()
    gx.step(4)
    outs[6].start()
    for copy in outs:
        copy.wait()


def front(tok, cot, wq, wo, small, seg, routes_t, turn):
    vmem = pl.BlockSpec(memory_space=pltpu.VMEM)
    anywhere = pl.BlockSpec(memory_space=pl.ANY)
    return pl.pallas_call(
        front_kernel,
        out_shape=(
            jax.ShapeDtypeStruct((2, 4, 4, 128, 1024), BF),
            jax.ShapeDtypeStruct((4, 4, 128, 1024), BF),
            jax.ShapeDtypeStruct((2, 4, 2, 128, 1024), BF),
            jax.ShapeDtypeStruct((4, 2, 128, 1024), BF),
            jax.ShapeDtypeStruct((2, 4, 2, 8, 128, 128), BF),
            jax.ShapeDtypeStruct((2, 2048, 128), F32),
            jax.ShapeDtypeStruct((64, 1024), F32),
            jax.ShapeDtypeStruct((2, 1024, 128), BF),
            jax.ShapeDtypeStruct((2, 1024, 128), BF),
            jax.ShapeDtypeStruct((2, 8, 1, 256), F32),
            jax.ShapeDtypeStruct((2, 128, 1024), F32),
            jax.ShapeDtypeStruct((2, 128, 1024), BF),
            jax.ShapeDtypeStruct((2, 32, 128), F32),
            jax.ShapeDtypeStruct((16, 8, 128), F32),
        ),
        in_specs=[vmem, vmem, anywhere, anywhere, anywhere, vmem, vmem, anywhere],
        out_specs=(anywhere,) * 6 + (vmem,) * 8,
        scratch_shapes=[
            pltpu.VMEM((2, 4, 4, 128, 1024), BF),
            pltpu.VMEM((4, 4, 128, 1024), BF),
            pltpu.VMEM((2, 4, 2, 128, 1024), BF),
            pltpu.VMEM((4, 2, 128, 1024), BF),
            pltpu.VMEM((2, 4, 2, 8, 128, 128), BF),
            pltpu.VMEM((2, 2048, 128), F32),
            pltpu.VMEM((4, 2, 64, 128), BF),
            pltpu.VMEM((256, 1024), BF),
            pltpu.VMEM((2, 1024, 128), F32),
            pltpu.VMEM((64, 128), F32),
            pltpu.SemaphoreType.DMA((3, 2, 2, 8)),
            pltpu.SemaphoreType.DMA((6, 2, 8)),
            pltpu.VMEM((16, 8, 128), F32),
            pltpu.SemaphoreType.DMA((16,)),
            pltpu.SemaphoreType.DMA((16,)),
            pltpu.SemaphoreType.DMA((12,)),
        ],
        compiler_params=pltpu.CompilerParams(
            collective_id=0, has_side_effects=True, vmem_limit_bytes=56 * MIB
        ),
        cost_estimate=pl.CostEstimate(
            flops=5_000_000_000, bytes_accessed=30_000_000, transcendentals=5_000_000
        ),
    )(tok, cot, wq, wo, small, seg, routes_t, turn)


def moe_kernel(
    ffn_ref, x0_hbm, dy_hbm, g_all, wgu_hbm, wd_hbm,
    out_hbm, dx_ref, h_ref, dw_own,
    dw, x_all, dy_all, r1, r2, r3, r4, xs, ds, os, gc, act, a1, a2, ggu, ranks, hcol, hs,
    wgu, wd, ra, rb, rc, sems, column_sems, hsend, hrecv, free, local,
):
    plane, column = Plane(), Column()
    me, z, x = plane.me, plane.z, plane.x
    own = [
        pltpu.make_async_copy(ffn_ref.at[1], x_all.at[1, z, x], local.at[0]),
        pltpu.make_async_copy(x0_hbm, x_all.at[0], local.at[2]),
        pltpu.make_async_copy(dy_hbm.at[0], dy_all.at[0], local.at[3]),
        pltpu.make_async_copy(wgu_hbm, wgu, local.at[4]),
        pltpu.make_async_copy(wd_hbm, wd, local.at[5]),
        pltpu.make_async_copy(dy_hbm.at[1], dy_all.at[1], local.at[1]),
    ]
    outs = [pltpu.make_async_copy(x_all.at[mb], out_hbm.at[mb], local.at[6 + mb]) for mb in range(2)]
    for copy in own:
        copy.start()
    greet(plane.others() + column.neighbours())
    own[0].wait()

    def h_message(step):
        to = (me + step) % 16
        return pltpu.make_async_remote_copy(
            src_ref=hs.at[to], dst_ref=h_ref.at[me],
            send_sem=hsend.at[step], recv_sem=hrecv.at[step], device_id={"expert": to},
        )

    gx = Gather(plane, x_all.at[1], sems.at[0])

    def into(mb):
        def store(place, rows, total):
            dx_ref[mb, rows] = total

        return store

    sdx = [
        Scatter(plane, dy_all.at[mb], (r1, r2, r3, r4), sems.at[1 + mb], into(mb), free)
        for mb in range(2)
    ]

    def own_part(k):
        def store(r, total):
            dw_own[k, r] = total.astype(BF)

        return store

    dsum = [
        ColumnScatter(
            column, dw.at[k], (ra.at[k], rb.at[k], rc.at[k]), column_sems.at[k], 128, own_part(k)
        )
        for k in range(3)
    ]
    earlier = (
        lax.broadcasted_iota(jnp.int32, (128, 128), 0)
        < lax.broadcasted_iota(jnp.int32, (128, 128), 1)
    ).astype(F32).astype(BF)

    @pl.loop(0, 16)
    def _(s):
        named = g_all[s] > 0.0
        before = nn(named.astype(F32).astype(BF), earlier)
        ranks[s] = jnp.where(named, before, -1.0)

    slot_ids = lax.broadcasted_iota(jnp.int32, (SLOTS, 128), 0).astype(F32)

    def places(p, mb):
        ranked = [ranks[2 * p + k] for k in range(2)]
        return [
            [(slot_ids == ranked[k][2 * mb + e : 2 * mb + e + 1]).astype(F32) for k in range(2)]
            for e in range(2)
        ]

    def gated(p, mb, hot):
        gates = [g_all[2 * p + k] for k in range(2)]
        return [
            [hot[e][k] * gates[k][2 * mb + e : 2 * mb + e + 1] for k in range(2)] for e in range(2)
        ]

    def spread(hot):
        blank = jnp.zeros((SLOTS, 128), F32)
        rows = []
        for e in range(2):
            rows.append(jnp.concatenate([hot[e][0], blank], axis=1))
            rows.append(jnp.concatenate([blank, hot[e][1]], axis=1))
        return jnp.concatenate(rows, axis=0).astype(BF)

    def span(p):
        return pl.ds(pl.multiple_of(p * 2 * SLOTS, 32), 2 * SLOTS)

    def pair(p):
        return p // 2, pl.ds(2 * (p % 2), 2)

    def select(mb):
        @pl.loop(0, 8)
        def _(p):
            hot = places(p, mb)
            line, two = pair(p)
            rows = nn(spread(hot), x_all[mb, line, two].reshape(256, 1024)).astype(BF)
            drows = nn(spread(gated(p, mb, hot)), dy_all[mb, line, two].reshape(256, 1024)).astype(BF)
            for e in range(2):
                xs[e, span(p)] = rows[2 * SLOTS * e : 2 * SLOTS * (e + 1)]
                ds[e, span(p)] = drows[2 * SLOTS * e : 2 * SLOTS * (e + 1)]

    chunks = 16 * SLOTS // CHUNK

    def forward(e):
        @pl.loop(0, chunks)
        def _(c):
            r = pl.ds(pl.multiple_of(c * CHUNK, CHUNK), CHUNK)
            gu = nn(xs[e, r], wgu[e])
            g, u = gu[:, :512], gu[:, 512:]
            sig = 1.0 / (1.0 + jnp.exp(-g))
            silu = g * sig
            active = (silu * u).astype(BF)
            act[e, r] = active
            a1[e, r] = (u * sig * (1.0 + g * (1.0 - sig))).astype(BF)
            a2[e, r] = silu.astype(BF)
            o = nn(active, wd[e]).astype(BF)
            os[e, r] = o
            hcol[e, r] = jnp.sum(o.astype(F32) * ds[e, r].astype(F32), axis=-1, keepdims=True)

    def combine_out(mb):
        @pl.loop(0, 8)
        def _(p):
            hot = places(p, mb)
            line, two = pair(p)
            both = jnp.concatenate([os[0, span(p)], os[1, span(p)]], axis=0)
            got = tn(spread(gated(p, mb, hot)), both).astype(BF)
            x_all[mb, line, two] = got.reshape(2, 128, 1024)
            for e in range(2):
                column_of = hcol[e, span(p)]
                for k in range(2):
                    row = 2 * mb + e
                    part = hot[e][k] * column_of[SLOTS * k : SLOTS * (k + 1)]
                    hs[2 * p + k, row : row + 1] = jnp.sum(part, axis=0, keepdims=True)

    def add_part(mb, k, n, fresh):
        fresh = fresh.reshape(2, 128, 1024)
        if mb == 1:
            fresh += dw[k, n].astype(F32)
        dw[k, n] = fresh.astype(BF)

    def backward(mb, e):
        @pl.loop(0, chunks)
        def _(c):
            r = pl.ds(pl.multiple_of(c * CHUNK, CHUNK), CHUNK)
            ga = nt(ds[e, r], wd[e])
            grad = jnp.concatenate(
                [ga * a1[e, r].astype(F32), ga * a2[e, r].astype(F32)], axis=1
            ).astype(BF)
            ggu[r] = grad
            gc[e, r] = nt(grad, wgu[e]).astype(BF)

        @pl.loop(0, 4)
        def _(m):
            cols = pl.ds(pl.multiple_of(m * 256, 256), 256)
            add_part(mb, e, m, tn(xs[e, :, cols], ggu[...]))

        @pl.loop(0, 2)
        def _(m):
            cols = pl.ds(pl.multiple_of(m * 256, 256), 256)
            add_part(mb, 2, 2 * e + m, tn(act[e, :, cols], ds[e]))

    def combine_dx(mb):
        @pl.loop(0, 8)
        def _(p):
            line, two = pair(p)
            both = jnp.concatenate([gc[0, span(p)], gc[1, span(p)]], axis=0)
            got = tn(spread(places(p, mb)), both).astype(BF)
            dy_all[mb, line, two] = got.reshape(2, 128, 1024)

    gx.step(0)
    own[1].wait()
    own[2].wait()
    select(0)
    gx.step(1)
    own[3].wait()
    own[4].wait()
    forward(0)
    gx.step(2)
    forward(1)
    combine_out(0)
    outs[0].start()
    backward(0, 0)
    gx.step(3)
    backward(0, 1)
    combine_dx(0)
    sdx[0].step(0)
    gx.step(4)
    own[5].wait()
    select(1)
    forward(1)
    sdx[0].step(1)
    forward(0)
    backward(1, 0)
    dsum[0].step(0)
    sdx[0].step(2)
    backward(1, 1)
    sdx[0].step(3)
    dsum[1].step(0)
    dsum[2].step(0)
    dsum[0].step(1)
    combine_dx(1)
    sdx[0].step(4)
    sdx[0].give_credit()
    sdx[1].take_credit()
    sdx[1].step(0)
    dsum[2].step(1)
    combine_out(1)
    outs[1].start()
    dsum[1].step(1)
    sdx[1].step(1)
    dsum[0].step(2)
    dsum[1].step(2)
    dsum[2].step(2)
    sdx[1].step(2)
    h_ref[me] = hs[me]
    for step in range(1, 16):
        h_message(step).start()
    sdx[1].step(3)
    dsum[0].step(3)
    dsum[2].step(3)
    dsum[1].step(3)
    sdx[1].step(4)
    for step in range(1, 16):
        h_message(step).wait_recv()
    for step in range(1, 16):
        h_message(step).wait_send()
    for copy in outs:
        copy.wait()


def moe(ffn, x0, dy, gates, w_gate_up, w_down):
    vmem = pl.BlockSpec(memory_space=pltpu.VMEM)
    anywhere = pl.BlockSpec(memory_space=pl.ANY)
    rows = 16 * SLOTS
    return pl.pallas_call(
        moe_kernel,
        out_shape=(
            jax.ShapeDtypeStruct((2, 4, 4, 128, 1024), BF),
            jax.ShapeDtypeStruct((2, 128, 1024), F32),
            jax.ShapeDtypeStruct((16, 8, 128), F32),
            jax.ShapeDtypeStruct((3, 128, 1024), BF),
        ),
        in_specs=[anywhere, anywhere, anywhere, vmem, anywhere, anywhere],
        out_specs=(anywhere,) + (vmem,) * 3,
        scratch_shapes=[
            pltpu.VMEM((3, 4, 2, 128, 1024), BF),
            pltpu.VMEM((2, 4, 4, 128, 1024), BF),
            pltpu.VMEM((2, 4, 4, 128, 1024), BF),
            *scatter_slots(128, 1024),
            pltpu.VMEM((2, rows, 1024), BF),
            pltpu.VMEM((2, rows, 1024), BF),
            pltpu.VMEM((2, rows, 1024), BF),
            pltpu.VMEM((2, rows, 1024), BF),
            pltpu.VMEM((2, rows, 512), BF),
            pltpu.VMEM((2, rows, 512), BF),
            pltpu.VMEM((2, rows, 512), BF),
            pltpu.VMEM((rows, 1024), BF),
            pltpu.VMEM((16, 8, 128), F32),
            pltpu.VMEM((2, rows, 1), F32),
            pltpu.VMEM((16, 8, 128), F32),
            pltpu.VMEM((2, 1024, 1024), BF),
            pltpu.VMEM((2, 512, 1024), BF),
            *column_slots((128, 1024), lead=(3,)),
            pltpu.SemaphoreType.DMA((3, 2, 2, 8)),
            pltpu.SemaphoreType.DMA((3, 2, 8)),
            pltpu.SemaphoreType.DMA((16,)),
            pltpu.SemaphoreType.DMA((16,)),
            pltpu.SemaphoreType.REGULAR,
            pltpu.SemaphoreType.DMA((8,)),
        ],
        compiler_params=pltpu.CompilerParams(
            collective_id=1, has_side_effects=True, vmem_limit_bytes=63 * MIB
        ),
        cost_estimate=pl.CostEstimate(
            flops=30_000_000_000, bytes_accessed=30_000_000, transcendentals=2_000_000
        ),
    )(ffn, x0, dy, gates, w_gate_up, w_down)


def norm_grad(grad, v, inverse, gain, axis):
    scaled = grad * gain
    moment = jnp.mean(scaled * v, axis=axis, keepdims=True)
    return inverse * (scaled - v * (inverse * inverse * moment)), grad * (v * inverse)


def back_kernel(
    tok, cot, seg_ref, turn_hbm, wq_hbm, wo_hbm, small_t, raw_hbm, q_t, kv_hbm, mix_t, lsum,
    res, ffn, gates_t, share_ref, dx, out_hbm, dw_own,
    dgu_all, dd_all, output, in_grad, gq, go, gs,
    wq_all, wo_all, kv_all, raw_t, turn, bias, gres, branch, gm_t, dq_t, own_kv, gp, normed_t, gn,
    part_kv, part_w, part_s, q_sum, k_sum, ra, rb, rc, sa, sb, sc, plane_buf, plane_all, p1, p2, p3, p4, ta, tb, tc,
    logits, routers, router_sum, out_part, r1, r2, r3, r4, parcels, got_parcels, small_own, kv_total,
    column_sems, plane_sems, far_send, far_recv, all_send, all_recv, free, local, gain_sums,
):
    plane, column = Plane(), Column()
    y, c = column.y, column.c
    copies = [
        pltpu.make_async_copy(wo_hbm, wo_all, local.at[0]),
        pltpu.make_async_copy(kv_hbm, kv_all, local.at[1]),
        pltpu.make_async_copy(raw_hbm, raw_t, local.at[2]),
        pltpu.make_async_copy(wq_hbm, wq_all, local.at[3]),
        pltpu.make_async_copy(turn_hbm.at[column.me], turn, local.at[4]),
    ]
    parts = [pltpu.make_async_copy(out_hbm.at[mb], out_part, local.at[5 + mb]) for mb in range(2)]
    dw_refs = [dgu_all.at[0], dgu_all.at[1], dd_all]
    owns = [pltpu.make_async_copy(dw_own.at[n], dw_refs[n].at[y, c], local.at[7 + n]) for n in range(3)]
    for copy in parts[:1] + owns + copies:
        copy.start()
    greet(plane.others() + column.neighbours())
    dall = [ColumnGather(column, dw_refs[n], column_sems.at[8 + n], 128, dw_own.at[n]) for n in range(3)]

    def add_residual(mb):
        def store(place, rows, total):
            output[mb, rows] = (res[mb, rows] + total).astype(BF)

        return store

    sout = [
        Scatter(plane, out_part, (r1, r2, r3, r4), plane_sems.at[mb], add_residual(mb), free)
        for mb in range(2)
    ]
    part_s[...] = jnp.zeros_like(part_s)
    q_sum[...] = jnp.zeros_like(q_sum)
    k_sum[...] = jnp.zeros_like(k_sum)
    for mb in range(2):
        document_bias(seg_ref, bias, mb, column.me)

    def place_w(which):
        def store(r, total):
            low = total.astype(BF)
            half = r.start // 64
            some = pl.ds(pl.multiple_of(r.start % 64, 16), 16)
            for k in range(8):
                n = half * 8 + k
                piece = low[:, 128 * k : 128 * (k + 1)]
                if which == 2:
                    parcels[n, some] = piece
                else:
                    plane_buf[n // 4, n % 4, some, 128 * which : 128 * (which + 1)] = piece

        return store

    def place_s(r, total):
        small_own[r] = total.astype(BF)

    def place_kv(mb, half):
        def store(r, total):
            own_kv[mb, pl.ds(r.start + 4 * half, 1)] = total

        return store

    w_sums = [
        ColumnScatter(
            column, part_w.at[n], (ra.at[n], rb.at[n], rc.at[n]), column_sems.at[n], 128, place_w(n)
        )
        for n in range(3)
    ]
    kv_sums = [
        [
            ColumnScatter(
                column, part_kv.at[mb, half],
                (sa.at[mb, half], sb.at[mb, half], sc.at[mb, half]),
                column_sems.at[4 + 2 * mb + half], 4, place_kv(mb, half), group=1,
            )
            for half in range(2)
        ]
        for mb in range(2)
    ]
    s_sum = ColumnScatter(column, part_s, (ta, tb, tc), column_sems.at[3], 64, place_s)

    def keep(place, rows, total):
        plane_all[place] = total.astype(BF)

    over = Scatter(plane, plane_buf, (p1, p2, p3, p4), plane_sems.at[2], keep, height=64)
    spread = Gather(plane, plane_all, plane_sems.at[3], height=64)

    def tokens_of(mb):
        return pl.ds(128 * mb, 128)

    router = small_t[:32].astype(BF)
    ffn_gain, attn_gain = small_t[33:34], small_t[32:33]
    routers[0:32] = router
    routers[32:64] = router
    def router_and_norm():
        ffn_gain_grad = jnp.zeros((1, 1024), F32)
        for mb in range(2):
            share = jnp.concatenate([share_ref[k, 2 * mb : 2 * mb + 2] for k in range(16)], axis=0)
            logit = share - gates_t[mb] * jnp.sum(share, axis=0, keepdims=True)
            high = logit.astype(BF)
            logits[0:32, tokens_of(mb)] = high
            logits[32:64, tokens_of(mb)] = (logit - high.astype(F32)).astype(BF)

        @pl.loop(0, 4)
        def _(n):
            cols = pl.ds(pl.multiple_of(n * 256, 256), 256)
            gn[:, cols] = tn(logits[...], routers[:, cols])
            router_sum[:, cols] = nn(logits[...], ffn[:, :, cols].reshape(256, 256))

        for mb in range(2):
            into = dx[mb] + gn[tokens_of(mb)]
            v = res[mb]
            inv = inverse_rms(v, 1)
            grad, gain = norm_grad(into, v, inv, ffn_gain, 1)
            ffn_gain_grad += jnp.sum(gain, axis=0, keepdims=True)
            total = cot[mb].astype(F32) + grad
            gres[mb] = total
            branch[128 * mb : 128 * (mb + 1)] = total.astype(BF)
        gain_sums[1:2] = ffn_gain_grad

    def out_projection():
        copies[0].wait()

        @pl.loop(0, 4)
        def _(n):
            rows = pl.ds(pl.multiple_of(n * 256, 256), 256)
            got = nt(wo_all[n].reshape(256, 1024), branch[...])
            gm_t[0, rows] = got[:, :128].astype(BF)
            gm_t[1, rows] = got[:, 128:].astype(BF)
            mixed = jnp.concatenate([mix_t[0, rows], mix_t[1, rows]], axis=1)
            part_w[0, n] = nn(mixed, branch[...]).astype(BF).reshape(2, 128, 1024)

    def attend(mb, start, stop):
        @pl.loop(start, stop)
        def _(g):
            query = pair_columns(q_t, mb, g)
            grad = pair_columns(gm_t, mb, g)
            mixed = pair_columns(mix_t, mb, g)
            blank = jnp.zeros_like(query)
            inner = jnp.sum(grad.astype(F32) * mixed.astype(F32), axis=0, keepdims=True)
            query = jnp.concatenate([query, blank], axis=0)
            grad = jnp.concatenate([blank, grad], axis=0)
            both = jnp.concatenate([query, grad], axis=1)
            scale = 1.0 / lsum[mb, g]
            dq = jnp.zeros((128, 256), F32)
            for j in range(4):
                keys = kv_all[mb, j, :, g].reshape(256, 128)
                there = bias[mb, 256 * j : 256 * (j + 1)].astype(F32)
                got = nn(keys, both)
                p = jnp.exp(got[:, :256] + jnp.concatenate([there, there], axis=1)) * scale
                ds = (p * (got[:, 256:] - inner)).astype(BF)
                dq += tn(keys, ds)
                dkv = nt(jnp.concatenate([ds, p.astype(BF)], axis=1), both)
                part_kv[mb, g // 4, j, :, g % 4] = dkv.astype(BF).reshape(2, 128, 128)
            dq = dq[:64] * HD ** (-0.5)
            rows = pl.ds(pl.multiple_of(g * 128, 128), 128)
            dq_t[mb, rows] = jnp.concatenate([dq[:, :128], dq[:, 128:]], axis=0)

    copies[4].wait()
    cosine, sine = turn[:32], turn[32:]
    query_gain = head_gain(small_t[...], 34)
    key_gain = head_gain(small_t[...], 35)

    def head_back(grad, v, gain, total):
        inv = inverse_rms(v, 0)
        grad = turned(grad, cosine, -sine)
        grad_v, gain_part = norm_grad(grad, v, inv, gain, 0)
        total[...] += gain_part
        return grad_v

    def queries_back(mb):
        @pl.loop(0, 8)
        def _(g):
            pieces = []
            for r in range(2):
                rows = pl.ds(pl.multiple_of(g * 128 + r * 64, 64), 64)
                pieces.append(head_back(dq_t[mb, rows], raw_t[mb, rows], query_gain, q_sum))
            cols = pl.ds(pl.multiple_of(g * 128, 128), 128)
            gp[tokens_of(mb), cols] = jnp.concatenate(pieces, axis=0).T.astype(BF)

    def turn_normed():
        for mb in range(2):
            v = tok[mb].astype(F32)
            normed = (v * inverse_rms(v, 1) * attn_gain).astype(BF).astype(F32)
            for k in range(8):
                normed_t[128 * k : 128 * (k + 1), tokens_of(mb)] = (
                    normed[:, 128 * k : 128 * (k + 1)].T.astype(BF)
                )

    def weight_part(which):
        cols = pl.ds(1024 * (which - 1), 1024)

        @pl.loop(0, 4)
        def _(n):
            rows = pl.ds(pl.multiple_of(n * 256, 256), 256)
            part_w[which, n] = nn(normed_t[rows], gp[:, cols]).astype(BF).reshape(2, 128, 1024)

    def keys_back(mb):
        @pl.loop(0, 4)
        def _(k):
            keys, values = [], []
            for r in range(2):
                g = 2 * k + r
                grad = own_kv[mb, g].T
                rows = pl.ds(pl.multiple_of(1024 + g * 64, 64), 64)
                keys.append(head_back(grad[:64], raw_t[mb, rows], key_gain, k_sum))
                values.append(grad[64:])
            cols = pl.ds(pl.multiple_of(1024 + k * 128, 128), 128)
            gp[tokens_of(mb), cols] = jnp.concatenate(keys, axis=0).T.astype(BF)
            cols = pl.ds(pl.multiple_of(1536 + k * 128, 128), 128)
            gp[tokens_of(mb), cols] = jnp.concatenate(values, axis=0).T.astype(BF)

    def normed_grad(k):
        @pl.loop(0, 4)
        def _(n):
            cols = pl.ds(pl.multiple_of(n * 256, 256), 256)
            got = nt(gp[:, 1024 * k : 1024 * (k + 1)], wq_all[k, n].reshape(256, 1024))
            gn[:, cols] = got if k == 0 else gn[:, cols] + got

    def finish():
        attn_gain_grad = jnp.zeros((1, 1024), F32)
        for mb in range(2):
            v = tok[mb].astype(F32)
            grad, gain = norm_grad(gn[tokens_of(mb)], v, inverse_rms(v, 1), attn_gain, 1)
            attn_gain_grad += jnp.sum(gain, axis=0, keepdims=True)
            in_grad[mb] = (gres[mb] + grad).astype(BF)
        for b in range(8):
            cols = slice(128 * b, 128 * (b + 1))
            heads = slice(8 * b, 8 * (b + 1))
            part_s[b // 2, b % 2, 0:32] = router_sum[0:32, cols] + router_sum[32:64, cols]
            part_s[b // 2, b % 2, 32:33] = attn_gain_grad[:, cols]
            part_s[b // 2, b % 2, 33:34] = gain_sums[1:2, cols]
            part_s[b // 2, b % 2, 40:48] = jnp.broadcast_to(
                jnp.sum(q_sum[heads], axis=1, keepdims=True), (8, 128)
            )
            part_s[b // 2, b % 2, 48:56] = jnp.broadcast_to(
                jnp.sum(k_sum[heads], axis=1, keepdims=True), (8, 128)
            )

    me = plane.me

    def parcel(step):
        to = (me + step) % 16
        return send(
            parcels.at[to], got_parcels.at[me], far_send.at[step], far_recv.at[step], {"expert": to}
        )

    def total_message(step):
        to = (me + step) % 16
        return send(
            kv_total.at[me], kv_total.at[me], all_send.at[step], all_recv.at[step], {"expert": to}
        )

    def send_parcels():
        @pl.loop(0, 16)
        def _(n):
            parcels[n, 64:128] = small_own[...]

        for step in range(1, 16):
            parcel(step).start()
        got_parcels[me] = parcels[me]

    def add_parcels():
        for step in range(1, 16):
            parcel(step).wait_recv()
        total = got_parcels[0].astype(F32)
        for n in range(1, 16):
            total += got_parcels[n].astype(F32)
        kv_total[me] = total[:64].astype(BF)
        for step in range(1, 16):
            total_message(step).start()
        gs[...] = total[64:]

    def write_out(k):
        for n in range(16):
            rows = slice(64 * (n // 8), 64 * (n // 8) + 64)
            cols = slice(128 * (n % 8), 128 * (n % 8) + 128)
            (go, gq)[k][rows, cols] = plane_all[n // 4, n % 4, :, 128 * k : 128 * (k + 1)].astype(F32)

    def take_totals():
        for step in range(1, 16):
            total_message(step).wait_recv()
        for n in range(16):
            first = 1024 + 128 * (n % 8)
            gq[64 * (n // 8) : 64 * (n // 8) + 64, first : first + 128] = kv_total[n].astype(F32)

    dall[2].step(0)
    router_and_norm()
    parts[0].wait()
    sout[0].step(0)
    dall[0].step(0)
    out_projection()
    dall[1].step(0)
    copies[1].wait()
    attend(1, 0, 2)
    attend(1, 2, 4)
    attend(0, 0, 2)
    kv_sums[1][0].step(0)
    w_sums[0].step(0)
    sout[0].step(1)
    attend(1, 4, 6)
    attend(1, 6, 8)
    dall[0].step(1)
    kv_sums[1][0].step(1)
    kv_sums[1][1].step(0)
    attend(0, 2, 4)
    w_sums[0].step(1)
    attend(0, 4, 6)
    dall[2].step(1)
    kv_sums[1][1].step(1)
    sout[0].step(2)
    w_sums[0].step(2)
    attend(0, 6, 8)
    sout[0].step(3)
    kv_sums[0][1].step(0)
    kv_sums[0][0].step(0)
    kv_sums[1][1].step(2)
    turn_normed()
    copies[2].wait()
    queries_back(1)
    queries_back(0)
    kv_sums[1][0].step(2)
    kv_sums[0][1].step(1)
    weight_part(1)
    copies[3].wait()
    normed_grad(0)
    sout[0].step(4)
    parts[1].start()
    sout[0].give_credit()
    w_sums[1].step(0)
    kv_sums[0][0].step(1)
    kv_sums[0][1].step(2)
    parts[1].wait()
    sout[1].take_credit()
    sout[1].step(0)
    dall[0].step(2)
    w_sums[1].step(1)
    kv_sums[1][1].step(3)
    kv_sums[0][1].step(3)
    kv_sums[0][0].step(2)
    w_sums[1].step(2)
    sout[1].step(1)
    kv_sums[0][0].step(3)
    kv_sums[1][0].step(3)
    keys_back(0)
    dall[2].step(2)
    keys_back(1)
    dall[1].step(1)
    weight_part(2)
    w_sums[2].step(0)
    w_sums[0].step(3)
    normed_grad(1)
    w_sums[1].step(3)
    over.step(0)
    finish()
    dall[0].step(3)
    dall[1].step(2)
    s_sum.step(0)
    w_sums[2].step(1)
    over.step(1)
    dall[2].step(3)
    sout[1].step(2)
    s_sum.step(1)
    w_sums[2].step(2)
    over.step(2)
    over.step(3)
    s_sum.step(2)
    sout[1].step(3)
    dall[1].step(3)
    over.step(4)
    s_sum.step(3)
    spread.step(0)
    w_sums[2].step(3)
    send_parcels()
    spread.step(1)
    spread.step(2)
    sout[1].step(4)
    add_parcels()
    spread.step(3)
    spread.step(4)
    write_out(0)
    write_out(1)
    take_totals()
    for step in range(1, 16):
        parcel(step).wait_send()
        total_message(step).wait_send()
    for copy in owns:
        copy.wait()


def back(tok, cot, seg, turn, wq_all, wo_all, small_t, raw_t, q_t, kv_all, mix_t, lsum, res, ffn, gates_t, share, dx, out_part, dw_own):
    vmem = pl.BlockSpec(memory_space=pltpu.VMEM)
    anywhere = pl.BlockSpec(memory_space=pl.ANY)
    kv_slots = column_slots((4, 128, 128), lead=(2, 2))
    return pl.pallas_call(
        back_kernel,
        out_shape=(
            jax.ShapeDtypeStruct((2, 4, 2, 128, 1024), BF),
            jax.ShapeDtypeStruct((4, 2, 128, 1024), BF),
            jax.ShapeDtypeStruct((2, 128, 1024), BF),
            jax.ShapeDtypeStruct((2, 128, 1024), BF),
            jax.ShapeDtypeStruct((128, 2048), F32),
            jax.ShapeDtypeStruct((128, 1024), F32),
            jax.ShapeDtypeStruct((64, 128), F32),
        ),
        in_specs=[
            vmem, vmem, vmem, anywhere, anywhere, anywhere, vmem, anywhere, vmem, anywhere,
            vmem, vmem, vmem, vmem, vmem, vmem, vmem, anywhere, vmem,
        ],
        out_specs=(anywhere,) * 2 + (vmem,) * 5,
        scratch_shapes=[
            pltpu.VMEM((2, 4, 2, 128, 1024), BF),
            pltpu.VMEM((4, 2, 128, 1024), BF),
            pltpu.VMEM((2, 4, 2, 8, 128, 128), BF),
            pltpu.VMEM((2, 2048, 128), F32),
            pltpu.VMEM((64, 128), F32),
            pltpu.VMEM((2, 1024, 128), BF),
            pltpu.VMEM((2, 128, 1024), F32),
            pltpu.VMEM((256, 1024), BF),
            pltpu.VMEM((2, 1024, 128), BF),
            pltpu.VMEM((2, 1024, 128), F32),
            pltpu.VMEM((2, 8, 128, 128), F32),
            pltpu.VMEM((256, 2048), BF),
            pltpu.VMEM((1024, 256), BF),
            pltpu.VMEM((256, 1024), F32),
            pltpu.VMEM((2, 2, 4, 2, 4, 128, 128), BF),
            pltpu.VMEM((3, 4, 2, 128, 1024), BF),
            pltpu.VMEM((4, 2, 64, 128), F32),
            pltpu.VMEM((64, 128), F32),
            pltpu.VMEM((64, 128), F32),
            *column_slots((128, 1024), lead=(3,)),
            *kv_slots,
            pltpu.VMEM((4, 4, 64, 256), BF),
            pltpu.VMEM((4, 4, 64, 256), BF),
            *scatter_slots(64, 256),
            *column_slots((64, 128), F32),
            pltpu.VMEM((64, 256), BF),
            pltpu.VMEM((64, 1024), BF),
            pltpu.VMEM((64, 1024), F32),
            pltpu.VMEM((4, 4, 128, 1024), BF),
            *scatter_slots(128, 1024),
            pltpu.VMEM((16, 128, 128), BF),
            pltpu.VMEM((16, 128, 128), BF),
            pltpu.VMEM((64, 128), BF),
            pltpu.VMEM((16, 64, 128), BF),
            pltpu.SemaphoreType.DMA((11, 2, 8)),
            pltpu.SemaphoreType.DMA((4, 2, 2, 8)),
            pltpu.SemaphoreType.DMA((16,)),
            pltpu.SemaphoreType.DMA((16,)),
            pltpu.SemaphoreType.DMA((16,)),
            pltpu.SemaphoreType.DMA((16,)),
            pltpu.SemaphoreType.REGULAR,
            pltpu.SemaphoreType.DMA((10,)),
            pltpu.VMEM((8, 1024), F32),
        ],
        compiler_params=pltpu.CompilerParams(
            collective_id=2, has_side_effects=True, vmem_limit_bytes=63 * MIB
        ),
        cost_estimate=pl.CostEstimate(
            flops=12_000_000_000, bytes_accessed=30_000_000, transcendentals=5_000_000
        ),
    )(tok, cot, seg, turn, wq_all, wo_all, small_t, raw_t, q_t, kv_all, mix_t, lsum, res, ffn, gates_t, share, dx, out_part, dw_own)


def last_kernel(
    dgu_ref, dd_ref, out_ref, in_ref, gq_ref, go_ref, gs_ref,
    dgu_f, dd_f, out_f, in_f, gq_f, go_f, attn_f, ffn_f, q_f, k_f, router_f,
):
    dgu_f[...] = dgu_ref[...].astype(F32)
    dd_f[...] = dd_ref[...].astype(F32)
    out_f[...] = out_ref[...]
    in_f[...] = in_ref[...]
    gq_f[...] = gq_ref[...]
    go_f[...] = go_ref[...]
    attn_f[...] = gs_ref[32:33]
    ffn_f[...] = gs_ref[33:34]
    q_f[...] = gs_ref[40:48].T[0:1]
    k_f[...] = gs_ref[48:56].T[0:1]
    router_f[...] = gs_ref[0:32]


def last(dgu, dd, output, in_grad, gq, go, gs):
    def rows(count, width):
        return pl.BlockSpec((count, width), lambda n: (n, 0))

    def whole(*shape):
        return pl.BlockSpec(shape, lambda n: (0, 0))

    return pl.pallas_call(
        last_kernel,
        grid=(8,),
        out_shape=(
            jax.ShapeDtypeStruct((2048, 1024), F32),
            jax.ShapeDtypeStruct((1024, 1024), F32),
            jax.ShapeDtypeStruct((256, 1024), BF),
            jax.ShapeDtypeStruct((256, 1024), BF),
            jax.ShapeDtypeStruct((128, 2048), F32),
            jax.ShapeDtypeStruct((128, 1024), F32),
            jax.ShapeDtypeStruct((1, 128), F32),
            jax.ShapeDtypeStruct((1, 128), F32),
            jax.ShapeDtypeStruct((1, 8), F32),
            jax.ShapeDtypeStruct((1, 8), F32),
            jax.ShapeDtypeStruct((32, 128), F32),
        ),
        in_specs=[
            rows(256, 1024), rows(128, 1024), rows(32, 1024), rows(32, 1024), rows(16, 2048),
            rows(16, 1024), whole(64, 128),
        ],
        out_specs=(
            rows(256, 1024), rows(128, 1024), rows(32, 1024), rows(32, 1024), rows(16, 2048),
            rows(16, 1024), whole(1, 128), whole(1, 128), whole(1, 8), whole(1, 8), whole(32, 128),
        ),
        cost_estimate=pl.CostEstimate(flops=0, bytes_accessed=24_000_000, transcendentals=0),
    )(
        dgu.reshape(2048, 1024), dd.reshape(1024, 1024), output.reshape(256, 1024),
        in_grad.reshape(256, 1024), gq, go, gs,
    )


def turn_table(length):
    frequency = np.power(np.float32(THETA), -2.0 * np.arange(HD // 2, dtype=np.float32) / HD)
    angle = np.arange(length, dtype=np.float32)[:, None] * frequency.astype(np.float32)[None, :]
    both = np.concatenate([np.cos(angle), np.sin(angle)], axis=1).astype(np.float32)
    return both.reshape(length // 128, 128, HD).transpose(0, 2, 1)


def body(
    tokens,
    cotangent,
    segments,
    routes,
    w_qkv,
    w_out,
    attn_norm,
    ffn_norm,
    q_gain,
    k_gain,
    router,
    w_gate_up,
    w_down,
):
    tok = tokens.reshape(2, 128, 1024)
    cot = cotangent.reshape(2, 128, 1024)
    seg = segments.reshape(2, 8, 1, 128)
    routes_t = routes.reshape(2, 128, 8).transpose(0, 2, 1)
    turn = jnp.asarray(turn_table(1024))
    gains = jnp.pad(jnp.stack([q_gain, k_gain]), ((0, 28), (0, 120)))
    small = jnp.concatenate([router.T, attn_norm[None], ffn_norm[None], gains])
    (
        dy_all, x0, wq_all, wo_all, kv_all, raw_t, small_t, q_t, mix_t, lsum, res, ffn, gates_t, sent
    ) = front(tok, cot, w_qkv, w_out, small, seg, routes_t, turn)
    out_part, moved_dx, share, dw_own = moe(ffn, x0, dy_all, sent, w_gate_up, w_down)
    dgu, dd, output, in_grad, gq, go, gs = back(
        tok, cot, seg, turn, wq_all, wo_all, small_t, raw_t, q_t, kv_all, mix_t, lsum, res, ffn,
        gates_t, share, moved_dx, out_part, dw_own,
    )
    dgu, dd, output, in_grad, gq, go, attn, ffn_gain, q_grad, k_grad, router_grad = last(
        dgu, dd, output, in_grad, gq, go, gs
    )
    return (
        output.reshape(tokens.shape),
        in_grad.reshape(tokens.shape),
        gq,
        go,
        attn.reshape(128),
        ffn_gain.reshape(128),
        q_grad.reshape(8),
        k_grad.reshape(8),
        router_grad.T,
        dgu.reshape(2, 1024, 1024),
        dd.reshape(2, 512, 1024),
    )


def solution(mesh):
    return jax.shard_map(
        body,
        mesh=mesh,
        in_specs=(
            P(None, "expert", "dp", None),
            P(None, "expert", "dp", None),
            P(None, "expert", None),
            P(None, "expert", "dp", None),
            P("dp", None),
            P("dp", None),
            P("dp"),
            P("dp"),
            P("dp"),
            P("dp"),
            P("dp", None),
            P("expert", None, None),
            P("expert", None, None),
        ),
        out_specs=(
            P(None, "expert", "dp", None),
            P(None, "expert", "dp", None),
            P("dp", None),
            P("dp", None),
            P("dp"),
            P("dp"),
            P("dp"),
            P("dp"),
            P("dp", None),
            P("expert", None, None),
            P("expert", None, None),
        ),
        check_vma=False,
    )
```

```python
import jax
import jax.numpy as jnp
import numpy as np
from jax import lax
from jax.experimental import pallas as pl
from jax.experimental.pallas import tpu as pltpu
from jax.sharding import PartitionSpec as P

HD = 64
EPSILON = 1e-06
THETA = 10000.0
MASKED = -1e30

BF = jnp.bfloat16
F32 = jnp.float32
SLOTS = 48
CHUNK = 256
MIB = 1024 * 1024


def nn(a, b):
    return lax.dot_general(a, b, (((1,), (0,)), ((), ())), preferred_element_type=F32)


def nt(a, b):
    return lax.dot_general(a, b, (((1,), (1,)), ((), ())), preferred_element_type=F32)


def tn(a, b):
    return lax.dot_general(a, b, (((0,), (0,)), ((), ())), preferred_element_type=F32)


def send(src, dst, send_sem, recv_sem, device):
    return pltpu.make_async_remote_copy(
        src_ref=src, dst_ref=dst, send_sem=send_sem, recv_sem=recv_sem, device_id=device
    )


def next_to(p):
    return (p + 1) % 4, (p + 3) % 4, (p + 2) % 4


def greet(devices):
    sem = pltpu.get_barrier_semaphore()
    for device in devices:
        pl.semaphore_signal(sem, inc=1, device_id=device)
    pl.semaphore_wait(sem, len(devices))


class Plane:
    def __init__(self):
        self.me = lax.axis_index("expert")
        self.z = self.me // 4
        self.x = self.me % 4

    def own(self, half):
        return (self.x, self.z) if half == 0 else (self.z, self.x)

    def device(self, half, p, q):
        return {"expert": q * 4 + p if half == 0 else p * 4 + q}

    def others(self):
        return [{"expert": (self.me + step) % 16} for step in range(1, 16)]

    def neighbours(self):
        zn, zp, _ = next_to(self.z)
        xn, xp, _ = next_to(self.x)
        return [{"expert": k} for k in (zn * 4 + self.x, zp * 4 + self.x, self.z * 4 + xn, self.z * 4 + xp)]


class Column:
    def __init__(self):
        self.me = lax.axis_index("dp")
        self.y = self.me // 2
        self.c = self.me % 2

    def neighbours(self):
        yn, yp, _ = next_to(self.y)
        return [self.to(yn), self.to(yp), self.other()]

    def to(self, y):
        return {"dp": y * 2 + self.c}

    def other(self):
        return {"dp": self.y * 2 + 1 - self.c}


class PlaneStep:
    def at(self, half, p, q, rows):
        return self.ref.at[q, p, rows] if half == 0 else self.ref.at[p, q, rows]

    def line(self, half, q, rows):
        return self.ref.at[q, :, rows] if half == 0 else self.ref.at[:, q, rows]

    def rows(self, half):
        quarter = self.height // 4
        base = 2 * quarter * half
        return pl.ds(base, 2 * quarter), pl.ds(base, quarter), pl.ds(base + quarter, quarter)


class Gather(PlaneStep):
    def __init__(self, plane, ref, sems, height=128):
        self.plane, self.ref, self.sems, self.height = plane, ref, sems, height

    def message(self, half, i):
        p, q = self.plane.own(half)
        pn, pp, _ = next_to(p)
        qn, qp, _ = next_to(q)
        full, first, second = self.rows(half)
        view, to = [
            lambda: (self.at(half, p, q, full), (pn, q)),
            lambda: (self.at(half, p, q, full), (pp, q)),
            lambda: (self.at(half, pp, q, first), (pn, q)),
            lambda: (self.at(half, pn, q, second), (pp, q)),
            lambda: (self.line(half, q, full), (p, qn)),
            lambda: (self.line(half, q, full), (p, qp)),
            lambda: (self.line(half, qp, first), (p, qn)),
            lambda: (self.line(half, qn, second), (p, qp)),
        ][i]()
        sems = self.sems
        return send(view, view, sems.at[0, half, i], sems.at[1, half, i], self.plane.device(half, *to))

    def step(self, n):
        waits, starts = [
            ((), (0, 1)),
            ((0, 1), (2, 3)),
            ((2, 3), (4, 5)),
            ((4, 5), (6, 7)),
            ((6, 7), ()),
        ][n]
        for half in range(2):
            for i in waits:
                self.message(half, i).wait_recv()
            for i in starts:
                self.message(half, i).start()
        if n == 4:
            for half in range(2):
                for i in range(8):
                    self.message(half, i).wait_send()


class Scatter(PlaneStep):
    def __init__(self, plane, ref, slots, sems, store, free=None, height=128):
        self.plane, self.ref, self.slots, self.sems = plane, ref, slots, sems
        self.store, self.free, self.height = store, free, height

    def message(self, half, i):
        p, q = self.plane.own(half)
        pn, pp, po = next_to(p)
        qn, qp, qo = next_to(q)
        full, first, second = self.rows(half)
        r1, r2, r3, r4 = self.slots
        view, slot, to = [
            lambda: (self.line(half, qo, first), r1.at[half, 0], (p, qn)),
            lambda: (self.line(half, qo, second), r1.at[half, 1], (p, qp)),
            lambda: (self.line(half, qn, full), r2.at[half, 0], (p, qn)),
            lambda: (self.line(half, qp, full), r2.at[half, 1], (p, qp)),
            lambda: (self.at(half, po, q, first), r3.at[half, 0], (pn, q)),
            lambda: (self.at(half, po, q, second), r3.at[half, 1], (pp, q)),
            lambda: (self.at(half, pn, q, full), r4.at[half, 0], (pn, q)),
            lambda: (self.at(half, pp, q, full), r4.at[half, 1], (pp, q)),
        ][i]()
        sems = self.sems
        return send(view, slot, sems.at[0, half, i], sems.at[1, half, i], self.plane.device(half, *to))

    def add_line(self, half, q, part, parts, slots):
        quarter = self.height // 4
        offset = quarter * (2 * half + part)
        groups = quarter * parts // 16

        @pl.loop(0, 4 * groups)
        def _(n):
            j, k = n // groups, n % groups
            rows = pl.ds(pl.multiple_of(offset + k * 16, 16), 16)
            some = pl.ds(pl.multiple_of(k * 16, 16), 16)
            place = (q, j, rows) if half == 0 else (j, q, rows)
            total = self.ref[place].astype(F32)
            for ref, side in slots:
                total += ref[half, side, j, some].astype(F32)
            self.ref[place] = total.astype(BF)

    def add_at(self, half, p, q, part, slot):
        quarter = self.height // 4
        ref, side = slot

        @pl.loop(0, quarter // 16)
        def _(k):
            rows = pl.ds(pl.multiple_of(quarter * (2 * half + part) + k * 16, 16), 16)
            place = (q, p, rows) if half == 0 else (p, q, rows)
            got = ref[half, side, pl.ds(pl.multiple_of(k * 16, 16), 16)].astype(F32)
            self.ref[place] = (self.ref[place].astype(F32) + got).astype(BF)

    def step(self, n):
        r1, r2, r3, r4 = self.slots
        for half in range(2):
            p, q = self.plane.own(half)
            pn, pp, po = next_to(p)
            qn, qp, qo = next_to(q)
            if n == 0:
                self.message(half, 0).start()
                self.message(half, 1).start()
            elif n == 1:
                self.message(half, 0).wait_recv()
                self.add_line(half, qn, 0, 1, [(r1, 0)])
                self.message(half, 2).start()
                self.message(half, 1).wait_recv()
                self.add_line(half, qp, 1, 1, [(r1, 1)])
                self.message(half, 3).start()
            elif n == 2:
                self.message(half, 2).wait_recv()
                self.message(half, 3).wait_recv()
                self.add_line(half, q, 0, 2, [(r2, 0), (r2, 1)])
                self.message(half, 4).start()
                self.message(half, 5).start()
            elif n == 3:
                self.message(half, 4).wait_recv()
                self.add_at(half, pn, q, 0, (r3, 0))
                self.message(half, 6).start()
                self.message(half, 5).wait_recv()
                self.add_at(half, pp, q, 1, (r3, 1))
                self.message(half, 7).start()
            elif n == 4:
                self.message(half, 6).wait_recv()
                self.message(half, 7).wait_recv()

                @pl.loop(0, self.height // 32)
                def _(k):
                    rows = pl.ds(pl.multiple_of(self.height // 2 * half + k * 16, 16), 16)
                    place = (q, p, rows) if half == 0 else (p, q, rows)
                    some = pl.ds(pl.multiple_of(k * 16, 16), 16)
                    total = self.ref[place].astype(F32)
                    total += r4[half, 0, some].astype(F32)
                    total += r4[half, 1, some].astype(F32)
                    self.store(place, rows, total)
        if n == 4:
            for half in range(2):
                for i in range(8):
                    self.message(half, i).wait_send()

    def give_credit(self):
        for device in self.plane.neighbours():
            pl.semaphore_signal(self.free, inc=1, device_id=device)

    def take_credit(self):
        pl.semaphore_wait(self.free, 4)


def scatter_slots(height, width, lead=()):
    quarter = height // 4
    return [
        pltpu.VMEM((*lead, 2, 2, 4, quarter, width), BF),
        pltpu.VMEM((*lead, 2, 2, 4, 2 * quarter, width), BF),
        pltpu.VMEM((*lead, 2, 2, quarter, width), BF),
        pltpu.VMEM((*lead, 2, 2, 2 * quarter, width), BF),
    ]


class ColumnGather:
    def __init__(self, column, ref, sems, count, own=None):
        self.column, self.ref, self.sems, self.count = column, ref, sems, count
        self.own = own

    def message(self, i):
        y, c = self.column.y, self.column.c
        yn, yp, yo = next_to(y)
        half = self.count // 2
        ref, column = self.ref, self.column
        view, device = [
            lambda: (ref.at[y, c], column.to(yn)),
            lambda: (ref.at[y, c], column.to(yp)),
            lambda: (ref.at[y, c], column.other()),
            lambda: (ref.at[yp, c, pl.ds(0, half)], column.to(yn)),
            lambda: (ref.at[yn, c, pl.ds(half, half)], column.to(yp)),
            lambda: (ref.at[yp, c], column.other()),
            lambda: (ref.at[yn, c], column.other()),
            lambda: (ref.at[yo, c], column.other()),
        ][i]()
        source = self.own if i < 3 and self.own is not None else view
        return send(source, view, self.sems.at[0, i], self.sems.at[1, i], device)

    def step(self, n):
        order = [
            [("s", 0), ("s", 1), ("s", 2)],
            [("w", 0), ("s", 3), ("s", 5), ("w", 1), ("s", 4), ("s", 6)],
            [("w", 3), ("w", 4), ("s", 7)],
            [("w", 2), ("w", 5), ("w", 6), ("w", 7)],
        ][n]
        for what, i in order:
            if what == "s":
                self.message(i).start()
            else:
                self.message(i).wait_recv()
        if n == 3:
            for i in range(8):
                self.message(i).wait_send()


class ColumnScatter:
    def __init__(self, column, ref, slots, sems, count, store, group=16):
        self.column, self.ref, self.slots, self.sems = column, ref, slots, sems
        self.count, self.store, self.group = count, store, group

    def message(self, i):
        y, c = self.column.y, self.column.c
        yn, yp, yo = next_to(y)
        half = self.count // 2
        ref, column = self.ref, self.column
        ra, rb, rc = self.slots
        view, slot, device = [
            lambda: (ref.at[:, 1 - c], ra, column.other()),
            lambda: (ref.at[yo, c, pl.ds(0, half)], rb.at[0], column.to(yn)),
            lambda: (ref.at[yo, c, pl.ds(half, half)], rb.at[1], column.to(yp)),
            lambda: (ref.at[yn, c], rc.at[0], column.to(yn)),
            lambda: (ref.at[yp, c], rc.at[1], column.to(yp)),
        ][i]()
        return send(view, slot, self.sems.at[0, i], self.sems.at[1, i], device)

    def some(self, k, base=0):
        return pl.ds(pl.multiple_of(base + k * self.group, self.group), self.group)

    def step(self, n):
        y, c = self.column.y, self.column.c
        yn, yp, yo = next_to(y)
        ref, (ra, rb, rc) = self.ref, self.slots
        low = ref.dtype
        half = self.count // 2
        groups = self.count // self.group
        if n == 0:
            self.message(0).start()
        elif n == 1:
            self.message(0).wait_recv()

            @pl.loop(0, 4 * groups)
            def _(k):
                j, r = k // groups, self.some(k % groups)
                ref[j, c, r] = (ref[j, c, r].astype(F32) + ra[j, r].astype(F32)).astype(low)

            self.message(1).start()
            self.message(2).start()
        elif n == 2:
            for side, to in ((0, yn), (1, yp)):
                self.message(1 + side).wait_recv()

                @pl.loop(0, groups // 2)
                def _(k):
                    r = self.some(k, side * half)
                    got = rb[side, self.some(k)].astype(F32)
                    ref[to, c, r] = (ref[to, c, r].astype(F32) + got).astype(low)

                self.message(3 + side).start()
        else:
            self.message(3).wait_recv()
            self.message(4).wait_recv()

            @pl.loop(0, groups)
            def _(k):
                r = self.some(k)
                total = ref[y, c, r].astype(F32) + rc[0, r].astype(F32) + rc[1, r].astype(F32)
                self.store(r, total)

            for i in range(5):
                self.message(i).wait_send()


def column_slots(shape, dtype=BF, lead=()):
    count, rest = shape[0], shape[1:]
    return [
        pltpu.VMEM((*lead, 4, count, *rest), dtype),
        pltpu.VMEM((*lead, 2, count // 2, *rest), dtype),
        pltpu.VMEM((*lead, 2, count, *rest), dtype),
    ]


def turned(v, cosine, sine):
    a, b = v[:32], v[32:]
    return jnp.concatenate([a * cosine - b * sine, b * cosine + a * sine], axis=0)


def inverse_rms(v, axis):
    return lax.rsqrt(jnp.mean(v * v, axis=axis, keepdims=True) + EPSILON)


def head_gain(small_t, row):
    pieces = [small_t[:, 128 * b : 128 * (b + 1)] for b in range(8)]
    tall = jnp.concatenate([piece.T[:8] for piece in pieces], axis=0)
    return jnp.broadcast_to(tall[:, row : row + 1], (64, 128))


def document_bias(seg_ref, bias, mb, mine):
    own = seg_ref[mb, mine].astype(F32)
    for b in range(8):
        keys = jnp.broadcast_to(seg_ref[mb, b].astype(F32), (128, 128)).T
        bias[mb, 128 * b : 128 * (b + 1)] = jnp.where(keys == own, 0.0, MASKED).astype(bias.dtype)


def pair_columns(ref, mb, g):
    both = ref[mb, pl.ds(pl.multiple_of(g * 128, 128), 128)]
    return jnp.concatenate([both[:64], both[64:]], axis=1)


def front_kernel(
    tok, cot, wq, wo, small, seg_ref, routes_ref, turn_hbm,
    dy_out, x0_out, wq_out, wo_out, kv_out, raw_out,
    small_t, q_t, mix_t, lsum, res, ffn, gates_t, g_all,
    dy_all, x0_all, wq_all, wo_all, kv_all, raw_t, small_all, normed, bias, turn, plane_sems, column_sems,
    sent, gsend, grecv, local,
):
    plane, column = Plane(), Column()
    y, c = column.y, column.c
    copies = [
        pltpu.make_async_copy(small, small_all.at[y, c], local.at[0]),
        pltpu.make_async_copy(wq.at[:, 1024:2048], wq_all.at[1, y, c], local.at[1]),
        pltpu.make_async_copy(wq.at[:, 0:1024], wq_all.at[0, y, c], local.at[3]),
        pltpu.make_async_copy(wo, wo_all.at[y, c], local.at[5]),
        pltpu.make_async_copy(turn_hbm.at[column.me], turn, local.at[6]),
    ]
    for copy in copies:
        copy.start()
    outs = [
        pltpu.make_async_copy(wq_all, wq_out, local.at[7]),
        pltpu.make_async_copy(wo_all, wo_out, local.at[8]),
        pltpu.make_async_copy(kv_all, kv_out, local.at[9]),
        pltpu.make_async_copy(raw_t, raw_out, local.at[10]),
        pltpu.make_async_copy(dy_all.at[0], dy_out.at[0], local.at[11]),
        pltpu.make_async_copy(dy_all.at[1], dy_out.at[1], local.at[2]),
        pltpu.make_async_copy(x0_all, x0_out, local.at[4]),
    ]
    for mb in range(2):
        dy_all[mb, plane.z, plane.x] = cot[mb]
    greet(plane.others() + column.neighbours())
    gdy = [Gather(plane, dy_all.at[mb], plane_sems.at[mb]) for mb in range(2)]
    gx = Gather(plane, x0_all, plane_sems.at[2])
    w_small = ColumnGather(column, small_all, column_sems.at[0], 64)
    w_q = ColumnGather(column, wq_all.at[0], column_sems.at[1], 128)
    w_kv = ColumnGather(column, wq_all.at[1], column_sems.at[2], 128)
    w_o = ColumnGather(column, wo_all, column_sems.at[3], 128)
    kv = [ColumnGather(column, kv_all.at[mb], column_sems.at[4 + mb], 8) for mb in range(2)]
    def both_biases():
        for mb in range(2):
            document_bias(seg_ref, bias, mb, column.me)

    def norm_tokens():
        for b in range(8):
            small_t[:, 128 * b : 128 * (b + 1)] = small_all[b // 2, b % 2].astype(F32)
        attn_gain = small_t[32:33]
        for mb in range(2):
            v = tok[mb].astype(F32)
            normed[128 * mb : 128 * (mb + 1)] = (v * inverse_rms(v, 1) * attn_gain).astype(BF)

    def project(k):
        @pl.loop(0, 2)
        def _(n):
            cols = pl.ds(pl.multiple_of(n * 512, 512), 512)
            rows = pl.ds(pl.multiple_of(1024 * k + n * 512, 512), 512)
            got = nn(normed[...], wq_all[k, :, :, :, cols].reshape(1024, 512))
            for mb in range(2):
                raw_t[mb, rows] = got[128 * mb : 128 * (mb + 1)].T

    def key_heads(mb):
        @pl.loop(0, 8)
        def _(g):
            v = raw_t[mb, pl.ds(pl.multiple_of(1024 + g * 64, 64), 64)]
            key = turned(v * inverse_rms(v, 0) * key_gain, cosine, sine)
            value = raw_t[mb, pl.ds(pl.multiple_of(1536 + g * 64, 64), 64)]
            kv_all[mb, y, c, g] = jnp.concatenate([key, value], axis=0).T.astype(BF)

    def query_heads(mb):
        @pl.loop(0, 16)
        def _(h):
            rows = pl.ds(pl.multiple_of(h * 64, 64), 64)
            v = raw_t[mb, rows]
            query = turned(v * inverse_rms(v, 0) * query_gain, cosine, sine)
            q_t[mb, rows] = (query.astype(BF).astype(F32) * HD ** (-0.5)).astype(BF)

    def attend(mb, start, stop):
        @pl.loop(start, stop)
        def _(g):
            query = pair_columns(q_t, mb, g)
            query = jnp.concatenate([query, jnp.zeros_like(query)], axis=0)
            total = jnp.zeros((1, 256), F32)
            mixed = jnp.zeros((128, 256), F32)
            for j in range(4):
                keys = kv_all[mb, j, :, g].reshape(256, 128)
                there = bias[mb, 256 * j : 256 * (j + 1)].astype(F32)
                p = jnp.exp(nn(keys, query) + jnp.concatenate([there, there], axis=1))
                total += jnp.sum(p, axis=0, keepdims=True)
                mixed += tn(keys, p.astype(BF))
            lsum[mb, g] = total
            mixed = (mixed[64:] / total).astype(BF)
            both = jnp.concatenate([mixed[:, :128], mixed[:, 128:]], axis=0)
            mix_t[mb, pl.ds(pl.multiple_of(g * 128, 128), 128)] = both

    def finish(mb):
        @pl.loop(0, 2)
        def _(n):
            cols = pl.ds(pl.multiple_of(n * 512, 512), 512)
            got = tn(mix_t[mb], wo_all[:, :, :, cols].reshape(1024, 512))
            res[mb, :, cols] = tok[mb, :, cols].astype(F32) + got

        v = res[mb]
        low = (v * inverse_rms(v, 1) * small_t[33:34]).astype(BF)
        ffn[mb] = low
        logits = nt(small_t[:32].astype(BF), low)
        ids = lax.broadcasted_iota(jnp.int32, (32, 128), 0)
        routed = ids == routes_ref[mb, 0:1]
        for k in range(1, 8):
            routed = routed | (ids == routes_ref[mb, k : k + 1])
        top = jnp.max(jnp.where(routed, logits, MASKED), axis=0, keepdims=True)
        weight = jnp.where(routed, jnp.exp(logits - top), 0.0)
        gates = weight / jnp.sum(weight, axis=0, keepdims=True)
        gates_t[mb] = gates
        for k in range(16):
            sent[k, 2 * mb : 2 * mb + 2] = gates[2 * k : 2 * k + 2]

    def gate_message(step):
        to = (plane.me + step) % 16
        return send(
            sent.at[to], g_all.at[plane.me], gsend.at[step], grecv.at[step], {"expert": to}
        )

    def send_gates():
        for step in range(1, 16):
            gate_message(step).start()
        g_all[plane.me] = sent[plane.me]

    def take_gates():
        for step in range(1, 16):
            gate_message(step).wait_recv()
        for step in range(1, 16):
            gate_message(step).wait_send()

    sent[...] = jnp.zeros_like(sent)
    copies[0].wait()
    w_small.step(0)
    gdy[0].step(0)
    copies[1].wait()
    w_kv.step(0)
    w_small.step(1)
    gdy[1].step(0)
    copies[2].wait()
    w_q.step(0)
    gdy[0].step(1)
    gdy[0].step(2)
    w_small.step(2)
    w_kv.step(1)
    gdy[1].step(1)
    w_q.step(1)
    copies[3].wait()
    w_o.step(0)
    w_small.step(3)
    norm_tokens()
    w_kv.step(2)
    w_kv.step(3)
    project(1)
    gdy[1].step(2)
    query_gain = head_gain(small_t[...], 34)
    key_gain = head_gain(small_t[...], 35)
    copies[4].wait()
    cosine, sine = turn[:32], turn[32:]
    key_heads(0)
    kv[0].step(0)
    kv[0].step(1)
    both_biases()
    key_heads(1)
    w_q.step(2)
    gdy[0].step(3)
    w_o.step(1)
    kv[0].step(2)
    w_q.step(3)
    outs[0].start()
    project(0)
    outs[3].start()
    kv[1].step(0)
    w_o.step(2)
    gdy[1].step(3)
    query_heads(0)
    kv[0].step(3)
    attend(0, 0, 4)
    attend(0, 4, 8)
    w_o.step(3)
    outs[1].start()
    finish(0)
    x0_all[plane.z, plane.x] = ffn[0]
    gx.step(0)
    query_heads(1)
    kv[1].step(1)
    gx.step(1)
    kv[1].step(2)
    gdy[1].step(4)
    outs[5].start()
    gx.step(2)
    kv[1].step(3)
    outs[2].start()
    attend(1, 0, 4)
    gx.step(3)
    attend(1, 4, 8)
    finish(1)
    send_gates()
    gdy[0].step(4)
    outs[4].start()
    take_gates()
    gx.step(4)
    outs[6].start()
    for copy in outs:
        copy.wait()


def front(tok, cot, wq, wo, small, seg, routes_t, turn):
    vmem = pl.BlockSpec(memory_space=pltpu.VMEM)
    anywhere = pl.BlockSpec(memory_space=pl.ANY)
    return pl.pallas_call(
        front_kernel,
        out_shape=(
            jax.ShapeDtypeStruct((2, 4, 4, 128, 1024), BF),
            jax.ShapeDtypeStruct((4, 4, 128, 1024), BF),
            jax.ShapeDtypeStruct((2, 4, 2, 128, 1024), BF),
            jax.ShapeDtypeStruct((4, 2, 128, 1024), BF),
            jax.ShapeDtypeStruct((2, 4, 2, 8, 128, 128), BF),
            jax.ShapeDtypeStruct((2, 2048, 128), F32),
            jax.ShapeDtypeStruct((64, 1024), F32),
            jax.ShapeDtypeStruct((2, 1024, 128), BF),
            jax.ShapeDtypeStruct((2, 1024, 128), BF),
            jax.ShapeDtypeStruct((2, 8, 1, 256), F32),
            jax.ShapeDtypeStruct((2, 128, 1024), F32),
            jax.ShapeDtypeStruct((2, 128, 1024), BF),
            jax.ShapeDtypeStruct((2, 32, 128), F32),
            jax.ShapeDtypeStruct((16, 8, 128), F32),
        ),
        in_specs=[vmem, vmem, anywhere, anywhere, anywhere, vmem, vmem, anywhere],
        out_specs=(anywhere,) * 6 + (vmem,) * 8,
        scratch_shapes=[
            pltpu.VMEM((2, 4, 4, 128, 1024), BF),
            pltpu.VMEM((4, 4, 128, 1024), BF),
            pltpu.VMEM((2, 4, 2, 128, 1024), BF),
            pltpu.VMEM((4, 2, 128, 1024), BF),
            pltpu.VMEM((2, 4, 2, 8, 128, 128), BF),
            pltpu.VMEM((2, 2048, 128), F32),
            pltpu.VMEM((4, 2, 64, 128), BF),
            pltpu.VMEM((256, 1024), BF),
            pltpu.VMEM((2, 1024, 128), F32),
            pltpu.VMEM((64, 128), F32),
            pltpu.SemaphoreType.DMA((3, 2, 2, 8)),
            pltpu.SemaphoreType.DMA((6, 2, 8)),
            pltpu.VMEM((16, 8, 128), F32),
            pltpu.SemaphoreType.DMA((16,)),
            pltpu.SemaphoreType.DMA((16,)),
            pltpu.SemaphoreType.DMA((12,)),
        ],
        compiler_params=pltpu.CompilerParams(
            collective_id=0, has_side_effects=True, vmem_limit_bytes=56 * MIB
        ),
        cost_estimate=pl.CostEstimate(
            flops=5_000_000_000, bytes_accessed=30_000_000, transcendentals=5_000_000
        ),
    )(tok, cot, wq, wo, small, seg, routes_t, turn)


def moe_kernel(
    ffn_ref, x0_hbm, dy_hbm, g_all, wgu_hbm, wd_hbm,
    out_hbm, dx_ref, h_ref, dw_own,
    dw, x_all, dy_all, r1, r2, r3, r4, xs, ds, os, gc, act, a1, a2, ggu, ranks, hcol, hs,
    wgu, wd, ra, rb, rc, sems, column_sems, hsend, hrecv, free, local,
):
    plane, column = Plane(), Column()
    me, z, x = plane.me, plane.z, plane.x
    own = [
        pltpu.make_async_copy(ffn_ref.at[1], x_all.at[1, z, x], local.at[0]),
        pltpu.make_async_copy(x0_hbm, x_all.at[0], local.at[2]),
        pltpu.make_async_copy(dy_hbm.at[0], dy_all.at[0], local.at[3]),
        pltpu.make_async_copy(wgu_hbm, wgu, local.at[4]),
        pltpu.make_async_copy(wd_hbm, wd, local.at[5]),
        pltpu.make_async_copy(dy_hbm.at[1], dy_all.at[1], local.at[1]),
    ]
    outs = [pltpu.make_async_copy(x_all.at[mb], out_hbm.at[mb], local.at[6 + mb]) for mb in range(2)]
    for copy in own:
        copy.start()
    greet(plane.others() + column.neighbours())
    own[0].wait()

    def h_message(step):
        to = (me + step) % 16
        return pltpu.make_async_remote_copy(
            src_ref=hs.at[to], dst_ref=h_ref.at[me],
            send_sem=hsend.at[step], recv_sem=hrecv.at[step], device_id={"expert": to},
        )

    gx = Gather(plane, x_all.at[1], sems.at[0])

    def into(mb):
        def store(place, rows, total):
            dx_ref[mb, rows] = total

        return store

    sdx = [
        Scatter(plane, dy_all.at[mb], (r1, r2, r3, r4), sems.at[1 + mb], into(mb), free)
        for mb in range(2)
    ]

    def own_part(k):
        def store(r, total):
            dw_own[k, r] = total.astype(BF)

        return store

    dsum = [
        ColumnScatter(
            column, dw.at[k], (ra.at[k], rb.at[k], rc.at[k]), column_sems.at[k], 128, own_part(k)
        )
        for k in range(3)
    ]
    earlier = (
        lax.broadcasted_iota(jnp.int32, (128, 128), 0)
        < lax.broadcasted_iota(jnp.int32, (128, 128), 1)
    ).astype(F32).astype(BF)

    @pl.loop(0, 16)
    def _(s):
        named = g_all[s] > 0.0
        before = nn(named.astype(F32).astype(BF), earlier)
        ranks[s] = jnp.where(named, before, -1.0)

    slot_ids = lax.broadcasted_iota(jnp.int32, (SLOTS, 128), 0).astype(F32)

    def places(p, mb):
        ranked = [ranks[2 * p + k] for k in range(2)]
        return [
            [(slot_ids == ranked[k][2 * mb + e : 2 * mb + e + 1]).astype(F32) for k in range(2)]
            for e in range(2)
        ]

    def gated(p, mb, hot):
        gates = [g_all[2 * p + k] for k in range(2)]
        return [
            [hot[e][k] * gates[k][2 * mb + e : 2 * mb + e + 1] for k in range(2)] for e in range(2)
        ]

    def spread(hot):
        blank = jnp.zeros((SLOTS, 128), F32)
        rows = []
        for e in range(2):
            rows.append(jnp.concatenate([hot[e][0], blank], axis=1))
            rows.append(jnp.concatenate([blank, hot[e][1]], axis=1))
        return jnp.concatenate(rows, axis=0).astype(BF)

    def span(p):
        return pl.ds(pl.multiple_of(p * 2 * SLOTS, 32), 2 * SLOTS)

    def pair(p):
        return p // 2, pl.ds(2 * (p % 2), 2)

    def select(mb):
        @pl.loop(0, 8)
        def _(p):
            hot = places(p, mb)
            line, two = pair(p)
            rows = nn(spread(hot), x_all[mb, line, two].reshape(256, 1024)).astype(BF)
            drows = nn(spread(gated(p, mb, hot)), dy_all[mb, line, two].reshape(256, 1024)).astype(BF)
            for e in range(2):
                xs[e, span(p)] = rows[2 * SLOTS * e : 2 * SLOTS * (e + 1)]
                ds[e, span(p)] = drows[2 * SLOTS * e : 2 * SLOTS * (e + 1)]

    chunks = 16 * SLOTS // CHUNK

    def forward(e):
        @pl.loop(0, chunks)
        def _(c):
            r = pl.ds(pl.multiple_of(c * CHUNK, CHUNK), CHUNK)
            gu = nn(xs[e, r], wgu[e])
            g, u = gu[:, :512], gu[:, 512:]
            sig = 1.0 / (1.0 + jnp.exp(-g))
            silu = g * sig
            active = (silu * u).astype(BF)
            act[e, r] = active
            a1[e, r] = (u * sig * (1.0 + g * (1.0 - sig))).astype(BF)
            a2[e, r] = silu.astype(BF)
            o = nn(active, wd[e]).astype(BF)
            os[e, r] = o
            hcol[e, r] = jnp.sum(o.astype(F32) * ds[e, r].astype(F32), axis=-1, keepdims=True)

    def combine_out(mb):
        @pl.loop(0, 8)
        def _(p):
            hot = places(p, mb)
            line, two = pair(p)
            both = jnp.concatenate([os[0, span(p)], os[1, span(p)]], axis=0)
            got = tn(spread(gated(p, mb, hot)), both).astype(BF)
            x_all[mb, line, two] = got.reshape(2, 128, 1024)
            for e in range(2):
                column_of = hcol[e, span(p)]
                for k in range(2):
                    row = 2 * mb + e
                    part = hot[e][k] * column_of[SLOTS * k : SLOTS * (k + 1)]
                    hs[2 * p + k, row : row + 1] = jnp.sum(part, axis=0, keepdims=True)

    def add_part(mb, k, n, fresh):
        fresh = fresh.reshape(2, 128, 1024)
        if mb == 1:
            fresh += dw[k, n].astype(F32)
        dw[k, n] = fresh.astype(BF)

    def backward(mb, e):
        @pl.loop(0, chunks)
        def _(c):
            r = pl.ds(pl.multiple_of(c * CHUNK, CHUNK), CHUNK)
            ga = nt(ds[e, r], wd[e])
            grad = jnp.concatenate(
                [ga * a1[e, r].astype(F32), ga * a2[e, r].astype(F32)], axis=1
            ).astype(BF)
            ggu[r] = grad
            gc[e, r] = nt(grad, wgu[e]).astype(BF)

        @pl.loop(0, 4)
        def _(m):
            cols = pl.ds(pl.multiple_of(m * 256, 256), 256)
            add_part(mb, e, m, tn(xs[e, :, cols], ggu[...]))

        @pl.loop(0, 2)
        def _(m):
            cols = pl.ds(pl.multiple_of(m * 256, 256), 256)
            add_part(mb, 2, 2 * e + m, tn(act[e, :, cols], ds[e]))

    def combine_dx(mb):
        @pl.loop(0, 8)
        def _(p):
            line, two = pair(p)
            both = jnp.concatenate([gc[0, span(p)], gc[1, span(p)]], axis=0)
            got = tn(spread(places(p, mb)), both).astype(BF)
            dy_all[mb, line, two] = got.reshape(2, 128, 1024)

    gx.step(0)
    own[1].wait()
    own[2].wait()
    select(0)
    gx.step(1)
    own[3].wait()
    own[4].wait()
    forward(0)
    gx.step(2)
    forward(1)
    combine_out(0)
    outs[0].start()
    backward(0, 0)
    gx.step(3)
    backward(0, 1)
    combine_dx(0)
    sdx[0].step(0)
    gx.step(4)
    own[5].wait()
    select(1)
    forward(1)
    sdx[0].step(1)
    forward(0)
    backward(1, 0)
    dsum[0].step(0)
    sdx[0].step(2)
    backward(1, 1)
    sdx[0].step(3)
    dsum[1].step(0)
    dsum[2].step(0)
    dsum[0].step(1)
    combine_dx(1)
    sdx[0].step(4)
    sdx[0].give_credit()
    sdx[1].take_credit()
    sdx[1].step(0)
    dsum[2].step(1)
    combine_out(1)
    outs[1].start()
    dsum[1].step(1)
    sdx[1].step(1)
    dsum[0].step(2)
    dsum[1].step(2)
    dsum[2].step(2)
    sdx[1].step(2)
    h_ref[me] = hs[me]
    for step in range(1, 16):
        h_message(step).start()
    sdx[1].step(3)
    dsum[0].step(3)
    dsum[2].step(3)
    dsum[1].step(3)
    sdx[1].step(4)
    for step in range(1, 16):
        h_message(step).wait_recv()
    for step in range(1, 16):
        h_message(step).wait_send()
    for copy in outs:
        copy.wait()


def moe(ffn, x0, dy, gates, w_gate_up, w_down):
    vmem = pl.BlockSpec(memory_space=pltpu.VMEM)
    anywhere = pl.BlockSpec(memory_space=pl.ANY)
    rows = 16 * SLOTS
    return pl.pallas_call(
        moe_kernel,
        out_shape=(
            jax.ShapeDtypeStruct((2, 4, 4, 128, 1024), BF),
            jax.ShapeDtypeStruct((2, 128, 1024), F32),
            jax.ShapeDtypeStruct((16, 8, 128), F32),
            jax.ShapeDtypeStruct((3, 128, 1024), BF),
        ),
        in_specs=[anywhere, anywhere, anywhere, vmem, anywhere, anywhere],
        out_specs=(anywhere,) + (vmem,) * 3,
        scratch_shapes=[
            pltpu.VMEM((3, 4, 2, 128, 1024), BF),
            pltpu.VMEM((2, 4, 4, 128, 1024), BF),
            pltpu.VMEM((2, 4, 4, 128, 1024), BF),
            *scatter_slots(128, 1024),
            pltpu.VMEM((2, rows, 1024), BF),
            pltpu.VMEM((2, rows, 1024), BF),
            pltpu.VMEM((2, rows, 1024), BF),
            pltpu.VMEM((2, rows, 1024), BF),
            pltpu.VMEM((2, rows, 512), BF),
            pltpu.VMEM((2, rows, 512), BF),
            pltpu.VMEM((2, rows, 512), BF),
            pltpu.VMEM((rows, 1024), BF),
            pltpu.VMEM((16, 8, 128), F32),
            pltpu.VMEM((2, rows, 1), F32),
            pltpu.VMEM((16, 8, 128), F32),
            pltpu.VMEM((2, 1024, 1024), BF),
            pltpu.VMEM((2, 512, 1024), BF),
            *column_slots((128, 1024), lead=(3,)),
            pltpu.SemaphoreType.DMA((3, 2, 2, 8)),
            pltpu.SemaphoreType.DMA((3, 2, 8)),
            pltpu.SemaphoreType.DMA((16,)),
            pltpu.SemaphoreType.DMA((16,)),
            pltpu.SemaphoreType.REGULAR,
            pltpu.SemaphoreType.DMA((8,)),
        ],
        compiler_params=pltpu.CompilerParams(
            collective_id=1, has_side_effects=True, vmem_limit_bytes=63 * MIB
        ),
        cost_estimate=pl.CostEstimate(
            flops=30_000_000_000, bytes_accessed=30_000_000, transcendentals=2_000_000
        ),
    )(ffn, x0, dy, gates, w_gate_up, w_down)


def norm_grad(grad, v, inverse, gain, axis):
    scaled = grad * gain
    moment = jnp.mean(scaled * v, axis=axis, keepdims=True)
    return inverse * (scaled - v * (inverse * inverse * moment)), grad * (v * inverse)


def back_kernel(
    tok, cot, seg_ref, turn_hbm, wq_hbm, wo_hbm, small_t, raw_hbm, q_t, kv_hbm, mix_t, lsum,
    res, ffn, gates_t, share_ref, dx, out_hbm, dw_own,
    dgu_all, dd_all, output, in_grad, gq, go, gs,
    wq_all, wo_all, kv_all, raw_t, turn, bias, gres, branch, gm_t, dq_t, own_kv, gp, normed_t, gn,
    part_kv, part_w, part_s, q_sum, k_sum, ra, rb, rc, sa, sb, sc, plane_buf, plane_all, p1, p2, p3, p4, ta, tb, tc,
    logits, routers, router_sum, out_part, r1, r2, r3, r4, parcels, got_parcels, small_own, kv_total,
    column_sems, plane_sems, far_send, far_recv, all_send, all_recv, free, local, gain_sums,
):
    plane, column = Plane(), Column()
    y, c = column.y, column.c
    copies = [
        pltpu.make_async_copy(wo_hbm, wo_all, local.at[0]),
        pltpu.make_async_copy(kv_hbm, kv_all, local.at[1]),
        pltpu.make_async_copy(raw_hbm, raw_t, local.at[2]),
        pltpu.make_async_copy(wq_hbm, wq_all, local.at[3]),
        pltpu.make_async_copy(turn_hbm.at[column.me], turn, local.at[4]),
    ]
    parts = [pltpu.make_async_copy(out_hbm.at[mb], out_part, local.at[5 + mb]) for mb in range(2)]
    dw_refs = [dgu_all.at[0], dgu_all.at[1], dd_all]
    owns = [pltpu.make_async_copy(dw_own.at[n], dw_refs[n].at[y, c], local.at[7 + n]) for n in range(3)]
    for copy in parts[:1] + owns + copies:
        copy.start()
    greet(plane.others() + column.neighbours())
    dall = [ColumnGather(column, dw_refs[n], column_sems.at[8 + n], 128, dw_own.at[n]) for n in range(3)]

    def add_residual(mb):
        def store(place, rows, total):
            output[mb, rows] = (res[mb, rows] + total).astype(BF)

        return store

    sout = [
        Scatter(plane, out_part, (r1, r2, r3, r4), plane_sems.at[mb], add_residual(mb), free)
        for mb in range(2)
    ]
    part_s[...] = jnp.zeros_like(part_s)
    q_sum[...] = jnp.zeros_like(q_sum)
    k_sum[...] = jnp.zeros_like(k_sum)
    for mb in range(2):
        document_bias(seg_ref, bias, mb, column.me)

    def place_w(which):
        def store(r, total):
            low = total.astype(BF)
            half = r.start // 64
            some = pl.ds(pl.multiple_of(r.start % 64, 16), 16)
            for k in range(8):
                n = half * 8 + k
                piece = low[:, 128 * k : 128 * (k + 1)]
                if which == 2:
                    parcels[n, some] = piece
                else:
                    plane_buf[n // 4, n % 4, some, 128 * which : 128 * (which + 1)] = piece

        return store

    def place_s(r, total):
        small_own[r] = total.astype(BF)

    def place_kv(mb, half):
        def store(r, total):
            own_kv[mb, pl.ds(r.start + 4 * half, 1)] = total

        return store

    w_sums = [
        ColumnScatter(
            column, part_w.at[n], (ra.at[n], rb.at[n], rc.at[n]), column_sems.at[n], 128, place_w(n)
        )
        for n in range(3)
    ]
    kv_sums = [
        [
            ColumnScatter(
                column, part_kv.at[mb, half],
                (sa.at[mb, half], sb.at[mb, half], sc.at[mb, half]),
                column_sems.at[4 + 2 * mb + half], 4, place_kv(mb, half), group=1,
            )
            for half in range(2)
        ]
        for mb in range(2)
    ]
    s_sum = ColumnScatter(column, part_s, (ta, tb, tc), column_sems.at[3], 64, place_s)

    def keep(place, rows, total):
        plane_all[place] = total.astype(BF)

    over = Scatter(plane, plane_buf, (p1, p2, p3, p4), plane_sems.at[2], keep, height=64)
    spread = Gather(plane, plane_all, plane_sems.at[3], height=64)

    def tokens_of(mb):
        return pl.ds(128 * mb, 128)

    router = small_t[:32].astype(BF)
    ffn_gain, attn_gain = small_t[33:34], small_t[32:33]
    routers[0:32] = router
    routers[32:64] = router
    def router_and_norm():
        ffn_gain_grad = jnp.zeros((1, 1024), F32)
        for mb in range(2):
            share = jnp.concatenate([share_ref[k, 2 * mb : 2 * mb + 2] for k in range(16)], axis=0)
            logit = share - gates_t[mb] * jnp.sum(share, axis=0, keepdims=True)
            high = logit.astype(BF)
            logits[0:32, tokens_of(mb)] = high
            logits[32:64, tokens_of(mb)] = (logit - high.astype(F32)).astype(BF)

        @pl.loop(0, 4)
        def _(n):
            cols = pl.ds(pl.multiple_of(n * 256, 256), 256)
            gn[:, cols] = tn(logits[...], routers[:, cols])
            router_sum[:, cols] = nn(logits[...], ffn[:, :, cols].reshape(256, 256))

        for mb in range(2):
            into = dx[mb] + gn[tokens_of(mb)]
            v = res[mb]
            inv = inverse_rms(v, 1)
            grad, gain = norm_grad(into, v, inv, ffn_gain, 1)
            ffn_gain_grad += jnp.sum(gain, axis=0, keepdims=True)
            total = cot[mb].astype(F32) + grad
            gres[mb] = total
            branch[128 * mb : 128 * (mb + 1)] = total.astype(BF)
        gain_sums[1:2] = ffn_gain_grad

    def out_projection():
        copies[0].wait()

        @pl.loop(0, 4)
        def _(n):
            rows = pl.ds(pl.multiple_of(n * 256, 256), 256)
            got = nt(wo_all[n].reshape(256, 1024), branch[...])
            gm_t[0, rows] = got[:, :128].astype(BF)
            gm_t[1, rows] = got[:, 128:].astype(BF)
            mixed = jnp.concatenate([mix_t[0, rows], mix_t[1, rows]], axis=1)
            part_w[0, n] = nn(mixed, branch[...]).astype(BF).reshape(2, 128, 1024)

    def attend(mb, start, stop):
        @pl.loop(start, stop)
        def _(g):
            query = pair_columns(q_t, mb, g)
            grad = pair_columns(gm_t, mb, g)
            mixed = pair_columns(mix_t, mb, g)
            blank = jnp.zeros_like(query)
            inner = jnp.sum(grad.astype(F32) * mixed.astype(F32), axis=0, keepdims=True)
            query = jnp.concatenate([query, blank], axis=0)
            grad = jnp.concatenate([blank, grad], axis=0)
            both = jnp.concatenate([query, grad], axis=1)
            scale = 1.0 / lsum[mb, g]
            dq = jnp.zeros((128, 256), F32)
            for j in range(4):
                keys = kv_all[mb, j, :, g].reshape(256, 128)
                there = bias[mb, 256 * j : 256 * (j + 1)].astype(F32)
                got = nn(keys, both)
                p = jnp.exp(got[:, :256] + jnp.concatenate([there, there], axis=1)) * scale
                ds = (p * (got[:, 256:] - inner)).astype(BF)
                dq += tn(keys, ds)
                dkv = nt(jnp.concatenate([ds, p.astype(BF)], axis=1), both)
                part_kv[mb, g // 4, j, :, g % 4] = dkv.astype(BF).reshape(2, 128, 128)
            dq = dq[:64] * HD ** (-0.5)
            rows = pl.ds(pl.multiple_of(g * 128, 128), 128)
            dq_t[mb, rows] = jnp.concatenate([dq[:, :128], dq[:, 128:]], axis=0)

    copies[4].wait()
    cosine, sine = turn[:32], turn[32:]
    query_gain = head_gain(small_t[...], 34)
    key_gain = head_gain(small_t[...], 35)

    def head_back(grad, v, gain, total):
        inv = inverse_rms(v, 0)
        grad = turned(grad, cosine, -sine)
        grad_v, gain_part = norm_grad(grad, v, inv, gain, 0)
        total[...] += gain_part
        return grad_v

    def queries_back(mb):
        @pl.loop(0, 8)
        def _(g):
            pieces = []
            for r in range(2):
                rows = pl.ds(pl.multiple_of(g * 128 + r * 64, 64), 64)
                pieces.append(head_back(dq_t[mb, rows], raw_t[mb, rows], query_gain, q_sum))
            cols = pl.ds(pl.multiple_of(g * 128, 128), 128)
            gp[tokens_of(mb), cols] = jnp.concatenate(pieces, axis=0).T.astype(BF)

    def turn_normed():
        for mb in range(2):
            v = tok[mb].astype(F32)
            normed = (v * inverse_rms(v, 1) * attn_gain).astype(BF).astype(F32)
            for k in range(8):
                normed_t[128 * k : 128 * (k + 1), tokens_of(mb)] = (
                    normed[:, 128 * k : 128 * (k + 1)].T.astype(BF)
                )

    def weight_part(which):
        cols = pl.ds(1024 * (which - 1), 1024)

        @pl.loop(0, 4)
        def _(n):
            rows = pl.ds(pl.multiple_of(n * 256, 256), 256)
            part_w[which, n] = nn(normed_t[rows], gp[:, cols]).astype(BF).reshape(2, 128, 1024)

    def keys_back(mb):
        @pl.loop(0, 4)
        def _(k):
            keys, values = [], []
            for r in range(2):
                g = 2 * k + r
                grad = own_kv[mb, g].T
                rows = pl.ds(pl.multiple_of(1024 + g * 64, 64), 64)
                keys.append(head_back(grad[:64], raw_t[mb, rows], key_gain, k_sum))
                values.append(grad[64:])
            cols = pl.ds(pl.multiple_of(1024 + k * 128, 128), 128)
            gp[tokens_of(mb), cols] = jnp.concatenate(keys, axis=0).T.astype(BF)
            cols = pl.ds(pl.multiple_of(1536 + k * 128, 128), 128)
            gp[tokens_of(mb), cols] = jnp.concatenate(values, axis=0).T.astype(BF)

    def normed_grad(k):
        @pl.loop(0, 4)
        def _(n):
            cols = pl.ds(pl.multiple_of(n * 256, 256), 256)
            got = nt(gp[:, 1024 * k : 1024 * (k + 1)], wq_all[k, n].reshape(256, 1024))
            gn[:, cols] = got if k == 0 else gn[:, cols] + got

    def finish():
        attn_gain_grad = jnp.zeros((1, 1024), F32)
        for mb in range(2):
            v = tok[mb].astype(F32)
            grad, gain = norm_grad(gn[tokens_of(mb)], v, inverse_rms(v, 1), attn_gain, 1)
            attn_gain_grad += jnp.sum(gain, axis=0, keepdims=True)
            in_grad[mb] = (gres[mb] + grad).astype(BF)
        for b in range(8):
            cols = slice(128 * b, 128 * (b + 1))
            heads = slice(8 * b, 8 * (b + 1))
            part_s[b // 2, b % 2, 0:32] = router_sum[0:32, cols] + router_sum[32:64, cols]
            part_s[b // 2, b % 2, 32:33] = attn_gain_grad[:, cols]
            part_s[b // 2, b % 2, 33:34] = gain_sums[1:2, cols]
            part_s[b // 2, b % 2, 40:48] = jnp.broadcast_to(
                jnp.sum(q_sum[heads], axis=1, keepdims=True), (8, 128)
            )
            part_s[b // 2, b % 2, 48:56] = jnp.broadcast_to(
                jnp.sum(k_sum[heads], axis=1, keepdims=True), (8, 128)
            )

    me = plane.me

    def parcel(step):
        to = (me + step) % 16
        return send(
            parcels.at[to], got_parcels.at[me], far_send.at[step], far_recv.at[step], {"expert": to}
        )

    def total_message(step):
        to = (me + step) % 16
        return send(
            kv_total.at[me], kv_total.at[me], all_send.at[step], all_recv.at[step], {"expert": to}
        )

    def send_parcels():
        @pl.loop(0, 16)
        def _(n):
            parcels[n, 64:128] = small_own[...]

        for step in range(1, 16):
            parcel(step).start()
        got_parcels[me] = parcels[me]

    def add_parcels():
        for step in range(1, 16):
            parcel(step).wait_recv()
        total = got_parcels[0].astype(F32)
        for n in range(1, 16):
            total += got_parcels[n].astype(F32)
        kv_total[me] = total[:64].astype(BF)
        for step in range(1, 16):
            total_message(step).start()
        gs[...] = total[64:]

    def write_out(k):
        for n in range(16):
            rows = slice(64 * (n // 8), 64 * (n // 8) + 64)
            cols = slice(128 * (n % 8), 128 * (n % 8) + 128)
            (go, gq)[k][rows, cols] = plane_all[n // 4, n % 4, :, 128 * k : 128 * (k + 1)].astype(F32)

    def take_totals():
        for step in range(1, 16):
            total_message(step).wait_recv()
        for n in range(16):
            first = 1024 + 128 * (n % 8)
            gq[64 * (n // 8) : 64 * (n // 8) + 64, first : first + 128] = kv_total[n].astype(F32)

    dall[2].step(0)
    router_and_norm()
    parts[0].wait()
    sout[0].step(0)
    dall[0].step(0)
    out_projection()
    dall[1].step(0)
    copies[1].wait()
    attend(1, 0, 2)
    attend(1, 2, 4)
    attend(0, 0, 2)
    kv_sums[1][0].step(0)
    w_sums[0].step(0)
    sout[0].step(1)
    attend(1, 4, 6)
    attend(1, 6, 8)
    dall[0].step(1)
    kv_sums[1][0].step(1)
    kv_sums[1][1].step(0)
    attend(0, 2, 4)
    w_sums[0].step(1)
    attend(0, 4, 6)
    dall[2].step(1)
    kv_sums[1][1].step(1)
    sout[0].step(2)
    w_sums[0].step(2)
    attend(0, 6, 8)
    sout[0].step(3)
    kv_sums[0][1].step(0)
    kv_sums[0][0].step(0)
    kv_sums[1][1].step(2)
    turn_normed()
    copies[2].wait()
    queries_back(1)
    queries_back(0)
    kv_sums[1][0].step(2)
    kv_sums[0][1].step(1)
    weight_part(1)
    copies[3].wait()
    normed_grad(0)
    sout[0].step(4)
    parts[1].start()
    sout[0].give_credit()
    w_sums[1].step(0)
    kv_sums[0][0].step(1)
    kv_sums[0][1].step(2)
    parts[1].wait()
    sout[1].take_credit()
    sout[1].step(0)
    dall[0].step(2)
    w_sums[1].step(1)
    kv_sums[1][1].step(3)
    kv_sums[0][1].step(3)
    kv_sums[0][0].step(2)
    w_sums[1].step(2)
    sout[1].step(1)
    kv_sums[0][0].step(3)
    kv_sums[1][0].step(3)
    keys_back(0)
    dall[2].step(2)
    keys_back(1)
    dall[1].step(1)
    weight_part(2)
    w_sums[2].step(0)
    w_sums[0].step(3)
    normed_grad(1)
    w_sums[1].step(3)
    over.step(0)
    finish()
    dall[0].step(3)
    dall[1].step(2)
    s_sum.step(0)
    w_sums[2].step(1)
    over.step(1)
    dall[2].step(3)
    sout[1].step(2)
    s_sum.step(1)
    w_sums[2].step(2)
    over.step(2)
    over.step(3)
    s_sum.step(2)
    sout[1].step(3)
    dall[1].step(3)
    over.step(4)
    s_sum.step(3)
    spread.step(0)
    w_sums[2].step(3)
    send_parcels()
    spread.step(1)
    spread.step(2)
    sout[1].step(4)
    add_parcels()
    spread.step(3)
    spread.step(4)
    write_out(0)
    write_out(1)
    take_totals()
    for step in range(1, 16):
        parcel(step).wait_send()
        total_message(step).wait_send()
    for copy in owns:
        copy.wait()


def back(tok, cot, seg, turn, wq_all, wo_all, small_t, raw_t, q_t, kv_all, mix_t, lsum, res, ffn, gates_t, share, dx, out_part, dw_own):
    vmem = pl.BlockSpec(memory_space=pltpu.VMEM)
    anywhere = pl.BlockSpec(memory_space=pl.ANY)
    kv_slots = column_slots((4, 128, 128), lead=(2, 2))
    return pl.pallas_call(
        back_kernel,
        out_shape=(
            jax.ShapeDtypeStruct((2, 4, 2, 128, 1024), BF),
            jax.ShapeDtypeStruct((4, 2, 128, 1024), BF),
            jax.ShapeDtypeStruct((2, 128, 1024), BF),
            jax.ShapeDtypeStruct((2, 128, 1024), BF),
            jax.ShapeDtypeStruct((128, 2048), F32),
            jax.ShapeDtypeStruct((128, 1024), F32),
            jax.ShapeDtypeStruct((64, 128), F32),
        ),
        in_specs=[
            vmem, vmem, vmem, anywhere, anywhere, anywhere, vmem, anywhere, vmem, anywhere,
            vmem, vmem, vmem, vmem, vmem, vmem, vmem, anywhere, vmem,
        ],
        out_specs=(anywhere,) * 2 + (vmem,) * 5,
        scratch_shapes=[
            pltpu.VMEM((2, 4, 2, 128, 1024), BF),
            pltpu.VMEM((4, 2, 128, 1024), BF),
            pltpu.VMEM((2, 4, 2, 8, 128, 128), BF),
            pltpu.VMEM((2, 2048, 128), F32),
            pltpu.VMEM((64, 128), F32),
            pltpu.VMEM((2, 1024, 128), BF),
            pltpu.VMEM((2, 128, 1024), F32),
            pltpu.VMEM((256, 1024), BF),
            pltpu.VMEM((2, 1024, 128), BF),
            pltpu.VMEM((2, 1024, 128), F32),
            pltpu.VMEM((2, 8, 128, 128), F32),
            pltpu.VMEM((256, 2048), BF),
            pltpu.VMEM((1024, 256), BF),
            pltpu.VMEM((256, 1024), F32),
            pltpu.VMEM((2, 2, 4, 2, 4, 128, 128), BF),
            pltpu.VMEM((3, 4, 2, 128, 1024), BF),
            pltpu.VMEM((4, 2, 64, 128), F32),
            pltpu.VMEM((64, 128), F32),
            pltpu.VMEM((64, 128), F32),
            *column_slots((128, 1024), lead=(3,)),
            *kv_slots,
            pltpu.VMEM((4, 4, 64, 256), BF),
            pltpu.VMEM((4, 4, 64, 256), BF),
            *scatter_slots(64, 256),
            *column_slots((64, 128), F32),
            pltpu.VMEM((64, 256), BF),
            pltpu.VMEM((64, 1024), BF),
            pltpu.VMEM((64, 1024), F32),
            pltpu.VMEM((4, 4, 128, 1024), BF),
            *scatter_slots(128, 1024),
            pltpu.VMEM((16, 128, 128), BF),
            pltpu.VMEM((16, 128, 128), BF),
            pltpu.VMEM((64, 128), BF),
            pltpu.VMEM((16, 64, 128), BF),
            pltpu.SemaphoreType.DMA((11, 2, 8)),
            pltpu.SemaphoreType.DMA((4, 2, 2, 8)),
            pltpu.SemaphoreType.DMA((16,)),
            pltpu.SemaphoreType.DMA((16,)),
            pltpu.SemaphoreType.DMA((16,)),
            pltpu.SemaphoreType.DMA((16,)),
            pltpu.SemaphoreType.REGULAR,
            pltpu.SemaphoreType.DMA((10,)),
            pltpu.VMEM((8, 1024), F32),
        ],
        compiler_params=pltpu.CompilerParams(
            collective_id=2, has_side_effects=True, vmem_limit_bytes=63 * MIB
        ),
        cost_estimate=pl.CostEstimate(
            flops=12_000_000_000, bytes_accessed=30_000_000, transcendentals=5_000_000
        ),
    )(tok, cot, seg, turn, wq_all, wo_all, small_t, raw_t, q_t, kv_all, mix_t, lsum, res, ffn, gates_t, share, dx, out_part, dw_own)


def last_kernel(
    dgu_ref, dd_ref, out_ref, in_ref, gq_ref, go_ref, gs_ref,
    dgu_f, dd_f, out_f, in_f, gq_f, go_f, attn_f, ffn_f, q_f, k_f, router_f,
):
    dgu_f[...] = dgu_ref[...].astype(F32)
    dd_f[...] = dd_ref[...].astype(F32)
    out_f[...] = out_ref[...]
    in_f[...] = in_ref[...]
    gq_f[...] = gq_ref[...]
    go_f[...] = go_ref[...]
    attn_f[...] = gs_ref[32:33]
    ffn_f[...] = gs_ref[33:34]
    q_f[...] = gs_ref[40:48].T[0:1]
    k_f[...] = gs_ref[48:56].T[0:1]
    router_f[...] = gs_ref[0:32]


def last(dgu, dd, output, in_grad, gq, go, gs):
    def rows(count, width):
        return pl.BlockSpec((count, width), lambda n: (n, 0))

    def whole(*shape):
        return pl.BlockSpec(shape, lambda n: (0, 0))

    return pl.pallas_call(
        last_kernel,
        grid=(8,),
        out_shape=(
            jax.ShapeDtypeStruct((2048, 1024), F32),
            jax.ShapeDtypeStruct((1024, 1024), F32),
            jax.ShapeDtypeStruct((256, 1024), BF),
            jax.ShapeDtypeStruct((256, 1024), BF),
            jax.ShapeDtypeStruct((128, 2048), F32),
            jax.ShapeDtypeStruct((128, 1024), F32),
            jax.ShapeDtypeStruct((1, 128), F32),
            jax.ShapeDtypeStruct((1, 128), F32),
            jax.ShapeDtypeStruct((1, 8), F32),
            jax.ShapeDtypeStruct((1, 8), F32),
            jax.ShapeDtypeStruct((32, 128), F32),
        ),
        in_specs=[
            rows(256, 1024), rows(128, 1024), rows(32, 1024), rows(32, 1024), rows(16, 2048),
            rows(16, 1024), whole(64, 128),
        ],
        out_specs=(
            rows(256, 1024), rows(128, 1024), rows(32, 1024), rows(32, 1024), rows(16, 2048),
            rows(16, 1024), whole(1, 128), whole(1, 128), whole(1, 8), whole(1, 8), whole(32, 128),
        ),
        cost_estimate=pl.CostEstimate(flops=0, bytes_accessed=24_000_000, transcendentals=0),
    )(
        dgu.reshape(2048, 1024), dd.reshape(1024, 1024), output.reshape(256, 1024),
        in_grad.reshape(256, 1024), gq, go, gs,
    )


def turn_table(length):
    frequency = np.power(np.float32(THETA), -2.0 * np.arange(HD // 2, dtype=np.float32) / HD)
    angle = np.arange(length, dtype=np.float32)[:, None] * frequency.astype(np.float32)[None, :]
    both = np.concatenate([np.cos(angle), np.sin(angle)], axis=1).astype(np.float32)
    return both.reshape(length // 128, 128, HD).transpose(0, 2, 1)


def body(
    tokens,
    cotangent,
    segments,
    routes,
    w_qkv,
    w_out,
    attn_norm,
    ffn_norm,
    q_gain,
    k_gain,
    router,
    w_gate_up,
    w_down,
):
    tok = tokens.reshape(2, 128, 1024)
    cot = cotangent.reshape(2, 128, 1024)
    seg = segments.reshape(2, 8, 1, 128)
    routes_t = routes.reshape(2, 128, 8).transpose(0, 2, 1)
    turn = jnp.asarray(turn_table(1024))
    gains = jnp.pad(jnp.stack([q_gain, k_gain]), ((0, 28), (0, 120)))
    small = jnp.concatenate([router.T, attn_norm[None], ffn_norm[None], gains])
    (
        dy_all, x0, wq_all, wo_all, kv_all, raw_t, small_t, q_t, mix_t, lsum, res, ffn, gates_t, sent
    ) = front(tok, cot, w_qkv, w_out, small, seg, routes_t, turn)
    out_part, moved_dx, share, dw_own = moe(ffn, x0, dy_all, sent, w_gate_up, w_down)
    dgu, dd, output, in_grad, gq, go, gs = back(
        tok, cot, seg, turn, wq_all, wo_all, small_t, raw_t, q_t, kv_all, mix_t, lsum, res, ffn,
        gates_t, share, moved_dx, out_part, dw_own,
    )
    dgu, dd, output, in_grad, gq, go, attn, ffn_gain, q_grad, k_grad, router_grad = last(
        dgu, dd, output, in_grad, gq, go, gs
    )
    return (
        output.reshape(tokens.shape),
        in_grad.reshape(tokens.shape),
        gq,
        go,
        attn.reshape(128),
        ffn_gain.reshape(128),
        q_grad.reshape(8),
        k_grad.reshape(8),
        router_grad.T,
        dgu.reshape(2, 1024, 1024),
        dd.reshape(2, 512, 1024),
    )


def solution(mesh):
    return jax.shard_map(
        body,
        mesh=mesh,
        in_specs=(
            P(None, "expert", "dp", None),
            P(None, "expert", "dp", None),
            P(None, "expert", None),
            P(None, "expert", "dp", None),
            P("dp", None),
            P("dp", None),
            P("dp"),
            P("dp"),
            P("dp"),
            P("dp"),
            P("dp", None),
            P("expert", None, None),
            P("expert", None, None),
        ),
        out_specs=(
            P(None, "expert", "dp", None),
            P(None, "expert", "dp", None),
            P("dp", None),
            P("dp", None),
            P("dp"),
            P("dp"),
            P("dp"),
            P("dp"),
            P("dp", None),
            P("expert", None, None),
            P("expert", None, None),
        ),
        check_vma=False,
    )
```

```python
import jax
import jax.numpy as jnp
import numpy as np
from jax import lax
from jax.experimental import pallas as pl
from jax.experimental.pallas import tpu as pltpu
from jax.sharding import PartitionSpec as P

HD = 64
EPSILON = 1e-06
THETA = 10000.0
MASKED = -1e30

BF = jnp.bfloat16
F32 = jnp.float32
SLOTS = 48
CHUNK = 256
MIB = 1024 * 1024


def nn(a, b):
    return lax.dot_general(a, b, (((1,), (0,)), ((), ())), preferred_element_type=F32)


def nt(a, b):
    return lax.dot_general(a, b, (((1,), (1,)), ((), ())), preferred_element_type=F32)


def tn(a, b):
    return lax.dot_general(a, b, (((0,), (0,)), ((), ())), preferred_element_type=F32)


def send(src, dst, send_sem, recv_sem, device):
    return pltpu.make_async_remote_copy(
        src_ref=src, dst_ref=dst, send_sem=send_sem, recv_sem=recv_sem, device_id=device
    )


def next_to(p):
    return (p + 1) % 4, (p + 3) % 4, (p + 2) % 4


def greet(devices):
    sem = pltpu.get_barrier_semaphore()
    for device in devices:
        pl.semaphore_signal(sem, inc=1, device_id=device)
    pl.semaphore_wait(sem, len(devices))


class Plane:
    def __init__(self):
        self.me = lax.axis_index("expert")
        self.z = self.me // 4
        self.x = self.me % 4

    def own(self, half):
        return (self.x, self.z) if half == 0 else (self.z, self.x)

    def device(self, half, p, q):
        return {"expert": q * 4 + p if half == 0 else p * 4 + q}

    def others(self):
        return [{"expert": (self.me + step) % 16} for step in range(1, 16)]

    def neighbours(self):
        zn, zp, _ = next_to(self.z)
        xn, xp, _ = next_to(self.x)
        return [{"expert": k} for k in (zn * 4 + self.x, zp * 4 + self.x, self.z * 4 + xn, self.z * 4 + xp)]


class Column:
    def __init__(self):
        self.me = lax.axis_index("dp")
        self.y = self.me // 2
        self.c = self.me % 2

    def neighbours(self):
        yn, yp, _ = next_to(self.y)
        return [self.to(yn), self.to(yp), self.other()]

    def to(self, y):
        return {"dp": y * 2 + self.c}

    def other(self):
        return {"dp": self.y * 2 + 1 - self.c}


class PlaneStep:
    def at(self, half, p, q, rows):
        return self.ref.at[q, p, rows] if half == 0 else self.ref.at[p, q, rows]

    def line(self, half, q, rows):
        return self.ref.at[q, :, rows] if half == 0 else self.ref.at[:, q, rows]

    def rows(self, half):
        quarter = self.height // 4
        base = 2 * quarter * half
        return pl.ds(base, 2 * quarter), pl.ds(base, quarter), pl.ds(base + quarter, quarter)


class Gather(PlaneStep):
    def __init__(self, plane, ref, sems, height=128):
        self.plane, self.ref, self.sems, self.height = plane, ref, sems, height

    def message(self, half, i):
        p, q = self.plane.own(half)
        pn, pp, _ = next_to(p)
        qn, qp, _ = next_to(q)
        full, first, second = self.rows(half)
        view, to = [
            lambda: (self.at(half, p, q, full), (pn, q)),
            lambda: (self.at(half, p, q, full), (pp, q)),
            lambda: (self.at(half, pp, q, first), (pn, q)),
            lambda: (self.at(half, pn, q, second), (pp, q)),
            lambda: (self.line(half, q, full), (p, qn)),
            lambda: (self.line(half, q, full), (p, qp)),
            lambda: (self.line(half, qp, first), (p, qn)),
            lambda: (self.line(half, qn, second), (p, qp)),
        ][i]()
        sems = self.sems
        return send(view, view, sems.at[0, half, i], sems.at[1, half, i], self.plane.device(half, *to))

    def step(self, n):
        waits, starts = [
            ((), (0, 1)),
            ((0, 1), (2, 3)),
            ((2, 3), (4, 5)),
            ((4, 5), (6, 7)),
            ((6, 7), ()),
        ][n]
        for half in range(2):
            for i in waits:
                self.message(half, i).wait_recv()
            for i in starts:
                self.message(half, i).start()
        if n == 4:
            for half in range(2):
                for i in range(8):
                    self.message(half, i).wait_send()


class Scatter(PlaneStep):
    def __init__(self, plane, ref, slots, sems, store, free=None, height=128):
        self.plane, self.ref, self.slots, self.sems = plane, ref, slots, sems
        self.store, self.free, self.height = store, free, height

    def message(self, half, i):
        p, q = self.plane.own(half)
        pn, pp, po = next_to(p)
        qn, qp, qo = next_to(q)
        full, first, second = self.rows(half)
        r1, r2, r3, r4 = self.slots
        view, slot, to = [
            lambda: (self.line(half, qo, first), r1.at[half, 0], (p, qn)),
            lambda: (self.line(half, qo, second), r1.at[half, 1], (p, qp)),
            lambda: (self.line(half, qn, full), r2.at[half, 0], (p, qn)),
            lambda: (self.line(half, qp, full), r2.at[half, 1], (p, qp)),
            lambda: (self.at(half, po, q, first), r3.at[half, 0], (pn, q)),
            lambda: (self.at(half, po, q, second), r3.at[half, 1], (pp, q)),
            lambda: (self.at(half, pn, q, full), r4.at[half, 0], (pn, q)),
            lambda: (self.at(half, pp, q, full), r4.at[half, 1], (pp, q)),
        ][i]()
        sems = self.sems
        return send(view, slot, sems.at[0, half, i], sems.at[1, half, i], self.plane.device(half, *to))

    def add_line(self, half, q, part, parts, slots):
        quarter = self.height // 4
        offset = quarter * (2 * half + part)
        groups = quarter * parts // 16

        @pl.loop(0, 4 * groups)
        def _(n):
            j, k = n // groups, n % groups
            rows = pl.ds(pl.multiple_of(offset + k * 16, 16), 16)
            some = pl.ds(pl.multiple_of(k * 16, 16), 16)
            place = (q, j, rows) if half == 0 else (j, q, rows)
            total = self.ref[place].astype(F32)
            for ref, side in slots:
                total += ref[half, side, j, some].astype(F32)
            self.ref[place] = total.astype(BF)

    def add_at(self, half, p, q, part, slot):
        quarter = self.height // 4
        ref, side = slot

        @pl.loop(0, quarter // 16)
        def _(k):
            rows = pl.ds(pl.multiple_of(quarter * (2 * half + part) + k * 16, 16), 16)
            place = (q, p, rows) if half == 0 else (p, q, rows)
            got = ref[half, side, pl.ds(pl.multiple_of(k * 16, 16), 16)].astype(F32)
            self.ref[place] = (self.ref[place].astype(F32) + got).astype(BF)

    def step(self, n):
        r1, r2, r3, r4 = self.slots
        for half in range(2):
            p, q = self.plane.own(half)
            pn, pp, po = next_to(p)
            qn, qp, qo = next_to(q)
            if n == 0:
                self.message(half, 0).start()
                self.message(half, 1).start()
            elif n == 1:
                self.message(half, 0).wait_recv()
                self.add_line(half, qn, 0, 1, [(r1, 0)])
                self.message(half, 2).start()
                self.message(half, 1).wait_recv()
                self.add_line(half, qp, 1, 1, [(r1, 1)])
                self.message(half, 3).start()
            elif n == 2:
                self.message(half, 2).wait_recv()
                self.message(half, 3).wait_recv()
                self.add_line(half, q, 0, 2, [(r2, 0), (r2, 1)])
                self.message(half, 4).start()
                self.message(half, 5).start()
            elif n == 3:
                self.message(half, 4).wait_recv()
                self.add_at(half, pn, q, 0, (r3, 0))
                self.message(half, 6).start()
                self.message(half, 5).wait_recv()
                self.add_at(half, pp, q, 1, (r3, 1))
                self.message(half, 7).start()
            elif n == 4:
                self.message(half, 6).wait_recv()
                self.message(half, 7).wait_recv()

                @pl.loop(0, self.height // 32)
                def _(k):
                    rows = pl.ds(pl.multiple_of(self.height // 2 * half + k * 16, 16), 16)
                    place = (q, p, rows) if half == 0 else (p, q, rows)
                    some = pl.ds(pl.multiple_of(k * 16, 16), 16)
                    total = self.ref[place].astype(F32)
                    total += r4[half, 0, some].astype(F32)
                    total += r4[half, 1, some].astype(F32)
                    self.store(place, rows, total)
        if n == 4:
            for half in range(2):
                for i in range(8):
                    self.message(half, i).wait_send()

    def give_credit(self):
        for device in self.plane.neighbours():
            pl.semaphore_signal(self.free, inc=1, device_id=device)

    def take_credit(self):
        pl.semaphore_wait(self.free, 4)


def scatter_slots(height, width, lead=()):
    quarter = height // 4
    return [
        pltpu.VMEM((*lead, 2, 2, 4, quarter, width), BF),
        pltpu.VMEM((*lead, 2, 2, 4, 2 * quarter, width), BF),
        pltpu.VMEM((*lead, 2, 2, quarter, width), BF),
        pltpu.VMEM((*lead, 2, 2, 2 * quarter, width), BF),
    ]


class ColumnGather:
    def __init__(self, column, ref, sems, count, own=None):
        self.column, self.ref, self.sems, self.count = column, ref, sems, count
        self.own = own

    def message(self, i):
        y, c = self.column.y, self.column.c
        yn, yp, yo = next_to(y)
        half = self.count // 2
        ref, column = self.ref, self.column
        view, device = [
            lambda: (ref.at[y, c], column.to(yn)),
            lambda: (ref.at[y, c], column.to(yp)),
            lambda: (ref.at[y, c], column.other()),
            lambda: (ref.at[yp, c, pl.ds(0, half)], column.to(yn)),
            lambda: (ref.at[yn, c, pl.ds(half, half)], column.to(yp)),
            lambda: (ref.at[yp, c], column.other()),
            lambda: (ref.at[yn, c], column.other()),
            lambda: (ref.at[yo, c], column.other()),
        ][i]()
        source = self.own if i < 3 and self.own is not None else view
        return send(source, view, self.sems.at[0, i], self.sems.at[1, i], device)

    def step(self, n):
        order = [
            [("s", 0), ("s", 1), ("s", 2)],
            [("w", 0), ("s", 3), ("s", 5), ("w", 1), ("s", 4), ("s", 6)],
            [("w", 3), ("w", 4), ("s", 7)],
            [("w", 2), ("w", 5), ("w", 6), ("w", 7)],
        ][n]
        for what, i in order:
            if what == "s":
                self.message(i).start()
            else:
                self.message(i).wait_recv()
        if n == 3:
            for i in range(8):
                self.message(i).wait_send()


class ColumnScatter:
    def __init__(self, column, ref, slots, sems, count, store, group=16):
        self.column, self.ref, self.slots, self.sems = column, ref, slots, sems
        self.count, self.store, self.group = count, store, group

    def message(self, i):
        y, c = self.column.y, self.column.c
        yn, yp, yo = next_to(y)
        half = self.count // 2
        ref, column = self.ref, self.column
        ra, rb, rc = self.slots
        view, slot, device = [
            lambda: (ref.at[:, 1 - c], ra, column.other()),
            lambda: (ref.at[yo, c, pl.ds(0, half)], rb.at[0], column.to(yn)),
            lambda: (ref.at[yo, c, pl.ds(half, half)], rb.at[1], column.to(yp)),
            lambda: (ref.at[yn, c], rc.at[0], column.to(yn)),
            lambda: (ref.at[yp, c], rc.at[1], column.to(yp)),
        ][i]()
        return send(view, slot, self.sems.at[0, i], self.sems.at[1, i], device)

    def some(self, k, base=0):
        return pl.ds(pl.multiple_of(base + k * self.group, self.group), self.group)

    def step(self, n):
        y, c = self.column.y, self.column.c
        yn, yp, yo = next_to(y)
        ref, (ra, rb, rc) = self.ref, self.slots
        low = ref.dtype
        half = self.count // 2
        groups = self.count // self.group
        if n == 0:
            self.message(0).start()
        elif n == 1:
            self.message(0).wait_recv()

            @pl.loop(0, 4 * groups)
            def _(k):
                j, r = k // groups, self.some(k % groups)
                ref[j, c, r] = (ref[j, c, r].astype(F32) + ra[j, r].astype(F32)).astype(low)

            self.message(1).start()
            self.message(2).start()
        elif n == 2:
            for side, to in ((0, yn), (1, yp)):
                self.message(1 + side).wait_recv()

                @pl.loop(0, groups // 2)
                def _(k):
                    r = self.some(k, side * half)
                    got = rb[side, self.some(k)].astype(F32)
                    ref[to, c, r] = (ref[to, c, r].astype(F32) + got).astype(low)

                self.message(3 + side).start()
        else:
            self.message(3).wait_recv()
            self.message(4).wait_recv()

            @pl.loop(0, groups)
            def _(k):
                r = self.some(k)
                total = ref[y, c, r].astype(F32) + rc[0, r].astype(F32) + rc[1, r].astype(F32)
                self.store(r, total)

            for i in range(5):
                self.message(i).wait_send()


def column_slots(shape, dtype=BF, lead=()):
    count, rest = shape[0], shape[1:]
    return [
        pltpu.VMEM((*lead, 4, count, *rest), dtype),
        pltpu.VMEM((*lead, 2, count // 2, *rest), dtype),
        pltpu.VMEM((*lead, 2, count, *rest), dtype),
    ]


def turned(v, cosine, sine):
    a, b = v[:32], v[32:]
    return jnp.concatenate([a * cosine - b * sine, b * cosine + a * sine], axis=0)


def inverse_rms(v, axis):
    return lax.rsqrt(jnp.mean(v * v, axis=axis, keepdims=True) + EPSILON)


def head_gain(small_t, row):
    pieces = [small_t[:, 128 * b : 128 * (b + 1)] for b in range(8)]
    tall = jnp.concatenate([piece.T[:8] for piece in pieces], axis=0)
    return jnp.broadcast_to(tall[:, row : row + 1], (64, 128))


def document_bias(seg_ref, bias, mb, mine):
    own = seg_ref[mb, mine].astype(F32)
    for b in range(8):
        keys = jnp.broadcast_to(seg_ref[mb, b].astype(F32), (128, 128)).T
        bias[mb, 128 * b : 128 * (b + 1)] = jnp.where(keys == own, 0.0, MASKED).astype(bias.dtype)


def pair_columns(ref, mb, g):
    both = ref[mb, pl.ds(pl.multiple_of(g * 128, 128), 128)]
    return jnp.concatenate([both[:64], both[64:]], axis=1)


def front_kernel(
    tok, cot, wq, wo, small, seg_ref, routes_ref, turn_hbm,
    dy_out, x0_out, wq_out, wo_out, kv_out, raw_out,
    small_t, q_t, mix_t, lsum, res, ffn, gates_t, g_all,
    dy_all, x0_all, wq_all, wo_all, kv_all, raw_t, small_all, normed, bias, turn, plane_sems, column_sems,
    sent, gsend, grecv, local,
):
    plane, column = Plane(), Column()
    y, c = column.y, column.c
    copies = [
        pltpu.make_async_copy(small, small_all.at[y, c], local.at[0]),
        pltpu.make_async_copy(wq.at[:, 1024:2048], wq_all.at[1, y, c], local.at[1]),
        pltpu.make_async_copy(wq.at[:, 0:1024], wq_all.at[0, y, c], local.at[3]),
        pltpu.make_async_copy(wo, wo_all.at[y, c], local.at[5]),
        pltpu.make_async_copy(turn_hbm.at[column.me], turn, local.at[6]),
    ]
    for copy in copies:
        copy.start()
    outs = [
        pltpu.make_async_copy(wq_all, wq_out, local.at[7]),
        pltpu.make_async_copy(wo_all, wo_out, local.at[8]),
        pltpu.make_async_copy(kv_all, kv_out, local.at[9]),
        pltpu.make_async_copy(raw_t, raw_out, local.at[10]),
        pltpu.make_async_copy(dy_all.at[0], dy_out.at[0], local.at[11]),
        pltpu.make_async_copy(dy_all.at[1], dy_out.at[1], local.at[2]),
        pltpu.make_async_copy(x0_all, x0_out, local.at[4]),
    ]
    for mb in range(2):
        dy_all[mb, plane.z, plane.x] = cot[mb]
    greet(plane.others() + column.neighbours())
    gdy = [Gather(plane, dy_all.at[mb], plane_sems.at[mb]) for mb in range(2)]
    gx = Gather(plane, x0_all, plane_sems.at[2])
    w_small = ColumnGather(column, small_all, column_sems.at[0], 64)
    w_q = ColumnGather(column, wq_all.at[0], column_sems.at[1], 128)
    w_kv = ColumnGather(column, wq_all.at[1], column_sems.at[2], 128)
    w_o = ColumnGather(column, wo_all, column_sems.at[3], 128)
    kv = [ColumnGather(column, kv_all.at[mb], column_sems.at[4 + mb], 8) for mb in range(2)]
    def both_biases():
        for mb in range(2):
            document_bias(seg_ref, bias, mb, column.me)

    def norm_tokens():
        for b in range(8):
            small_t[:, 128 * b : 128 * (b + 1)] = small_all[b // 2, b % 2].astype(F32)
        attn_gain = small_t[32:33]
        for mb in range(2):
            v = tok[mb].astype(F32)
            normed[128 * mb : 128 * (mb + 1)] = (v * inverse_rms(v, 1) * attn_gain).astype(BF)

    def project(k):
        @pl.loop(0, 2)
        def _(n):
            cols = pl.ds(pl.multiple_of(n * 512, 512), 512)
            rows = pl.ds(pl.multiple_of(1024 * k + n * 512, 512), 512)
            got = nn(normed[...], wq_all[k, :, :, :, cols].reshape(1024, 512))
            for mb in range(2):
                raw_t[mb, rows] = got[128 * mb : 128 * (mb + 1)].T

    def key_heads(mb):
        @pl.loop(0, 8)
        def _(g):
            v = raw_t[mb, pl.ds(pl.multiple_of(1024 + g * 64, 64), 64)]
            key = turned(v * inverse_rms(v, 0) * key_gain, cosine, sine)
            value = raw_t[mb, pl.ds(pl.multiple_of(1536 + g * 64, 64), 64)]
            kv_all[mb, y, c, g] = jnp.concatenate([key, value], axis=0).T.astype(BF)

    def query_heads(mb):
        @pl.loop(0, 16)
        def _(h):
            rows = pl.ds(pl.multiple_of(h * 64, 64), 64)
            v = raw_t[mb, rows]
            query = turned(v * inverse_rms(v, 0) * query_gain, cosine, sine)
            q_t[mb, rows] = (query.astype(BF).astype(F32) * HD ** (-0.5)).astype(BF)

    def attend(mb, start, stop):
        @pl.loop(start, stop)
        def _(g):
            query = pair_columns(q_t, mb, g)
            query = jnp.concatenate([query, jnp.zeros_like(query)], axis=0)
            total = jnp.zeros((1, 256), F32)
            mixed = jnp.zeros((128, 256), F32)
            for j in range(4):
                keys = kv_all[mb, j, :, g].reshape(256, 128)
                there = bias[mb, 256 * j : 256 * (j + 1)].astype(F32)
                p = jnp.exp(nn(keys, query) + jnp.concatenate([there, there], axis=1))
                total += jnp.sum(p, axis=0, keepdims=True)
                mixed += tn(keys, p.astype(BF))
            lsum[mb, g] = total
            mixed = (mixed[64:] / total).astype(BF)
            both = jnp.concatenate([mixed[:, :128], mixed[:, 128:]], axis=0)
            mix_t[mb, pl.ds(pl.multiple_of(g * 128, 128), 128)] = both

    def finish(mb):
        @pl.loop(0, 2)
        def _(n):
            cols = pl.ds(pl.multiple_of(n * 512, 512), 512)
            got = tn(mix_t[mb], wo_all[:, :, :, cols].reshape(1024, 512))
            res[mb, :, cols] = tok[mb, :, cols].astype(F32) + got

        v = res[mb]
        low = (v * inverse_rms(v, 1) * small_t[33:34]).astype(BF)
        ffn[mb] = low
        logits = nt(small_t[:32].astype(BF), low)
        ids = lax.broadcasted_iota(jnp.int32, (32, 128), 0)
        routed = ids == routes_ref[mb, 0:1]
        for k in range(1, 8):
            routed = routed | (ids == routes_ref[mb, k : k + 1])
        top = jnp.max(jnp.where(routed, logits, MASKED), axis=0, keepdims=True)
        weight = jnp.where(routed, jnp.exp(logits - top), 0.0)
        gates = weight / jnp.sum(weight, axis=0, keepdims=True)
        gates_t[mb] = gates
        for k in range(16):
            sent[k, 2 * mb : 2 * mb + 2] = gates[2 * k : 2 * k + 2]

    def gate_message(step):
        to = (plane.me + step) % 16
        return send(
            sent.at[to], g_all.at[plane.me], gsend.at[step], grecv.at[step], {"expert": to}
        )

    def send_gates():
        for step in range(1, 16):
            gate_message(step).start()
        g_all[plane.me] = sent[plane.me]

    def take_gates():
        for step in range(1, 16):
            gate_message(step).wait_recv()
        for step in range(1, 16):
            gate_message(step).wait_send()

    sent[...] = jnp.zeros_like(sent)
    copies[0].wait()
    w_small.step(0)
    gdy[0].step(0)
    copies[1].wait()
    w_kv.step(0)
    w_small.step(1)
    gdy[1].step(0)
    copies[2].wait()
    w_q.step(0)
    gdy[0].step(1)
    gdy[0].step(2)
    w_small.step(2)
    w_kv.step(1)
    gdy[1].step(1)
    w_q.step(1)
    copies[3].wait()
    w_o.step(0)
    w_small.step(3)
    norm_tokens()
    w_kv.step(2)
    w_kv.step(3)
    project(1)
    gdy[1].step(2)
    query_gain = head_gain(small_t[...], 34)
    key_gain = head_gain(small_t[...], 35)
    copies[4].wait()
    cosine, sine = turn[:32], turn[32:]
    key_heads(0)
    kv[0].step(0)
    kv[0].step(1)
    both_biases()
    key_heads(1)
    w_q.step(2)
    gdy[0].step(3)
    w_o.step(1)
    kv[0].step(2)
    w_q.step(3)
    outs[0].start()
    project(0)
    outs[3].start()
    kv[1].step(0)
    w_o.step(2)
    gdy[1].step(3)
    query_heads(0)
    kv[0].step(3)
    attend(0, 0, 4)
    attend(0, 4, 8)
    w_o.step(3)
    outs[1].start()
    finish(0)
    x0_all[plane.z, plane.x] = ffn[0]
    gx.step(0)
    query_heads(1)
    kv[1].step(1)
    gx.step(1)
    kv[1].step(2)
    gdy[1].step(4)
    outs[5].start()
    gx.step(2)
    kv[1].step(3)
    outs[2].start()
    attend(1, 0, 4)
    gx.step(3)
    attend(1, 4, 8)
    finish(1)
    send_gates()
    gdy[0].step(4)
    outs[4].start()
    take_gates()
    gx.step(4)
    outs[6].start()
    for copy in outs:
        copy.wait()


def front(tok, cot, wq, wo, small, seg, routes_t, turn):
    vmem = pl.BlockSpec(memory_space=pltpu.VMEM)
    anywhere = pl.BlockSpec(memory_space=pl.ANY)
    return pl.pallas_call(
        front_kernel,
        out_shape=(
            jax.ShapeDtypeStruct((2, 4, 4, 128, 1024), BF),
            jax.ShapeDtypeStruct((4, 4, 128, 1024), BF),
            jax.ShapeDtypeStruct((2, 4, 2, 128, 1024), BF),
            jax.ShapeDtypeStruct((4, 2, 128, 1024), BF),
            jax.ShapeDtypeStruct((2, 4, 2, 8, 128, 128), BF),
            jax.ShapeDtypeStruct((2, 2048, 128), F32),
            jax.ShapeDtypeStruct((64, 1024), F32),
            jax.ShapeDtypeStruct((2, 1024, 128), BF),
            jax.ShapeDtypeStruct((2, 1024, 128), BF),
            jax.ShapeDtypeStruct((2, 8, 1, 256), F32),
            jax.ShapeDtypeStruct((2, 128, 1024), F32),
            jax.ShapeDtypeStruct((2, 128, 1024), BF),
            jax.ShapeDtypeStruct((2, 32, 128), F32),
            jax.ShapeDtypeStruct((16, 8, 128), F32),
        ),
        in_specs=[vmem, vmem, anywhere, anywhere, anywhere, vmem, vmem, anywhere],
        out_specs=(anywhere,) * 6 + (vmem,) * 8,
        scratch_shapes=[
            pltpu.VMEM((2, 4, 4, 128, 1024), BF),
            pltpu.VMEM((4, 4, 128, 1024), BF),
            pltpu.VMEM((2, 4, 2, 128, 1024), BF),
            pltpu.VMEM((4, 2, 128, 1024), BF),
            pltpu.VMEM((2, 4, 2, 8, 128, 128), BF),
            pltpu.VMEM((2, 2048, 128), F32),
            pltpu.VMEM((4, 2, 64, 128), BF),
            pltpu.VMEM((256, 1024), BF),
            pltpu.VMEM((2, 1024, 128), F32),
            pltpu.VMEM((64, 128), F32),
            pltpu.SemaphoreType.DMA((3, 2, 2, 8)),
            pltpu.SemaphoreType.DMA((6, 2, 8)),
            pltpu.VMEM((16, 8, 128), F32),
            pltpu.SemaphoreType.DMA((16,)),
            pltpu.SemaphoreType.DMA((16,)),
            pltpu.SemaphoreType.DMA((12,)),
        ],
        compiler_params=pltpu.CompilerParams(
            collective_id=0, has_side_effects=True, vmem_limit_bytes=56 * MIB
        ),
        cost_estimate=pl.CostEstimate(
            flops=5_000_000_000, bytes_accessed=30_000_000, transcendentals=5_000_000
        ),
    )(tok, cot, wq, wo, small, seg, routes_t, turn)


def moe_kernel(
    ffn_ref, x0_hbm, dy_hbm, g_all, wgu_hbm, wd_hbm,
    out_hbm, dx_ref, h_ref, dw_own,
    dw, x_all, dy_all, r1, r2, r3, r4, xs, ds, os, gc, act, a1, a2, ggu, ranks, hcol, hs,
    wgu, wd, ra, rb, rc, sems, column_sems, hsend, hrecv, free, local,
):
    plane, column = Plane(), Column()
    me, z, x = plane.me, plane.z, plane.x
    own = [
        pltpu.make_async_copy(ffn_ref.at[1], x_all.at[1, z, x], local.at[0]),
        pltpu.make_async_copy(x0_hbm, x_all.at[0], local.at[2]),
        pltpu.make_async_copy(dy_hbm.at[0], dy_all.at[0], local.at[3]),
        pltpu.make_async_copy(wgu_hbm, wgu, local.at[4]),
        pltpu.make_async_copy(wd_hbm, wd, local.at[5]),
        pltpu.make_async_copy(dy_hbm.at[1], dy_all.at[1], local.at[1]),
    ]
    outs = [pltpu.make_async_copy(x_all.at[mb], out_hbm.at[mb], local.at[6 + mb]) for mb in range(2)]
    for copy in own:
        copy.start()
    greet(plane.others() + column.neighbours())
    own[0].wait()

    def h_message(step):
        to = (me + step) % 16
        return pltpu.make_async_remote_copy(
            src_ref=hs.at[to], dst_ref=h_ref.at[me],
            send_sem=hsend.at[step], recv_sem=hrecv.at[step], device_id={"expert": to},
        )

    gx = Gather(plane, x_all.at[1], sems.at[0])

    def into(mb):
        def store(place, rows, total):
            dx_ref[mb, rows] = total

        return store

    sdx = [
        Scatter(plane, dy_all.at[mb], (r1, r2, r3, r4), sems.at[1 + mb], into(mb), free)
        for mb in range(2)
    ]

    def own_part(k):
        def store(r, total):
            dw_own[k, r] = total.astype(BF)

        return store

    dsum = [
        ColumnScatter(
            column, dw.at[k], (ra.at[k], rb.at[k], rc.at[k]), column_sems.at[k], 128, own_part(k)
        )
        for k in range(3)
    ]
    earlier = (
        lax.broadcasted_iota(jnp.int32, (128, 128), 0)
        < lax.broadcasted_iota(jnp.int32, (128, 128), 1)
    ).astype(F32).astype(BF)

    @pl.loop(0, 16)
    def _(s):
        named = g_all[s] > 0.0
        before = nn(named.astype(F32).astype(BF), earlier)
        ranks[s] = jnp.where(named, before, -1.0)

    slot_ids = lax.broadcasted_iota(jnp.int32, (SLOTS, 128), 0).astype(F32)

    def places(p, mb):
        ranked = [ranks[2 * p + k] for k in range(2)]
        return [
            [(slot_ids == ranked[k][2 * mb + e : 2 * mb + e + 1]).astype(F32) for k in range(2)]
            for e in range(2)
        ]

    def gated(p, mb, hot):
        gates = [g_all[2 * p + k] for k in range(2)]
        return [
            [hot[e][k] * gates[k][2 * mb + e : 2 * mb + e + 1] for k in range(2)] for e in range(2)
        ]

    def spread(hot):
        blank = jnp.zeros((SLOTS, 128), F32)
        rows = []
        for e in range(2):
            rows.append(jnp.concatenate([hot[e][0], blank], axis=1))
            rows.append(jnp.concatenate([blank, hot[e][1]], axis=1))
        return jnp.concatenate(rows, axis=0).astype(BF)

    def span(p):
        return pl.ds(pl.multiple_of(p * 2 * SLOTS, 32), 2 * SLOTS)

    def pair(p):
        return p // 2, pl.ds(2 * (p % 2), 2)

    def select(mb):
        @pl.loop(0, 8)
        def _(p):
            hot = places(p, mb)
            line, two = pair(p)
            rows = nn(spread(hot), x_all[mb, line, two].reshape(256, 1024)).astype(BF)
            drows = nn(spread(gated(p, mb, hot)), dy_all[mb, line, two].reshape(256, 1024)).astype(BF)
            for e in range(2):
                xs[e, span(p)] = rows[2 * SLOTS * e : 2 * SLOTS * (e + 1)]
                ds[e, span(p)] = drows[2 * SLOTS * e : 2 * SLOTS * (e + 1)]

    chunks = 16 * SLOTS // CHUNK

    def forward(e):
        @pl.loop(0, chunks)
        def _(c):
            r = pl.ds(pl.multiple_of(c * CHUNK, CHUNK), CHUNK)
            gu = nn(xs[e, r], wgu[e])
            g, u = gu[:, :512], gu[:, 512:]
            sig = 1.0 / (1.0 + jnp.exp(-g))
            silu = g * sig
            active = (silu * u).astype(BF)
            act[e, r] = active
            a1[e, r] = (u * sig * (1.0 + g * (1.0 - sig))).astype(BF)
            a2[e, r] = silu.astype(BF)
            o = nn(active, wd[e]).astype(BF)
            os[e, r] = o
            hcol[e, r] = jnp.sum(o.astype(F32) * ds[e, r].astype(F32), axis=-1, keepdims=True)

    def combine_out(mb):
        @pl.loop(0, 8)
        def _(p):
            hot = places(p, mb)
            line, two = pair(p)
            both = jnp.concatenate([os[0, span(p)], os[1, span(p)]], axis=0)
            got = tn(spread(gated(p, mb, hot)), both).astype(BF)
            x_all[mb, line, two] = got.reshape(2, 128, 1024)
            for e in range(2):
                column_of = hcol[e, span(p)]
                for k in range(2):
                    row = 2 * mb + e
                    part = hot[e][k] * column_of[SLOTS * k : SLOTS * (k + 1)]
                    hs[2 * p + k, row : row + 1] = jnp.sum(part, axis=0, keepdims=True)

    def add_part(mb, k, n, fresh):
        fresh = fresh.reshape(2, 128, 1024)
        if mb == 1:
            fresh += dw[k, n].astype(F32)
        dw[k, n] = fresh.astype(BF)

    def backward(mb, e):
        @pl.loop(0, chunks)
        def _(c):
            r = pl.ds(pl.multiple_of(c * CHUNK, CHUNK), CHUNK)
            ga = nt(ds[e, r], wd[e])
            grad = jnp.concatenate(
                [ga * a1[e, r].astype(F32), ga * a2[e, r].astype(F32)], axis=1
            ).astype(BF)
            ggu[r] = grad
            gc[e, r] = nt(grad, wgu[e]).astype(BF)

        @pl.loop(0, 4)
        def _(m):
            cols = pl.ds(pl.multiple_of(m * 256, 256), 256)
            add_part(mb, e, m, tn(xs[e, :, cols], ggu[...]))

        @pl.loop(0, 2)
        def _(m):
            cols = pl.ds(pl.multiple_of(m * 256, 256), 256)
            add_part(mb, 2, 2 * e + m, tn(act[e, :, cols], ds[e]))

    def combine_dx(mb):
        @pl.loop(0, 8)
        def _(p):
            line, two = pair(p)
            both = jnp.concatenate([gc[0, span(p)], gc[1, span(p)]], axis=0)
            got = tn(spread(places(p, mb)), both).astype(BF)
            dy_all[mb, line, two] = got.reshape(2, 128, 1024)

    gx.step(0)
    own[1].wait()
    own[2].wait()
    select(0)
    gx.step(1)
    own[3].wait()
    own[4].wait()
    forward(0)
    gx.step(2)
    forward(1)
    combine_out(0)
    outs[0].start()
    backward(0, 0)
    gx.step(3)
    backward(0, 1)
    combine_dx(0)
    sdx[0].step(0)
    gx.step(4)
    own[5].wait()
    select(1)
    forward(1)
    sdx[0].step(1)
    forward(0)
    backward(1, 0)
    dsum[0].step(0)
    sdx[0].step(2)
    backward(1, 1)
    sdx[0].step(3)
    dsum[1].step(0)
    dsum[2].step(0)
    dsum[0].step(1)
    combine_dx(1)
    sdx[0].step(4)
    sdx[0].give_credit()
    sdx[1].take_credit()
    sdx[1].step(0)
    dsum[2].step(1)
    combine_out(1)
    outs[1].start()
    dsum[1].step(1)
    sdx[1].step(1)
    dsum[0].step(2)
    dsum[1].step(2)
    dsum[2].step(2)
    sdx[1].step(2)
    h_ref[me] = hs[me]
    for step in range(1, 16):
        h_message(step).start()
    sdx[1].step(3)
    dsum[0].step(3)
    dsum[2].step(3)
    dsum[1].step(3)
    sdx[1].step(4)
    for step in range(1, 16):
        h_message(step).wait_recv()
    for step in range(1, 16):
        h_message(step).wait_send()
    for copy in outs:
        copy.wait()


def moe(ffn, x0, dy, gates, w_gate_up, w_down):
    vmem = pl.BlockSpec(memory_space=pltpu.VMEM)
    anywhere = pl.BlockSpec(memory_space=pl.ANY)
    rows = 16 * SLOTS
    return pl.pallas_call(
        moe_kernel,
        out_shape=(
            jax.ShapeDtypeStruct((2, 4, 4, 128, 1024), BF),
            jax.ShapeDtypeStruct((2, 128, 1024), F32),
            jax.ShapeDtypeStruct((16, 8, 128), F32),
            jax.ShapeDtypeStruct((3, 128, 1024), BF),
        ),
        in_specs=[anywhere, anywhere, anywhere, vmem, anywhere, anywhere],
        out_specs=(anywhere,) + (vmem,) * 3,
        scratch_shapes=[
            pltpu.VMEM((3, 4, 2, 128, 1024), BF),
            pltpu.VMEM((2, 4, 4, 128, 1024), BF),
            pltpu.VMEM((2, 4, 4, 128, 1024), BF),
            *scatter_slots(128, 1024),
            pltpu.VMEM((2, rows, 1024), BF),
            pltpu.VMEM((2, rows, 1024), BF),
            pltpu.VMEM((2, rows, 1024), BF),
            pltpu.VMEM((2, rows, 1024), BF),
            pltpu.VMEM((2, rows, 512), BF),
            pltpu.VMEM((2, rows, 512), BF),
            pltpu.VMEM((2, rows, 512), BF),
            pltpu.VMEM((rows, 1024), BF),
            pltpu.VMEM((16, 8, 128), F32),
            pltpu.VMEM((2, rows, 1), F32),
            pltpu.VMEM((16, 8, 128), F32),
            pltpu.VMEM((2, 1024, 1024), BF),
            pltpu.VMEM((2, 512, 1024), BF),
            *column_slots((128, 1024), lead=(3,)),
            pltpu.SemaphoreType.DMA((3, 2, 2, 8)),
            pltpu.SemaphoreType.DMA((3, 2, 8)),
            pltpu.SemaphoreType.DMA((16,)),
            pltpu.SemaphoreType.DMA((16,)),
            pltpu.SemaphoreType.REGULAR,
            pltpu.SemaphoreType.DMA((8,)),
        ],
        compiler_params=pltpu.CompilerParams(
            collective_id=1, has_side_effects=True, vmem_limit_bytes=63 * MIB
        ),
        cost_estimate=pl.CostEstimate(
            flops=30_000_000_000, bytes_accessed=30_000_000, transcendentals=2_000_000
        ),
    )(ffn, x0, dy, gates, w_gate_up, w_down)


def norm_grad(grad, v, inverse, gain, axis):
    scaled = grad * gain
    moment = jnp.mean(scaled * v, axis=axis, keepdims=True)
    return inverse * (scaled - v * (inverse * inverse * moment)), grad * (v * inverse)


def back_kernel(
    tok, cot, seg_ref, turn_hbm, wq_hbm, wo_hbm, small_t, raw_hbm, q_t, kv_hbm, mix_t, lsum,
    res, ffn, gates_t, share_ref, dx, out_hbm, dw_own,
    dgu_all, dd_all, output, in_grad, gq, go, gs,
    wq_all, wo_all, kv_all, raw_t, turn, bias, gres, branch, gm_t, dq_t, own_kv, gp, normed_t, gn,
    part_kv, part_w, part_s, q_sum, k_sum, ra, rb, rc, sa, sb, sc, plane_buf, plane_all, p1, p2, p3, p4, ta, tb, tc,
    logits, routers, router_sum, out_part, r1, r2, r3, r4, parcels, got_parcels, small_own, kv_total,
    column_sems, plane_sems, far_send, far_recv, all_send, all_recv, free, local, gain_sums,
):
    plane, column = Plane(), Column()
    y, c = column.y, column.c
    copies = [
        pltpu.make_async_copy(wo_hbm, wo_all, local.at[0]),
        pltpu.make_async_copy(kv_hbm, kv_all, local.at[1]),
        pltpu.make_async_copy(raw_hbm, raw_t, local.at[2]),
        pltpu.make_async_copy(wq_hbm, wq_all, local.at[3]),
        pltpu.make_async_copy(turn_hbm.at[column.me], turn, local.at[4]),
    ]
    parts = [pltpu.make_async_copy(out_hbm.at[mb], out_part, local.at[5 + mb]) for mb in range(2)]
    dw_refs = [dgu_all.at[0], dgu_all.at[1], dd_all]
    owns = [pltpu.make_async_copy(dw_own.at[n], dw_refs[n].at[y, c], local.at[7 + n]) for n in range(3)]
    for copy in parts[:1] + owns + copies:
        copy.start()
    greet(plane.others() + column.neighbours())
    dall = [ColumnGather(column, dw_refs[n], column_sems.at[8 + n], 128, dw_own.at[n]) for n in range(3)]

    def add_residual(mb):
        def store(place, rows, total):
            output[mb, rows] = (res[mb, rows] + total).astype(BF)

        return store

    sout = [
        Scatter(plane, out_part, (r1, r2, r3, r4), plane_sems.at[mb], add_residual(mb), free)
        for mb in range(2)
    ]
    part_s[...] = jnp.zeros_like(part_s)
    q_sum[...] = jnp.zeros_like(q_sum)
    k_sum[...] = jnp.zeros_like(k_sum)
    for mb in range(2):
        document_bias(seg_ref, bias, mb, column.me)

    def place_w(which):
        def store(r, total):
            low = total.astype(BF)
            half = r.start // 64
            some = pl.ds(pl.multiple_of(r.start % 64, 16), 16)
            for k in range(8):
                n = half * 8 + k
                piece = low[:, 128 * k : 128 * (k + 1)]
                if which == 2:
                    parcels[n, some] = piece
                else:
                    plane_buf[n // 4, n % 4, some, 128 * which : 128 * (which + 1)] = piece

        return store

    def place_s(r, total):
        small_own[r] = total.astype(BF)

    def place_kv(mb, half):
        def store(r, total):
            own_kv[mb, pl.ds(r.start + 4 * half, 1)] = total

        return store

    w_sums = [
        ColumnScatter(
            column, part_w.at[n], (ra.at[n], rb.at[n], rc.at[n]), column_sems.at[n], 128, place_w(n)
        )
        for n in range(3)
    ]
    kv_sums = [
        [
            ColumnScatter(
                column, part_kv.at[mb, half],
                (sa.at[mb, half], sb.at[mb, half], sc.at[mb, half]),
                column_sems.at[4 + 2 * mb + half], 4, place_kv(mb, half), group=1,
            )
            for half in range(2)
        ]
        for mb in range(2)
    ]
    s_sum = ColumnScatter(column, part_s, (ta, tb, tc), column_sems.at[3], 64, place_s)

    def keep(place, rows, total):
        plane_all[place] = total.astype(BF)

    over = Scatter(plane, plane_buf, (p1, p2, p3, p4), plane_sems.at[2], keep, height=64)
    spread = Gather(plane, plane_all, plane_sems.at[3], height=64)

    def tokens_of(mb):
        return pl.ds(128 * mb, 128)

    router = small_t[:32].astype(BF)
    ffn_gain, attn_gain = small_t[33:34], small_t[32:33]
    routers[0:32] = router
    routers[32:64] = router
    def router_and_norm():
        ffn_gain_grad = jnp.zeros((1, 1024), F32)
        for mb in range(2):
            share = jnp.concatenate([share_ref[k, 2 * mb : 2 * mb + 2] for k in range(16)], axis=0)
            logit = share - gates_t[mb] * jnp.sum(share, axis=0, keepdims=True)
            high = logit.astype(BF)
            logits[0:32, tokens_of(mb)] = high
            logits[32:64, tokens_of(mb)] = (logit - high.astype(F32)).astype(BF)

        @pl.loop(0, 4)
        def _(n):
            cols = pl.ds(pl.multiple_of(n * 256, 256), 256)
            gn[:, cols] = tn(logits[...], routers[:, cols])
            router_sum[:, cols] = nn(logits[...], ffn[:, :, cols].reshape(256, 256))

        for mb in range(2):
            into = dx[mb] + gn[tokens_of(mb)]
            v = res[mb]
            inv = inverse_rms(v, 1)
            grad, gain = norm_grad(into, v, inv, ffn_gain, 1)
            ffn_gain_grad += jnp.sum(gain, axis=0, keepdims=True)
            total = cot[mb].astype(F32) + grad
            gres[mb] = total
            branch[128 * mb : 128 * (mb + 1)] = total.astype(BF)
        gain_sums[1:2] = ffn_gain_grad

    def out_projection():
        copies[0].wait()

        @pl.loop(0, 4)
        def _(n):
            rows = pl.ds(pl.multiple_of(n * 256, 256), 256)
            got = nt(wo_all[n].reshape(256, 1024), branch[...])
            gm_t[0, rows] = got[:, :128].astype(BF)
            gm_t[1, rows] = got[:, 128:].astype(BF)
            mixed = jnp.concatenate([mix_t[0, rows], mix_t[1, rows]], axis=1)
            part_w[0, n] = nn(mixed, branch[...]).astype(BF).reshape(2, 128, 1024)

    def attend(mb, start, stop):
        @pl.loop(start, stop)
        def _(g):
            query = pair_columns(q_t, mb, g)
            grad = pair_columns(gm_t, mb, g)
            mixed = pair_columns(mix_t, mb, g)
            blank = jnp.zeros_like(query)
            inner = jnp.sum(grad.astype(F32) * mixed.astype(F32), axis=0, keepdims=True)
            query = jnp.concatenate([query, blank], axis=0)
            grad = jnp.concatenate([blank, grad], axis=0)
            both = jnp.concatenate([query, grad], axis=1)
            scale = 1.0 / lsum[mb, g]
            dq = jnp.zeros((128, 256), F32)
            for j in range(4):
                keys = kv_all[mb, j, :, g].reshape(256, 128)
                there = bias[mb, 256 * j : 256 * (j + 1)].astype(F32)
                got = nn(keys, both)
                p = jnp.exp(got[:, :256] + jnp.concatenate([there, there], axis=1)) * scale
                ds = (p * (got[:, 256:] - inner)).astype(BF)
                dq += tn(keys, ds)
                dkv = nt(jnp.concatenate([ds, p.astype(BF)], axis=1), both)
                part_kv[mb, g // 4, j, :, g % 4] = dkv.astype(BF).reshape(2, 128, 128)
            dq = dq[:64] * HD ** (-0.5)
            rows = pl.ds(pl.multiple_of(g * 128, 128), 128)
            dq_t[mb, rows] = jnp.concatenate([dq[:, :128], dq[:, 128:]], axis=0)

    copies[4].wait()
    cosine, sine = turn[:32], turn[32:]
    query_gain = head_gain(small_t[...], 34)
    key_gain = head_gain(small_t[...], 35)

    def head_back(grad, v, gain, total):
        inv = inverse_rms(v, 0)
        grad = turned(grad, cosine, -sine)
        grad_v, gain_part = norm_grad(grad, v, inv, gain, 0)
        total[...] += gain_part
        return grad_v

    def queries_back(mb):
        @pl.loop(0, 8)
        def _(g):
            pieces = []
            for r in range(2):
                rows = pl.ds(pl.multiple_of(g * 128 + r * 64, 64), 64)
                pieces.append(head_back(dq_t[mb, rows], raw_t[mb, rows], query_gain, q_sum))
            cols = pl.ds(pl.multiple_of(g * 128, 128), 128)
            gp[tokens_of(mb), cols] = jnp.concatenate(pieces, axis=0).T.astype(BF)

    def turn_normed():
        for mb in range(2):
            v = tok[mb].astype(F32)
            normed = (v * inverse_rms(v, 1) * attn_gain).astype(BF).astype(F32)
            for k in range(8):
                normed_t[128 * k : 128 * (k + 1), tokens_of(mb)] = (
                    normed[:, 128 * k : 128 * (k + 1)].T.astype(BF)
                )

    def weight_part(which):
        cols = pl.ds(1024 * (which - 1), 1024)

        @pl.loop(0, 4)
        def _(n):
            rows = pl.ds(pl.multiple_of(n * 256, 256), 256)
            part_w[which, n] = nn(normed_t[rows], gp[:, cols]).astype(BF).reshape(2, 128, 1024)

    def keys_back(mb):
        @pl.loop(0, 4)
        def _(k):
            keys, values = [], []
            for r in range(2):
                g = 2 * k + r
                grad = own_kv[mb, g].T
                rows = pl.ds(pl.multiple_of(1024 + g * 64, 64), 64)
                keys.append(head_back(grad[:64], raw_t[mb, rows], key_gain, k_sum))
                values.append(grad[64:])
            cols = pl.ds(pl.multiple_of(1024 + k * 128, 128), 128)
            gp[tokens_of(mb), cols] = jnp.concatenate(keys, axis=0).T.astype(BF)
            cols = pl.ds(pl.multiple_of(1536 + k * 128, 128), 128)
            gp[tokens_of(mb), cols] = jnp.concatenate(values, axis=0).T.astype(BF)

    def normed_grad(k):
        @pl.loop(0, 4)
        def _(n):
            cols = pl.ds(pl.multiple_of(n * 256, 256), 256)
            got = nt(gp[:, 1024 * k : 1024 * (k + 1)], wq_all[k, n].reshape(256, 1024))
            gn[:, cols] = got if k == 0 else gn[:, cols] + got

    def finish():
        attn_gain_grad = jnp.zeros((1, 1024), F32)
        for mb in range(2):
            v = tok[mb].astype(F32)
            grad, gain = norm_grad(gn[tokens_of(mb)], v, inverse_rms(v, 1), attn_gain, 1)
            attn_gain_grad += jnp.sum(gain, axis=0, keepdims=True)
            in_grad[mb] = (gres[mb] + grad).astype(BF)
        for b in range(8):
            cols = slice(128 * b, 128 * (b + 1))
            heads = slice(8 * b, 8 * (b + 1))
            part_s[b // 2, b % 2, 0:32] = router_sum[0:32, cols] + router_sum[32:64, cols]
            part_s[b // 2, b % 2, 32:33] = attn_gain_grad[:, cols]
            part_s[b // 2, b % 2, 33:34] = gain_sums[1:2, cols]
            part_s[b // 2, b % 2, 40:48] = jnp.broadcast_to(
                jnp.sum(q_sum[heads], axis=1, keepdims=True), (8, 128)
            )
            part_s[b // 2, b % 2, 48:56] = jnp.broadcast_to(
                jnp.sum(k_sum[heads], axis=1, keepdims=True), (8, 128)
            )

    me = plane.me

    def parcel(step):
        to = (me + step) % 16
        return send(
            parcels.at[to], got_parcels.at[me], far_send.at[step], far_recv.at[step], {"expert": to}
        )

    def total_message(step):
        to = (me + step) % 16
        return send(
            kv_total.at[me], kv_total.at[me], all_send.at[step], all_recv.at[step], {"expert": to}
        )

    def send_parcels():
        @pl.loop(0, 16)
        def _(n):
            parcels[n, 64:128] = small_own[...]

        for step in range(1, 16):
            parcel(step).start()
        got_parcels[me] = parcels[me]

    def add_parcels():
        for step in range(1, 16):
            parcel(step).wait_recv()
        total = got_parcels[0].astype(F32)
        for n in range(1, 16):
            total += got_parcels[n].astype(F32)
        kv_total[me] = total[:64].astype(BF)
        for step in range(1, 16):
            total_message(step).start()
        gs[...] = total[64:]

    def write_out(k):
        for n in range(16):
            rows = slice(64 * (n // 8), 64 * (n // 8) + 64)
            cols = slice(128 * (n % 8), 128 * (n % 8) + 128)
            (go, gq)[k][rows, cols] = plane_all[n // 4, n % 4, :, 128 * k : 128 * (k + 1)].astype(F32)

    def take_totals():
        for step in range(1, 16):
            total_message(step).wait_recv()
        for n in range(16):
            first = 1024 + 128 * (n % 8)
            gq[64 * (n // 8) : 64 * (n // 8) + 64, first : first + 128] = kv_total[n].astype(F32)

    dall[2].step(0)
    router_and_norm()
    parts[0].wait()
    sout[0].step(0)
    dall[0].step(0)
    out_projection()
    dall[1].step(0)
    copies[1].wait()
    attend(1, 0, 2)
    attend(1, 2, 4)
    attend(0, 0, 2)
    kv_sums[1][0].step(0)
    w_sums[0].step(0)
    sout[0].step(1)
    attend(1, 4, 6)
    attend(1, 6, 8)
    dall[0].step(1)
    kv_sums[1][0].step(1)
    kv_sums[1][1].step(0)
    attend(0, 2, 4)
    w_sums[0].step(1)
    attend(0, 4, 6)
    dall[2].step(1)
    kv_sums[1][1].step(1)
    sout[0].step(2)
    w_sums[0].step(2)
    attend(0, 6, 8)
    sout[0].step(3)
    kv_sums[0][1].step(0)
    kv_sums[0][0].step(0)
    kv_sums[1][1].step(2)
    turn_normed()
    copies[2].wait()
    queries_back(1)
    queries_back(0)
    kv_sums[1][0].step(2)
    kv_sums[0][1].step(1)
    weight_part(1)
    copies[3].wait()
    normed_grad(0)
    sout[0].step(4)
    parts[1].start()
    sout[0].give_credit()
    w_sums[1].step(0)
    kv_sums[0][0].step(1)
    kv_sums[0][1].step(2)
    parts[1].wait()
    sout[1].take_credit()
    sout[1].step(0)
    dall[0].step(2)
    w_sums[1].step(1)
    kv_sums[1][1].step(3)
    kv_sums[0][1].step(3)
    kv_sums[0][0].step(2)
    w_sums[1].step(2)
    sout[1].step(1)
    kv_sums[0][0].step(3)
    kv_sums[1][0].step(3)
    keys_back(0)
    dall[2].step(2)
    keys_back(1)
    dall[1].step(1)
    weight_part(2)
    w_sums[2].step(0)
    w_sums[0].step(3)
    normed_grad(1)
    w_sums[1].step(3)
    over.step(0)
    finish()
    dall[0].step(3)
    dall[1].step(2)
    s_sum.step(0)
    w_sums[2].step(1)
    over.step(1)
    dall[2].step(3)
    sout[1].step(2)
    s_sum.step(1)
    w_sums[2].step(2)
    over.step(2)
    over.step(3)
    s_sum.step(2)
    sout[1].step(3)
    dall[1].step(3)
    over.step(4)
    s_sum.step(3)
    spread.step(0)
    w_sums[2].step(3)
    send_parcels()
    spread.step(1)
    spread.step(2)
    sout[1].step(4)
    add_parcels()
    spread.step(3)
    spread.step(4)
    write_out(0)
    write_out(1)
    take_totals()
    for step in range(1, 16):
        parcel(step).wait_send()
        total_message(step).wait_send()
    for copy in owns:
        copy.wait()


def back(tok, cot, seg, turn, wq_all, wo_all, small_t, raw_t, q_t, kv_all, mix_t, lsum, res, ffn, gates_t, share, dx, out_part, dw_own):
    vmem = pl.BlockSpec(memory_space=pltpu.VMEM)
    anywhere = pl.BlockSpec(memory_space=pl.ANY)
    kv_slots = column_slots((4, 128, 128), lead=(2, 2))
    return pl.pallas_call(
        back_kernel,
        out_shape=(
            jax.ShapeDtypeStruct((2, 4, 2, 128, 1024), BF),
            jax.ShapeDtypeStruct((4, 2, 128, 1024), BF),
            jax.ShapeDtypeStruct((2, 128, 1024), BF),
            jax.ShapeDtypeStruct((2, 128, 1024), BF),
            jax.ShapeDtypeStruct((128, 2048), F32),
            jax.ShapeDtypeStruct((128, 1024), F32),
            jax.ShapeDtypeStruct((64, 128), F32),
        ),
        in_specs=[
            vmem, vmem, vmem, anywhere, anywhere, anywhere, vmem, anywhere, vmem, anywhere,
            vmem, vmem, vmem, vmem, vmem, vmem, vmem, anywhere, vmem,
        ],
        out_specs=(anywhere,) * 2 + (vmem,) * 5,
        scratch_shapes=[
            pltpu.VMEM((2, 4, 2, 128, 1024), BF),
            pltpu.VMEM((4, 2, 128, 1024), BF),
            pltpu.VMEM((2, 4, 2, 8, 128, 128), BF),
            pltpu.VMEM((2, 2048, 128), F32),
            pltpu.VMEM((64, 128), F32),
            pltpu.VMEM((2, 1024, 128), BF),
            pltpu.VMEM((2, 128, 1024), F32),
            pltpu.VMEM((256, 1024), BF),
            pltpu.VMEM((2, 1024, 128), BF),
            pltpu.VMEM((2, 1024, 128), F32),
            pltpu.VMEM((2, 8, 128, 128), F32),
            pltpu.VMEM((256, 2048), BF),
            pltpu.VMEM((1024, 256), BF),
            pltpu.VMEM((256, 1024), F32),
            pltpu.VMEM((2, 2, 4, 2, 4, 128, 128), BF),
            pltpu.VMEM((3, 4, 2, 128, 1024), BF),
            pltpu.VMEM((4, 2, 64, 128), F32),
            pltpu.VMEM((64, 128), F32),
            pltpu.VMEM((64, 128), F32),
            *column_slots((128, 1024), lead=(3,)),
            *kv_slots,
            pltpu.VMEM((4, 4, 64, 256), BF),
            pltpu.VMEM((4, 4, 64, 256), BF),
            *scatter_slots(64, 256),
            *column_slots((64, 128), F32),
            pltpu.VMEM((64, 256), BF),
            pltpu.VMEM((64, 1024), BF),
            pltpu.VMEM((64, 1024), F32),
            pltpu.VMEM((4, 4, 128, 1024), BF),
            *scatter_slots(128, 1024),
            pltpu.VMEM((16, 128, 128), BF),
            pltpu.VMEM((16, 128, 128), BF),
            pltpu.VMEM((64, 128), BF),
            pltpu.VMEM((16, 64, 128), BF),
            pltpu.SemaphoreType.DMA((11, 2, 8)),
            pltpu.SemaphoreType.DMA((4, 2, 2, 8)),
            pltpu.SemaphoreType.DMA((16,)),
            pltpu.SemaphoreType.DMA((16,)),
            pltpu.SemaphoreType.DMA((16,)),
            pltpu.SemaphoreType.DMA((16,)),
            pltpu.SemaphoreType.REGULAR,
            pltpu.SemaphoreType.DMA((10,)),
            pltpu.VMEM((8, 1024), F32),
        ],
        compiler_params=pltpu.CompilerParams(
            collective_id=2, has_side_effects=True, vmem_limit_bytes=63 * MIB
        ),
        cost_estimate=pl.CostEstimate(
            flops=12_000_000_000, bytes_accessed=30_000_000, transcendentals=5_000_000
        ),
    )(tok, cot, seg, turn, wq_all, wo_all, small_t, raw_t, q_t, kv_all, mix_t, lsum, res, ffn, gates_t, share, dx, out_part, dw_own)


def last_kernel(
    dgu_ref, dd_ref, out_ref, in_ref, gq_ref, go_ref, gs_ref,
    dgu_f, dd_f, out_f, in_f, gq_f, go_f, attn_f, ffn_f, q_f, k_f, router_f,
):
    dgu_f[...] = dgu_ref[...].astype(F32)
    dd_f[...] = dd_ref[...].astype(F32)
    out_f[...] = out_ref[...]
    in_f[...] = in_ref[...]
    gq_f[...] = gq_ref[...]
    go_f[...] = go_ref[...]
    attn_f[...] = gs_ref[32:33]
    ffn_f[...] = gs_ref[33:34]
    q_f[...] = gs_ref[40:48].T[0:1]
    k_f[...] = gs_ref[48:56].T[0:1]
    router_f[...] = gs_ref[0:32]


def last(dgu, dd, output, in_grad, gq, go, gs):
    def rows(count, width):
        return pl.BlockSpec((count, width), lambda n: (n, 0))

    def whole(*shape):
        return pl.BlockSpec(shape, lambda n: (0, 0))

    return pl.pallas_call(
        last_kernel,
        grid=(4,),
        out_shape=(
            jax.ShapeDtypeStruct((2048, 1024), F32),
            jax.ShapeDtypeStruct((1024, 1024), F32),
            jax.ShapeDtypeStruct((256, 1024), BF),
            jax.ShapeDtypeStruct((256, 1024), BF),
            jax.ShapeDtypeStruct((128, 2048), F32),
            jax.ShapeDtypeStruct((128, 1024), F32),
            jax.ShapeDtypeStruct((1, 128), F32),
            jax.ShapeDtypeStruct((1, 128), F32),
            jax.ShapeDtypeStruct((1, 8), F32),
            jax.ShapeDtypeStruct((1, 8), F32),
            jax.ShapeDtypeStruct((32, 128), F32),
        ),
        in_specs=[
            rows(512, 1024), rows(256, 1024), rows(64, 1024), rows(64, 1024), rows(32, 2048),
            rows(32, 1024), whole(64, 128),
        ],
        out_specs=(
            rows(512, 1024), rows(256, 1024), rows(64, 1024), rows(64, 1024), rows(32, 2048),
            rows(32, 1024), whole(1, 128), whole(1, 128), whole(1, 8), whole(1, 8), whole(32, 128),
        ),
        compiler_params=pltpu.CompilerParams(vmem_limit_bytes=40 * MIB),
        cost_estimate=pl.CostEstimate(flops=0, bytes_accessed=24_000_000, transcendentals=0),
    )(
        dgu.reshape(2048, 1024), dd.reshape(1024, 1024), output.reshape(256, 1024),
        in_grad.reshape(256, 1024), gq, go, gs,
    )


def turn_table(length):
    frequency = np.power(np.float32(THETA), -2.0 * np.arange(HD // 2, dtype=np.float32) / HD)
    angle = np.arange(length, dtype=np.float32)[:, None] * frequency.astype(np.float32)[None, :]
    both = np.concatenate([np.cos(angle), np.sin(angle)], axis=1).astype(np.float32)
    return both.reshape(length // 128, 128, HD).transpose(0, 2, 1)


def body(
    tokens,
    cotangent,
    segments,
    routes,
    w_qkv,
    w_out,
    attn_norm,
    ffn_norm,
    q_gain,
    k_gain,
    router,
    w_gate_up,
    w_down,
):
    tok = tokens.reshape(2, 128, 1024)
    cot = cotangent.reshape(2, 128, 1024)
    seg = segments.reshape(2, 8, 1, 128)
    routes_t = routes.reshape(2, 128, 8).transpose(0, 2, 1)
    turn = jnp.asarray(turn_table(1024))
    gains = jnp.pad(jnp.stack([q_gain, k_gain]), ((0, 28), (0, 120)))
    small = jnp.concatenate([router.T, attn_norm[None], ffn_norm[None], gains])
    (
        dy_all, x0, wq_all, wo_all, kv_all, raw_t, small_t, q_t, mix_t, lsum, res, ffn, gates_t, sent
    ) = front(tok, cot, w_qkv, w_out, small, seg, routes_t, turn)
    out_part, moved_dx, share, dw_own = moe(ffn, x0, dy_all, sent, w_gate_up, w_down)
    dgu, dd, output, in_grad, gq, go, gs = back(
        tok, cot, seg, turn, wq_all, wo_all, small_t, raw_t, q_t, kv_all, mix_t, lsum, res, ffn,
        gates_t, share, moved_dx, out_part, dw_own,
    )
    dgu, dd, output, in_grad, gq, go, attn, ffn_gain, q_grad, k_grad, router_grad = last(
        dgu, dd, output, in_grad, gq, go, gs
    )
    return (
        output.reshape(tokens.shape),
        in_grad.reshape(tokens.shape),
        gq,
        go,
        attn.reshape(128),
        ffn_gain.reshape(128),
        q_grad.reshape(8),
        k_grad.reshape(8),
        router_grad.T,
        dgu.reshape(2, 1024, 1024),
        dd.reshape(2, 512, 1024),
    )


def solution(mesh):
    return jax.shard_map(
        body,
        mesh=mesh,
        in_specs=(
            P(None, "expert", "dp", None),
            P(None, "expert", "dp", None),
            P(None, "expert", None),
            P(None, "expert", "dp", None),
            P("dp", None),
            P("dp", None),
            P("dp"),
            P("dp"),
            P("dp"),
            P("dp"),
            P("dp", None),
            P("expert", None, None),
            P("expert", None, None),
        ),
        out_specs=(
            P(None, "expert", "dp", None),
            P(None, "expert", "dp", None),
            P("dp", None),
            P("dp", None),
            P("dp"),
            P("dp"),
            P("dp"),
            P("dp"),
            P("dp", None),
            P("expert", None, None),
            P("expert", None, None),
        ),
        check_vma=False,
    )
```
